32 devices in a mesh: section: 2 (over core), dp: 16 (over z, y, x).
Axes of the slice: x: 2, y: 2, z: 4, core: 2. Of those that a mesh axis runs over, the one named last changes fastest.
Arguments:
- clips_in: bfloat16 [32, 8, 14, 14, 528], P('dp')
- frames: int32 [32], P('dp'), may hold values from 2 to 8
- voxel_mask: int32 [32, 8, 14, 14], P('dp'), may hold values from 0 to 1, as said below
- micro_order: int32 [16, 2], P('dp'), may hold values from 0 to 1, each once within a row
- inproj_4f: bfloat16 [528, 576], replicated, may hold values from -0.25 to 0.25
- conv_mid_4f: bfloat16 [27, 160, 320], replicated, may hold values from -0.09375 to 0.09375
- conv_small_4f: bfloat16 [27, 32, 128], replicated, may hold values from -0.21875 to 0.21875
- gain_4f: float32 [1024], replicated, may hold values from 0.25 to 1.75
- bias_4f: float32 [1024], replicated, may hold values from -2.5 to 2.5
- inproj_5b: bfloat16 [832, 576], replicated, may hold values from -0.21875 to 0.21875
- conv_mid_5b: bfloat16 [27, 160, 320], replicated, may hold values from -0.09375 to 0.09375
- conv_small_5b: bfloat16 [27, 32, 128], replicated, may hold values from -0.21875 to 0.21875
- gain_5b: float32 [1024], replicated, may hold values from 0.25 to 1.75
- bias_5b: float32 [1024], replicated, may hold values from -2.5 to 2.5
- cotangent: bfloat16 [32, 4, 7, 7, 832], P('dp'), may hold values from -6 to 6
Outputs:
- block_out: bfloat16 [32, 4, 7, 7, 832], P('dp', 'section')
- clips_grad: bfloat16 [32, 8, 14, 14, 528], P('dp', 'section')
- inproj_4f_grad: float32 [528, 576], replicated
- conv_mid_4f_grad: float32 [27, 160, 320], replicated
- conv_small_4f_grad: float32 [27, 32, 128], replicated
- norm_4f_grad: float32 [2, 1024], replicated
- moments_4f: float32 [2, 2, 1024], replicated
- inproj_5b_grad: float32 [832, 576], replicated
- conv_mid_5b_grad: float32 [27, 160, 320], replicated
- conv_small_5b_grad: float32 [27, 32, 128], replicated
- norm_5b_grad: float32 [2, 1024], replicated
- moments_5b: float32 [2, 2, 1024], replicated
The draws below stay inside these ranges and needn't reach their ends.
Inputs may be any that keep to these rules, and one draw needn't show every extreme that they name: `voxel_mask`: in every frame of every clip the voxel at height 0 and width 0 is valid. `micro_order`: each dp index's row orders its 2 clips; micro-batch m takes entries m * 1 to (m + 1) - 1.
All inputs are finite; a program needn't handle non-finite values.
Results may differ from the reference program's by a relative error of at most 0.015.
Values may be sent and summed in bfloat16 or wider, within the bound.
No kernel may reach another device: no remote copies, remote signals or barrier semaphores. Data moves between devices by JAX's collectives and lax.ppermute only.
A program may use at most 448 MiB of HBM per device.

```python
import jax
import jax.numpy as jnp
from jax import lax

C4 = 528
B0 = 256
B1A = 160
B1 = 320
B2A = 32
B2 = 128
C5 = 832
NX = 448
NB1 = 576
NB = 1024
T0 = 8
H0 = 14
T1 = 4
H1 = 7
MICRO = 2
CMB = 1
CLIPS_DEV = 2
CLIPS = 32
N_DP = 16


def draw_clips_in(key, part):
    first_key = jax.random.fold_in(key, 0)
    shape = (CLIPS, T0, H0, H0, C4)
    ramp = 1.0 + 2.0 * jnp.arange(CLIPS, dtype=jnp.float32) / max(CLIPS - 1, 1)
    ramp = ramp.reshape(CLIPS, 1, 1, 1, 1)
    return (jax.random.uniform(first_key, shape, jnp.float32, 0.0, 2.0) * ramp).astype(jnp.bfloat16)


def draw_voxel_mask(key, part):
    shape = (CLIPS, T0, H0, H0)
    coin = jax.random.randint(key, shape, 0, 8)
    corner = jnp.arange(H0)[:, None] + jnp.arange(H0)[None, :] == 0
    return jnp.where((coin > 0) | corner[None, None], 1, 0).astype(jnp.int32)


def with_ends(entries, own_key, smallest, top_value):
    shape = entries.shape
    place = [jax.random.randint(jax.random.fold_in(own_key, axis), (), 0, shape[axis]) for axis in range(len(shape))]
    entries = entries.at[tuple(place)].set(smallest)
    longest = shape.index(max(shape))
    place[longest] = (place[longest] + 1) % shape[longest]
    return entries.at[tuple(place)].set(top_value)


def level_of(stream_key, dims, shards, smallest, top_value):
    factor_of, own = 1.0, jax.random.fold_in(stream_key, 6)
    for position, shards_of in shards:
        draws = jnp.exp(jax.random.uniform(jax.random.fold_in(own, position), (shards_of,), jnp.float32, smallest / len(shards), top_value / len(shards)))
        factor_of = factor_of * jnp.repeat(draws, dims[position] // shards_of).reshape([-1 if axis == position else 1 for axis in range(len(dims))])
    return factor_of


def scatter_about(key, dims, scale, bound, cuts=(), held_as=jnp.bfloat16):
    values = scale * jax.random.normal(key, dims, jnp.float32)
    if cuts:
        values = values * level_of(key, dims, cuts, -0.22, 0.18)
    return jnp.clip(values, -bound, bound).astype(held_as)


def setup_inputs(seed: int = 0) -> dict:
    splits = jax.random.split(jax.random.key(seed), 16)
    return {
        "clips_in": draw_clips_in(jax.random.fold_in(splits[15], 71), 0),
        "frames": with_ends(jax.random.randint(splits[1], (CLIPS,), 2, T0 + 1), jax.random.fold_in(splits[1], 1), 2, T0).astype(jnp.int32),
        "voxel_mask": draw_voxel_mask(jax.random.fold_in(splits[15], 71), 0),
        "micro_order": jax.vmap(lambda own: jax.random.permutation(own, CLIPS_DEV))(jax.random.split(splits[3], N_DP)).reshape((N_DP, CLIPS_DEV)).astype(jnp.int32),
        "inproj_4f": scatter_about(splits[4], (C4, NB1), C4 ** -0.5, 0.25),
        "conv_mid_4f": scatter_about(splits[5], (27, B1A, B1), (27 * B1A) ** -0.5, 0.09375),
        "conv_small_4f": scatter_about(splits[6], (27, B2A, B2), (27 * B2A) ** -0.5, 0.21875),
        "gain_4f": jnp.clip(1.0 + 0.15 * jax.random.normal(splits[7], (NB,), jnp.float32), 0.25, 1.75),
        "bias_4f": scatter_about(splits[8], (NB,), 0.5, 2.5, (), jnp.float32),
        "inproj_5b": scatter_about(splits[9], (C5, NB1), C5 ** -0.5, 0.21875),
        "conv_mid_5b": scatter_about(splits[10], (27, B1A, B1), (27 * B1A) ** -0.5, 0.09375),
        "conv_small_5b": scatter_about(splits[11], (27, B2A, B2), (27 * B2A) ** -0.5, 0.21875),
        "gain_5b": jnp.clip(1.0 + 0.15 * jax.random.normal(splits[12], (NB,), jnp.float32), 0.25, 1.75),
        "bias_5b": scatter_about(splits[13], (NB,), 0.5, 2.5, (), jnp.float32),
        "cotangent": scatter_about(splits[14], (CLIPS, T1, H1, H1, C5), 1.0, 6.0, ((0, 16),)),
    }


EPSILON = 0.001
HIGHEST_PRECISION = lax.Precision.HIGHEST
SUM_AXES = (0, 1, 2, 3)

@jax.custom_vjp
def low(v):
    return lax.optimization_barrier(v.astype(jnp.bfloat16)).astype(jnp.float32)

@jax.custom_vjp
def low_back(v):
    return v

def low_keep(v):
    return (low(v), None)

def low_pass(kept, grad):
    return (grad,)

def back_keep(v):
    return (v, None)

def back_low(kept, grad):
    return (low(grad),)
low.defvjp(low_keep, low_pass)
low_back.defvjp(back_keep, back_low)

def three_sum(values, axis):
    extent = values.shape[axis]
    widths = [(0, 0)] * values.ndim
    widths[axis] = (1, 1)
    padded = jnp.pad(values, widths)
    return lax.slice_in_dim(padded, 0, extent, axis=axis) + lax.slice_in_dim(padded, 1, extent + 1, axis=axis) + lax.slice_in_dim(padded, 2, extent + 2, axis=axis)

def window_mean(values):
    return three_sum(three_sum(three_sum(values, 1), 2), 3) / 27.0

def paired(values):
    count, extent_t, extent_h, extent_w, channels = values.shape
    return values.reshape(count, extent_t // 2, 2, extent_h // 2, 2, extent_w // 2, 2, channels)

def halve_mean(values):
    return lax.optimization_barrier(jnp.sum(paired(values), axis=(2, 4, 6))) / 8.0

def halve_max(values):
    return lax.optimization_barrier(jnp.max(paired(values), axis=(2, 4, 6)))

def project(values, weight):
    return jnp.dot(values, weight, precision=HIGHEST_PRECISION)

def convolve(values, weight):
    kernel = weight.reshape(3, 3, 3, weight.shape[1], weight.shape[2])
    return lax.conv_general_dilated(values, kernel, (1, 1, 1), 'SAME', dimension_numbers=('NDHWC', 'DHWIO', 'NDHWC'), precision=HIGHEST_PRECISION)

def normalize(values, keep_mask, norm_gain, norm_bias):
    voxel_count = jnp.sum(keep_mask)
    mean_value = lax.optimization_barrier(jnp.sum(values * keep_mask, axis=SUM_AXES)) / voxel_count
    variance = lax.optimization_barrier(jnp.sum(values * values * keep_mask, axis=SUM_AXES)) / voxel_count - mean_value * mean_value
    scaled = (values - mean_value) * lax.rsqrt(variance + EPSILON)
    return (jax.nn.silu(norm_gain * scaled + norm_bias) * keep_mask, jnp.stack([mean_value, variance]))

def inception(inputs, keep_mask, inproj, conv_mid, conv_small, norm_gain, norm_bias):
    inputs = inputs * keep_mask
    pooled = low(window_mean(inputs))
    first_out = jnp.concatenate([project(inputs, inproj[:, :NX]), project(pooled, inproj[:, NX:])], -1)
    first_out = low_back(first_out)
    act_first, moments_first = normalize(first_out, keep_mask, norm_gain[:NB1], norm_bias[:NB1])
    middle = low(act_first[..., B0:NX])
    second_out = jnp.concatenate([convolve(middle[..., :B1A], conv_mid), convolve(middle[..., B1A:], conv_small)], -1)
    second_out = low_back(second_out)
    act_second, moments_second = normalize(second_out, keep_mask, norm_gain[NB1:], norm_bias[NB1:])
    result = low(jnp.concatenate([act_first[..., :B0], act_second, act_first[..., NX:]], -1))
    return (result, jnp.concatenate([moments_first, moments_second], 1))

def reference(clips_in, frames, voxel_mask, micro_order, inproj_4f, conv_mid_4f, conv_small_4f, gain_4f, bias_4f, inproj_5b, conv_mid_5b, conv_small_5b, gain_5b, bias_5b, cotangent):
    frame_index = jnp.arange(T0, dtype=jnp.int32)
    frame_valid = (frame_index[None, :] < frames[:, None]).astype(jnp.float32)
    keep_first = (frame_valid[:, :, None, None] * voxel_mask.astype(jnp.float32))[..., None]
    keep_second = halve_max(keep_first)
    owners = jnp.arange(N_DP, dtype=jnp.int32)[:, None] * CLIPS_DEV
    chosen = [(owners + micro_order[:, micro_step * CMB:(micro_step + 1) * CMB]).reshape(-1).astype(jnp.int32) for micro_step in range(MICRO)]

    def forward(inputs, params_first, params_second):
        output = jnp.zeros((CLIPS, T1, H1, H1, C5), jnp.float32)
        moments = []
        for micro_step in range(MICRO):
            chosen_rows = chosen[micro_step]
            result_first, moments_first = inception(inputs[chosen_rows], keep_first[chosen_rows], *params_first)
            pooled = low(low_back(halve_mean(result_first)))
            result_second, moments_second = inception(pooled, keep_second[chosen_rows], *params_second)
            output = output.at[chosen_rows].set(result_second)
            moments.append((moments_first, moments_second))
        return (output, moments)
    params_first = tuple((value.astype(jnp.float32) for value in (inproj_4f, conv_mid_4f, conv_small_4f, gain_4f, bias_4f)))
    params_second = tuple((value.astype(jnp.float32) for value in (inproj_5b, conv_mid_5b, conv_small_5b, gain_5b, bias_5b)))
    output, pullback, moments = jax.vjp(forward, clips_in.astype(jnp.float32), params_first, params_second, has_aux=True)
    grad_inputs, grads_first, grads_second = pullback(cotangent.astype(jnp.float32))
    moments_first = jnp.stack([moments[micro_step][0] for micro_step in range(MICRO)])
    moments_second = jnp.stack([moments[micro_step][1] for micro_step in range(MICRO)])
    return (output.astype(jnp.bfloat16), grad_inputs.astype(jnp.bfloat16), grads_first[0], grads_first[1], grads_first[2], jnp.stack([grads_first[3], grads_first[4]]), moments_first, grads_second[0], grads_second[1], grads_second[2], jnp.stack([grads_second[3], grads_second[4]]), moments_second)
```

```python
import jax
import jax.numpy as jnp
from jax import lax
from jax.sharding import PartitionSpec as P

B0 = 256
B1A = 160
B1 = 320
B2A = 32
B2 = 128
B3 = 128
C5 = 832
NX = 448
NB1 = 576
NB = 1024
MICRO = 2
CMB = 1


EPSILON = 0.001
SUM_AXES = (0, 1, 2, 3)


def three_sum(values, axis):
    extent = values.shape[axis]
    widths = [(0, 0)] * values.ndim
    widths[axis] = (1, 1)
    padded = jnp.pad(values, widths)
    return (
        lax.slice_in_dim(padded, 0, extent, axis=axis)
        + lax.slice_in_dim(padded, 1, extent + 1, axis=axis)
        + lax.slice_in_dim(padded, 2, extent + 2, axis=axis)
    )


def window_mean(values):
    return three_sum(three_sum(three_sum(values, 1), 2), 3) / 27.0


def paired(values):
    count, extent_t, extent_h, extent_w, channels = values.shape
    return values.reshape(count, extent_t // 2, 2, extent_h // 2, 2, extent_w // 2, 2, channels)


def halve_mean(values):
    return jnp.sum(paired(values), axis=(2, 4, 6)) / 8.0


def halve_max(values):
    return jnp.max(paired(values), axis=(2, 4, 6))


def windows(values):
    extent_t, extent_h, extent_w = values.shape[1:4]
    padded = jnp.pad(values, ((0, 0), (1, 1), (1, 1), (1, 1), (0, 0)))
    pieces = [
        padded[
            :,
            shift_t : shift_t + extent_t,
            shift_h : shift_h + extent_h,
            shift_w : shift_w + extent_w,
        ]
        for shift_t in range(3)
        for shift_h in range(3)
        for shift_w in range(3)
    ]
    return jnp.concatenate(pieces, -1)


def project(values, weight):
    return jnp.dot(values, weight, preferred_element_type=jnp.float32)


def convolve(values, weight):
    return project(windows(values), weight.reshape(-1, weight.shape[2]))


def convolve_back(grad_values, weight):
    flipped = jnp.transpose(weight[::-1], (0, 2, 1))
    return project(windows(grad_values), flipped.reshape(-1, flipped.shape[2]))


def outer_sum(left_side, right_side):
    flat_left = left_side.reshape(-1, left_side.shape[-1])
    flat_right = right_side.reshape(-1, right_side.shape[-1])
    return lax.dot_general(
        flat_left, flat_right, (((0,), (0,)), ((), ())), preferred_element_type=jnp.float32
    )


def moments_of(value_sum, square_sum, voxel_count):
    mean_value = value_sum / voxel_count
    return (mean_value, square_sum / voxel_count - mean_value * mean_value)


def normalized(values, keep_mask, mean_value, variance, norm_gain, norm_bias):
    scaled = (values - mean_value) * lax.rsqrt(variance + EPSILON)
    shifted = norm_gain * scaled + norm_bias
    return (jax.nn.silu(shifted) * keep_mask, scaled, shifted)


def slope_terms(grad_values, keep_mask, scaled, shifted):
    sigmoid_value = jax.nn.sigmoid(shifted)
    derivative = sigmoid_value * (1.0 + shifted * (1.0 - sigmoid_value))
    slope_grad = grad_values * keep_mask * derivative
    return (slope_grad, (jnp.sum(slope_grad, SUM_AXES), jnp.sum(slope_grad * scaled, SUM_AXES)))


def norm_back(slope_grad, scaled, keep_mask, norm_gain, variance, totals, voxel_count):
    slope_sum, cross_sum = totals
    return (
        norm_gain
        * lax.rsqrt(variance + EPSILON)
        * (slope_grad - slope_sum / voxel_count - scaled * cross_sum / voxel_count)
        * keep_mask
    )


def total_of(vectors):
    count = lax.axis_size("dp")
    sizes = [vector.shape[0] for vector in vectors]
    joined = jnp.concatenate(vectors)
    spread = jnp.broadcast_to(joined[None], (count,) + joined.shape)
    summed = jnp.sum(lax.all_to_all(spread, "dp", 0, 0), 0)
    pieces, start = [], 0
    for size in sizes:
        pieces.append(summed[start : start + size])
        start += size
    return pieces


def swapped(value):
    return lax.ppermute(value, "section", [(0, 1), (1, 0)])


def block_forward(inputs, keep, params):
    inproj, conv_mid, conv_small, gain, bias = params
    inputs = (inputs.astype(jnp.float32) * keep).astype(jnp.bfloat16)
    pooled = window_mean(inputs.astype(jnp.float32)).astype(jnp.bfloat16)
    first_out = jnp.concatenate(
        [project(inputs, inproj[:, :NX]), project(pooled, inproj[:, NX:])], -1
    )
    masked = first_out * keep
    sum_first, square_first, count = total_of(
        [
            jnp.sum(masked, SUM_AXES),
            jnp.sum(masked * first_out, SUM_AXES),
            jnp.sum(keep).reshape(1),
        ]
    )
    count = count[0]
    mean_first, var_first = moments_of(sum_first, square_first, count)
    act_first, scaled_first, shifted_first = normalized(
        first_out, keep, mean_first, var_first, gain[:NB1], bias[:NB1]
    )
    rounded = act_first.astype(jnp.bfloat16)
    middle = rounded[..., B0:NX]
    second_out = jnp.concatenate(
        [convolve(middle[..., :B1A], conv_mid), convolve(middle[..., B1A:], conv_small)], -1
    )
    masked = second_out * keep
    sum_second, square_second = total_of(
        [jnp.sum(masked, SUM_AXES), jnp.sum(masked * second_out, SUM_AXES)]
    )
    mean_second, var_second = moments_of(sum_second, square_second, count)
    act_second, scaled_second, shifted_second = normalized(
        second_out, keep, mean_second, var_second, gain[NB1:], bias[NB1:]
    )
    result = jnp.concatenate(
        [rounded[..., :B0], act_second.astype(jnp.bfloat16), rounded[..., NX:]], -1
    )
    moments = jnp.stack(
        [
            jnp.concatenate([mean_first, mean_second]),
            jnp.concatenate([var_first, var_second]),
        ]
    )
    kept = (
        inputs,
        pooled,
        middle,
        scaled_first,
        shifted_first,
        scaled_second,
        shifted_second,
        moments,
        count,
    )
    return result, moments, kept


def block_backward(upstream, keep, params, kept):
    inproj, conv_mid, conv_small, gain, bias = params
    (
        inputs,
        pooled,
        middle,
        scaled_first,
        shifted_first,
        scaled_second,
        shifted_second,
        moments,
        count,
    ) = kept
    slope_second, sums = slope_terms(
        upstream[..., B0 : B0 + B1 + B2], keep, scaled_second, shifted_second
    )
    totals_second = total_of(list(sums))
    grad_second = norm_back(
        slope_second, scaled_second, keep, gain[NB1:], moments[1, NB1:], totals_second, count
    ).astype(jnp.bfloat16)
    back_mid = convolve_back(grad_second[..., :B1], conv_mid)
    back_small = convolve_back(grad_second[..., B1:], conv_small)
    grad_first = jnp.concatenate(
        [upstream[..., :B0], back_mid, back_small, upstream[..., C5 - B3 :]], -1
    )
    slope_first, sums = slope_terms(grad_first, keep, scaled_first, shifted_first)
    mid_grad = outer_sum(windows(middle[..., :B1A]), grad_second[..., :B1])
    small_grad = outer_sum(windows(middle[..., B1A:]), grad_second[..., B1:])
    totals_first = total_of(list(sums))
    grad_first = norm_back(
        slope_first, scaled_first, keep, gain[:NB1], moments[1, :NB1], totals_first, count
    ).astype(jnp.bfloat16)
    direct = project(grad_first[..., :NX], inproj[:, :NX].T)
    through = project(grad_first[..., NX:], inproj[:, NX:].T)
    unused, pool_back = jax.vjp(window_mean, inputs.astype(jnp.float32))
    grad_inputs = ((direct + pool_back(through)[0]) * keep).astype(jnp.bfloat16)
    inproj_grad = jnp.concatenate(
        [
            outer_sum(inputs, grad_first[..., :NX]),
            outer_sum(pooled, grad_first[..., NX:]),
        ],
        -1,
    )
    norm_grad = jnp.stack(
        [
            jnp.concatenate([totals_first[1], totals_second[1]]),
            jnp.concatenate([totals_first[0], totals_second[0]]),
        ]
    )
    return grad_inputs, norm_grad, (inproj_grad, mid_grad, small_grad)


def halves_exchanged(mine, section, own_clip, clips):
    half = mine.shape[1] // 2
    to_keep = lax.dynamic_slice_in_dim(mine, section * half, half, 1)
    to_send = lax.dynamic_slice_in_dim(mine, (1 - section) * half, half, 1)
    got = swapped(to_send)
    own_first = (own_clip == 0)
    return jnp.concatenate(
        [jnp.where(own_first, to_keep, got), jnp.where(own_first, got, to_keep)]
    )


def local(
    clips_in,
    frames,
    voxel_mask,
    micro_order,
    inproj_4f,
    conv_mid_4f,
    conv_small_4f,
    gain_4f,
    bias_4f,
    inproj_5b,
    conv_mid_5b,
    conv_small_5b,
    gain_5b,
    bias_5b,
    cotangent,
):
    section = lax.axis_index("section")
    own_clip = micro_order[0, section]
    grid = clips_in.shape[1:4]

    def own(array):
        return lax.dynamic_slice_in_dim(array, own_clip, 1, 0)

    frame_index = jnp.arange(grid[0], dtype=jnp.int32)
    frame_valid = (frame_index[None, :] < own(frames)[:, None]).astype(jnp.float32)
    keep_first = (frame_valid[:, :, None, None] * own(voxel_mask).astype(jnp.float32))[..., None]
    keep_second = halve_max(keep_first)
    params_first = (inproj_4f, conv_mid_4f, conv_small_4f, gain_4f, bias_4f)
    params_second = (inproj_5b, conv_mid_5b, conv_small_5b, gain_5b, bias_5b)
    result_first, moments_first, kept_first = block_forward(own(clips_in), keep_first, params_first)
    between = halve_mean(result_first.astype(jnp.float32)).astype(jnp.bfloat16)
    result_second, moments_second, kept_second = block_forward(between, keep_second, params_second)
    block_out = halves_exchanged(result_second, section, own_clip, clips_in.shape[0])
    grad_between, norm_second, grads_second = block_backward(
        own(cotangent).astype(jnp.float32), keep_second, params_second, kept_second
    )
    unused, pool_back = jax.vjp(halve_mean, result_first.astype(jnp.float32))
    upstream = pool_back(grad_between.astype(jnp.float32))[0]
    grad_in, norm_first, grads_first = block_backward(
        upstream, keep_first, params_first, kept_first
    )
    clips_grad = halves_exchanged(grad_in, section, own_clip, clips_in.shape[0])
    small = jnp.stack([moments_first, moments_second, norm_first, norm_second])
    other = swapped(small)
    ordered = jnp.where(section == 0, jnp.stack([small, other]), jnp.stack([other, small]))
    norms = ordered[0] + ordered[1]
    summed_second = lax.psum(grads_second, ("section", "dp"))
    summed_first = lax.psum(grads_first, ("section", "dp"))
    return (
        block_out,
        clips_grad,
        summed_first[0],
        summed_first[1].reshape(conv_mid_4f.shape),
        summed_first[2].reshape(conv_small_4f.shape),
        norms[2],
        ordered[:, 0],
        summed_second[0],
        summed_second[1].reshape(conv_mid_5b.shape),
        summed_second[2].reshape(conv_small_5b.shape),
        norms[3],
        ordered[:, 1],
    )


def solution(mesh):
    placed = (
        P("dp", None, None, None, None),
        P("dp"),
        P("dp", None, None, None),
        P("dp", None),
        P(),
        P(),
        P(),
        P(),
        P(),
        P(),
        P(),
        P(),
        P(),
        P(),
        P("dp", None, None, None, None),
    )
    return jax.shard_map(
        local,
        mesh=mesh,
        in_specs=placed,
        out_specs=(
            P("dp", "section", None, None, None),
            P("dp", "section", None, None, None),
            P(),
            P(),
            P(),
            P(),
            P(),
            P(),
            P(),
            P(),
            P(),
            P(),
        ),
        check_vma=False,
    )
```

```python
import functools

import jax
import jax.numpy as jnp
from jax import lax
from jax.experimental import pallas as pl
from jax.experimental.pallas import tpu as pltpu
from jax.sharding import PartitionSpec as P

B0 = 256
B1A = 160
B1 = 320
B2A = 32
B2 = 128
B3 = 128
C5 = 832
NX = 448
NB1 = 576
NB = 1024
NB2 = NB - NB1
NM = B1A + B2A
ND = B0 + B3
WP = 16

EPSILON = 0.001
F32 = jnp.float32
BF16 = jnp.bfloat16

FIRST_PIECES = ((0, 0, B0), (B0, NX, B3), (ND, B0, NM))
SECOND_PIECES = ((0, B1, B2), (B2, 0, B1))
RESULT_PIECES = ((0, 0, B0), (B0, C5 - B3, B3), (ND, B0 + B1, B2), (ND + B2, B0, B1))

CONV_ROWS = 11776
CONV_NARROW = 10800


def shape_of(*dims, dtype=F32):
    return jax.ShapeDtypeStruct(dims, dtype)


def tiles_of(start, stop):
    return [(first, min(first + 128, stop)) for first in range(start, stop, 128)]


def call(body, outs, scratch, args, name, mib, scalars=None, specs=None, flops=0):
    params = pltpu.CompilerParams(vmem_limit_bytes=mib * 2**20)
    cost = pl.CostEstimate(
        flops=flops, transcendentals=0, bytes_accessed=sum(a.size * a.dtype.itemsize for a in args)
    )
    if scalars is None:
        return pl.pallas_call(
            body,
            out_shape=outs,
            scratch_shapes=scratch,
            compiler_params=params,
            cost_estimate=cost,
            name=name,
        )(*args)
    whole = [
        pl.BlockSpec(a.shape, functools.partial(lambda nd, i, s: (0,) * nd, a.ndim)) for a in args
    ]
    for place, spec in specs.items():
        whole[place] = spec
    return pl.pallas_call(
        body,
        out_shape=outs,
        grid_spec=pltpu.PrefetchScalarGridSpec(
            num_scalar_prefetch=1,
            grid=(1,),
            in_specs=whole,
            out_specs=[
                pl.BlockSpec(o.shape, functools.partial(lambda nd, i, s: (0,) * nd, len(o.shape)))
                for o in outs
            ],
            scratch_shapes=scratch,
        ),
        compiler_params=params,
        cost_estimate=cost,
        name=name,
    )(scalars, *args)


def sigmoid(value):
    return 0.5 * jnp.tanh(0.5 * value) + 0.5


def rows_summed(value):
    return value.reshape(value.shape[0] // 8, 8, value.shape[1]).sum(0)


def put_permuted(target, row, source, pieces, offset=0):
    for inner, outer, width in pieces:
        target[row : row + 1, inner : inner + width] = source[
            :, offset + outer : offset + outer + width
        ]


def put_original(target, row, value, pieces):
    for inner, outer, width in pieces:
        target[row : row + 1, outer : outer + width] = value[:, inner : inner + width]


def put_stats(stat_ref, acc_ref, count=None):
    peers, rows, width = stat_ref.shape
    for row in range(2):
        line = jnp.sum(acc_ref[row], axis=0, keepdims=True)
        stat_ref[:, row : row + 1, :] = jnp.broadcast_to(line[None], (peers, 1, width))
    if count is not None:
        stat_ref[:, 2:3, :] = jnp.broadcast_to(count.reshape(1, 1, 1), (peers, 1, width))


def masked_stats(value_ref, keep_ref, acc_ref):
    frames, rows, width = value_ref.shape
    acc_ref[...] = jnp.zeros_like(acc_ref)

    def step(t, carry):
        keep = keep_ref[t]
        for first, last in tiles_of(0, width):
            value = value_ref[t, :, first:last]
            masked = value * keep
            acc_ref[0, :, first:last] += rows_summed(masked)
            acc_ref[1, :, first:last] += rows_summed(masked * value)
        return carry

    lax.fori_loop(0, frames, step, 0)


def window_sums(source_ref, between_ref, put):
    frames, rows, width = source_ref.shape
    edge = jnp.zeros((WP, width), F32)
    between_ref[0] = jnp.zeros((rows, width), F32)
    between_ref[frames + 1] = jnp.zeros((rows, width), F32)

    def plane(t, carry):
        value = source_ref[t]
        value = value + pltpu.roll(value, 1, 0) + pltpu.roll(value, rows - 1, 0)
        up = jnp.concatenate([value[WP:], edge], 0)
        down = jnp.concatenate([edge, value[:-WP]], 0)
        between_ref[t + 1] = value + up + down
        return carry

    lax.fori_loop(0, frames, plane, 0)

    def through(t, carry):
        put(t, (between_ref[t] + between_ref[t + 1] + between_ref[t + 2]) * (1.0 / 27.0))
        return carry

    lax.fori_loop(0, frames, through, 0)


def weight_ordered(weight_ref, ordered_ref, row_pieces):
    for row_to, row_from, height in row_pieces:
        for inner, outer, width in FIRST_PIECES:
            ordered_ref[row_to : row_to + height, inner : inner + width] = weight_ref[
                row_from : row_from + height, outer : outer + width
            ]


def step_frames(frames, rows):
    together = max(1, min(frames, 448 // rows))
    return together, frames // together


def first_outputs(x_ref, ordered_ref, z_ref, pool_ref, between_ref):
    frames, rows, channels = x_ref.shape
    together, steps = step_frames(frames, rows)

    def product(i, carry):
        at = pl.ds(i * together, together)
        value = x_ref[at].reshape(together * rows, channels)
        out = jnp.dot(value, ordered_ref[...], preferred_element_type=F32)
        z_ref[at] = out.reshape(together, rows, NB1)
        pool_ref[at] = out[:, B0:ND].reshape(together, rows, B3)
        return carry

    lax.fori_loop(0, steps, product, 0)

    def put(t, value):
        z_ref[t, :, B0:ND] = value

    window_sums(pool_ref, between_ref, put)


def project_body(
    index_ref, x_in, keep_ref, weight_ref, x_ref, z_ref, stat_ref, padded, ordered, pool, between, acc
):
    frames, rows, channels = x_ref.shape
    width = x_in.shape[3]
    padded[...] = jnp.zeros_like(padded)
    weight_ordered(weight_ref, ordered, ((0, 0, channels),))

    def load(t, carry):
        padded[:, 0:width, :] = x_in[0, t]
        value = padded[...].reshape(rows, channels)
        x_ref[t] = value * keep_ref[t].astype(BF16)
        return carry

    lax.fori_loop(0, frames, load, 0)
    first_outputs(x_ref, ordered, z_ref, pool, between)
    masked_stats(z_ref, keep_ref, acc)
    put_stats(stat_ref, acc, jnp.sum(keep_ref[...]))


def project_first(clips, own_clip, keep, weight, peers):
    clip_count, frames, height, width, channels = clips.shape
    rows = height * WP
    return call(
        project_body,
        [
            shape_of(frames, rows, channels, dtype=BF16),
            shape_of(frames, rows, NB1),
            shape_of(peers, 3, NB1),
        ],
        [
            pltpu.VMEM((height, WP, channels), BF16),
            pltpu.VMEM((channels, NB1), BF16),
            pltpu.VMEM((frames, rows, B3), F32),
            pltpu.VMEM((frames + 2, rows, B3), F32),
            pltpu.VMEM((2, 8, NB1), F32),
        ],
        (clips, keep, weight),
        "project_first",
        40,
        own_clip.reshape(1),
        {0: pl.BlockSpec((1,) + clips.shape[1:], lambda i, s: (s[0], 0, 0, 0, 0))},
        2 * frames * rows * channels * NB1,
    )


def first_rows(vec, gain_ref, bias_ref, mom_ref):
    put_permuted(vec, 4, gain_ref, FIRST_PIECES)
    put_permuted(vec, 5, bias_ref, FIRST_PIECES)
    mean, var = mom_ref[0:1, :], mom_ref[1:2, :]
    inverse = lax.rsqrt(var + EPSILON)
    scale = vec[4:5, :] * inverse
    vec[0:1, :] = scale
    vec[1:2, :] = vec[5:6, :] - mean * scale
    vec[2:3, :] = inverse
    vec[3:4, :] = -mean * inverse


def second_rows(vec, gain_ref, bias_ref, mom_ref):
    put_permuted(vec, 4, gain_ref, SECOND_PIECES, NB1)
    put_permuted(vec, 5, bias_ref, SECOND_PIECES, NB1)
    mean, var = mom_ref[0:1, :], mom_ref[1:2, :]
    inverse = lax.rsqrt(var + EPSILON)
    scale = vec[4:5, :] * inverse
    vec[0:1, :] = scale
    vec[1:2, :] = vec[5:6, :] - mean * scale
    vec[2:3, :] = inverse
    vec[3:4, :] = -mean * inverse


def put_moments(tot_ref, mom_ref, count):
    total = jnp.sum(tot_ref[...], axis=0)
    if count is None:
        count = total[2:3, :]
        mom_ref[2:3, :] = count
    mean = total[0:1, :] / count
    mom_ref[0:1, :] = mean
    mom_ref[1:2, :] = total[1:2, :] / count - mean * mean


def shifted_in(shifts, t, lanes, value):
    rows = value.shape[0]
    first, last = lanes
    shifts[0, t, WP : WP + rows, first:last] = pltpu.roll(value, 1, 0).astype(BF16)
    shifts[1, t, WP : WP + rows, first:last] = value.astype(BF16)
    shifts[2, t, WP : WP + rows, first:last] = pltpu.roll(value, rows - 1, 0).astype(BF16)


def clear_edges(shifts):
    frames, rows = shifts.shape[1], shifts.shape[2] - 2 * WP
    edge = jnp.zeros(shifts.shape[:2] + (WP, shifts.shape[3]), BF16)
    shifts[:, :, 0:WP, :] = edge
    shifts[:, :, WP + rows :, :] = edge


def spread_windows(shifts, targets):
    frames, rows = shifts.shape[1], shifts.shape[2] - 2 * WP
    for target, first, last in targets:
        target[0] = jnp.zeros(target.shape[1:], BF16)
        target[frames + 1] = jnp.zeros(target.shape[1:], BF16)

    def frame(t, carry):
        for high in range(3):
            for wide in range(3):
                place = high * 3 + wide
                for target, first, last in targets:
                    width = last - first
                    target[t + 1, :, place * width : (place + 1) * width] = shifts[
                        wide, t, high * WP : high * WP + rows, first:last
                    ]
        return carry

    lax.fori_loop(0, frames, frame, 0)


def second_body(
    tot_ref,
    z_ref,
    keep_ref,
    gain_ref,
    bias_ref,
    wide_ref,
    narrow_ref,
    act_ref,
    mid_ref,
    out_ref,
    stat_ref,
    mom_ref,
    vec,
    shifts,
    im_wide,
    im_narrow,
    acc,
):
    frames, rows, unused = z_ref.shape
    put_moments(tot_ref, mom_ref, None)
    first_rows(vec, gain_ref, bias_ref, mom_ref)
    clear_edges(shifts)

    def activate(t, carry):
        keep = keep_ref[t]
        for first, last in tiles_of(0, NB1):
            shifted = z_ref[t, :, first:last] * vec[0:1, first:last] + vec[1:2, first:last]
            value = shifted * sigmoid(shifted) * keep
            if first < ND:
                act_ref[t, :, first:last] = value.astype(BF16)
            else:
                mid_ref[t, :, first - ND : last - ND] = value.astype(BF16)
                shifted_in(shifts, t, (first - ND, last - ND), value)
        return carry

    lax.fori_loop(0, frames, activate, 0)
    spread_windows(shifts, ((im_wide, 0, B1A), (im_narrow, B1A, NM)))
    together, steps = step_frames(frames, rows)

    def convolve(i, carry):
        at = pl.ds(i * together, together)
        for im_ref, weight_ref, first, last in (
            (im_narrow, narrow_ref, 0, B2),
            (im_wide, wide_ref, B2, NB2),
        ):
            total = None
            for depth in range(3):
                value = im_ref[pl.ds(i * together + depth, together)]
                value = value.reshape(together * rows, value.shape[2])
                part = jnp.dot(value, weight_ref[depth], preferred_element_type=F32)
                total = part if total is None else total + part
            out_ref[at, :, first:last] = total.reshape(together, rows, last - first)
        return carry

    lax.fori_loop(0, steps, convolve, 0)
    masked_stats(out_ref, keep_ref, acc)
    put_stats(stat_ref, acc)


def second_level(totals, first_out, keep, params, peers):
    unused, conv_mid, conv_small, gain, bias = params
    frames, rows, unused = first_out.shape
    return call(
        second_body,
        [
            shape_of(frames, rows, ND, dtype=BF16),
            shape_of(frames, rows, NM, dtype=BF16),
            shape_of(frames, rows, NB2),
            shape_of(peers, 2, NB2),
            shape_of(3, NB1),
        ],
        [
            pltpu.VMEM((8, NB1), F32),
            pltpu.VMEM((3, frames, rows + 2 * WP, NM), BF16),
            pltpu.VMEM((frames + 2, rows, 9 * B1A), BF16),
            pltpu.VMEM((frames + 2, rows, 9 * B2A), BF16),
            pltpu.VMEM((2, 8, NB2), F32),
        ],
        (
            totals,
            first_out,
            keep,
            gain,
            bias,
            conv_mid.reshape(3, 9 * B1A, B1),
            conv_small.reshape(3, 9 * B2A, B2),
        ),
        "second_level",
        48,
        flops=2 * frames * rows * 27 * (B1A * B1 + B2A * B2),
    )


def between_body(
    tot_ref,
    z_ref,
    keep_ref,
    gain_ref,
    bias_ref,
    act_ref,
    first_mom_ref,
    keep_next_ref,
    weight_ref,
    x_ref,
    z_next_ref,
    stat_ref,
    mom_ref,
    vec,
    pair,
    ordered,
    pool,
    between,
    acc,
):
    frames, rows, channels = x_ref.shape
    source_rows = z_ref.shape[1]
    high = source_rows // (2 * WP)
    put_moments(tot_ref, mom_ref, first_mom_ref[2:3, 0:NB2])
    second_rows(vec, gain_ref, bias_ref, mom_ref)
    weight_ordered(weight_ref, ordered, RESULT_PIECES)

    def pooling(t, carry):
        keeps = [keep_ref[2 * t], keep_ref[2 * t + 1]]
        keep_next = keep_next_ref[t].reshape(high, WP, 1)[:, 0 : WP // 2]
        for first, last in tiles_of(0, C5):
            total = None
            for step in range(2):
                if first < ND:
                    part = act_ref[2 * t + step, :, first:last].astype(F32)
                else:
                    at = slice(first - ND, last - ND)
                    shifted = z_ref[2 * t + step, :, at] * vec[0:1, at] + vec[1:2, at]
                    part = (shifted * sigmoid(shifted) * keeps[step]).astype(BF16).astype(F32)
                total = part if total is None else total + part
            width = last - first
            total = total.reshape(high, 2, WP, width).sum(1)
            pair[:, :, 0:width] = total
            mean = (
                pair[:, pl.ds(0, WP // 2, stride=2), :] + pair[:, pl.ds(1, WP // 2, stride=2), :]
            ) * 0.125
            mean = (mean.astype(BF16).astype(F32) * keep_next)[:, :, 0:width]
            mean = jnp.concatenate([mean, jnp.zeros_like(mean)], 1)
            x_ref[t, :, first:last] = mean.reshape(rows, width).astype(BF16)
        return carry

    lax.fori_loop(0, frames, pooling, 0)
    first_outputs(x_ref, ordered, z_next_ref, pool, between)
    masked_stats(z_next_ref, keep_next_ref, acc)
    put_stats(stat_ref, acc, jnp.sum(keep_next_ref[...]))


def between_blocks(totals, second_out, keep, params, act, first_mom, keep_next, weight, peers):
    frames, rows = keep_next.shape[:2]
    high = second_out.shape[1] // (2 * WP)
    return call(
        between_body,
        [
            shape_of(frames, rows, C5, dtype=BF16),
            shape_of(frames, rows, NB1),
            shape_of(peers, 3, NB1),
            shape_of(2, NB2),
        ],
        [
            pltpu.VMEM((8, NB2), F32),
            pltpu.VMEM((high, WP, 128), F32),
            pltpu.VMEM((C5, NB1), BF16),
            pltpu.VMEM((frames, rows, B3), F32),
            pltpu.VMEM((frames + 2, rows, B3), F32),
            pltpu.VMEM((2, 8, NB1), F32),
        ],
        (totals, second_out, keep, params[3], params[4], act, first_mom, keep_next, weight),
        "between_blocks",
        32,
        flops=2 * frames * rows * C5 * NB1,
    )


def turn_body(
    index_ref,
    tot_ref,
    z_ref,
    keep_ref,
    gain_ref,
    bias_ref,
    act_ref,
    first_mom_ref,
    grad_ref,
    out_ref,
    slope_ref,
    direct_ref,
    stat_ref,
    mom_ref,
    vec,
    grad,
    result,
    acc,
):
    frames, rows, unused = z_ref.shape
    high = rows // WP
    width = grad_ref.shape[3]
    put_moments(tot_ref, mom_ref, first_mom_ref[2:3, 0:NB2])
    second_rows(vec, gain_ref, bias_ref, mom_ref)
    acc[...] = jnp.zeros_like(acc)
    grad[...] = jnp.zeros_like(grad)

    def frame(t, carry):
        keep = keep_ref[t]
        grad[:, 0:width, :] = grad_ref[0, t].astype(F32)
        upstream = grad[...].reshape(rows, C5)
        direct_ref[t, :, 0:B0] = upstream[:, 0:B0].astype(BF16)
        direct_ref[t, :, B0:ND] = upstream[:, C5 - B3 :].astype(BF16)
        result[:, :, 0:B0] = act_ref[t, :, 0:B0].astype(F32).reshape(high, WP, B0)
        result[:, :, C5 - B3 :] = act_ref[t, :, B0:ND].astype(F32).reshape(high, WP, B3)
        for inner, outer, size in SECOND_PIECES:
            at = slice(inner, inner + size)
            place = slice(B0 + outer, B0 + outer + size)
            value = z_ref[t, :, at]
            shifted = value * vec[0:1, at] + vec[1:2, at]
            gate = sigmoid(shifted)
            result[:, :, place] = (shifted * gate * keep).reshape(high, WP, size)
            slope = upstream[:, place] * keep * gate * (1.0 + shifted * (1.0 - gate))
            slope_ref[t, :, at] = slope
            acc[0, :, at] += rows_summed(slope)
            acc[1, :, at] += rows_summed(slope * (value * vec[2:3, at] + vec[3:4, at]))
        out_ref[t] = result[:, 0:width, :].astype(BF16)
        return carry

    lax.fori_loop(0, frames, frame, 0)
    put_stats(stat_ref, acc)


def turn(totals, second_out, keep, params, act, first_mom, cotangent, own_clip, peers):
    frames, rows, unused = second_out.shape
    high = rows // WP
    return call(
        turn_body,
        [
            shape_of(*cotangent.shape[1:], dtype=BF16),
            shape_of(frames, rows, NB2),
            shape_of(frames, rows, ND, dtype=BF16),
            shape_of(peers, 2, NB2),
            shape_of(2, NB2),
        ],
        [
            pltpu.VMEM((8, NB2), F32),
            pltpu.VMEM((high, WP, C5), F32),
            pltpu.VMEM((high, WP, C5), F32),
            pltpu.VMEM((2, 8, NB2), F32),
        ],
        (totals, second_out, keep, params[3], params[4], act, first_mom, cotangent),
        "turn",
        24,
        own_clip.reshape(1),
        {7: pl.BlockSpec((1,) + cotangent.shape[1:], lambda i, s: (s[0], 0, 0, 0, 0))},
    )


def upsampled(up_ref, t, first, last):
    value = up_ref[t // 2, :, first:last].astype(F32) * 0.125
    high = value.shape[0] // WP
    width = last - first
    value = value.reshape(high, 1, WP, width)
    return jnp.broadcast_to(value, (high, 2, WP, width)).reshape(2 * high * WP, width)


def back_second_body(
    halved,
    tot_ref,
    slope_in,
    z_second,
    z_first,
    keep_ref,
    gain_ref,
    bias_ref,
    first_mom_ref,
    mom_ref,
    direct_ref,
    wide_ref,
    narrow_ref,
    grad_ref,
    slope_ref,
    stat_ref,
    norm_ref,
    vec,
    vec_first,
    shifts,
    windows,
    weights,
    acc,
):
    frames, rows, unused = z_first.shape
    total = jnp.sum(tot_ref[...], axis=0)
    put_original(norm_ref, 0, total[1:2], SECOND_PIECES)
    put_original(norm_ref, 1, total[0:1], SECOND_PIECES)
    second_rows(vec, gain_ref, bias_ref, mom_ref)
    first_rows(vec_first, gain_ref, bias_ref, first_mom_ref)
    count = first_mom_ref[2:3, 0:NB2]
    cross = vec[0:1, :] * total[1:2] / count
    vec[6:7, :] = -(vec[0:1, :] * total[0:1] / count) - cross * vec[3:4, :]
    vec[7:8, :] = -cross * vec[2:3, :]
    clear_edges(shifts)
    weights[...] = jnp.zeros_like(weights)
    for depth in range(3):
        for place in range(9):
            source = 26 - (depth * 9 + place)
            weights[depth, 0:B1A, place * NB2 + B2 : (place + 1) * NB2] = wide_ref[source]
            weights[depth, B1A:NM, place * NB2 : place * NB2 + B2] = narrow_ref[source]

    def gradient(t, carry):
        keep = keep_ref[t]
        for first, last in tiles_of(0, NB2):
            at = slice(first, last)
            value = (
                slope_in[t, :, at] * vec[0:1, at]
                + z_second[t, :, at] * vec[7:8, at]
                + vec[6:7, at]
            ) * keep
            grad_ref[t, :, at] = value.astype(BF16)
            shifted_in(shifts, t, (first, last), value)
        return carry

    lax.fori_loop(0, frames, gradient, 0)
    spread_windows(shifts, ((windows, 0, NB2),))
    together, steps = step_frames(frames, rows)

    def convolve(i, carry):
        at = pl.ds(i * together, together)
        total = None
        for depth in range(3):
            value = windows[pl.ds(i * together + depth, together)]
            value = value.reshape(together * rows, 9 * NB2)
            part = lax.dot_general(
                value, weights[depth], (((1,), (1,)), ((), ())), preferred_element_type=F32
            )
            total = part if total is None else total + part
        slope_ref[at, :, ND:NB1] = total.reshape(together, rows, NM)
        return carry

    lax.fori_loop(0, steps, convolve, 0)
    acc[...] = jnp.zeros_like(acc)

    def slopes(t, carry):
        keep = keep_ref[t]
        for first, last in tiles_of(0, NB1):
            at = slice(first, last)
            value = z_first[t, :, at]
            shifted = value * vec_first[0:1, at] + vec_first[1:2, at]
            gate = sigmoid(shifted)
            if first >= ND:
                upstream = slope_ref[t, :, at]
            elif halved:
                upstream = upsampled(direct_ref, t, first, last)
            else:
                upstream = direct_ref[t, :, at].astype(F32)
            slope = upstream * keep * gate * (1.0 + shifted * (1.0 - gate))
            slope_ref[t, :, at] = slope
            acc[0, :, at] += rows_summed(slope)
            acc[1, :, at] += rows_summed(slope * (value * vec_first[2:3, at] + vec_first[3:4, at]))
        return carry

    lax.fori_loop(0, frames, slopes, 0)
    put_stats(stat_ref, acc)


def back_second(
    totals, slope, second_out, first_out, keep, params, first_mom, mom, direct, halved, peers
):
    unused, conv_mid, conv_small, gain, bias = params
    frames, rows, unused = first_out.shape
    return call(
        functools.partial(back_second_body, halved),
        [
            shape_of(frames, rows, NB2, dtype=BF16),
            shape_of(frames, rows, NB1),
            shape_of(peers, 2, NB1),
            shape_of(2, NB2),
        ],
        [
            pltpu.VMEM((8, NB2), F32),
            pltpu.VMEM((8, NB1), F32),
            pltpu.VMEM((3, frames, rows + 2 * WP, NB2), BF16),
            pltpu.VMEM((frames + 2, rows, 9 * NB2), BF16),
            pltpu.VMEM((3, NM, 9 * NB2), BF16),
            pltpu.VMEM((2, 8, NB1), F32),
        ],
        (
            totals,
            slope,
            second_out,
            first_out,
            keep,
            gain,
            bias,
            first_mom,
            mom,
            direct,
            conv_mid,
            conv_small,
        ),
        "back_second",
        62,
        flops=2 * frames * rows * 27 * (B1A * B1 + B2A * B2),
    )


def conv_grad_body(mid_ref, grad_ref, packed_ref, shifts, im_wide, im_narrow, turned):
    frames, rows, unused = mid_ref.shape
    clear_edges(shifts)

    def shift(t, carry):
        for first, last in tiles_of(0, NM):
            shifted_in(shifts, t, (first, last), mid_ref[t, :, first:last].astype(F32))
        return carry

    lax.fori_loop(0, frames, shift, 0)
    spread_windows(shifts, ((im_wide, 0, B1A), (im_narrow, B1A, NM)))
    turned[...] = grad_ref[...].reshape(frames * rows, NB2).T
    step = 9 * B1A
    half = 27 * B1A // 2
    tail = 54 * B1A
    packed_ref[CONV_NARROW + 27 * B2A :, :] = jnp.zeros(
        (CONV_ROWS - CONV_NARROW - 27 * B2A, 128), BF16
    )
    for depth in range(3):
        value = im_wide[depth : depth + frames].reshape(frames * rows, step)
        part = jnp.dot(turned[B2:NB2, :], value, preferred_element_type=F32)
        part = part.T.astype(BF16)
        packed_ref[depth * step : (depth + 1) * step, :] = part[:, 0:128]
        packed_ref[27 * B1A + depth * step : 27 * B1A + (depth + 1) * step, :] = part[:, 128:256]
        low = max(0, min(step, half - depth * step))
        if low > 0:
            packed_ref[tail + depth * step : tail + depth * step + low, 0:64] = part[:low, 256:B1]
        if low < step:
            start = tail + depth * step + low - half
            packed_ref[start : start + step - low, 64:128] = part[low:, 256:B1]
        value = im_narrow[depth : depth + frames].reshape(frames * rows, 9 * B2A)
        part = jnp.dot(turned[0:B2, :], value, preferred_element_type=F32)
        start = CONV_NARROW + depth * 9 * B2A
        packed_ref[start : start + 9 * B2A, :] = part.T.astype(BF16)


def conv_grad(mid, grad):
    frames, rows, unused = mid.shape
    return call(
        conv_grad_body,
        [shape_of(CONV_ROWS, 128, dtype=BF16)],
        [
            pltpu.VMEM((3, frames, rows + 2 * WP, NM), BF16),
            pltpu.VMEM((frames + 2, rows, 9 * B1A), BF16),
            pltpu.VMEM((frames + 2, rows, 9 * B2A), BF16),
            pltpu.VMEM((NB2, frames * rows), BF16),
        ],
        (mid, grad),
        "conv_grad",
        48,
        flops=2 * frames * rows * 27 * (B1A * B1 + B2A * B2),
    )[0]


def first_gradient(
    tot_ref, slope_ref, z_ref, keep_ref, vec, count, grad_ref, pool_ref, between_ref
):
    frames, rows, unused = z_ref.shape
    total = jnp.sum(tot_ref[...], axis=0)
    cross = vec[0:1, :] * total[1:2] / count
    vec[6:7, :] = -(vec[0:1, :] * total[0:1] / count) - cross * vec[3:4, :]
    vec[7:8, :] = -cross * vec[2:3, :]

    def gradient(t, carry):
        keep = keep_ref[t]
        for first, last in tiles_of(0, NB1):
            at = slice(first, last)
            value = (
                slope_ref[t, :, at] * vec[0:1, at] + z_ref[t, :, at] * vec[7:8, at] + vec[6:7, at]
            ) * keep
            if first == B0:
                pool_ref[t] = value
            else:
                grad_ref[t, :, at] = value.astype(BF16)
        return carry

    lax.fori_loop(0, frames, gradient, 0)

    def put(t, value):
        grad_ref[t, :, B0:ND] = value.astype(BF16)

    window_sums(pool_ref, between_ref, put)
    return total


def back_first_last_body(
    tot_ref,
    slope_ref,
    z_ref,
    keep_ref,
    gain_ref,
    bias_ref,
    mom_ref,
    weight_ref,
    du_ref,
    grad_ref,
    norm_ref,
    vec,
    ordered,
    pool,
    between,
):
    frames, rows, unused = z_ref.shape
    width = du_ref.shape[2]
    first_rows(vec, gain_ref, bias_ref, mom_ref)
    total = first_gradient(
        tot_ref, slope_ref, z_ref, keep_ref, vec, mom_ref[2:3, :], grad_ref, pool, between
    )
    put_original(norm_ref, 0, total[1:2], FIRST_PIECES)
    put_original(norm_ref, 1, total[0:1], FIRST_PIECES)
    channels = du_ref.shape[3]
    weight_ordered(weight_ref, ordered, ((0, 0, channels),))
    together, steps = step_frames(frames, rows)

    def product(i, carry):
        at = pl.ds(i * together, together)
        value = grad_ref[at].reshape(together * rows, NB1)
        out = lax.dot_general(
            value, ordered[...], (((1,), (1,)), ((), ())), preferred_element_type=F32
        )
        out = out.reshape(together, rows, channels) * keep_ref[at]
        out = out.reshape(together, rows // WP, WP, channels)[:, :, 0:width, :]
        du_ref[at] = out.astype(BF16)
        return carry

    lax.fori_loop(0, steps, product, 0)


def back_first_last(totals, slope, first_out, keep, params, mom, width):
    inproj, unused, unused, gain, bias = params
    frames, rows, unused = first_out.shape
    channels = inproj.shape[0]
    return call(
        back_first_last_body,
        [
            shape_of(frames, rows // WP, width, channels, dtype=BF16),
            shape_of(frames, rows, NB1, dtype=BF16),
            shape_of(2, NB1),
        ],
        [
            pltpu.VMEM((8, NB1), F32),
            pltpu.VMEM((channels, NB1), BF16),
            pltpu.VMEM((frames, rows, B3), F32),
            pltpu.VMEM((frames + 2, rows, B3), F32),
        ],
        (totals, slope, first_out, keep, gain, bias, mom, inproj),
        "back_first_last",
        48,
        flops=2 * frames * rows * channels * NB1,
    )


def back_between_body(
    tot_ref,
    slope_ref,
    z_ref,
    keep_ref,
    gain_ref,
    bias_ref,
    mom_ref,
    weight_ref,
    z_prev,
    keep_prev,
    gain_prev,
    bias_prev,
    mom_prev,
    up_ref,
    grad_ref,
    slope_prev,
    stat_ref,
    norm_ref,
    vec,
    vec_prev,
    ordered,
    pool,
    between,
    double,
    acc,
):
    frames, rows, unused = z_ref.shape
    high = rows // WP
    first_rows(vec, gain_ref, bias_ref, mom_ref)
    second_rows(vec_prev, gain_prev, bias_prev, mom_prev)
    total = first_gradient(
        tot_ref, slope_ref, z_ref, keep_ref, vec, mom_ref[2:3, :], grad_ref, pool, between
    )
    put_original(norm_ref, 0, total[1:2], FIRST_PIECES)
    put_original(norm_ref, 1, total[0:1], FIRST_PIECES)
    weight_ordered(weight_ref, ordered, RESULT_PIECES)
    together, steps = step_frames(frames, rows)

    def product(i, carry):
        value = grad_ref[pl.ds(i * together, together)].reshape(together * rows, NB1)
        out = lax.dot_general(
            value, ordered[...], (((1,), (1,)), ((), ())), preferred_element_type=F32
        )
        out = out.reshape(together, rows, C5)
        for inner in range(together):
            t = i * together + inner
            keep = keep_ref[t]
            for first, last in tiles_of(0, C5):
                width = last - first
                value = (out[inner, :, first:last] * keep).astype(BF16).astype(F32)
                value = value.reshape(high, WP, width)[:, 0 : WP // 2, :]
                double[:, pl.ds(0, WP // 2, stride=2), :] = jnp.pad(
                    value, ((0, 0), (0, 0), (0, 128 - width))
                )
                double[:, pl.ds(1, WP // 2, stride=2), :] = jnp.pad(
                    value, ((0, 0), (0, 0), (0, 128 - width))
                )
                up_ref[t, :, first:last] = double[...].reshape(rows, 128)[:, 0:width].astype(BF16)
        return carry

    lax.fori_loop(0, steps, product, 0)
    acc[...] = jnp.zeros_like(acc)

    def slopes(t, carry):
        keep = keep_prev[t]
        for first, last in tiles_of(0, NB2):
            at = slice(first, last)
            value = z_prev[t, :, at]
            shifted = value * vec_prev[0:1, at] + vec_prev[1:2, at]
            gate = sigmoid(shifted)
            upstream = upsampled(up_ref, t, ND + first, ND + last)
            slope = upstream * keep * gate * (1.0 + shifted * (1.0 - gate))
            slope_prev[t, :, at] = slope
            acc[0, :, at] += rows_summed(slope)
            acc[1, :, at] += rows_summed(slope * (value * vec_prev[2:3, at] + vec_prev[3:4, at]))
        return carry

    lax.fori_loop(0, z_prev.shape[0], slopes, 0)
    put_stats(stat_ref, acc)


def back_between(
    totals, slope, first_out, keep, params, mom, second_prev, keep_prev, params_prev, mom_prev, peers
):
    inproj, unused, unused, gain, bias = params
    frames, rows, unused = first_out.shape
    return call(
        back_between_body,
        [
            shape_of(frames, rows, C5, dtype=BF16),
            shape_of(frames, rows, NB1, dtype=BF16),
            shape_of(*second_prev.shape),
            shape_of(peers, 2, NB2),
            shape_of(2, NB1),
        ],
        [
            pltpu.VMEM((8, NB1), F32),
            pltpu.VMEM((8, NB2), F32),
            pltpu.VMEM((C5, NB1), BF16),
            pltpu.VMEM((frames, rows, B3), F32),
            pltpu.VMEM((frames + 2, rows, B3), F32),
            pltpu.VMEM((rows // WP, WP, 128), F32),
            pltpu.VMEM((2, 8, NB2), F32),
        ],
        (
            totals,
            slope,
            first_out,
            keep,
            gain,
            bias,
            mom,
            inproj,
            second_prev,
            keep_prev,
            params_prev[3],
            params_prev[4],
            mom_prev,
        ),
        "back_between",
        40,
        flops=2 * frames * rows * C5 * NB1,
    )


def inproj_rows(channels):
    first = -(-channels // 32) * 16
    rows = 4 * channels + first
    return first, rows, -(-rows // 512) * 512


def inproj_grad_body(row_pieces, x_ref, grad_ref, packed_ref, product, ordered):
    frames, rows, channels = x_ref.shape
    first, used, padded = inproj_rows(channels)
    product[...] = lax.dot_general(
        x_ref[...].reshape(frames * rows, channels),
        grad_ref[...].reshape(frames * rows, NB1),
        (((0,), (0,)), ((), ())),
        preferred_element_type=F32,
    ).astype(product.dtype)
    for row_to, row_from, height in row_pieces:
        for inner, outer, width in FIRST_PIECES:
            ordered[row_from : row_from + height, outer : outer + width] = product[
                row_to : row_to + height, inner : inner + width
            ]
    for place in range(4):
        packed_ref[place * channels : (place + 1) * channels, :] = ordered[
            :, place * 128 : (place + 1) * 128
        ]
    start = 4 * channels
    packed_ref[start : start + first, 0:64] = ordered[0:first, 512:NB1]
    packed_ref[start : start + channels - first, 64:128] = ordered[first:channels, 512:NB1]
    if 2 * first > channels:
        packed_ref[start + channels - first : start + first, 64:128] = jnp.zeros(
            (2 * first - channels, 64), packed_ref.dtype
        )
    if padded > used:
        packed_ref[used:padded, :] = jnp.zeros((padded - used, 128), packed_ref.dtype)


def inproj_grad(x, grad, row_pieces, dtype=BF16):
    frames, rows, channels = x.shape
    return call(
        functools.partial(inproj_grad_body, row_pieces),
        [shape_of(inproj_rows(channels)[2], 128, dtype=dtype)],
        [pltpu.VMEM((channels, NB1), dtype), pltpu.VMEM((channels, NB1), dtype)],
        (x, grad),
        "inproj_grad",
        32,
        flops=2 * frames * rows * channels * NB1,
    )[0]


def unpack_conv_body(packed_ref, wide_ref, narrow_ref):
    step = 27 * B1A
    half = step // 2
    wide_ref[:, 0:128] = packed_ref[0:step, :].astype(F32)
    wide_ref[:, 128:256] = packed_ref[step : 2 * step, :].astype(F32)
    wide_ref[0:half, 256:B1] = packed_ref[2 * step : 2 * step + half, 0:64].astype(F32)
    wide_ref[half:step, 256:B1] = packed_ref[2 * step : 2 * step + half, 64:128].astype(F32)
    narrow_ref[...] = packed_ref[CONV_NARROW : CONV_NARROW + 27 * B2A, :].astype(F32)


def unpack_conv(packed):
    wide, narrow = call(
        unpack_conv_body,
        [shape_of(27 * B1A, B1), shape_of(27 * B2A, B2)],
        [],
        (packed,),
        "unpack_conv",
        32,
    )
    return wide.reshape(27, B1A, B1), narrow.reshape(27, B2A, B2)


def unpack_inproj_body(packed_ref, out_ref):
    channels = out_ref.shape[0]
    first = inproj_rows(channels)[0]
    for place in range(4):
        out_ref[:, place * 128 : (place + 1) * 128] = packed_ref[
            place * channels : (place + 1) * channels, :
        ].astype(F32)
    start = 4 * channels
    out_ref[0:first, 512:NB1] = packed_ref[start : start + first, 0:64].astype(F32)
    out_ref[first:channels, 512:NB1] = packed_ref[start : start + channels - first, 64:128].astype(
        F32
    )


def unpack_inproj(packed, channels):
    return call(
        unpack_inproj_body, [shape_of(channels, NB1)], [], (packed,), "unpack_inproj", 24
    )[0]


def sent_to_all(spread):
    return lax.all_to_all(spread, "dp", 0, 0)


def swapped(value):
    return lax.ppermute(value, "section", [(0, 1), (1, 0)])


def partner(value, distance):
    count = lax.axis_size("dp")
    return lax.ppermute(value, "dp", [(place, place ^ distance) for place in range(count)])


def summed_halves(value, order):
    place = lax.axis_index("dp")
    for distance in order:
        upper = (place // distance) % 2
        halves = value.reshape(2, value.shape[0] // 2, 128)
        kept = lax.dynamic_index_in_dim(halves, upper, 0, False)
        sent = lax.dynamic_index_in_dim(halves, 1 - upper, 0, False)
        value = (kept.astype(F32) + partner(sent, distance).astype(F32)).astype(value.dtype)
    for distance in order[::-1]:
        upper = (place // distance) % 2
        other = partner(value, distance)
        value = jnp.where(
            upper == 0,
            jnp.concatenate([value, other]),
            jnp.concatenate([other, value]),
        )
    return value


def summed_over_all(packed):
    section = lax.axis_index("section")
    halves = packed.reshape(2, packed.shape[0] // 2, 128)
    kept = lax.dynamic_index_in_dim(halves, section, 0, False)
    sent = lax.dynamic_index_in_dim(halves, 1 - section, 0, False)
    value = (kept.astype(F32) + swapped(sent).astype(F32)).astype(packed.dtype)
    distances = []
    while 2 ** len(distances) < lax.axis_size("dp"):
        distances.append(2 ** len(distances))
    middle = value.shape[0] // 2
    other_order = [distances[1], distances[0]] + distances[2:]
    value = jnp.concatenate(
        [summed_halves(value[:middle], distances), summed_halves(value[middle:], other_order)]
    )
    other = swapped(value)
    return jnp.where(
        section == 0, jnp.concatenate([value, other]), jnp.concatenate([other, value])
    )


def halves_exchanged(mine, section, own_clip):
    half = mine.shape[0] // 2
    kept = lax.dynamic_slice_in_dim(mine, section * half, half, 0)
    sent = lax.dynamic_slice_in_dim(mine, (1 - section) * half, half, 0)
    got = swapped(sent)
    own_first = own_clip == 0
    return jnp.stack([jnp.where(own_first, kept, got), jnp.where(own_first, got, kept)])


def level_first(rows):
    return jnp.concatenate(
        [rows[..., inner : inner + width] for inner, outer, width in sorted(FIRST_PIECES, key=lambda p: p[1])],
        -1,
    )


def level_second(rows):
    return jnp.concatenate(
        [rows[..., inner : inner + width] for inner, outer, width in sorted(SECOND_PIECES, key=lambda p: p[1])],
        -1,
    )


def local(
    clips_in,
    frames,
    voxel_mask,
    micro_order,
    inproj_4f,
    conv_mid_4f,
    conv_small_4f,
    gain_4f,
    bias_4f,
    inproj_5b,
    conv_mid_5b,
    conv_small_5b,
    gain_5b,
    bias_5b,
    cotangent,
):
    section = lax.axis_index("section")
    peers = lax.axis_size("dp")
    own_clip = micro_order[0, section]
    depth, height, width = clips_in.shape[1:4]

    frame_index = jnp.arange(depth, dtype=jnp.int32)
    own_frames = lax.dynamic_index_in_dim(frames, own_clip, 0, False)
    own_mask = lax.dynamic_index_in_dim(voxel_mask, own_clip, 0, False)
    keep = jnp.where(frame_index[:, None, None] < own_frames, own_mask, 0).astype(F32)
    paired = keep.reshape(depth // 2, 2, height // 2, 2, width // 2, 2)
    keep_next = jnp.max(paired, axis=(1, 3, 5))

    def laid_out(mask):
        padded = jnp.pad(mask, ((0, 0), (0, 0), (0, WP - mask.shape[2])))
        return padded.reshape(mask.shape[0], mask.shape[1] * WP, 1)

    keep, keep_next = laid_out(keep), laid_out(keep_next)
    first = (inproj_4f, conv_mid_4f, conv_small_4f, gain_4f.reshape(1, NB), bias_4f.reshape(1, NB))
    second = (inproj_5b, conv_mid_5b, conv_small_5b, gain_5b.reshape(1, NB), bias_5b.reshape(1, NB))

    x_a, z1_a, stat = project_first(clips_in, own_clip, keep, inproj_4f, peers)
    act_a, mid_a, z2_a, stat, mom1_a = second_level(sent_to_all(stat), z1_a, keep, first, peers)
    x_b, z1_b, stat, mom2_a = between_blocks(
        sent_to_all(stat), z2_a, keep, first, act_a, mom1_a, keep_next, inproj_5b, peers
    )
    act_b, mid_b, z2_b, stat, mom1_b = second_level(
        sent_to_all(stat), z1_b, keep_next, second, peers
    )
    result, slope, direct, stat, mom2_b = turn(
        sent_to_all(stat), z2_b, keep_next, second, act_b, mom1_b, cotangent, own_clip, peers
    )
    dz2_b, slope, stat, norm2_b = back_second(
        sent_to_all(stat), slope, z2_b, z1_b, keep_next, second, mom1_b, mom2_b, direct, False, peers
    )
    up, dz1_b, slope, stat, norm1_b = back_between(
        sent_to_all(stat), slope, z1_b, keep_next, second, mom1_b, z2_a, keep, first, mom2_a, peers
    )
    packed_b = jnp.concatenate([conv_grad(mid_b, dz2_b), inproj_grad(x_b, dz1_b, RESULT_PIECES)])
    dz2_a, slope, stat, norm2_a = back_second(
        sent_to_all(stat), slope, z2_a, z1_a, keep, first, mom1_a, mom2_a, up, True, peers
    )
    packed_a = conv_grad(mid_a, dz2_a)
    du, dz1_a, norm1_a = back_first_last(
        sent_to_all(stat), slope, z1_a, keep, first, mom1_a, width
    )
    packed_i = inproj_grad(x_a, dz1_a, ((0, 0, x_a.shape[2]),), F32)

    summed_b = summed_over_all(packed_b)
    summed_a = summed_over_all(packed_a)
    summed_i = summed_over_all(packed_i)
    conv_a = unpack_conv(summed_a)
    conv_b = unpack_conv(summed_b[:CONV_ROWS])
    inproj_a = unpack_inproj(summed_i, inproj_4f.shape[0])
    inproj_b = unpack_inproj(summed_b[CONV_ROWS:], inproj_5b.shape[0])

    block_out = halves_exchanged(result, section, own_clip)
    clips_grad = halves_exchanged(du, section, own_clip)
    small = jnp.stack(
        [
            jnp.concatenate([level_first(mom1_a[:2]), level_second(mom2_a)], -1),
            jnp.concatenate([level_first(mom1_b[:2]), level_second(mom2_b)], -1),
            jnp.concatenate([norm1_a, norm2_a], -1),
            jnp.concatenate([norm1_b, norm2_b], -1),
        ]
    )
    other = swapped(small)
    ordered = jnp.where(section == 0, jnp.stack([small, other]), jnp.stack([other, small]))
    norms = ordered[0] + ordered[1]
    return (
        block_out,
        clips_grad,
        inproj_a,
        conv_a[0],
        conv_a[1],
        norms[2],
        ordered[:, 0],
        inproj_b,
        conv_b[0],
        conv_b[1],
        norms[3],
        ordered[:, 1],
    )


def solution(mesh):
    placed = (
        P("dp", None, None, None, None),
        P("dp"),
        P("dp", None, None, None),
        P("dp", None),
        P(),
        P(),
        P(),
        P(),
        P(),
        P(),
        P(),
        P(),
        P(),
        P(),
        P("dp", None, None, None, None),
    )
    return jax.shard_map(
        local,
        mesh=mesh,
        in_specs=placed,
        out_specs=(
            P("dp", "section", None, None, None),
            P("dp", "section", None, None, None),
            P(),
            P(),
            P(),
            P(),
            P(),
            P(),
            P(),
            P(),
            P(),
            P(),
        ),
        check_vma=False,
    )
```

```python
import functools

import jax
import jax.numpy as jnp
from jax import lax
from jax.experimental import pallas as pl
from jax.experimental.pallas import tpu as pltpu
from jax.sharding import PartitionSpec as P

B0 = 256
B1A = 160
B1 = 320
B2A = 32
B2 = 128
B3 = 128
C5 = 832
NX = 448
NB1 = 576
NB = 1024
NB2 = NB - NB1
NM = B1A + B2A
ND = B0 + B3
WP = 16

EPSILON = 0.001
F32 = jnp.float32
BF16 = jnp.bfloat16

FIRST_PIECES = ((0, 0, B0), (B0, NX, B3), (ND, B0, NM))
SECOND_PIECES = ((0, B1, B2), (B2, 0, B1))
RESULT_PIECES = ((0, 0, B0), (B0, C5 - B3, B3), (ND, B0 + B1, B2), (ND + B2, B0, B1))

CONV_NARROW = 10800


def padded_rows(rows, peers):
    whole = 32 * peers
    return -(-rows // whole) * whole


def conv_rows(peers):
    return padded_rows(CONV_NARROW + 27 * B2A, peers)


def shape_of(*dims, dtype=F32):
    return jax.ShapeDtypeStruct(dims, dtype)


def tiles_of(start, stop):
    return [(first, min(first + 128, stop)) for first in range(start, stop, 128)]


def call(body, outs, scratch, args, name, mib, scalars=None, specs=None, flops=0):
    params = pltpu.CompilerParams(vmem_limit_bytes=mib * 2**20)
    cost = pl.CostEstimate(
        flops=flops, transcendentals=0, bytes_accessed=sum(a.size * a.dtype.itemsize for a in args)
    )
    if scalars is None:
        return pl.pallas_call(
            body,
            out_shape=outs,
            scratch_shapes=scratch,
            compiler_params=params,
            cost_estimate=cost,
            name=name,
        )(*args)
    whole = [
        pl.BlockSpec(a.shape, functools.partial(lambda nd, i, s: (0,) * nd, a.ndim)) for a in args
    ]
    for place, spec in specs.items():
        whole[place] = spec
    return pl.pallas_call(
        body,
        out_shape=outs,
        grid_spec=pltpu.PrefetchScalarGridSpec(
            num_scalar_prefetch=1,
            grid=(1,),
            in_specs=whole,
            out_specs=[
                pl.BlockSpec(o.shape, functools.partial(lambda nd, i, s: (0,) * nd, len(o.shape)))
                for o in outs
            ],
            scratch_shapes=scratch,
        ),
        compiler_params=params,
        cost_estimate=cost,
        name=name,
    )(scalars, *args)


def sigmoid(value):
    return 0.5 * jnp.tanh(0.5 * value) + 0.5


def rows_summed(value):
    return value.reshape(value.shape[0] // 8, 8, value.shape[1]).sum(0)


def put_permuted(target, row, source, pieces, offset=0):
    for inner, outer, width in pieces:
        target[row : row + 1, inner : inner + width] = source[
            :, offset + outer : offset + outer + width
        ]


def put_original(target, row, value, pieces):
    for inner, outer, width in pieces:
        target[row : row + 1, outer : outer + width] = value[:, inner : inner + width]


def put_stats(stat_ref, acc_ref, count=None):
    peers, rows, width = stat_ref.shape
    for row in range(2):
        line = jnp.sum(acc_ref[row], axis=0, keepdims=True)
        stat_ref[:, row : row + 1, :] = jnp.broadcast_to(line[None], (peers, 1, width))
    if count is not None:
        stat_ref[:, 2:3, :] = jnp.broadcast_to(count.reshape(1, 1, 1), (peers, 1, width))


def masked_stats(value_ref, keep_ref, acc_ref):
    frames, rows, width = value_ref.shape
    acc_ref[...] = jnp.zeros_like(acc_ref)

    def step(t, carry):
        keep = keep_ref[t]
        for first, last in tiles_of(0, width):
            value = value_ref[t, :, first:last]
            masked = value * keep
            acc_ref[0, :, first:last] += rows_summed(masked)
            acc_ref[1, :, first:last] += rows_summed(masked * value)
        return carry

    lax.fori_loop(0, frames, step, 0)


def window_sums(source_ref, between_ref, put):
    frames, rows, width = source_ref.shape
    edge = jnp.zeros((WP, width), F32)
    between_ref[0] = jnp.zeros((rows, width), F32)
    between_ref[frames + 1] = jnp.zeros((rows, width), F32)

    def plane(t, carry):
        value = source_ref[t]
        value = value + pltpu.roll(value, 1, 0) + pltpu.roll(value, rows - 1, 0)
        up = jnp.concatenate([value[WP:], edge], 0)
        down = jnp.concatenate([edge, value[:-WP]], 0)
        between_ref[t + 1] = value + up + down
        return carry

    lax.fori_loop(0, frames, plane, 0)

    def through(t, carry):
        put(t, (between_ref[t] + between_ref[t + 1] + between_ref[t + 2]) * (1.0 / 27.0))
        return carry

    lax.fori_loop(0, frames, through, 0)


def turned_ordered(turned_ref, ordered_ref):
    for row_to, row_from, height in FIRST_PIECES:
        for inner, outer, width in RESULT_PIECES:
            ordered_ref[row_to : row_to + height, inner : inner + width] = turned_ref[
                row_from : row_from + height, outer : outer + width
            ]


def weight_ordered(weight_ref, ordered_ref, row_pieces):
    for row_to, row_from, height in row_pieces:
        for inner, outer, width in FIRST_PIECES:
            ordered_ref[row_to : row_to + height, inner : inner + width] = weight_ref[
                row_from : row_from + height, outer : outer + width
            ]


def step_frames(frames, rows):
    together = max(1, min(frames, 448 // rows))
    return together, frames // together


def first_outputs(x_ref, ordered_ref, axis, z_ref, pool_ref, between_ref):
    frames, rows, channels = x_ref.shape
    together, steps = step_frames(frames, rows)

    def product(i, carry):
        at = pl.ds(i * together, together)
        value = x_ref[at].reshape(together * rows, channels)
        out = lax.dot_general(
            value, ordered_ref[...], (((1,), (axis,)), ((), ())), preferred_element_type=F32
        )
        z_ref[at] = out.reshape(together, rows, NB1)
        pool_ref[at] = out[:, B0:ND].reshape(together, rows, B3)
        return carry

    lax.fori_loop(0, steps, product, 0)

    def put(t, value):
        z_ref[t, :, B0:ND] = value

    window_sums(pool_ref, between_ref, put)


def project_body(
    index_ref, x_in, keep_ref, weight_ref, x_ref, z_ref, stat_ref, padded, ordered, pool, between, acc
):
    frames, rows, channels = x_ref.shape
    width = x_in.shape[3]
    padded[...] = jnp.zeros_like(padded)
    weight_ordered(weight_ref, ordered, ((0, 0, channels),))

    def load(t, carry):
        padded[:, 0:width, :] = x_in[0, t]
        value = padded[...].reshape(rows, channels)
        x_ref[t] = value * keep_ref[t].astype(BF16)
        return carry

    lax.fori_loop(0, frames, load, 0)
    first_outputs(x_ref, ordered, 0, z_ref, pool, between)
    masked_stats(z_ref, keep_ref, acc)
    put_stats(stat_ref, acc, jnp.sum(keep_ref[...]))


def project_first(clips, own_clip, keep, weight, peers):
    clip_count, frames, height, width, channels = clips.shape
    rows = height * WP
    return call(
        project_body,
        [
            shape_of(frames, rows, channels, dtype=BF16),
            shape_of(frames, rows, NB1),
            shape_of(peers, 3, NB1),
        ],
        [
            pltpu.VMEM((height, WP, channels), BF16),
            pltpu.VMEM((channels, NB1), BF16),
            pltpu.VMEM((frames, rows, B3), F32),
            pltpu.VMEM((frames + 2, rows, B3), F32),
            pltpu.VMEM((2, 8, NB1), F32),
        ],
        (clips, keep, weight),
        "project_first",
        14,
        own_clip.reshape(1),
        {0: pl.BlockSpec((1,) + clips.shape[1:], lambda i, s: (s[0], 0, 0, 0, 0))},
        2 * frames * rows * channels * NB1,
    )


def first_rows(vec, gain_ref, bias_ref, mom_ref):
    put_permuted(vec, 4, gain_ref, FIRST_PIECES)
    put_permuted(vec, 5, bias_ref, FIRST_PIECES)
    mean, var = mom_ref[0:1, :], mom_ref[1:2, :]
    inverse = lax.rsqrt(var + EPSILON)
    scale = vec[4:5, :] * inverse
    vec[0:1, :] = scale
    vec[1:2, :] = vec[5:6, :] - mean * scale
    vec[2:3, :] = inverse
    vec[3:4, :] = -mean * inverse


def second_rows(vec, gain_ref, bias_ref, mom_ref):
    put_permuted(vec, 4, gain_ref, SECOND_PIECES, NB1)
    put_permuted(vec, 5, bias_ref, SECOND_PIECES, NB1)
    mean, var = mom_ref[0:1, :], mom_ref[1:2, :]
    inverse = lax.rsqrt(var + EPSILON)
    scale = vec[4:5, :] * inverse
    vec[0:1, :] = scale
    vec[1:2, :] = vec[5:6, :] - mean * scale
    vec[2:3, :] = inverse
    vec[3:4, :] = -mean * inverse


def put_moments(tot_ref, mom_ref, count):
    total = jnp.sum(tot_ref[...], axis=0)
    if count is None:
        count = total[2:3, :]
        mom_ref[2:3, :] = count
    mean = total[0:1, :] / count
    mom_ref[0:1, :] = mean
    mom_ref[1:2, :] = total[1:2, :] / count - mean * mean


def shifted_in(shifts, t, lanes, value):
    rows = value.shape[0]
    first, last = lanes
    shifts[0, t, WP : WP + rows, first:last] = pltpu.roll(value, 1, 0).astype(BF16)
    shifts[1, t, WP : WP + rows, first:last] = value.astype(BF16)
    shifts[2, t, WP : WP + rows, first:last] = pltpu.roll(value, rows - 1, 0).astype(BF16)


def clear_edges(shifts):
    frames, rows = shifts.shape[1], shifts.shape[2] - 2 * WP
    edge = jnp.zeros(shifts.shape[:2] + (WP, shifts.shape[3]), BF16)
    shifts[:, :, 0:WP, :] = edge
    shifts[:, :, WP + rows :, :] = edge


def spread_windows(shifts, targets, low, high):
    rows = shifts.shape[2] - 2 * WP

    def frame(t, carry):
        for high in range(3):
            for wide in range(3):
                place = high * 3 + wide
                for target, first, last in targets:
                    width = last - first
                    target[t, :, place * width : (place + 1) * width] = shifts[
                        wide, t, high * WP : high * WP + rows, first:last
                    ]
        return carry

    lax.fori_loop(low, high, frame, 0)


def spread_all(shifts, targets):
    frames = shifts.shape[1] - 2
    for target, first, last in targets:
        target[0] = jnp.zeros(target.shape[1:], BF16)
        target[frames + 1] = jnp.zeros(target.shape[1:], BF16)
    spread_windows(shifts, targets, 1, frames + 1)


def second_body(
    tot_ref,
    z_ref,
    keep_ref,
    gain_ref,
    bias_ref,
    wide_ref,
    narrow_ref,
    act_ref,
    mid_ref,
    out_ref,
    stat_ref,
    mom_ref,
    vec,
    shifts,
    im_wide,
    im_narrow,
    acc,
):
    frames, rows, unused = z_ref.shape
    put_moments(tot_ref, mom_ref, None)
    first_rows(vec, gain_ref, bias_ref, mom_ref)
    clear_edges(shifts)

    def activate(t, carry):
        keep = keep_ref[t]
        for first, last in tiles_of(0, NB1):
            shifted = z_ref[t, :, first:last] * vec[0:1, first:last] + vec[1:2, first:last]
            value = shifted * sigmoid(shifted) * keep
            if first < ND:
                act_ref[t, :, first:last] = value.astype(BF16)
            else:
                mid_ref[t, :, first - ND : last - ND] = value.astype(BF16)
                shifted_in(shifts, t + 1, (first - ND, last - ND), value)
        return carry

    lax.fori_loop(0, frames, activate, 0)
    spread_all(shifts, ((im_wide, 0, B1A), (im_narrow, B1A, NM)))
    together, steps = step_frames(frames, rows)

    def convolve(i, carry):
        at = pl.ds(i * together, together)
        for im_ref, weight_ref, first, last in (
            (im_narrow, narrow_ref, 0, B2),
            (im_wide, wide_ref, B2, NB2),
        ):
            total = None
            for depth in range(3):
                value = im_ref[pl.ds(i * together + depth, together)]
                value = value.reshape(together * rows, value.shape[2])
                part = jnp.dot(value, weight_ref[depth], preferred_element_type=F32)
                total = part if total is None else total + part
            out_ref[at, :, first:last] = total.reshape(together, rows, last - first)
        return carry

    lax.fori_loop(0, steps, convolve, 0)
    masked_stats(out_ref, keep_ref, acc)
    put_stats(stat_ref, acc)


def second_level(totals, first_out, keep, params, peers):
    unused, conv_mid, conv_small, gain, bias = params
    frames, rows, unused = first_out.shape
    return call(
        second_body,
        [
            shape_of(frames, rows, ND, dtype=BF16),
            shape_of(frames, rows, NM, dtype=BF16),
            shape_of(frames, rows, NB2),
            shape_of(peers, 2, NB2),
            shape_of(3, NB1),
        ],
        [
            pltpu.VMEM((8, NB1), F32),
            pltpu.VMEM((3, frames + 2, rows + 2 * WP, NM), BF16),
            pltpu.VMEM((frames + 2, rows, 9 * B1A), BF16),
            pltpu.VMEM((frames + 2, rows, 9 * B2A), BF16),
            pltpu.VMEM((2, 8, NB2), F32),
        ],
        (
            totals,
            first_out,
            keep,
            gain,
            bias,
            conv_mid.reshape(3, 9 * B1A, B1),
            conv_small.reshape(3, 9 * B2A, B2),
        ),
        "second_level",
        20,
        flops=2 * frames * rows * 27 * (B1A * B1 + B2A * B2),
    )


def between_body(
    tot_ref,
    z_ref,
    keep_ref,
    gain_ref,
    bias_ref,
    act_ref,
    first_mom_ref,
    keep_next_ref,
    weight_ref,
    x_ref,
    z_next_ref,
    stat_ref,
    mom_ref,
    vec,
    pair,
    ordered,
    pool,
    between,
    acc,
):
    frames, rows, channels = x_ref.shape
    source_rows = z_ref.shape[1]
    high = source_rows // (2 * WP)
    put_moments(tot_ref, mom_ref, first_mom_ref[2:3, 0:NB2])
    second_rows(vec, gain_ref, bias_ref, mom_ref)
    turned_ordered(weight_ref, ordered)

    def pooling(t, carry):
        keeps = [keep_ref[2 * t], keep_ref[2 * t + 1]]
        keep_next = keep_next_ref[t].reshape(high, WP, 1)[:, 0 : WP // 2]
        for first, last in tiles_of(0, C5):
            total = None
            for step in range(2):
                if first < ND:
                    part = act_ref[2 * t + step, :, first:last].astype(F32)
                else:
                    at = slice(first - ND, last - ND)
                    shifted = z_ref[2 * t + step, :, at] * vec[0:1, at] + vec[1:2, at]
                    part = (shifted * sigmoid(shifted) * keeps[step]).astype(BF16).astype(F32)
                total = part if total is None else total + part
            width = last - first
            total = total.reshape(high, 2, WP, width).sum(1)
            pair[:, :, 0:width] = total
            mean = (
                pair[:, pl.ds(0, WP // 2, stride=2), :] + pair[:, pl.ds(1, WP // 2, stride=2), :]
            ) * 0.125
            mean = (mean.astype(BF16).astype(F32) * keep_next)[:, :, 0:width]
            mean = jnp.concatenate([mean, jnp.zeros_like(mean)], 1)
            x_ref[t, :, first:last] = mean.reshape(rows, width).astype(BF16)
        return carry

    lax.fori_loop(0, frames, pooling, 0)
    first_outputs(x_ref, ordered, 1, z_next_ref, pool, between)
    masked_stats(z_next_ref, keep_next_ref, acc)
    put_stats(stat_ref, acc, jnp.sum(keep_next_ref[...]))


def between_blocks(totals, second_out, keep, params, act, first_mom, keep_next, weight, peers):
    frames, rows = keep_next.shape[:2]
    high = second_out.shape[1] // (2 * WP)
    return call(
        between_body,
        [
            shape_of(frames, rows, C5, dtype=BF16),
            shape_of(frames, rows, NB1),
            shape_of(peers, 3, NB1),
            shape_of(2, NB2),
        ],
        [
            pltpu.VMEM((8, NB2), F32),
            pltpu.VMEM((high, WP, 128), F32),
            pltpu.VMEM((NB1, C5), BF16),
            pltpu.VMEM((frames, rows, B3), F32),
            pltpu.VMEM((frames + 2, rows, B3), F32),
            pltpu.VMEM((2, 8, NB1), F32),
        ],
        (totals, second_out, keep, params[3], params[4], act, first_mom, keep_next, weight),
        "between_blocks",
        10,
        flops=2 * frames * rows * C5 * NB1,
    )


def turn_body(
    index_ref,
    tot_ref,
    z_ref,
    keep_ref,
    gain_ref,
    bias_ref,
    act_ref,
    first_mom_ref,
    grad_ref,
    out_ref,
    slope_ref,
    direct_ref,
    stat_ref,
    mom_ref,
    vec,
    grad,
    result,
    acc,
):
    frames, rows, unused = z_ref.shape
    high = rows // WP
    width = grad_ref.shape[3]
    put_moments(tot_ref, mom_ref, first_mom_ref[2:3, 0:NB2])
    second_rows(vec, gain_ref, bias_ref, mom_ref)
    acc[...] = jnp.zeros_like(acc)
    grad[...] = jnp.zeros_like(grad)

    def frame(t, carry):
        keep = keep_ref[t]
        grad[:, 0:width, :] = grad_ref[0, t].astype(F32)
        upstream = grad[...].reshape(rows, C5)
        direct_ref[t, :, 0:B0] = upstream[:, 0:B0].astype(BF16)
        direct_ref[t, :, B0:ND] = upstream[:, C5 - B3 :].astype(BF16)
        result[:, :, 0:B0] = act_ref[t, :, 0:B0].astype(F32).reshape(high, WP, B0)
        result[:, :, C5 - B3 :] = act_ref[t, :, B0:ND].astype(F32).reshape(high, WP, B3)
        for inner, outer, size in SECOND_PIECES:
            at = slice(inner, inner + size)
            place = slice(B0 + outer, B0 + outer + size)
            value = z_ref[t, :, at]
            shifted = value * vec[0:1, at] + vec[1:2, at]
            gate = sigmoid(shifted)
            result[:, :, place] = (shifted * gate * keep).reshape(high, WP, size)
            slope = upstream[:, place] * keep * gate * (1.0 + shifted * (1.0 - gate))
            slope_ref[t, :, at] = slope
            acc[0, :, at] += rows_summed(slope)
            acc[1, :, at] += rows_summed(slope * (value * vec[2:3, at] + vec[3:4, at]))
        out_ref[t] = result[:, 0:width, :].astype(BF16)
        return carry

    lax.fori_loop(0, frames, frame, 0)
    put_stats(stat_ref, acc)


def turn(totals, second_out, keep, params, act, first_mom, cotangent, own_clip, peers):
    frames, rows, unused = second_out.shape
    high = rows // WP
    return call(
        turn_body,
        [
            shape_of(*cotangent.shape[1:], dtype=BF16),
            shape_of(frames, rows, NB2),
            shape_of(frames, rows, ND, dtype=BF16),
            shape_of(peers, 2, NB2),
            shape_of(2, NB2),
        ],
        [
            pltpu.VMEM((8, NB2), F32),
            pltpu.VMEM((high, WP, C5), F32),
            pltpu.VMEM((high, WP, C5), F32),
            pltpu.VMEM((2, 8, NB2), F32),
        ],
        (totals, second_out, keep, params[3], params[4], act, first_mom, cotangent),
        "turn",
        8,
        own_clip.reshape(1),
        {7: pl.BlockSpec((1,) + cotangent.shape[1:], lambda i, s: (s[0], 0, 0, 0, 0))},
    )


def upsampled(up_ref, t, first, last):
    value = up_ref[t // 2, :, first:last].astype(F32) * 0.125
    high = value.shape[0] // WP
    width = last - first
    value = value.reshape(high, 1, WP, width)
    return jnp.broadcast_to(value, (high, 2, WP, width)).reshape(2 * high * WP, width)


def second_gradient_body(
    tot_ref,
    slope_in,
    z_second,
    keep_ref,
    gain_ref,
    bias_ref,
    first_mom_ref,
    mom_ref,
    grad_ref,
    norm_ref,
    vec,
):
    frames, rows, unused = z_second.shape
    total = jnp.sum(tot_ref[...], axis=0)
    put_original(norm_ref, 0, total[1:2], SECOND_PIECES)
    put_original(norm_ref, 1, total[0:1], SECOND_PIECES)
    second_rows(vec, gain_ref, bias_ref, mom_ref)
    count = first_mom_ref[2:3, 0:NB2]
    cross = vec[0:1, :] * total[1:2] / count
    vec[6:7, :] = -(vec[0:1, :] * total[0:1] / count) - cross * vec[3:4, :]
    vec[7:8, :] = -cross * vec[2:3, :]

    def gradient(t, carry):
        keep = keep_ref[t]
        for first, last in tiles_of(0, NB2):
            at = slice(first, last)
            value = (
                slope_in[t, :, at] * vec[0:1, at]
                + z_second[t, :, at] * vec[7:8, at]
                + vec[6:7, at]
            ) * keep
            grad_ref[t, :, at] = value.astype(BF16)
        return carry

    lax.fori_loop(0, frames, gradient, 0)


def second_gradient(totals, slope, second_out, keep, params, first_mom, mom):
    frames, rows, unused = second_out.shape
    return call(
        second_gradient_body,
        [shape_of(frames, rows, NB2, dtype=BF16), shape_of(2, NB2)],
        [pltpu.VMEM((8, NB2), F32)],
        (totals, slope, second_out, keep, params[3], params[4], first_mom, mom),
        "second_gradient",
        8,
        flops=frames * rows * NB2 * 10,
    )


def back_conv_body(
    halved,
    start,
    grad_ref,
    z_first,
    keep_ref,
    gain_ref,
    bias_ref,
    first_mom_ref,
    direct_ref,
    wide_ref,
    narrow_ref,
    before_ref,
    slope_ref,
    stat_ref,
    acc,
    vec_first,
    shifts,
    windows,
    weights,
):
    frames, rows, unused = z_first.shape
    count = slope_ref.shape[0]
    first_rows(vec_first, gain_ref, bias_ref, first_mom_ref)
    clear_edges(shifts)
    weights[...] = jnp.zeros_like(weights)
    for depth in range(3):
        for place in range(9):
            source = 26 - (depth * 9 + place)
            weights[depth, 0:B1A, place * NB2 + B2 : (place + 1) * NB2] = wide_ref[source]
            weights[depth, B1A:NM, place * NB2 : place * NB2 + B2] = narrow_ref[source]
    low = 1 if start == 0 else 0
    high = count + 1 if start + count == frames else count + 2

    def shift(j, carry):
        for first, last in tiles_of(0, NB2):
            value = grad_ref[start - 1 + j, :, first:last].astype(F32)
            shifted_in(shifts, j, (first, last), value)
        return carry

    lax.fori_loop(low, high, shift, 0)
    for edge in [0] * low + [count + 1] * (count + 2 - high):
        windows[edge] = jnp.zeros(windows.shape[1:], BF16)
    spread_windows(shifts, ((windows, 0, NB2),), low, high)
    together, steps = step_frames(count, rows)

    def convolve(i, carry):
        at = pl.ds(i * together, together)
        total = None
        for depth in range(3):
            value = windows[pl.ds(i * together + depth, together)]
            value = value.reshape(together * rows, 9 * NB2)
            part = lax.dot_general(
                value, weights[depth], (((1,), (1,)), ((), ())), preferred_element_type=F32
            )
            total = part if total is None else total + part
        slope_ref[at, :, ND:NB1] = total.reshape(together, rows, NM)
        return carry

    lax.fori_loop(0, steps, convolve, 0)
    acc[...] = before_ref[...]

    def slopes(t, carry):
        frame = start + t
        keep = keep_ref[frame]
        for first, last in tiles_of(0, NB1):
            at = slice(first, last)
            value = z_first[frame, :, at]
            shifted = value * vec_first[0:1, at] + vec_first[1:2, at]
            gate = sigmoid(shifted)
            if first >= ND:
                upstream = slope_ref[t, :, at]
            elif halved:
                upstream = upsampled(direct_ref, frame, first, last)
            else:
                upstream = direct_ref[frame, :, at].astype(F32)
            slope = upstream * keep * gate * (1.0 + shifted * (1.0 - gate))
            slope_ref[t, :, at] = slope
            acc[0, :, at] += rows_summed(slope)
            acc[1, :, at] += rows_summed(slope * (value * vec_first[2:3, at] + vec_first[3:4, at]))
        return carry

    lax.fori_loop(0, count, slopes, 0)
    put_stats(stat_ref, acc)


def back_conv(grad, first_out, keep, params, first_mom, direct, halved, peers, part, before):
    unused, conv_mid, conv_small, gain, bias = params
    frames, rows, unused = first_out.shape
    start, count = part
    return call(
        functools.partial(back_conv_body, halved, start),
        [
            shape_of(count, rows, NB1),
            shape_of(peers, 2, NB1),
            shape_of(2, 8, NB1),
        ],
        [
            pltpu.VMEM((8, NB1), F32),
            pltpu.VMEM((3, count + 2, rows + 2 * WP, NB2), BF16),
            pltpu.VMEM((count + 2, rows, 9 * NB2), BF16),
            pltpu.VMEM((3, NM, 9 * NB2), BF16),
        ],
        (grad, first_out, keep, gain, bias, first_mom, direct, conv_mid, conv_small, before),
        "back_conv",
        30,
        flops=2 * count * rows * 27 * (B1A * B1 + B2A * B2),
    )


def conv_grad_body(
    section_ref, mid_ref, grad_ref, kept_ref, sent_ref, shifts, im_wide, im_narrow, turned, packed_ref
):
    frames, rows, unused = mid_ref.shape
    clear_edges(shifts)

    def shift(t, carry):
        for first, last in tiles_of(0, NM):
            shifted_in(shifts, t + 1, (first, last), mid_ref[t, :, first:last].astype(F32))
        return carry

    lax.fori_loop(0, frames, shift, 0)
    spread_all(shifts, ((im_wide, 0, B1A), (im_narrow, B1A, NM)))
    turned[...] = grad_ref[...].reshape(frames * rows, NB2).T
    step = 9 * B1A
    half = 27 * B1A // 2
    tail = 54 * B1A
    used = CONV_NARROW + 27 * B2A
    packed_ref[used:, :] = jnp.zeros((packed_ref.shape[0] - used, 128), BF16)
    for depth in range(3):
        value = im_wide[depth : depth + frames].reshape(frames * rows, step)
        part = jnp.dot(turned[B2:NB2, :], value, preferred_element_type=F32)
        part = part.T.astype(BF16)
        packed_ref[depth * step : (depth + 1) * step, :] = part[:, 0:128]
        packed_ref[27 * B1A + depth * step : 27 * B1A + (depth + 1) * step, :] = part[:, 128:256]
        low = max(0, min(step, half - depth * step))
        if low > 0:
            packed_ref[tail + depth * step : tail + depth * step + low, 0:64] = part[:low, 256:B1]
        if low < step:
            start = tail + depth * step + low - half
            packed_ref[start : start + step - low, 64:128] = part[low:, 256:B1]
        value = im_narrow[depth : depth + frames].reshape(frames * rows, 9 * B2A)
        part = jnp.dot(turned[0:B2, :], value, preferred_element_type=F32)
        start = CONV_NARROW + depth * 9 * B2A
        packed_ref[start : start + 9 * B2A, :] = part.T.astype(BF16)
    put_halves(section_ref, packed_ref, kept_ref, sent_ref)


def put_halves(section_ref, packed_ref, kept_ref, sent_ref):
    half = packed_ref.shape[0] // 2
    section = section_ref[0]
    kept_ref[...] = packed_ref[pl.ds(pl.multiple_of(section * half, 16), half), :]
    sent_ref[...] = packed_ref[pl.ds(pl.multiple_of((1 - section) * half, 16), half), :]


def conv_grad(mid, grad, section, peers):
    frames, rows, unused = mid.shape
    packed = conv_rows(peers)
    return call(
        conv_grad_body,
        [shape_of(packed // 2, 128, dtype=BF16)] * 2,
        [
            pltpu.VMEM((3, frames + 2, rows + 2 * WP, NM), BF16),
            pltpu.VMEM((frames + 2, rows, 9 * B1A), BF16),
            pltpu.VMEM((frames + 2, rows, 9 * B2A), BF16),
            pltpu.VMEM((NB2, frames * rows), BF16),
            pltpu.VMEM((packed, 128), BF16),
        ],
        (mid, grad),
        "conv_grad",
        22,
        section,
        {},
        2 * frames * rows * 27 * (B1A * B1 + B2A * B2),
    )


def first_gradient(
    tot_ref, slope_refs, z_ref, keep_ref, vec, count, grad_ref, pool_ref, between_ref
):
    total = jnp.sum(tot_ref[...], axis=0)
    cross = vec[0:1, :] * total[1:2] / count
    vec[6:7, :] = -(vec[0:1, :] * total[0:1] / count) - cross * vec[3:4, :]
    vec[7:8, :] = -cross * vec[2:3, :]
    begin = 0
    for slope_ref in slope_refs:

        def gradient(t, carry, begin=begin, slope_ref=slope_ref):
            keep = keep_ref[begin + t]
            for first, last in tiles_of(0, NB1):
                at = slice(first, last)
                value = (
                    slope_ref[t, :, at] * vec[0:1, at]
                    + z_ref[begin + t, :, at] * vec[7:8, at]
                    + vec[6:7, at]
                ) * keep
                if first == B0:
                    pool_ref[begin + t] = value
                else:
                    grad_ref[begin + t, :, at] = value.astype(BF16)
            return carry

        lax.fori_loop(0, slope_ref.shape[0], gradient, 0)
        begin += slope_ref.shape[0]

    def put(t, value):
        grad_ref[t, :, B0:ND] = value.astype(BF16)

    window_sums(pool_ref, between_ref, put)
    return total


def last_gradient_body(
    tot_ref,
    low_ref,
    high_ref,
    z_ref,
    keep_ref,
    gain_ref,
    bias_ref,
    mom_ref,
    grad_ref,
    norm_ref,
    vec,
    pool,
    between,
):
    first_rows(vec, gain_ref, bias_ref, mom_ref)
    total = first_gradient(
        tot_ref, (low_ref, high_ref), z_ref, keep_ref, vec, mom_ref[2:3, :], grad_ref, pool, between
    )
    put_original(norm_ref, 0, total[1:2], FIRST_PIECES)
    put_original(norm_ref, 1, total[0:1], FIRST_PIECES)


def last_gradient(totals, slopes, first_out, keep, params, mom):
    frames, rows, unused = first_out.shape
    return call(
        last_gradient_body,
        [shape_of(frames, rows, NB1, dtype=BF16), shape_of(2, NB1)],
        [
            pltpu.VMEM((8, NB1), F32),
            pltpu.VMEM((frames, rows, B3), F32),
            pltpu.VMEM((frames + 2, rows, B3), F32),
        ],
        (totals, *slopes, first_out, keep, params[3], params[4], mom),
        "last_gradient",
        12,
        flops=frames * rows * NB1 * 10,
    )


def clip_gradient_body(grad_ref, keep_ref, weight_ref, du_ref, ordered):
    frames, rows, unused = grad_ref.shape
    width, channels = du_ref.shape[2:]
    weight_ordered(weight_ref, ordered, ((0, 0, channels),))
    together, steps = step_frames(frames, rows)

    def product(i, carry):
        at = pl.ds(i * together, together)
        value = grad_ref[at].reshape(together * rows, NB1)
        out = lax.dot_general(
            value, ordered[...], (((1,), (1,)), ((), ())), preferred_element_type=F32
        )
        out = out.reshape(together, rows, channels) * keep_ref[at]
        out = out.reshape(together, rows // WP, WP, channels)[:, :, 0:width, :]
        du_ref[at] = out.astype(BF16)
        return carry

    lax.fori_loop(0, steps, product, 0)


def clip_gradient(grad, keep, inproj, width):
    frames, rows, unused = grad.shape
    channels = inproj.shape[0]
    return call(
        clip_gradient_body,
        [shape_of(frames, rows // WP, width, channels, dtype=BF16)],
        [pltpu.VMEM((channels, NB1), BF16)],
        (grad, keep, inproj),
        "clip_gradient",
        6,
        flops=2 * frames * rows * channels * NB1,
    )[0]


def back_between_body(
    tot_ref,
    slope_ref,
    z_ref,
    keep_ref,
    gain_ref,
    bias_ref,
    mom_ref,
    weight_ref,
    z_prev,
    keep_prev,
    gain_prev,
    bias_prev,
    mom_prev,
    up_ref,
    grad_ref,
    slope_prev,
    stat_ref,
    norm_ref,
    vec,
    vec_prev,
    ordered,
    pool,
    between,
    double,
    acc,
):
    frames, rows, unused = z_ref.shape
    high = rows // WP
    first_rows(vec, gain_ref, bias_ref, mom_ref)
    second_rows(vec_prev, gain_prev, bias_prev, mom_prev)
    total = first_gradient(
        tot_ref, (slope_ref,), z_ref, keep_ref, vec, mom_ref[2:3, :], grad_ref, pool, between
    )
    put_original(norm_ref, 0, total[1:2], FIRST_PIECES)
    put_original(norm_ref, 1, total[0:1], FIRST_PIECES)
    turned_ordered(weight_ref, ordered)
    together, steps = step_frames(frames, rows)

    def product(i, carry):
        value = grad_ref[pl.ds(i * together, together)].reshape(together * rows, NB1)
        out = lax.dot_general(
            value, ordered[...], (((1,), (0,)), ((), ())), preferred_element_type=F32
        )
        out = out.reshape(together, rows, C5)
        for inner in range(together):
            t = i * together + inner
            keep = keep_ref[t]
            for first, last in tiles_of(0, C5):
                width = last - first
                value = (out[inner, :, first:last] * keep).astype(BF16).astype(F32)
                value = value.reshape(high, WP, width)[:, 0 : WP // 2, :]
                double[:, pl.ds(0, WP // 2, stride=2), :] = jnp.pad(
                    value, ((0, 0), (0, 0), (0, 128 - width))
                )
                double[:, pl.ds(1, WP // 2, stride=2), :] = jnp.pad(
                    value, ((0, 0), (0, 0), (0, 128 - width))
                )
                up_ref[t, :, first:last] = double[...].reshape(rows, 128)[:, 0:width].astype(BF16)
        return carry

    lax.fori_loop(0, steps, product, 0)
    acc[...] = jnp.zeros_like(acc)

    def slopes(t, carry):
        keep = keep_prev[t]
        for first, last in tiles_of(0, NB2):
            at = slice(first, last)
            value = z_prev[t, :, at]
            shifted = value * vec_prev[0:1, at] + vec_prev[1:2, at]
            gate = sigmoid(shifted)
            upstream = upsampled(up_ref, t, ND + first, ND + last)
            slope = upstream * keep * gate * (1.0 + shifted * (1.0 - gate))
            slope_prev[t, :, at] = slope
            acc[0, :, at] += rows_summed(slope)
            acc[1, :, at] += rows_summed(slope * (value * vec_prev[2:3, at] + vec_prev[3:4, at]))
        return carry

    lax.fori_loop(0, z_prev.shape[0], slopes, 0)
    put_stats(stat_ref, acc)


def back_between(
    totals, slope, first_out, keep, params, mom, second_prev, keep_prev, params_prev, mom_prev, peers
):
    inproj, unused, unused, gain, bias = params
    frames, rows, unused = first_out.shape
    return call(
        back_between_body,
        [
            shape_of(frames, rows, C5, dtype=BF16),
            shape_of(frames, rows, NB1, dtype=BF16),
            shape_of(*second_prev.shape),
            shape_of(peers, 2, NB2),
            shape_of(2, NB1),
        ],
        [
            pltpu.VMEM((8, NB1), F32),
            pltpu.VMEM((8, NB2), F32),
            pltpu.VMEM((NB1, C5), BF16),
            pltpu.VMEM((frames, rows, B3), F32),
            pltpu.VMEM((frames + 2, rows, B3), F32),
            pltpu.VMEM((rows // WP, WP, 128), F32),
            pltpu.VMEM((2, 8, NB2), F32),
        ],
        (
            totals,
            slope,
            first_out,
            keep,
            gain,
            bias,
            mom,
            inproj,
            second_prev,
            keep_prev,
            params_prev[3],
            params_prev[4],
            mom_prev,
        ),
        "back_between",
        12,
        flops=2 * frames * rows * C5 * NB1,
    )


def inproj_rows(channels):
    first = -(-channels // 32) * 16
    return first, 4 * channels + first


def inproj_grad_body(
    row_pieces, section_ref, x_ref, grad_ref, kept_ref, sent_ref, product, ordered, packed_ref
):
    frames, rows, channels = x_ref.shape
    first, used = inproj_rows(channels)
    padded = packed_ref.shape[0]
    product[...] = lax.dot_general(
        x_ref[...].reshape(frames * rows, channels),
        grad_ref[...].reshape(frames * rows, NB1),
        (((0,), (0,)), ((), ())),
        preferred_element_type=F32,
    ).astype(product.dtype)
    for row_to, row_from, height in row_pieces:
        for inner, outer, width in FIRST_PIECES:
            ordered[row_from : row_from + height, outer : outer + width] = product[
                row_to : row_to + height, inner : inner + width
            ]
    for place in range(4):
        packed_ref[place * channels : (place + 1) * channels, :] = ordered[
            :, place * 128 : (place + 1) * 128
        ]
    start = 4 * channels
    packed_ref[start : start + first, 0:64] = ordered[0:first, 512:NB1]
    packed_ref[start : start + channels - first, 64:128] = ordered[first:channels, 512:NB1]
    if 2 * first > channels:
        packed_ref[start + channels - first : start + first, 64:128] = jnp.zeros(
            (2 * first - channels, 64), packed_ref.dtype
        )
    if padded > used:
        packed_ref[used:padded, :] = jnp.zeros((padded - used, 128), packed_ref.dtype)
    put_halves(section_ref, packed_ref, kept_ref, sent_ref)


def inproj_grad(x, grad, row_pieces, section, peers, dtype=BF16):
    frames, rows, channels = x.shape
    packed = padded_rows(inproj_rows(channels)[1], peers)
    return call(
        functools.partial(inproj_grad_body, row_pieces),
        [shape_of(packed // 2, 128, dtype=dtype)] * 2,
        [
            pltpu.VMEM((channels, NB1), dtype),
            pltpu.VMEM((channels, NB1), dtype),
            pltpu.VMEM((packed, 128), dtype),
        ],
        (x, grad),
        "inproj_grad",
        14,
        section,
        {},
        2 * frames * rows * channels * NB1,
    )


def unpack_conv(packed_ref, wide_ref, narrow_ref):
    step = 27 * B1A
    half = step // 2
    wide_ref[:, 0:128] = packed_ref[0:step, :].astype(F32)
    wide_ref[:, 128:256] = packed_ref[step : 2 * step, :].astype(F32)
    wide_ref[0:half, 256:B1] = packed_ref[2 * step : 2 * step + half, 0:64].astype(F32)
    wide_ref[half:step, 256:B1] = packed_ref[2 * step : 2 * step + half, 64:128].astype(F32)
    narrow_ref[...] = packed_ref[CONV_NARROW : CONV_NARROW + 27 * B2A, :].astype(F32)


def unpack_inproj(packed_ref, out_ref):
    channels = out_ref.shape[0]
    first = inproj_rows(channels)[0]
    for place in range(4):
        out_ref[:, place * 128 : (place + 1) * 128] = packed_ref[
            place * channels : (place + 1) * channels, :
        ].astype(F32)
    start = 4 * channels
    out_ref[0:first, 512:NB1] = packed_ref[start : start + first, 0:64].astype(F32)
    out_ref[first:channels, 512:NB1] = packed_ref[start : start + channels - first, 64:128].astype(
        F32
    )


def unpack_alone_body(section_ref, value_ref, got_ref, wide_ref, narrow_ref, packed_ref):
    half = value_ref.shape[0]
    section = section_ref[0]
    packed_ref[pl.ds(pl.multiple_of(section * half, 16), half), :] = value_ref[...]
    packed_ref[pl.ds(pl.multiple_of((1 - section) * half, 16), half), :] = got_ref[...]
    unpack_conv(packed_ref, wide_ref, narrow_ref)


def unpack_alone(value, got, section):
    return call(
        unpack_alone_body,
        [shape_of(27 * B1A, B1), shape_of(27 * B2A, B2)],
        [pltpu.VMEM((2 * value.shape[0], 128), BF16)],
        (value, got),
        "unpack_alone",
        14,
        section,
        {},
    )


def halves_placed(section_ref, value_ref, got_ref, pieces):
    section = section_ref[0]
    for half_ref, half in ((value_ref, section), (got_ref, 1 - section)):
        for packed_ref, first, last in pieces:
            size = last - first
            packed_ref[pl.ds(pl.multiple_of(half * size, 16), size), :] = half_ref[first:last, :]


def unpack_joined_body(
    section_ref, value_ref, got_ref, wide_ref, narrow_ref, next_ref, conv_packed, next_packed, next_out
):
    half = conv_packed.shape[0] // 2
    halves_placed(
        section_ref,
        value_ref,
        got_ref,
        ((conv_packed, 0, half), (next_packed, half, value_ref.shape[0])),
    )
    unpack_conv(conv_packed, wide_ref, narrow_ref)
    unpack_inproj(next_packed, next_out)
    next_ref[...] = next_out[...].T


def unpack_joined(value, got, section, channels, peers):
    return call(
        unpack_joined_body,
        [shape_of(27 * B1A, B1), shape_of(27 * B2A, B2), shape_of(NB1, channels)],
        [
            pltpu.VMEM((conv_rows(peers), 128), BF16),
            pltpu.VMEM((padded_rows(inproj_rows(channels)[1], peers), 128), BF16),
            pltpu.VMEM((channels, NB1), F32),
        ],
        (value, got),
        "unpack_joined",
        32,
        section,
        {},
    )


def unpack_inproj_body(section_ref, value_ref, got_ref, out_ref, packed):
    halves_placed(section_ref, value_ref, got_ref, ((packed, 0, value_ref.shape[0]),))
    unpack_inproj(packed, out_ref)


def unpack_inproj_alone(value, got, section, channels):
    return call(
        unpack_inproj_body,
        [shape_of(channels, NB1)],
        [pltpu.VMEM((2 * value.shape[0], 128), BF16)],
        (value, got),
        "unpack_inproj",
        12,
        section,
        {},
    )[0]


def sent_to_all(spread):
    return lax.all_to_all(spread, "dp", 0, 0)


def swapped(value):
    return lax.ppermute(value, "section", [(0, 1), (1, 0)])


def distances_of():
    distances = []
    while 2 ** len(distances) < lax.axis_size("dp"):
        distances.append(2 ** len(distances))
    return list(zip(distances, [distances[1], distances[0]] + distances[2:]))


def exchanged(value, pair):
    count = lax.axis_size("dp")
    links = [
        (section * count + place, section * count + (place ^ pair[section]))
        for section in range(2)
        for place in range(count)
    ]
    return lax.ppermute(value, ("section", "dp"), links)


def upper_half(pair):
    place = lax.axis_index("dp")
    distance = jnp.where(lax.axis_index("section") == 0, pair[0], pair[1])
    return ((place // distance) % 2).astype(jnp.int32).reshape(1)


def added(kept, got):
    return (kept.astype(F32) + got.astype(F32)).astype(kept.dtype)


def split_sum_body(upper_ref, kept_ref, got_ref, left_ref, sent_ref):
    half = left_ref.shape[0]
    upper = upper_ref[0]
    for target, which in ((left_ref, upper), (sent_ref, 1 - upper)):
        at = pl.ds(pl.multiple_of(which * half, 16), half)
        target[...] = added(kept_ref[at, :], got_ref[at, :])


def split_sum(kept, got, pair):
    half = shape_of(kept.shape[0] // 2, 128, dtype=kept.dtype)
    return call(
        split_sum_body, [half, half], [], (kept, got), "split_sum", 6, upper_half(pair), {}
    )


def placed_body(upper_ref, value_ref, got_ref, out_ref):
    half = value_ref.shape[0]
    upper = upper_ref[0]
    out_ref[pl.ds(pl.multiple_of(upper * half, 16), half), :] = value_ref[...]
    out_ref[pl.ds(pl.multiple_of((1 - upper) * half, 16), half), :] = got_ref[...]


def placed(value, got, pair):
    whole = shape_of(value.shape[0] * 2, 128, dtype=value.dtype)
    return call(
        placed_body, [whole], [], (value, got), "placed", 6, upper_half(pair), {}
    )[0]


class Scatter:
    def __init__(self, kept, sent):
        self.kept = kept
        self.pairs = distances_of()
        self.place = 0
        self.got = swapped(sent)

    def step(self):
        pair = self.pairs[self.place]
        self.kept, sent = split_sum(self.kept, self.got, pair)
        self.got = exchanged(sent, pair)
        self.place += 1

    def result(self):
        while self.place < len(self.pairs):
            self.step()
        return added(self.kept, self.got)


class Gather:
    def __init__(self, value):
        self.value = value
        self.pairs = distances_of()[::-1]
        self.place = 0
        self.got = exchanged(value, self.pairs[0])

    def step(self):
        self.value = placed(self.value, self.got, self.pairs[self.place])
        self.place += 1
        if self.place < len(self.pairs):
            self.got = exchanged(self.value, self.pairs[self.place])
        else:
            self.got = swapped(self.value)

    def result(self):
        while self.place < len(self.pairs):
            self.step()
        return self.value, self.got


def lockstep(one, other):
    one.got, other.got = lax.optimization_barrier((one.got, other.got))


def tied(value, *exchanges):
    both = lax.optimization_barrier((value,) + tuple(e.got for e in exchanges))
    for exchange, got in zip(exchanges, both[1:]):
        exchange.got = got
    return both[0]


def halves_exchanged(mine, section, own_clip):
    half = mine.shape[0] // 2
    kept = lax.dynamic_slice_in_dim(mine, section * half, half, 0)
    sent = lax.dynamic_slice_in_dim(mine, (1 - section) * half, half, 0)
    got = swapped(sent)
    own_first = own_clip == 0
    return jnp.stack([jnp.where(own_first, kept, got), jnp.where(own_first, got, kept)])


def level_first(rows):
    return jnp.concatenate(
        [rows[..., inner : inner + width] for inner, outer, width in sorted(FIRST_PIECES, key=lambda p: p[1])],
        -1,
    )


def level_second(rows):
    return jnp.concatenate(
        [rows[..., inner : inner + width] for inner, outer, width in sorted(SECOND_PIECES, key=lambda p: p[1])],
        -1,
    )


def local(
    clips_in,
    frames,
    voxel_mask,
    micro_order,
    inproj_4f,
    conv_mid_4f,
    conv_small_4f,
    gain_4f,
    bias_4f,
    inproj_5b,
    conv_mid_5b,
    conv_small_5b,
    gain_5b,
    bias_5b,
    cotangent,
):
    section = lax.axis_index("section")
    peers = lax.axis_size("dp")
    own_clip = micro_order[0, section]
    which = section.astype(jnp.int32).reshape(1)
    depth, height, width = clips_in.shape[1:4]

    frame_index = jnp.arange(depth, dtype=jnp.int32)
    own_frames = lax.dynamic_index_in_dim(frames, own_clip, 0, False)
    own_mask = lax.dynamic_index_in_dim(voxel_mask, own_clip, 0, False)
    keep = jnp.where(frame_index[:, None, None] < own_frames, own_mask, 0).astype(F32)
    paired = keep.reshape(depth // 2, 2, height // 2, 2, width // 2, 2)
    keep_next = jnp.max(paired, axis=(1, 3, 5))

    def laid_out(mask):
        padded = jnp.pad(mask, ((0, 0), (0, 0), (0, WP - mask.shape[2])))
        return padded.reshape(mask.shape[0], mask.shape[1] * WP, 1)

    keep, keep_next = laid_out(keep), laid_out(keep_next)
    first = (inproj_4f, conv_mid_4f, conv_small_4f, gain_4f.reshape(1, NB), bias_4f.reshape(1, NB))
    second = (inproj_5b.T, conv_mid_5b, conv_small_5b, gain_5b.reshape(1, NB), bias_5b.reshape(1, NB))

    x_a, z1_a, stat = project_first(clips_in, own_clip, keep, inproj_4f, peers)
    act_a, mid_a, z2_a, stat, mom1_a = second_level(sent_to_all(stat), z1_a, keep, first, peers)
    x_b, z1_b, stat, mom2_a = between_blocks(
        sent_to_all(stat), z2_a, keep, first, act_a, mom1_a, keep_next, second[0], peers
    )
    act_b, mid_b, z2_b, stat, mom1_b = second_level(
        sent_to_all(stat), z1_b, keep_next, second, peers
    )
    result, slope, direct, stat, mom2_b = turn(
        sent_to_all(stat), z2_b, keep_next, second, act_b, mom1_b, cotangent, own_clip, peers
    )
    dz2_b, norm2_b = second_gradient(
        sent_to_all(stat), slope, z2_b, keep_next, second, mom1_b, mom2_b
    )
    kept, sent = conv_grad(mid_b, dz2_b, which, peers)
    dz2_b, sent = lax.optimization_barrier((dz2_b, sent))
    sum_b = Scatter(kept, sent)
    nothing = jnp.zeros((2, 8, NB1), F32)
    slope, stat, unused = back_conv(
        dz2_b, z1_b, keep_next, second, mom1_b, direct, False, peers, (0, depth // 2), nothing
    )
    stat = tied(stat, sum_b)
    sum_b.step()
    totals = sent_to_all(stat)
    totals = tied(totals, sum_b)
    sum_b.step()
    up, dz1_b, slope, stat, norm1_b = back_between(
        totals, slope, z1_b, keep_next, second, mom1_b, z2_a, keep, first, mom2_a, peers
    )
    stat = tied(stat, sum_b)
    sum_b.step()
    totals = sent_to_all(stat)
    inproj_halves = inproj_grad(x_b, dz1_b, RESULT_PIECES, which, peers)
    totals = tied(totals, sum_b)
    sum_b.step()
    dz2_a, norm2_a = second_gradient(totals, slope, z2_a, keep, first, mom1_a, mom2_a)
    conv_halves = conv_grad(mid_a, dz2_a, which, peers)
    kept, sent = [jnp.concatenate(pair) for pair in zip(conv_halves, inproj_halves)]
    dz2_a, sent = lax.optimization_barrier((dz2_a, sent))
    sum_a = Scatter(kept, sent)
    dz2_a = tied(dz2_a, sum_b)
    gather_b = Gather(sum_b.result())
    half = depth // 2
    slope_low, unused, part = back_conv(
        dz2_a, z1_a, keep, first, mom1_a, up, True, peers, (0, half), nothing
    )
    part = tied(part, sum_a, gather_b)
    sum_a.step()
    gather_b.step()
    slope_high, stat, unused = back_conv(
        dz2_a, z1_a, keep, first, mom1_a, up, True, peers, (half, depth - half), part
    )
    stat = tied(stat, sum_a, gather_b)
    sum_a.step()
    gather_b.step()
    totals = sent_to_all(stat)
    totals = tied(totals, sum_a, gather_b)
    sum_a.step()
    gather_b.step()
    dz1_a, norm1_a = last_gradient(totals, (slope_low, slope_high), z1_a, keep, first, mom1_a)
    sum_i = Scatter(*inproj_grad(x_a, dz1_a, ((0, 0, x_a.shape[2]),), which, peers, F32))
    dz1_a = tied(dz1_a, sum_a, gather_b)
    sum_a.step()
    gather_b.step()
    du = clip_gradient(dz1_a, keep, inproj_4f, width)
    du = tied(du, sum_a, sum_i, gather_b)
    gather_a = Gather(sum_a.result())

    conv_b = unpack_alone(*gather_b.result(), which)
    while sum_i.place < len(sum_i.pairs):
        sum_i.step()
        gather_a.step()
        lockstep(gather_a, sum_i)
    gather_i = Gather(sum_i.result().astype(BF16))
    wide_a, narrow_a, inproj_b = unpack_joined(
        *gather_a.result(), which, inproj_5b.shape[0], peers
    )
    inproj_a = unpack_inproj_alone(*gather_i.result(), which, inproj_4f.shape[0])

    block_out = halves_exchanged(result, section, own_clip)
    clips_grad = halves_exchanged(du, section, own_clip)
    small = jnp.stack(
        [
            jnp.concatenate([level_first(mom1_a[:2]), level_second(mom2_a)], -1),
            jnp.concatenate([level_first(mom1_b[:2]), level_second(mom2_b)], -1),
            jnp.concatenate([norm1_a, norm2_a], -1),
            jnp.concatenate([norm1_b, norm2_b], -1),
        ]
    )
    other = swapped(small)
    ordered = jnp.where(section == 0, jnp.stack([small, other]), jnp.stack([other, small]))
    norms = ordered[0] + ordered[1]
    return (
        block_out,
        clips_grad,
        inproj_a,
        wide_a.reshape(conv_mid_4f.shape),
        narrow_a.reshape(conv_small_4f.shape),
        norms[2],
        ordered[:, 0],
        inproj_b.T,
        conv_b[0].reshape(conv_mid_5b.shape),
        conv_b[1].reshape(conv_small_5b.shape),
        norms[3],
        ordered[:, 1],
    )


def solution(mesh):
    placed = (
        P("dp", None, None, None, None),
        P("dp"),
        P("dp", None, None, None),
        P("dp", None),
        P(),
        P(),
        P(),
        P(),
        P(),
        P(),
        P(),
        P(),
        P(),
        P(),
        P("dp", None, None, None, None),
    )
    return jax.shard_map(
        local,
        mesh=mesh,
        in_specs=placed,
        out_specs=(
            P("dp", "section", None, None, None),
            P("dp", "section", None, None, None),
            P(),
            P(),
            P(),
            P(),
            P(),
            P(),
            P(),
            P(),
            P(),
            P(),
        ),
        check_vma=False,
    )
```

```python
import functools

import jax
import jax.numpy as jnp
from jax import lax
from jax.experimental import pallas as pl
from jax.experimental.pallas import tpu as pltpu
from jax.sharding import PartitionSpec as P

B0 = 256
B1A = 160
B1 = 320
B2A = 32
B2 = 128
B3 = 128
C5 = 832
NX = 448
NB1 = 576
NB = 1024
NB2 = NB - NB1
NM = B1A + B2A
ND = B0 + B3

EPSILON = 0.001
F32 = jnp.float32
BF16 = jnp.bfloat16

FIRST_PIECES = ((0, 0, B0), (B0, NX, B3), (ND, B0, NM))
SECOND_PIECES = ((0, B1, B2), (B2, 0, B1))
RESULT_PIECES = ((0, 0, B0), (B0, C5 - B3, B3), (ND, B0 + B1, B2), (ND + B2, B0, B1))

CONV_NARROW = 10800
DMA = pltpu.SemaphoreType.DMA


def padded_rows(rows, peers):
    whole = 32 * peers
    return -(-rows // whole) * whole


def conv_rows(peers):
    return padded_rows(CONV_NARROW + 27 * B2A, peers)


def shape_of(*dims, dtype=F32):
    return jax.ShapeDtypeStruct(dims, dtype)


def tiles_of(start, stop):
    return [(first, min(first + 128, stop)) for first in range(start, stop, 128)]


def whole_block(shape):
    return pl.BlockSpec(shape, lambda *unused: (0,) * len(shape))


def call(body, outs, out_spaces, scratch, args, spaces, name, scalars=(), flops=0, mib=12):
    def spec(array, space):
        return whole_block(array.shape) if space == "v" else pl.BlockSpec(memory_space=pltpu.HBM)

    assert len(args) == len(spaces) and len(outs) == len(out_spaces)
    return pl.pallas_call(
        body,
        out_shape=[
            pltpu.HBM(o.shape, o.dtype) if s == "a" else o for o, s in zip(outs, out_spaces)
        ],
        grid_spec=pltpu.PrefetchScalarGridSpec(
            num_scalar_prefetch=len(scalars),
            grid=(1,),
            in_specs=[spec(a, s) for a, s in zip(args, spaces)],
            out_specs=[spec(o, s) for o, s in zip(outs, out_spaces)],
            scratch_shapes=scratch,
        ),
        compiler_params=pltpu.CompilerParams(vmem_limit_bytes=mib * 2**20),
        cost_estimate=pl.CostEstimate(
            flops=flops,
            transcendentals=0,
            bytes_accessed=sum(a.size * a.dtype.itemsize for a in list(args) + list(outs)),
        ),
        name=name,
    )(
        *scalars,
        *[
            pltpu.with_memory_space_constraint(a, pltpu.HBM) if s == "a" else a
            for a, s in zip(args, spaces)
        ],
    )


class Planes:
    def __init__(self, source, target, sem, start=0):
        self.source, self.target, self.sem, self.start_at = source, target, sem, start

    def copy(self, h):
        return pltpu.make_async_copy(
            self.source.at[h + self.start_at], self.target.at[h], self.sem.at[h]
        )

    def start(self, h):
        self.copy(h).start()

    def wait(self, h):
        self.copy(h).wait()

    def start_all(self):
        for h in range(self.sem.shape[0]):
            self.start(h)

    def wait_all(self):
        for h in range(self.sem.shape[0]):
            self.wait(h)


class Outwards(Planes):
    def copy(self, h):
        return pltpu.make_async_copy(
            self.source.at[h], self.target.at[h + self.start_at], self.sem.at[h]
        )


def sigmoid(value):
    return 0.5 * jnp.tanh(0.5 * value) + 0.5


def rows_summed(value):
    return value.reshape(value.shape[0] // 8, 8, value.shape[1]).sum(0)


def put_permuted(target, row, source, pieces, offset=0):
    for inner, outer, width in pieces:
        target[row : row + 1, inner : inner + width] = source[
            :, offset + outer : offset + outer + width
        ]


def put_original(target, row, value, pieces):
    for inner, outer, width in pieces:
        target[row : row + 1, outer : outer + width] = value[:, inner : inner + width]


def put_stats(stat_ref, acc_ref, count=None):
    peers, rows, width = stat_ref.shape
    for row in range(2):
        line = jnp.sum(acc_ref[row], axis=0, keepdims=True)
        stat_ref[:, row : row + 1, :] = jnp.broadcast_to(line[None], (peers, 1, width))
    if count is not None:
        stat_ref[:, 2:3, :] = jnp.broadcast_to(count.reshape(1, 1, 1), (peers, 1, width))


def plane_stats(value_ref, h, keep, acc_ref):
    for first, last in tiles_of(0, value_ref.shape[2]):
        value = value_ref[h, :, first:last]
        masked = value * keep
        acc_ref[0, :, first:last] += rows_summed(masked)
        acc_ref[1, :, first:last] += rows_summed(masked * value)


def times_of(rows, width, extent):
    return lax.broadcasted_iota(jnp.int32, (rows, width), 0) & (extent - 1)


def time_shifted(value, times, extent):
    rows = value.shape[0]
    earlier = jnp.where(times != 0, pltpu.roll(value, 1, 0), 0.0)
    later = jnp.where(times != extent - 1, pltpu.roll(value, rows - 1, 0), 0.0)
    return earlier, value, later


def width_shifted(value, extent):
    rows = value.shape[0]
    if extent % 8 == 0:
        edge = jnp.zeros((extent, value.shape[1]), value.dtype)
        left = jnp.concatenate([edge, value[:-extent]], 0)
        right = jnp.concatenate([value[extent:], edge], 0)
    else:
        left = pltpu.roll(value, extent, 0)
        right = pltpu.roll(value, rows - extent, 0)
    return left, value, right


def window_sums(source_ref, between_ref, extent, put):
    planes, rows, width = source_ref.shape
    between_ref[0] = jnp.zeros((rows, width), F32)
    between_ref[planes + 1] = jnp.zeros((rows, width), F32)
    times = times_of(rows, width, extent)

    def plane(h, carry):
        before, here, after = time_shifted(source_ref[h], times, extent)
        left, here, right = width_shifted(before + here + after, extent)
        between_ref[h + 1] = left + here + right
        return carry

    lax.fori_loop(0, planes, plane, 0)

    def through(h, carry):
        put(h, (between_ref[h] + between_ref[h + 1] + between_ref[h + 2]) * (1.0 / 27.0))
        return carry

    lax.fori_loop(0, planes, through, 0)


def turned_ordered(turned_ref, ordered_ref):
    for row_to, row_from, height in FIRST_PIECES:
        for inner, outer, width in RESULT_PIECES:
            ordered_ref[row_to : row_to + height, inner : inner + width] = turned_ref[
                row_from : row_from + height, outer : outer + width
            ]


def weight_ordered(weight_ref, ordered_ref):
    for inner, outer, width in FIRST_PIECES:
        ordered_ref[:, inner : inner + width] = weight_ref[:, outer : outer + width]


def step_planes(planes):
    return (planes // 2, 2) if planes % 2 == 0 else (planes, 1)


def project_body(
    clip_ref,
    x_hbm,
    keep_ref,
    weight_ref,
    z_hbm,
    stat_ref,
    x_v,
    z_v,
    ordered,
    pool,
    between,
    acc,
    x_sem,
    z_sem,
):
    planes, rows, channels = x_v.shape
    extent = 8
    arriving = Planes(x_hbm.at[clip_ref[0]], x_v, x_sem)
    leaving = Outwards(z_v, z_hbm, z_sem)
    arriving.start_all()
    weight_ordered(weight_ref, ordered)
    together, steps = step_planes(planes)

    def product(i, carry):
        def masked(k, carry):
            h = i * together + k
            arriving.wait(h)
            x_v[h] = x_v[h] * keep_ref[h].astype(BF16)
            return carry

        lax.fori_loop(0, together, masked, 0)
        at = pl.ds(i * together, together)
        value = x_v[at].reshape(together * rows, channels)
        out = jnp.dot(value, ordered[...], preferred_element_type=F32)
        z_v[at] = out.reshape(together, rows, NB1)
        pool[at] = out[:, B0:ND].reshape(together, rows, B3)
        return carry

    lax.fori_loop(0, steps, product, 0)
    acc[...] = jnp.zeros_like(acc)

    def put(h, value):
        z_v[h, :, B0:ND] = value
        leaving.start(h)
        plane_stats(z_v, h, keep_ref[h], acc)

    window_sums(pool, between, extent, put)
    put_stats(stat_ref, acc, jnp.sum(keep_ref[...]))
    leaving.wait_all()


def project_first(clips, own_clip, keep, weight, peers):
    unused, planes, rows, channels = clips.shape
    return call(
        project_body,
        [shape_of(planes, rows, NB1), shape_of(peers, 3, NB1)],
        "av",
        [
            pltpu.VMEM((planes, rows, channels), BF16),
            pltpu.VMEM((planes, rows, NB1), F32),
            pltpu.VMEM((channels, NB1), BF16),
            pltpu.VMEM((planes, rows, B3), F32),
            pltpu.VMEM((planes + 2, rows, B3), F32),
            pltpu.VMEM((2, 8, NB1), F32),
            DMA((planes,)),
            DMA((planes,)),
        ],
        (clips, keep, weight),
        "avv",
        "project_first",
        (own_clip,),
        flops=2 * planes * rows * channels * NB1,
        mib=16,
    )


def level_rows(vec, gain_ref, bias_ref, mom_ref, pieces, offset):
    put_permuted(vec, 4, gain_ref, pieces, offset)
    put_permuted(vec, 5, bias_ref, pieces, offset)
    mean, var = mom_ref[0:1, :], mom_ref[1:2, :]
    inverse = lax.rsqrt(var + EPSILON)
    scale = vec[4:5, :] * inverse
    vec[0:1, :] = scale
    vec[1:2, :] = vec[5:6, :] - mean * scale
    vec[2:3, :] = inverse
    vec[3:4, :] = -mean * inverse


def first_rows(vec, gain_ref, bias_ref, mom_ref):
    level_rows(vec, gain_ref, bias_ref, mom_ref, FIRST_PIECES, 0)


def second_rows(vec, gain_ref, bias_ref, mom_ref):
    level_rows(vec, gain_ref, bias_ref, mom_ref, SECOND_PIECES, NB1)


def back_rows(vec, total, count):
    cross = vec[0:1, :] * total[1:2] / count
    vec[6:7, :] = -(vec[0:1, :] * total[0:1] / count) - cross * vec[3:4, :]
    vec[7:8, :] = -cross * vec[2:3, :]


def put_moments(tot_ref, mom_ref, count):
    total = jnp.sum(tot_ref[...], axis=0)
    if count is None:
        count = total[2:3, :]
        mom_ref[2:3, :] = count
    mean = total[0:1, :] / count
    mom_ref[0:1, :] = mean
    mom_ref[1:2, :] = total[1:2, :] / count - mean * mean


def spread_plane(value, first, times, extent, targets, index):
    width = value.shape[1]
    for early, shifted in enumerate(time_shifted(value, times[:, 0:width], extent)):
        for side, moved in enumerate(width_shifted(shifted, extent)):
            place = early * 3 + side
            moved = moved.astype(BF16)
            for target, low, high in targets:
                begin, end = max(low, first), min(high, first + width)
                if begin < end:
                    start = place * (high - low) + begin - low
                    target[index, :, start : start + end - begin] = moved[
                        :, begin - first : end - first
                    ]


def clear_ends(targets, ends):
    for target, unused, unused in targets:
        for end in ends:
            target[end] = jnp.zeros(target.shape[1:], BF16)


def weight_copies(source, target, sems):
    return [
        pltpu.make_async_copy(
            source.at[pl.ds(time * 9 + height * 3, 3)],
            target.at[height, pl.ds(time * 3, 3)],
            sems.at[height * 3 + time],
        )
        for height in range(3)
        for time in range(3)
    ]


def second_body(
    extent,
    tot_ref,
    z_hbm,
    keep_ref,
    gain_ref,
    bias_ref,
    wide_hbm,
    narrow_hbm,
    act_hbm,
    mid_hbm,
    out_hbm,
    stat_ref,
    mom_ref,
    vec,
    z_v,
    act_v,
    mid_v,
    out_v,
    wide_v,
    narrow_v,
    im_wide,
    im_narrow,
    acc,
    z_sem,
    wide_sem,
    narrow_sem,
    act_sem,
    mid_sem,
    out_sem,
):
    planes, rows, unused = z_v.shape
    arriving = Planes(z_hbm, z_v, z_sem)
    arriving.start_all()
    weights = weight_copies(wide_hbm, wide_v, wide_sem) + weight_copies(
        narrow_hbm, narrow_v, narrow_sem
    )
    for copy in weights:
        copy.start()
    act_out = Outwards(act_v, act_hbm, act_sem)
    mid_out = Outwards(mid_v, mid_hbm, mid_sem)
    out_out = Outwards(out_v, out_hbm, out_sem)
    put_moments(tot_ref, mom_ref, None)
    first_rows(vec, gain_ref, bias_ref, mom_ref)
    targets = ((im_wide, 0, B1A), (im_narrow, B1A, NM))
    clear_ends(targets, (0, planes + 1))
    times = times_of(rows, 128, extent)

    def activate(h, carry):
        arriving.wait(h)
        keep = keep_ref[h]
        for first, last in tiles_of(0, NB1):
            shifted = z_v[h, :, first:last] * vec[0:1, first:last] + vec[1:2, first:last]
            value = shifted * sigmoid(shifted) * keep
            if first < ND:
                act_v[h, :, first:last] = value.astype(BF16)
            else:
                mid_v[h, :, first - ND : last - ND] = value.astype(BF16)
                spread_plane(value, first - ND, times, extent, targets, h + 1)
        act_out.start(h)
        mid_out.start(h)
        return carry

    lax.fori_loop(0, planes, activate, 0)
    for copy in weights:
        copy.wait()
    acc[...] = jnp.zeros_like(acc)
    together, steps = step_planes(planes)

    def convolve(i, carry):
        at = pl.ds(i * together, together)
        for im_ref, weight_ref, first, last in (
            (im_narrow, narrow_v, 0, B2),
            (im_wide, wide_v, B2, NB2),
        ):
            total = None
            for high in range(3):
                value = im_ref[pl.ds(i * together + high, together)]
                value = value.reshape(together * rows, value.shape[2])
                weight = weight_ref[high].reshape(value.shape[1], last - first)
                part = jnp.dot(value, weight, preferred_element_type=F32)
                total = part if total is None else total + part
            out_v[at, :, first:last] = total.reshape(together, rows, last - first)

        def finish(k, carry):
            h = i * together + k
            out_out.start(h)
            plane_stats(out_v, h, keep_ref[h], acc)
            return carry

        lax.fori_loop(0, together, finish, 0)
        return carry

    lax.fori_loop(0, steps, convolve, 0)
    put_stats(stat_ref, acc)
    act_out.wait_all()
    mid_out.wait_all()
    out_out.wait_all()


def second_level(totals, first_out, keep, params, extent, peers):
    unused, conv_mid, conv_small, gain, bias = params
    planes, rows, unused = first_out.shape
    return call(
        functools.partial(second_body, extent),
        [
            shape_of(planes, rows, ND, dtype=BF16),
            shape_of(planes, rows, NM, dtype=BF16),
            shape_of(planes, rows, NB2),
            shape_of(peers, 2, NB2),
            shape_of(3, NB1),
        ],
        "aaavv",
        [
            pltpu.VMEM((8, NB1), F32),
            pltpu.VMEM((planes, rows, NB1), F32),
            pltpu.VMEM((planes, rows, ND), BF16),
            pltpu.VMEM((planes, rows, NM), BF16),
            pltpu.VMEM((planes, rows, NB2), F32),
            pltpu.VMEM((3, 9, B1A, B1), BF16),
            pltpu.VMEM((3, 9, B2A, B2), BF16),
            pltpu.VMEM((planes + 2, rows, 9 * B1A), BF16),
            pltpu.VMEM((planes + 2, rows, 9 * B2A), BF16),
            pltpu.VMEM((2, 8, NB2), F32),
            DMA((planes,)),
            DMA((9,)),
            DMA((9,)),
            DMA((planes,)),
            DMA((planes,)),
            DMA((planes,)),
        ],
        (totals, first_out, keep, gain, bias, conv_mid, conv_small),
        "vavvvaa",
        "second_level",
        flops=2 * planes * rows * 27 * (B1A * B1 + B2A * B2),
        mib=30,
    )


def between_body(
    tot_ref,
    z_hbm,
    keep_ref,
    gain_ref,
    bias_ref,
    act_hbm,
    first_mom_ref,
    keep_next_ref,
    weight_ref,
    x_ref,
    z_next_ref,
    stat_ref,
    mom_ref,
    vec,
    z_v,
    act_v,
    summed,
    picked,
    ordered,
    pool,
    between,
    acc,
    z_sem,
    act_sem,
):
    planes, rows, channels = x_ref.shape
    z_in = Planes(z_hbm, z_v, z_sem)
    act_in = Planes(act_hbm, act_v, act_sem)
    for h in range(2 * planes):
        act_in.start(h)
        z_in.start(h)
    put_moments(tot_ref, mom_ref, first_mom_ref[2:3, 0:NB2])
    second_rows(vec, gain_ref, bias_ref, mom_ref)
    turned_ordered(weight_ref, ordered)
    picked[...] = jnp.zeros_like(picked)
    extent = 4
    wide = z_v.shape[1] // 16

    def pooling(h, carry):
        for step in range(2):
            act_in.wait(2 * h + step)
            z_in.wait(2 * h + step)
        keeps = [keep_ref[2 * h], keep_ref[2 * h + 1]]
        keep_next = keep_next_ref[h]
        for first, last in tiles_of(0, C5):
            width = last - first
            total = None
            for step in range(2):
                if first < ND:
                    part = act_v[2 * h + step, :, first:last].astype(F32)
                else:
                    at = slice(first - ND, last - ND)
                    shifted = z_v[2 * h + step, :, at] * vec[0:1, at] + vec[1:2, at]
                    part = (shifted * sigmoid(shifted) * keeps[step]).astype(BF16).astype(F32)
                total = part if total is None else total + part
            summed[:, 0:width] = total
            for time in range(extent):
                mean = None
                for offset in (2 * time, 2 * time + 1, 8 + 2 * time, 9 + 2 * time):
                    part = summed[pl.ds(offset, wide, stride=16), :]
                    mean = part if mean is None else mean + part
                picked[pl.ds(time, wide, stride=extent), :] = mean * 0.125
            mean = picked[...].astype(BF16).astype(F32) * keep_next
            x_ref[h, :, first:last] = mean[:, 0:width].astype(BF16)
        return carry

    lax.fori_loop(0, planes, pooling, 0)
    value = x_ref[...].reshape(planes * rows, channels)
    out = lax.dot_general(
        value, ordered[...], (((1,), (1,)), ((), ())), preferred_element_type=F32
    )
    z_next_ref[...] = out.reshape(planes, rows, NB1)
    pool[...] = out[:, B0:ND].reshape(planes, rows, B3)
    acc[...] = jnp.zeros_like(acc)

    def put(h, value):
        z_next_ref[h, :, B0:ND] = value
        plane_stats(z_next_ref, h, keep_next_ref[h], acc)

    window_sums(pool, between, extent, put)
    put_stats(stat_ref, acc, jnp.sum(keep_next_ref[...]))


def between_blocks(totals, second_out, keep, params, act, first_mom, keep_next, weight, peers):
    planes, rows = keep_next.shape[:2]
    above, source_rows = second_out.shape[:2]
    return call(
        between_body,
        [
            shape_of(planes, rows, C5, dtype=BF16),
            shape_of(planes, rows, NB1),
            shape_of(peers, 3, NB1),
            shape_of(2, NB2),
        ],
        "vvvv",
        [
            pltpu.VMEM((8, NB2), F32),
            pltpu.VMEM(second_out.shape, F32),
            pltpu.VMEM(act.shape, BF16),
            pltpu.VMEM((source_rows, 128), F32),
            pltpu.VMEM((rows, 128), F32),
            pltpu.VMEM((NB1, C5), BF16),
            pltpu.VMEM((planes, rows, B3), F32),
            pltpu.VMEM((planes + 2, rows, B3), F32),
            pltpu.VMEM((2, 8, NB1), F32),
            DMA((above,)),
            DMA((above,)),
        ],
        (totals, second_out, keep, params[3], params[4], act, first_mom, keep_next, weight),
        "vavvvavvv",
        "between_blocks",
        flops=2 * planes * rows * C5 * NB1,
        mib=16,
    )


def turn_body(
    clip_ref,
    tot_ref,
    z_ref,
    keep_ref,
    gain_ref,
    bias_ref,
    act_ref,
    first_mom_ref,
    grad_ref,
    out_ref,
    slope_ref,
    direct_ref,
    stat_ref,
    mom_ref,
    vec,
    grad,
    result,
    acc,
):
    planes, rows, unused = z_ref.shape
    unused, unused, width, extent, unused = grad_ref.shape
    clip = clip_ref[0]
    put_moments(tot_ref, mom_ref, first_mom_ref[2:3, 0:NB2])
    second_rows(vec, gain_ref, bias_ref, mom_ref)
    acc[...] = jnp.zeros_like(acc)
    grad[...] = jnp.zeros_like(grad)

    def plane(h, carry):
        keep = keep_ref[h]
        for column in range(width):
            at = slice(column * extent, (column + 1) * extent)
            grad[at, :] = grad_ref[clip, h, column].astype(F32)
        direct_ref[h, :, 0:B0] = grad[:, 0:B0].astype(BF16)
        direct_ref[h, :, B0:ND] = grad[:, C5 - B3 :].astype(BF16)
        result[:, 0:B0] = act_ref[h, :, 0:B0].astype(F32)
        result[:, C5 - B3 :] = act_ref[h, :, B0:ND].astype(F32)
        for inner, outer, size in SECOND_PIECES:
            at = slice(inner, inner + size)
            place = slice(B0 + outer, B0 + outer + size)
            value = z_ref[h, :, at]
            shifted = value * vec[0:1, at] + vec[1:2, at]
            gate = sigmoid(shifted)
            result[:, place] = shifted * gate * keep
            slope = grad[:, place] * keep * gate * (1.0 + shifted * (1.0 - gate))
            slope_ref[h, :, at] = slope
            acc[0, :, at] += rows_summed(slope)
            acc[1, :, at] += rows_summed(slope * (value * vec[2:3, at] + vec[3:4, at]))
        for column in range(width):
            at = slice(column * extent, (column + 1) * extent)
            out_ref[h, column] = result[at, :].astype(BF16)
        return carry

    lax.fori_loop(0, planes, plane, 0)
    put_stats(stat_ref, acc)


def turn(totals, second_out, keep, params, act, first_mom, cotangent, own_clip, peers):
    planes, rows, unused = second_out.shape
    return call(
        turn_body,
        [
            shape_of(*cotangent.shape[1:], dtype=BF16),
            shape_of(planes, rows, NB2),
            shape_of(planes, rows, ND, dtype=BF16),
            shape_of(peers, 2, NB2),
            shape_of(2, NB2),
        ],
        "vvvvv",
        [
            pltpu.VMEM((8, NB2), F32),
            pltpu.VMEM((rows, C5), F32),
            pltpu.VMEM((rows, C5), F32),
            pltpu.VMEM((2, 8, NB2), F32),
        ],
        (totals, second_out, keep, params[3], params[4], act, first_mom, cotangent),
        "vvvvvvvv",
        "turn",
        (own_clip,),
        mib=8,
    )


def slope_plane(
    upstream, z_ref, h, vec, keep, slope_ref, slope_at, acc, tiles
):
    for first, last in tiles:
        at = slice(first, last)
        value = z_ref[h, :, at]
        shifted = value * vec[0:1, at] + vec[1:2, at]
        gate = sigmoid(shifted)
        slope = upstream(first, last) * keep * gate * (1.0 + shifted * (1.0 - gate))
        slope_ref[slope_at, :, at] = slope
        acc[0, :, at] += rows_summed(slope)
        acc[1, :, at] += rows_summed(slope * (value * vec[2:3, at] + vec[3:4, at]))


def put_halves(section, packed, kept_hbm, sent_hbm, sems):
    half = kept_hbm.shape[0]
    copies = [
        pltpu.make_async_copy(
            packed.at[pl.ds(pl.multiple_of(which * half, 16), half)], target, sems.at[place]
        )
        for place, (which, target) in enumerate(((section, kept_hbm), (1 - section, sent_hbm)))
    ]
    for copy in copies:
        copy.start()
    return copies


def conv_grad_body(
    extent,
    section_ref,
    tot_ref,
    slope_hbm,
    z_hbm,
    mid_hbm,
    keep_ref,
    gain_ref,
    bias_ref,
    first_mom_ref,
    mom_ref,
    grad_hbm,
    kept_hbm,
    sent_hbm,
    norm_ref,
    vec,
    slope_v,
    z_v,
    mid_v,
    grad_v,
    im_wide,
    im_narrow,
    turned,
    packed,
    slope_sem,
    z_sem,
    mid_sem,
    grad_sem,
    half_sem,
):
    planes, rows, unused = z_v.shape
    slope_in = Planes(slope_hbm, slope_v, slope_sem)
    z_in = Planes(z_hbm, z_v, z_sem)
    mid_in = Planes(mid_hbm, mid_v, mid_sem)
    grad_out = Outwards(grad_v, grad_hbm, grad_sem)
    for h in range(planes):
        mid_in.start(h)
        slope_in.start(h)
        z_in.start(h)
    total = jnp.sum(tot_ref[...], axis=0)
    put_original(norm_ref, 0, total[1:2], SECOND_PIECES)
    put_original(norm_ref, 1, total[0:1], SECOND_PIECES)
    second_rows(vec, gain_ref, bias_ref, mom_ref)
    back_rows(vec, total, first_mom_ref[2:3, 0:NB2])
    targets = ((im_wide, 0, B1A), (im_narrow, B1A, NM))
    clear_ends(targets, (0, planes + 1))
    times = times_of(rows, 128, extent)

    def gradient(h, carry):
        mid_in.wait(h)
        for first, last in tiles_of(0, NM):
            value = mid_v[h, :, first:last].astype(F32)
            spread_plane(value, first, times, extent, targets, h + 1)
        slope_in.wait(h)
        z_in.wait(h)
        keep = keep_ref[h]
        for first, last in tiles_of(0, NB2):
            at = slice(first, last)
            value = slope_v[h, :, at] * vec[0:1, at] + z_v[h, :, at] * vec[7:8, at] + vec[6:7, at]
            grad_v[h, :, at] = (value * keep).astype(BF16)
        grad_out.start(h)
        return carry

    lax.fori_loop(0, planes, gradient, 0)
    turned[...] = grad_v[...].reshape(planes * rows, NB2).T
    wide_rows = 27 * B1A
    half = wide_rows // 2
    used = CONV_NARROW + 27 * B2A
    packed[used:, :] = jnp.zeros((packed.shape[0] - used, 128), BF16)
    step = 3 * B1A
    for high in range(3):
        value = im_wide[high : high + planes].reshape(planes * rows, 9 * B1A)
        part = jnp.dot(turned[B2:NB2, :], value, preferred_element_type=F32)
        part = part.T.astype(BF16)
        value = im_narrow[high : high + planes].reshape(planes * rows, 9 * B2A)
        small = jnp.dot(turned[0:B2, :], value, preferred_element_type=F32)
        small = small.T.astype(BF16)
        for time in range(3):
            chunk = time * 3 + high
            row = chunk * step
            piece = part[time * step : (time + 1) * step]
            packed[row : row + step, :] = piece[:, 0:128]
            packed[wide_rows + row : wide_rows + row + step, :] = piece[:, 128:256]
            low = max(0, min(step, half - row))
            tail = 2 * wide_rows + row
            if low > 0:
                packed[tail : tail + low, 0:64] = piece[:low, 256:B1]
            if low < step:
                tail = tail + low - half
                packed[tail : tail + step - low, 64:128] = piece[low:, 256:B1]
            row = CONV_NARROW + chunk * 3 * B2A
            packed[row : row + 3 * B2A, :] = small[time * 3 * B2A : (time + 1) * 3 * B2A]
    copies = put_halves(section_ref[0], packed, kept_hbm, sent_hbm, half_sem)
    grad_out.wait_all()
    for copy in copies:
        copy.wait()


def conv_grad(totals, slope, second_out, mid, keep, params, first_mom, mom, extent, section, peers):
    planes, rows, unused = second_out.shape
    packed = conv_rows(peers)
    return call(
        functools.partial(conv_grad_body, extent),
        [
            shape_of(planes, rows, NB2, dtype=BF16),
            shape_of(packed // 2, 128, dtype=BF16),
            shape_of(packed // 2, 128, dtype=BF16),
            shape_of(2, NB2),
        ],
        "aaav",
        [
            pltpu.VMEM((8, NB2), F32),
            pltpu.VMEM((planes, rows, NB2), F32),
            pltpu.VMEM((planes, rows, NB2), F32),
            pltpu.VMEM((planes, rows, NM), BF16),
            pltpu.VMEM((planes, rows, NB2), BF16),
            pltpu.VMEM((planes + 2, rows, 9 * B1A), BF16),
            pltpu.VMEM((planes + 2, rows, 9 * B2A), BF16),
            pltpu.VMEM((NB2, planes * rows), BF16),
            pltpu.VMEM((packed, 128), BF16),
            DMA((planes,)),
            DMA((planes,)),
            DMA((planes,)),
            DMA((planes,)),
            DMA((2,)),
        ],
        (totals, slope, second_out, mid, keep, params[3], params[4], first_mom, mom),
        "vaaavvvvv",
        "conv_grad",
        (section,),
        flops=2 * planes * rows * 27 * (B1A * B1 + B2A * B2),
        mib=30,
    )


def back_conv_body(
    extent,
    halved,
    start,
    grad_hbm,
    z_hbm,
    keep_ref,
    gain_ref,
    bias_ref,
    first_mom_ref,
    direct_hbm,
    wide_hbm,
    narrow_hbm,
    before_ref,
    slope_hbm,
    stat_ref,
    acc,
    vec,
    grad_v,
    z_v,
    direct_v,
    wide_v,
    narrow_v,
    slope_v,
    windows,
    weights,
    grad_sem,
    z_sem,
    direct_sem,
    weight_sem,
    slope_sem,
):
    planes = grad_hbm.shape[0]
    count, rows, unused = z_v.shape
    copies = [
        pltpu.make_async_copy(wide_hbm, wide_v, weight_sem.at[0]),
        pltpu.make_async_copy(narrow_hbm, narrow_v, weight_sem.at[1]),
    ]
    for copy in copies:
        copy.start()
    low = 1 if start == 0 else 0
    high = count + 1 if start + count == planes else count + 2
    grad_in = Planes(grad_hbm, grad_v, grad_sem, start - 1)
    for j in range(low, high):
        grad_in.start(j)
    z_in = Planes(z_hbm, z_v, z_sem, start)
    z_in.start_all()
    direct_in = Planes(direct_hbm, direct_v, direct_sem)
    direct_in.start_all()
    slope_out = Outwards(slope_v, slope_hbm, slope_sem)
    first_rows(vec, gain_ref, bias_ref, first_mom_ref)
    targets = ((windows, 0, NB2),)
    clear_ends(targets, [0] * low + [count + 1] * (count + 2 - high))
    weights[...] = jnp.zeros_like(weights)
    times = times_of(rows, 128, extent)

    def shift(j, carry):
        grad_in.wait(j)
        for first, last in tiles_of(0, NB2):
            value = grad_v[j, :, first:last].astype(F32)
            spread_plane(value, first, times, extent, targets, j)
        return carry

    lax.fori_loop(low, high, shift, 0)
    for copy in copies:
        copy.wait()
    for height in range(3):
        for place in range(9):
            source = 26 - ((place // 3) * 9 + height * 3 + place % 3)
            weights[height, 0:B1A, place * NB2 + B2 : (place + 1) * NB2] = wide_v[source]
            weights[height, B1A:NM, place * NB2 : place * NB2 + B2] = narrow_v[source]
    total = None
    for height in range(3):
        value = windows[height : height + count].reshape(count * rows, 9 * NB2)
        part = lax.dot_general(
            value, weights[height], (((1,), (1,)), ((), ())), preferred_element_type=F32
        )
        total = part if total is None else total + part
    slope_v[:, :, ND:NB1] = total.reshape(count, rows, NM)
    acc[...] = before_ref[...]
    direct_in.wait_all()

    def slopes(h, carry):
        z_in.wait(h)

        def upstream(first, last):
            if first >= ND:
                return slope_v[h, :, first:last]
            if halved:
                return direct_v[(start + h) // 2, :, first:last].astype(F32) * 0.125
            return direct_v[start + h, :, first:last].astype(F32)

        slope_plane(upstream, z_v, h, vec, keep_ref[start + h], slope_v, h, acc, tiles_of(0, NB1))
        slope_out.start(h)
        return carry

    lax.fori_loop(0, count, slopes, 0)
    put_stats(stat_ref, acc)
    slope_out.wait_all()


def back_conv(grad, first_out, keep, params, first_mom, direct, halved, extent, peers, part, before):
    unused, conv_mid, conv_small, gain, bias = params
    planes, rows, unused = first_out.shape
    start, count = part
    return call(
        functools.partial(back_conv_body, extent, halved, start),
        [shape_of(count, rows, NB1), shape_of(peers, 2, NB1), shape_of(2, 8, NB1)],
        "avv",
        [
            pltpu.VMEM((8, NB1), F32),
            pltpu.VMEM((count + 2, rows, NB2), BF16),
            pltpu.VMEM((count, rows, NB1), F32),
            pltpu.VMEM(direct.shape, BF16),
            pltpu.VMEM(conv_mid.shape, BF16),
            pltpu.VMEM(conv_small.shape, BF16),
            pltpu.VMEM((count, rows, NB1), F32),
            pltpu.VMEM((count + 2, rows, 9 * NB2), BF16),
            pltpu.VMEM((3, NM, 9 * NB2), BF16),
            DMA((count + 2,)),
            DMA((count,)),
            DMA((direct.shape[0],)),
            DMA((2,)),
            DMA((count,)),
        ],
        (grad, first_out, keep, gain, bias, first_mom, direct, conv_mid, conv_small, before),
        "aavvvvaaav",
        "back_conv",
        flops=2 * count * rows * 27 * (B1A * B1 + B2A * B2),
        mib=30,
    )


def first_gradient(slope_of, z_ref, keep_ref, vec, grad_ref, pool_ref, between_ref, extent, done):
    planes, rows, unused = z_ref.shape

    def gradient(h, carry):
        slope = slope_of(h)
        keep = keep_ref[h]
        for first, last in tiles_of(0, NB1):
            at = slice(first, last)
            value = (
                slope[h, :, at] * vec[0:1, at] + z_ref[h, :, at] * vec[7:8, at] + vec[6:7, at]
            ) * keep
            if first == B0:
                pool_ref[h] = value
            else:
                grad_ref[h, :, at] = value.astype(BF16)
        return carry

    lax.fori_loop(0, planes, gradient, 0)

    def put(h, value):
        grad_ref[h, :, B0:ND] = value.astype(BF16)
        done(h)

    window_sums(pool_ref, between_ref, extent, put)


def put_norms(norm_ref, total, pieces):
    put_original(norm_ref, 0, total[1:2], pieces)
    put_original(norm_ref, 1, total[0:1], pieces)


def last_gradient_body(
    clip_ref,
    section_ref,
    tot_ref,
    low_hbm,
    high_hbm,
    z_hbm,
    x_hbm,
    keep_ref,
    gain_ref,
    bias_ref,
    mom_ref,
    grad_hbm,
    kept_hbm,
    sent_hbm,
    norm_ref,
    vec,
    slope_v,
    z_v,
    x_v,
    grad_v,
    pool,
    between,
    product,
    ordered,
    packed,
    slope_sem,
    z_sem,
    x_sem,
    grad_sem,
    half_sem,
):
    planes, rows, channels = x_v.shape
    low_planes = low_hbm.shape[0]
    z_in = Planes(z_hbm, z_v, z_sem)
    x_in = Planes(x_hbm.at[clip_ref[0]], x_v, x_sem)
    grad_out = Outwards(grad_v, grad_hbm, grad_sem)
    for h in range(planes):
        source = low_hbm.at[h] if h < low_planes else high_hbm.at[h - low_planes]
        pltpu.make_async_copy(source, slope_v.at[h], slope_sem.at[h]).start()
        z_in.start(h)
    x_in.start_all()
    first_rows(vec, gain_ref, bias_ref, mom_ref)
    total = jnp.sum(tot_ref[...], axis=0)
    put_norms(norm_ref, total, FIRST_PIECES)
    back_rows(vec, total, mom_ref[2:3, :])

    def slope_of(h):
        pltpu.make_async_copy(low_hbm.at[0], slope_v.at[h], slope_sem.at[h]).wait()
        z_in.wait(h)
        return slope_v

    def done(h):
        grad_out.start(h)
        x_in.wait(h)
        x_v[h] = x_v[h] * keep_ref[h].astype(BF16)

    first_gradient(slope_of, z_v, keep_ref, vec, grad_v, pool, between, 8, done)
    product[...] = lax.dot_general(
        x_v[...].reshape(planes * rows, channels),
        grad_v[...].reshape(planes * rows, NB1),
        (((0,), (0,)), ((), ())),
        preferred_element_type=F32,
    )
    for inner, outer, width in FIRST_PIECES:
        ordered[:, outer : outer + width] = product[:, inner : inner + width]
    pack_inproj(ordered, packed)
    copies = put_halves(section_ref[0], packed, kept_hbm, sent_hbm, half_sem)
    grad_out.wait_all()
    for copy in copies:
        copy.wait()


def last_gradient(totals, slopes, first_out, clips, keep, params, mom, own_clip, section, peers):
    planes, rows, unused = first_out.shape
    channels = clips.shape[3]
    packed = padded_rows(inproj_rows(channels)[1], peers)
    return call(
        last_gradient_body,
        [
            shape_of(planes, rows, NB1, dtype=BF16),
            shape_of(packed // 2, 128),
            shape_of(packed // 2, 128),
            shape_of(2, NB1),
        ],
        "aaav",
        [
            pltpu.VMEM((8, NB1), F32),
            pltpu.VMEM((planes, rows, NB1), F32),
            pltpu.VMEM((planes, rows, NB1), F32),
            pltpu.VMEM((planes, rows, channels), BF16),
            pltpu.VMEM((planes, rows, NB1), BF16),
            pltpu.VMEM((planes, rows, B3), F32),
            pltpu.VMEM((planes + 2, rows, B3), F32),
            pltpu.VMEM((channels, NB1), F32),
            pltpu.VMEM((channels, NB1), F32),
            pltpu.VMEM((packed, 128), F32),
            DMA((planes,)),
            DMA((planes,)),
            DMA((planes,)),
            DMA((planes,)),
            DMA((2,)),
        ],
        (totals, *slopes, first_out, clips, keep, params[3], params[4], mom),
        "vaaaavvvv",
        "last_gradient",
        (own_clip, section),
        flops=2 * planes * rows * channels * NB1,
        mib=26,
    )


def clip_gradient_body(grad_hbm, keep_ref, weight_ref, du_hbm, grad_v, du_v, ordered, grad_sem, du_sem):
    planes, rows, channels = du_v.shape
    grad_in = Planes(grad_hbm, grad_v, grad_sem)
    du_out = Outwards(du_v, du_hbm, du_sem)
    grad_in.start_all()
    weight_ordered(weight_ref, ordered)
    together, steps = step_planes(planes)

    def product(i, carry):
        def ready(k, carry):
            grad_in.wait(i * together + k)
            return carry

        lax.fori_loop(0, together, ready, 0)
        at = pl.ds(i * together, together)
        value = grad_v[at].reshape(together * rows, NB1)
        out = lax.dot_general(
            value, ordered[...], (((1,), (1,)), ((), ())), preferred_element_type=F32
        )
        du_v[at] = (out.reshape(together, rows, channels) * keep_ref[at]).astype(BF16)

        def sent(k, carry):
            du_out.start(i * together + k)
            return carry

        lax.fori_loop(0, together, sent, 0)
        return carry

    lax.fori_loop(0, steps, product, 0)
    du_out.wait_all()


def clip_gradient(grad, keep, inproj):
    planes, rows, unused = grad.shape
    channels = inproj.shape[0]
    return call(
        clip_gradient_body,
        [shape_of(planes, rows, channels, dtype=BF16)],
        "a",
        [
            pltpu.VMEM((planes, rows, NB1), BF16),
            pltpu.VMEM((planes, rows, channels), BF16),
            pltpu.VMEM((channels, NB1), BF16),
            DMA((planes,)),
            DMA((planes,)),
        ],
        (grad, keep, inproj),
        "avv",
        "clip_gradient",
        flops=2 * planes * rows * channels * NB1,
        mib=10,
    )[0]


def back_between_body(
    tot_ref,
    slope_ref,
    z_ref,
    keep_ref,
    gain_ref,
    bias_ref,
    mom_ref,
    weight_ref,
    z_hbm,
    keep_prev,
    gain_prev,
    bias_prev,
    mom_prev,
    up_hbm,
    grad_ref,
    slope_hbm,
    stat_ref,
    norm_ref,
    vec,
    vec_prev,
    ordered,
    pool,
    between,
    single,
    double,
    up_v,
    z_v,
    slope_v,
    acc,
    z_sem,
    up_sem,
    slope_sem,
):
    planes, rows, unused = z_ref.shape
    extent = 4
    wide = z_v.shape[1] // 16
    z_in = Planes(z_hbm, z_v, z_sem)
    z_in.start_all()
    up_out = Outwards(up_v, up_hbm, up_sem)
    slope_out = Outwards(slope_v, slope_hbm, slope_sem)
    first_rows(vec, gain_ref, bias_ref, mom_ref)
    second_rows(vec_prev, gain_prev, bias_prev, mom_prev)
    total = jnp.sum(tot_ref[...], axis=0)
    put_norms(norm_ref, total, FIRST_PIECES)
    back_rows(vec, total, mom_ref[2:3, :])
    turned_ordered(weight_ref, ordered)
    first_gradient(
        lambda h: slope_ref, z_ref, keep_ref, vec, grad_ref, pool, between, extent, lambda h: None
    )
    value = grad_ref[...].reshape(planes * rows, NB1)
    out = lax.dot_general(
        value, ordered[...], (((1,), (0,)), ((), ())), preferred_element_type=F32
    )
    for h in range(planes):
        keep = keep_ref[h]
        for first, last in tiles_of(0, C5):
            width = last - first
            single[:, 0:width] = (
                (out[h * rows : (h + 1) * rows, first:last] * keep).astype(BF16).astype(F32)
            )
            for time in range(extent):
                row = single[pl.ds(time, wide, stride=extent), :]
                for offset in (2 * time, 2 * time + 1, 8 + 2 * time, 9 + 2 * time):
                    double[pl.ds(offset, wide, stride=16), :] = row
            up_v[h, :, first:last] = double[:, 0:width].astype(BF16)
        up_out.start(h)
    acc[...] = jnp.zeros_like(acc)

    def slopes(h, carry):
        z_in.wait(h)

        def upstream(first, last):
            return up_v[h // 2, :, ND + first : ND + last].astype(F32) * 0.125

        slope_plane(upstream, z_v, h, vec_prev, keep_prev[h], slope_v, h, acc, tiles_of(0, NB2))
        slope_out.start(h)
        return carry

    lax.fori_loop(0, 2 * planes, slopes, 0)
    put_stats(stat_ref, acc)
    up_out.wait_all()
    slope_out.wait_all()


def back_between(
    totals, slope, first_out, keep, params, mom, second_prev, keep_prev, params_prev, mom_prev, peers
):
    inproj, unused, unused, gain, bias = params
    planes, rows, unused = first_out.shape
    above, rows_prev, unused = second_prev.shape
    return call(
        back_between_body,
        [
            shape_of(planes, rows_prev, C5, dtype=BF16),
            shape_of(planes, rows, NB1, dtype=BF16),
            shape_of(*second_prev.shape),
            shape_of(peers, 2, NB2),
            shape_of(2, NB1),
        ],
        "avavv",
        [
            pltpu.VMEM((8, NB1), F32),
            pltpu.VMEM((8, NB2), F32),
            pltpu.VMEM((NB1, C5), BF16),
            pltpu.VMEM((planes, rows, B3), F32),
            pltpu.VMEM((planes + 2, rows, B3), F32),
            pltpu.VMEM((rows, 128), F32),
            pltpu.VMEM((rows_prev, 128), F32),
            pltpu.VMEM((planes, rows_prev, C5), BF16),
            pltpu.VMEM(second_prev.shape, F32),
            pltpu.VMEM(second_prev.shape, F32),
            pltpu.VMEM((2, 8, NB2), F32),
            DMA((above,)),
            DMA((planes,)),
            DMA((above,)),
        ],
        (
            totals,
            slope,
            first_out,
            keep,
            gain,
            bias,
            mom,
            inproj,
            second_prev,
            keep_prev,
            params_prev[3],
            params_prev[4],
            mom_prev,
        ),
        "vvvvvvvvavvvv",
        "back_between",
        flops=2 * planes * rows * C5 * NB1,
        mib=20,
    )


def inproj_rows(channels):
    first = -(-channels // 32) * 16
    return first, 4 * channels + first


def pack_inproj(ordered, packed):
    channels = ordered.shape[0]
    first, used = inproj_rows(channels)
    padded = packed.shape[0]
    for place in range(4):
        packed[place * channels : (place + 1) * channels, :] = ordered[
            :, place * 128 : (place + 1) * 128
        ]
    start = 4 * channels
    packed[start : start + first, 0:64] = ordered[0:first, 512:NB1]
    packed[start : start + channels - first, 64:128] = ordered[first:channels, 512:NB1]
    if 2 * first > channels:
        packed[start + channels - first : start + first, 64:128] = jnp.zeros(
            (2 * first - channels, 64), packed.dtype
        )
    if padded > used:
        packed[used:padded, :] = jnp.zeros((padded - used, 128), packed.dtype)


def inproj_grad_body(
    section_ref, x_ref, grad_ref, kept_hbm, sent_hbm, product, ordered, packed, half_sem
):
    planes, rows, channels = x_ref.shape
    product[...] = lax.dot_general(
        x_ref[...].reshape(planes * rows, channels),
        grad_ref[...].reshape(planes * rows, NB1),
        (((0,), (0,)), ((), ())),
        preferred_element_type=F32,
    ).astype(BF16)
    for row_to, row_from, height in RESULT_PIECES:
        for inner, outer, width in FIRST_PIECES:
            ordered[row_from : row_from + height, outer : outer + width] = product[
                row_to : row_to + height, inner : inner + width
            ]
    pack_inproj(ordered, packed)
    for copy in put_halves(section_ref[0], packed, kept_hbm, sent_hbm, half_sem):
        copy.wait()


def inproj_grad(x, grad, section, peers):
    planes, rows, channels = x.shape
    packed = padded_rows(inproj_rows(channels)[1], peers)
    return call(
        inproj_grad_body,
        [shape_of(packed // 2, 128, dtype=BF16)] * 2,
        "aa",
        [
            pltpu.VMEM((channels, NB1), BF16),
            pltpu.VMEM((channels, NB1), BF16),
            pltpu.VMEM((packed, 128), BF16),
            DMA((2,)),
        ],
        (x, grad),
        "vv",
        "inproj_grad",
        (section,),
        flops=2 * planes * rows * channels * NB1,
        mib=12,
    )


def unpack_conv(packed_ref, wide_ref, narrow_ref):
    step = 27 * B1A
    half = step // 2
    wide_ref[:, 0:128] = packed_ref[0:step, :].astype(F32)
    wide_ref[:, 128:256] = packed_ref[step : 2 * step, :].astype(F32)
    wide_ref[0:half, 256:B1] = packed_ref[2 * step : 2 * step + half, 0:64].astype(F32)
    wide_ref[half:step, 256:B1] = packed_ref[2 * step : 2 * step + half, 64:128].astype(F32)
    narrow_ref[...] = packed_ref[CONV_NARROW : CONV_NARROW + 27 * B2A, :].astype(F32)


def unpack_inproj(packed_ref, out_ref):
    channels = out_ref.shape[0]
    first = inproj_rows(channels)[0]
    for place in range(4):
        out_ref[:, place * 128 : (place + 1) * 128] = packed_ref[
            place * channels : (place + 1) * channels, :
        ].astype(F32)
    start = 4 * channels
    out_ref[0:first, 512:NB1] = packed_ref[start : start + first, 0:64].astype(F32)
    out_ref[first:channels, 512:NB1] = packed_ref[start : start + channels - first, 64:128].astype(
        F32
    )


def unpack_alone_body(section_ref, value_ref, got_ref, wide_ref, narrow_ref, packed_ref):
    half = value_ref.shape[0]
    section = section_ref[0]
    packed_ref[pl.ds(pl.multiple_of(section * half, 16), half), :] = value_ref[...]
    packed_ref[pl.ds(pl.multiple_of((1 - section) * half, 16), half), :] = got_ref[...]
    unpack_conv(packed_ref, wide_ref, narrow_ref)


def unpack_alone(value, got, section):
    return call(
        unpack_alone_body,
        [shape_of(27 * B1A, B1), shape_of(27 * B2A, B2)],
        "vv",
        [pltpu.VMEM((2 * value.shape[0], 128), BF16)],
        (value, got),
        "vv",
        "unpack_alone",
        (section,),
        mib=24,
    )


def halves_placed(section_ref, value_ref, got_ref, pieces):
    section = section_ref[0]
    for half_ref, half in ((value_ref, section), (got_ref, 1 - section)):
        for packed_ref, first, last in pieces:
            size = last - first
            packed_ref[pl.ds(pl.multiple_of(half * size, 16), size), :] = half_ref[first:last, :]


def unpack_joined_body(
    section_ref, value_ref, got_ref, wide_ref, narrow_ref, next_ref, conv_packed, next_packed, next_out
):
    half = conv_packed.shape[0] // 2
    halves_placed(
        section_ref,
        value_ref,
        got_ref,
        ((conv_packed, 0, half), (next_packed, half, value_ref.shape[0])),
    )
    unpack_conv(conv_packed, wide_ref, narrow_ref)
    unpack_inproj(next_packed, next_out)
    next_ref[...] = next_out[...].T


def unpack_joined(value, got, section, channels, peers):
    return call(
        unpack_joined_body,
        [shape_of(27 * B1A, B1), shape_of(27 * B2A, B2), shape_of(NB1, channels)],
        "vvv",
        [
            pltpu.VMEM((conv_rows(peers), 128), BF16),
            pltpu.VMEM((padded_rows(inproj_rows(channels)[1], peers), 128), BF16),
            pltpu.VMEM((channels, NB1), F32),
        ],
        (value, got),
        "vv",
        "unpack_joined",
        (section,),
        mib=32,
    )


def unpack_inproj_body(section_ref, value_ref, got_ref, out_ref, packed):
    halves_placed(section_ref, value_ref, got_ref, ((packed, 0, value_ref.shape[0]),))
    unpack_inproj(packed, out_ref)


def unpack_inproj_alone(value, got, section, channels):
    return call(
        unpack_inproj_body,
        [shape_of(channels, NB1)],
        "v",
        [pltpu.VMEM((2 * value.shape[0], 128), BF16)],
        (value, got),
        "vv",
        "unpack_inproj",
        (section,),
        mib=12,
    )[0]


def sent_to_all(spread):
    return lax.all_to_all(spread, "dp", 0, 0)


def swapped(value):
    return lax.ppermute(value, "section", [(0, 1), (1, 0)])


def distances_of():
    distances = []
    while 2 ** len(distances) < lax.axis_size("dp"):
        distances.append(2 ** len(distances))
    return list(zip(distances, [distances[1], distances[0]] + distances[2:]))


def exchanged(value, pair):
    count = lax.axis_size("dp")
    links = [
        (section * count + place, section * count + (place ^ pair[section]))
        for section in range(2)
        for place in range(count)
    ]
    return lax.ppermute(value, ("section", "dp"), links)


def upper_half(pair):
    place = lax.axis_index("dp")
    distance = jnp.where(lax.axis_index("section") == 0, pair[0], pair[1])
    return ((place // distance) % 2).astype(jnp.int32).reshape(1)


def added(kept, got):
    return (kept.astype(F32) + got.astype(F32)).astype(kept.dtype)


def split_sum_body(upper_ref, kept_ref, got_ref, left_ref, sent_ref):
    half = left_ref.shape[0]
    upper = upper_ref[0]
    for target, which in ((left_ref, upper), (sent_ref, 1 - upper)):
        at = pl.ds(pl.multiple_of(which * half, 16), half)
        target[...] = added(kept_ref[at, :], got_ref[at, :])


def split_sum(kept, got, pair):
    half = shape_of(kept.shape[0] // 2, 128, dtype=kept.dtype)
    return call(
        split_sum_body, [half, half], "vv", [], (kept, got), "vv", "split_sum", (upper_half(pair),)
    )


def placed_body(upper_ref, value_ref, got_ref, out_ref):
    half = value_ref.shape[0]
    upper = upper_ref[0]
    out_ref[pl.ds(pl.multiple_of(upper * half, 16), half), :] = value_ref[...]
    out_ref[pl.ds(pl.multiple_of((1 - upper) * half, 16), half), :] = got_ref[...]


def placed(value, got, pair):
    whole = shape_of(value.shape[0] * 2, 128, dtype=value.dtype)
    return call(
        placed_body, [whole], "v", [], (value, got), "vv", "placed", (upper_half(pair),)
    )[0]


class Scatter:
    def __init__(self, kept, sent):
        self.kept = kept
        self.pairs = distances_of()
        self.place = 0
        self.got = swapped(sent)

    def step(self):
        pair = self.pairs[self.place]
        self.kept, sent = split_sum(self.kept, self.got, pair)
        self.got = exchanged(sent, pair)
        self.place += 1

    def result(self):
        while self.place < len(self.pairs):
            self.step()
        return added(self.kept, self.got)


class Gather:
    def __init__(self, value):
        self.value = value
        self.pairs = distances_of()[::-1]
        self.place = 0
        self.got = exchanged(value, self.pairs[0])

    def step(self):
        self.value = placed(self.value, self.got, self.pairs[self.place])
        self.place += 1
        if self.place < len(self.pairs):
            self.got = exchanged(self.value, self.pairs[self.place])
        else:
            self.got = swapped(self.value)

    def result(self):
        while self.place < len(self.pairs):
            self.step()
        return self.value, self.got


def lockstep(one, other):
    one.got, other.got = lax.optimization_barrier((one.got, other.got))


def tied(value, *exchanges):
    both = lax.optimization_barrier((value,) + tuple(e.got for e in exchanges))
    for exchange, got in zip(exchanges, both[1:]):
        exchange.got = got
    return both[0]


def halves_exchanged(mine, section, own_clip):
    half = mine.shape[2] // 2
    kept = lax.dynamic_slice_in_dim(mine, section * half, half, 2)
    sent = lax.dynamic_slice_in_dim(mine, (1 - section) * half, half, 2)
    got = swapped(sent)
    own_first = own_clip == 0
    both = jnp.stack([jnp.where(own_first, kept, got), jnp.where(own_first, got, kept)])
    return jnp.transpose(both, (0, 3, 1, 2, 4))


def level_first(rows):
    return jnp.concatenate(
        [rows[..., inner : inner + width] for inner, outer, width in sorted(FIRST_PIECES, key=lambda p: p[1])],
        -1,
    )


def level_second(rows):
    return jnp.concatenate(
        [rows[..., inner : inner + width] for inner, outer, width in sorted(SECOND_PIECES, key=lambda p: p[1])],
        -1,
    )


def local(
    clips_in,
    frames,
    voxel_mask,
    micro_order,
    inproj_4f,
    conv_mid_4f,
    conv_small_4f,
    gain_4f,
    bias_4f,
    inproj_5b,
    conv_mid_5b,
    conv_small_5b,
    gain_5b,
    bias_5b,
    cotangent,
):
    section = lax.axis_index("section")
    peers = lax.axis_size("dp")
    own = micro_order[0, section]
    own_clip = own.reshape(1)
    which = section.astype(jnp.int32).reshape(1)
    count, depth, height, width, channels = clips_in.shape
    clips = jnp.transpose(clips_in, (0, 2, 3, 1, 4)).reshape(count, height, width * depth, channels)
    upstream = jnp.transpose(cotangent, (0, 2, 3, 1, 4))

    frame_index = jnp.arange(depth, dtype=jnp.int32)
    own_frames = lax.dynamic_index_in_dim(frames, own, 0, False)
    own_mask = lax.dynamic_index_in_dim(voxel_mask, own, 0, False)
    keep = jnp.where(frame_index[:, None, None] < own_frames, own_mask, 0).astype(F32)
    paired = keep.reshape(depth // 2, 2, height // 2, 2, width // 2, 2)
    keep_next = jnp.max(paired, axis=(1, 3, 5))
    keep_next = jnp.pad(keep_next, ((0, 0), (0, 0), (0, 1)))

    def laid_out(mask):
        extent, planes, columns = mask.shape
        return jnp.transpose(mask, (1, 2, 0)).reshape(planes, columns * extent, 1)

    keep, keep_next = laid_out(keep), laid_out(keep_next)
    first = (inproj_4f, conv_mid_4f, conv_small_4f, gain_4f.reshape(1, NB), bias_4f.reshape(1, NB))
    second = (inproj_5b.T, conv_mid_5b, conv_small_5b, gain_5b.reshape(1, NB), bias_5b.reshape(1, NB))
    long, short = depth, depth // 2

    z1_a, stat = project_first(clips, own_clip, keep, inproj_4f, peers)
    act_a, mid_a, z2_a, stat, mom1_a = second_level(
        sent_to_all(stat), z1_a, keep, first, long, peers
    )
    x_b, z1_b, stat, mom2_a = between_blocks(
        sent_to_all(stat), z2_a, keep, first, act_a, mom1_a, keep_next, second[0], peers
    )
    act_b, mid_b, z2_b, stat, mom1_b = second_level(
        sent_to_all(stat), z1_b, keep_next, second, short, peers
    )
    result, slope, direct, stat, mom2_b = turn(
        sent_to_all(stat), z2_b, keep_next, second, act_b, mom1_b, upstream, own_clip, peers
    )
    dz2_b, kept, sent, norm2_b = conv_grad(
        sent_to_all(stat), slope, z2_b, mid_b, keep_next, second, mom1_b, mom2_b, short, which, peers
    )
    sum_b = Scatter(kept, sent)
    nothing = jnp.zeros((2, 8, NB1), F32)
    slope, stat, unused = back_conv(
        dz2_b, z1_b, keep_next, second, mom1_b, direct, False, short, peers, (0, height // 2), nothing
    )
    stat = tied(stat, sum_b)
    sum_b.step()
    totals = sent_to_all(stat)
    totals = tied(totals, sum_b)
    sum_b.step()
    up, dz1_b, slope, stat, norm1_b = back_between(
        totals, slope, z1_b, keep_next, second, mom1_b, z2_a, keep, first, mom2_a, peers
    )
    stat = tied(stat, sum_b)
    sum_b.step()
    totals = sent_to_all(stat)
    inproj_halves = inproj_grad(x_b, dz1_b, which, peers)
    totals = tied(totals, sum_b)
    sum_b.step()
    dz2_a, kept, sent, norm2_a = conv_grad(
        totals, slope, z2_a, mid_a, keep, first, mom1_a, mom2_a, long, which, peers
    )
    kept = jnp.concatenate([kept, inproj_halves[0]])
    sent = jnp.concatenate([sent, inproj_halves[1]])
    sum_a = Scatter(kept, sent)
    dz2_a = tied(dz2_a, sum_b)
    gather_b = Gather(sum_b.result())
    half = height // 2
    slope_low, unused, part = back_conv(
        dz2_a, z1_a, keep, first, mom1_a, up, True, long, peers, (0, half), nothing
    )
    part = tied(part, sum_a, gather_b)
    sum_a.step()
    gather_b.step()
    slope_high, stat, unused = back_conv(
        dz2_a, z1_a, keep, first, mom1_a, up, True, long, peers, (half, height - half), part
    )
    stat = tied(stat, sum_a, gather_b)
    sum_a.step()
    gather_b.step()
    totals = sent_to_all(stat)
    totals = tied(totals, sum_a, gather_b)
    sum_a.step()
    gather_b.step()
    dz1_a, kept, sent, norm1_a = last_gradient(
        totals, (slope_low, slope_high), z1_a, clips, keep, first, mom1_a, own_clip, which, peers
    )
    sum_i = Scatter(kept, sent)
    dz1_a = tied(dz1_a, sum_a, gather_b)
    sum_a.step()
    gather_b.step()
    du = clip_gradient(dz1_a, keep, inproj_4f)
    du = tied(du, sum_a, sum_i, gather_b)
    gather_a = Gather(sum_a.result())

    conv_b = unpack_alone(*gather_b.result(), which)
    while sum_i.place < len(sum_i.pairs):
        sum_i.step()
        gather_a.step()
        lockstep(gather_a, sum_i)
    gather_i = Gather(sum_i.result().astype(BF16))
    wide_a, narrow_a, inproj_b = unpack_joined(
        *gather_a.result(), which, inproj_5b.shape[0], peers
    )
    inproj_a = unpack_inproj_alone(*gather_i.result(), which, inproj_4f.shape[0])

    block_out = halves_exchanged(result, section, own)
    clips_grad = halves_exchanged(
        du.reshape(height, width, depth, channels), section, own
    )
    small = jnp.stack(
        [
            jnp.concatenate([level_first(mom1_a[:2]), level_second(mom2_a)], -1),
            jnp.concatenate([level_first(mom1_b[:2]), level_second(mom2_b)], -1),
            jnp.concatenate([norm1_a, norm2_a], -1),
            jnp.concatenate([norm1_b, norm2_b], -1),
        ]
    )
    other = swapped(small)
    ordered = jnp.where(section == 0, jnp.stack([small, other]), jnp.stack([other, small]))
    norms = ordered[0] + ordered[1]
    return (
        block_out,
        clips_grad,
        inproj_a,
        wide_a.reshape(conv_mid_4f.shape),
        narrow_a.reshape(conv_small_4f.shape),
        norms[2],
        ordered[:, 0],
        inproj_b.T,
        conv_b[0].reshape(conv_mid_5b.shape),
        conv_b[1].reshape(conv_small_5b.shape),
        norms[3],
        ordered[:, 1],
    )


def solution(mesh):
    placed = (
        P("dp", None, None, None, None),
        P("dp"),
        P("dp", None, None, None),
        P("dp", None),
        P(),
        P(),
        P(),
        P(),
        P(),
        P(),
        P(),
        P(),
        P(),
        P(),
        P("dp", None, None, None, None),
    )
    return jax.shard_map(
        local,
        mesh=mesh,
        in_specs=placed,
        out_specs=(
            P("dp", "section", None, None, None),
            P("dp", "section", None, None, None),
            P(),
            P(),
            P(),
            P(),
            P(),
            P(),
            P(),
            P(),
            P(),
            P(),
        ),
        check_vma=False,
    )
```

```python
import functools

import jax
import jax.numpy as jnp
from jax import lax
from jax.experimental import pallas as pl
from jax.experimental.pallas import tpu as pltpu
from jax.sharding import PartitionSpec as P

B0 = 256
B1A = 160
B1 = 320
B2A = 32
B2 = 128
B3 = 128
C5 = 832
NX = 448
NB1 = 576
NB = 1024
NB2 = NB - NB1
NM = B1A + B2A
ND = B0 + B3

EPSILON = 0.001
F32 = jnp.float32
BF16 = jnp.bfloat16

FIRST_PIECES = ((0, 0, B0), (B0, NX, B3), (ND, B0, NM))
SECOND_PIECES = ((0, B1, B2), (B2, 0, B1))
RESULT_PIECES = ((0, 0, B0), (B0, C5 - B3, B3), (ND, B0 + B1, B2), (ND + B2, B0, B1))

CONV_NARROW = 10800
TURNED = 4096
DMA = pltpu.SemaphoreType.DMA


def padded_rows(rows, peers):
    whole = 32 * peers
    return -(-rows // whole) * whole


def conv_rows(peers):
    return padded_rows(CONV_NARROW + 27 * B2A, peers)


def shape_of(*dims, dtype=F32):
    return jax.ShapeDtypeStruct(dims, dtype)


def tiles_of(start, stop):
    return [(first, min(first + 128, stop)) for first in range(start, stop, 128)]


def whole_block(shape):
    return pl.BlockSpec(shape, lambda *unused: (0,) * len(shape))


def call(body, outs, out_spaces, scratch, args, spaces, name, scalars=(), flops=0, mib=12):
    def spec(array, space):
        return whole_block(array.shape) if space == "v" else pl.BlockSpec(memory_space=pltpu.HBM)

    assert len(args) == len(spaces) and len(outs) == len(out_spaces)
    return pl.pallas_call(
        body,
        out_shape=[
            pltpu.HBM(o.shape, o.dtype) if s == "a" else o for o, s in zip(outs, out_spaces)
        ],
        grid_spec=pltpu.PrefetchScalarGridSpec(
            num_scalar_prefetch=len(scalars),
            grid=(1,),
            in_specs=[spec(a, s) for a, s in zip(args, spaces)],
            out_specs=[spec(o, s) for o, s in zip(outs, out_spaces)],
            scratch_shapes=scratch,
        ),
        compiler_params=pltpu.CompilerParams(vmem_limit_bytes=mib * 2**20),
        cost_estimate=pl.CostEstimate(
            flops=flops,
            transcendentals=0,
            bytes_accessed=sum(a.size * a.dtype.itemsize for a in list(args) + list(outs)),
        ),
        name=name,
    )(
        *scalars,
        *[
            pltpu.with_memory_space_constraint(a, pltpu.HBM) if s == "a" else a
            for a, s in zip(args, spaces)
        ],
    )


class Planes:
    def __init__(self, source, target, sem, start=0):
        self.source, self.target, self.sem, self.start_at = source, target, sem, start

    def copy(self, h):
        return pltpu.make_async_copy(
            self.source.at[h + self.start_at], self.target.at[h], self.sem.at[h]
        )

    def start(self, h):
        self.copy(h).start()

    def wait(self, h):
        self.copy(h).wait()

    def start_all(self):
        for h in range(self.sem.shape[0]):
            self.start(h)

    def wait_all(self):
        for h in range(self.sem.shape[0]):
            self.wait(h)


class Outwards(Planes):
    def copy(self, h):
        return pltpu.make_async_copy(
            self.source.at[h], self.target.at[h + self.start_at], self.sem.at[h]
        )


def sigmoid(value):
    return 0.5 * jnp.tanh(0.5 * value) + 0.5


def rows_summed(value):
    return value.reshape(value.shape[0] // 8, 8, value.shape[1]).sum(0)


def put_permuted(target, row, source, pieces, offset=0):
    for inner, outer, width in pieces:
        target[row : row + 1, inner : inner + width] = source[
            :, offset + outer : offset + outer + width
        ]


def put_original(target, row, value, pieces):
    for inner, outer, width in pieces:
        target[row : row + 1, outer : outer + width] = value[:, inner : inner + width]


def put_stats(stat_ref, acc_ref, count=None):
    peers, rows, width = stat_ref.shape
    for row in range(2):
        line = jnp.sum(acc_ref[row], axis=0, keepdims=True)
        stat_ref[:, row : row + 1, :] = jnp.broadcast_to(line[None], (peers, 1, width))
    if count is not None:
        stat_ref[:, 2:3, :] = jnp.broadcast_to(count.reshape(1, 1, 1), (peers, 1, width))


def plane_stats(value_ref, h, keep, acc_ref):
    for first, last in tiles_of(0, value_ref.shape[2]):
        value = value_ref[h, :, first:last]
        masked = value * keep
        acc_ref[0, :, first:last] += rows_summed(masked)
        acc_ref[1, :, first:last] += rows_summed(masked * value)


def times_of(rows, width, extent):
    return lax.broadcasted_iota(jnp.int32, (rows, width), 0) & (extent - 1)


def time_shifted(value, times, extent):
    rows = value.shape[0]
    earlier = jnp.where(times != 0, pltpu.roll(value, 1, 0), 0.0)
    later = jnp.where(times != extent - 1, pltpu.roll(value, rows - 1, 0), 0.0)
    return earlier, value, later


def width_shifted(value, extent):
    rows = value.shape[0]
    if extent % 8 == 0:
        edge = jnp.zeros((extent, value.shape[1]), value.dtype)
        left = jnp.concatenate([edge, value[:-extent]], 0)
        right = jnp.concatenate([value[extent:], edge], 0)
    else:
        left = pltpu.roll(value, extent, 0)
        right = pltpu.roll(value, rows - extent, 0)
    return left, value, right


def window_sums(source_ref, between_ref, extent, put):
    planes, rows, width = source_ref.shape
    between_ref[0] = jnp.zeros((rows, width), F32)
    between_ref[planes + 1] = jnp.zeros((rows, width), F32)
    times = times_of(rows, width, extent)

    def plane(h, carry):
        before, here, after = time_shifted(source_ref[h], times, extent)
        left, here, right = width_shifted(before + here + after, extent)
        between_ref[h + 1] = left + here + right
        return carry

    lax.fori_loop(0, planes, plane, 0)

    def through(h, carry):
        put(h, (between_ref[h] + between_ref[h + 1] + between_ref[h + 2]) * (1.0 / 27.0))
        return carry

    lax.fori_loop(0, planes, through, 0)


def turned_ordered(turned_ref, ordered_ref):
    for row_to, row_from, height in FIRST_PIECES:
        for inner, outer, width in RESULT_PIECES:
            ordered_ref[row_to : row_to + height, inner : inner + width] = turned_ref[
                row_from : row_from + height, outer : outer + width
            ]


def weight_ordered(weight_ref, ordered_ref):
    for inner, outer, width in FIRST_PIECES:
        ordered_ref[:, inner : inner + width] = weight_ref[:, outer : outer + width]


def step_planes(planes):
    return (planes // 2, 2) if planes % 2 == 0 else (planes, 1)


def masks_body(clip_ref, frames_ref, mask_ref, keep_ref, next_ref):
    planes, rows, unused = keep_ref.shape
    unused, unused, extent, width = mask_ref.shape
    clip = clip_ref[0]
    valid = frames_ref[clip]

    def one_hot(shape, picked):
        places = lax.broadcasted_iota(jnp.int32, shape, 1)
        index = lax.broadcasted_iota(jnp.int32, shape, 0)
        return (places == picked(index)).astype(F32)

    times = one_hot((rows, extent), lambda r: r & (extent - 1))
    columns = one_hot((rows, width), lambda r: r // extent)
    frame = lax.broadcasted_iota(jnp.int32, (extent, width), 0)
    for h in range(planes):
        plane = jnp.where(frame < valid, mask_ref[clip, h], 0).astype(F32)
        picked = jnp.dot(times, plane, preferred_element_type=F32) * columns
        keep_ref[h] = jnp.sum(picked, axis=1, keepdims=True)
    rows_next = next_ref.shape[1]
    half = extent // 2
    index = lax.broadcasted_iota(jnp.int32, (rows_next, rows), 0)
    places = lax.broadcasted_iota(jnp.int32, (rows_next, rows), 1)
    same_time = (places & (extent - 1)) // 2 == (index & (half - 1))
    same_column = places // (2 * extent) == index // half
    pooled = (same_time & same_column).astype(F32)
    for h in range(next_ref.shape[0]):
        both = jnp.broadcast_to(keep_ref[2 * h] + keep_ref[2 * h + 1], (rows, 128))
        held = jnp.dot(pooled, both, preferred_element_type=F32)
        next_ref[h] = jnp.where(held[:, 0:1] > 0.5, 1.0, 0.0)


def masks(own_clip, frames, voxel_mask):
    unused, planes, extent, width = voxel_mask.shape
    return call(
        masks_body,
        [
            shape_of(planes, width * extent, 1),
            shape_of(planes // 2, (width // 2 + 1) * extent // 2, 1),
        ],
        "vv",
        [],
        (voxel_mask,),
        "v",
        "masks",
        (own_clip, frames),
    )


def project_body(
    clip_ref,
    x_hbm,
    keep_ref,
    weight_ref,
    z_hbm,
    stat_ref,
    x_v,
    z_v,
    ordered,
    pool,
    between,
    acc,
    x_sem,
    z_sem,
):
    planes, rows, channels = x_v.shape
    extent = 8
    arriving = Planes(x_hbm.at[clip_ref[0]], x_v, x_sem)
    leaving = Outwards(z_v, z_hbm, z_sem)
    arriving.start_all()
    weight_ordered(weight_ref, ordered)
    together, steps = step_planes(planes)

    def product(i, carry):
        def masked(k, carry):
            h = i * together + k
            arriving.wait(h)
            x_v[h] = x_v[h] * keep_ref[h].astype(BF16)
            return carry

        lax.fori_loop(0, together, masked, 0)
        at = pl.ds(i * together, together)
        value = x_v[at].reshape(together * rows, channels)
        out = jnp.dot(value, ordered[...], preferred_element_type=F32)
        z_v[at] = out.reshape(together, rows, NB1)
        pool[at] = out[:, B0:ND].reshape(together, rows, B3)
        return carry

    lax.fori_loop(0, steps, product, 0)
    acc[...] = jnp.zeros_like(acc)

    def put(h, value):
        z_v[h, :, B0:ND] = value
        leaving.start(h)
        plane_stats(z_v, h, keep_ref[h], acc)

    window_sums(pool, between, extent, put)
    put_stats(stat_ref, acc, jnp.sum(keep_ref[...]))
    leaving.wait_all()


def project_first(clips, own_clip, keep, weight, peers):
    unused, planes, rows, channels = clips.shape
    return call(
        project_body,
        [shape_of(planes, rows, NB1), shape_of(peers, 3, NB1)],
        "av",
        [
            pltpu.VMEM((planes, rows, channels), BF16),
            pltpu.VMEM((planes, rows, NB1), F32),
            pltpu.VMEM((channels, NB1), BF16),
            pltpu.VMEM((planes, rows, B3), F32),
            pltpu.VMEM((planes + 2, rows, B3), F32),
            pltpu.VMEM((2, 8, NB1), F32),
            DMA((planes,)),
            DMA((planes,)),
        ],
        (clips, keep, weight),
        "avv",
        "project_first",
        (own_clip,),
        flops=2 * planes * rows * channels * NB1,
        mib=16,
    )


def level_rows(vec, gain_ref, bias_ref, mom_ref, pieces, offset):
    put_permuted(vec, 4, gain_ref, pieces, offset)
    put_permuted(vec, 5, bias_ref, pieces, offset)
    mean, var = mom_ref[0:1, :], mom_ref[1:2, :]
    inverse = lax.rsqrt(var + EPSILON)
    scale = vec[4:5, :] * inverse
    vec[0:1, :] = scale
    vec[1:2, :] = vec[5:6, :] - mean * scale
    vec[2:3, :] = inverse
    vec[3:4, :] = -mean * inverse


def first_rows(vec, gain_ref, bias_ref, mom_ref):
    level_rows(vec, gain_ref, bias_ref, mom_ref, FIRST_PIECES, 0)


def second_rows(vec, gain_ref, bias_ref, mom_ref):
    level_rows(vec, gain_ref, bias_ref, mom_ref, SECOND_PIECES, NB1)


def back_rows(vec, total, count):
    cross = vec[0:1, :] * total[1:2] / count
    vec[6:7, :] = -(vec[0:1, :] * total[0:1] / count) - cross * vec[3:4, :]
    vec[7:8, :] = -cross * vec[2:3, :]


def put_moments(tot_ref, mom_ref, count):
    total = jnp.sum(tot_ref[...], axis=0)
    if count is None:
        count = total[2:3, :]
        mom_ref[2:3, :] = count
    mean = total[0:1, :] / count
    mom_ref[0:1, :] = mean
    mom_ref[1:2, :] = total[1:2, :] / count - mean * mean


def spread_plane(value, first, times, extent, targets, index):
    width = value.shape[1]
    for early, shifted in enumerate(time_shifted(value, times[:, 0:width], extent)):
        for side, moved in enumerate(width_shifted(shifted, extent)):
            place = early * 3 + side
            moved = moved.astype(BF16)
            for target, low, high in targets:
                begin, end = max(low, first), min(high, first + width)
                if begin < end:
                    start = place * (high - low) + begin - low
                    target[index, :, start : start + end - begin] = moved[
                        :, begin - first : end - first
                    ]


def clear_ends(targets, ends):
    for target, unused, unused in targets:
        for end in ends:
            target[end] = jnp.zeros(target.shape[1:], BF16)


def weight_copies(source, target, sems):
    return [
        pltpu.make_async_copy(
            source.at[pl.ds(time * 9 + height * 3, 3)],
            target.at[height, pl.ds(time * 3, 3)],
            sems.at[height * 3 + time],
        )
        for height in range(3)
        for time in range(3)
    ]


def second_body(
    extent,
    tot_ref,
    z_hbm,
    keep_ref,
    gain_ref,
    bias_ref,
    wide_hbm,
    narrow_hbm,
    act_hbm,
    mid_hbm,
    out_hbm,
    stat_ref,
    mom_ref,
    vec,
    z_v,
    act_v,
    mid_v,
    out_v,
    wide_v,
    narrow_v,
    im_wide,
    im_narrow,
    acc,
    z_sem,
    wide_sem,
    narrow_sem,
    act_sem,
    mid_sem,
    out_sem,
):
    planes, rows, unused = z_v.shape
    arriving = Planes(z_hbm, z_v, z_sem)
    arriving.start_all()
    weights = weight_copies(wide_hbm, wide_v, wide_sem) + weight_copies(
        narrow_hbm, narrow_v, narrow_sem
    )
    for copy in weights:
        copy.start()
    act_out = Outwards(act_v, act_hbm, act_sem)
    mid_out = Outwards(mid_v, mid_hbm, mid_sem)
    out_out = Outwards(out_v, out_hbm, out_sem)
    put_moments(tot_ref, mom_ref, None)
    first_rows(vec, gain_ref, bias_ref, mom_ref)
    targets = ((im_wide, 0, B1A), (im_narrow, B1A, NM))
    clear_ends(targets, (0, planes + 1))
    times = times_of(rows, 128, extent)

    def activate(h, carry):
        arriving.wait(h)
        keep = keep_ref[h]
        for first, last in tiles_of(0, NB1):
            shifted = z_v[h, :, first:last] * vec[0:1, first:last] + vec[1:2, first:last]
            value = shifted * sigmoid(shifted) * keep
            if first < ND:
                act_v[h, :, first:last] = value.astype(BF16)
            else:
                mid_v[h, :, first - ND : last - ND] = value.astype(BF16)
                spread_plane(value, first - ND, times, extent, targets, h + 1)
        act_out.start(h)
        mid_out.start(h)
        return carry

    lax.fori_loop(0, planes, activate, 0)
    for copy in weights:
        copy.wait()
    acc[...] = jnp.zeros_like(acc)
    together, steps = step_planes(planes)

    def convolve(i, carry):
        at = pl.ds(i * together, together)
        for im_ref, weight_ref, first, last in (
            (im_narrow, narrow_v, 0, B2),
            (im_wide, wide_v, B2, NB2),
        ):
            total = None
            for high in range(3):
                value = im_ref[pl.ds(i * together + high, together)]
                value = value.reshape(together * rows, value.shape[2])
                weight = weight_ref[high].reshape(value.shape[1], last - first)
                part = jnp.dot(value, weight, preferred_element_type=F32)
                total = part if total is None else total + part
            out_v[at, :, first:last] = total.reshape(together, rows, last - first)

        def finish(k, carry):
            h = i * together + k
            out_out.start(h)
            plane_stats(out_v, h, keep_ref[h], acc)
            return carry

        lax.fori_loop(0, together, finish, 0)
        return carry

    lax.fori_loop(0, steps, convolve, 0)
    put_stats(stat_ref, acc)
    act_out.wait_all()
    mid_out.wait_all()
    out_out.wait_all()


def second_level(totals, first_out, keep, params, extent, peers):
    unused, conv_mid, conv_small, gain, bias = params
    planes, rows, unused = first_out.shape
    return call(
        functools.partial(second_body, extent),
        [
            shape_of(planes, rows, ND, dtype=BF16),
            shape_of(planes, rows, NM, dtype=BF16),
            shape_of(planes, rows, NB2),
            shape_of(peers, 2, NB2),
            shape_of(3, NB1),
        ],
        "aaavv",
        [
            pltpu.VMEM((8, NB1), F32),
            pltpu.VMEM((planes, rows, NB1), F32),
            pltpu.VMEM((planes, rows, ND), BF16),
            pltpu.VMEM((planes, rows, NM), BF16),
            pltpu.VMEM((planes, rows, NB2), F32),
            pltpu.VMEM((3, 9, B1A, B1), BF16),
            pltpu.VMEM((3, 9, B2A, B2), BF16),
            pltpu.VMEM((planes + 2, rows, 9 * B1A), BF16),
            pltpu.VMEM((planes + 2, rows, 9 * B2A), BF16),
            pltpu.VMEM((2, 8, NB2), F32),
            DMA((planes,)),
            DMA((9,)),
            DMA((9,)),
            DMA((planes,)),
            DMA((planes,)),
            DMA((planes,)),
        ],
        (totals, first_out, keep, gain, bias, conv_mid, conv_small),
        "vavvvaa",
        "second_level",
        flops=2 * planes * rows * 27 * (B1A * B1 + B2A * B2),
        mib=30,
    )


def between_body(
    tot_ref,
    z_hbm,
    keep_ref,
    gain_ref,
    bias_ref,
    act_hbm,
    first_mom_ref,
    keep_next_ref,
    weight_ref,
    x_ref,
    z_next_ref,
    stat_ref,
    mom_ref,
    vec,
    z_v,
    act_v,
    summed,
    picked,
    ordered,
    pool,
    between,
    acc,
    z_sem,
    act_sem,
):
    planes, rows, channels = x_ref.shape
    z_in = Planes(z_hbm, z_v, z_sem)
    act_in = Planes(act_hbm, act_v, act_sem)
    for h in range(2 * planes):
        act_in.start(h)
        z_in.start(h)
    put_moments(tot_ref, mom_ref, first_mom_ref[2:3, 0:NB2])
    second_rows(vec, gain_ref, bias_ref, mom_ref)
    turned_ordered(weight_ref, ordered)
    picked[...] = jnp.zeros_like(picked)
    extent = 4
    wide = z_v.shape[1] // 16

    def pooling(h, carry):
        for step in range(2):
            act_in.wait(2 * h + step)
            z_in.wait(2 * h + step)
        keeps = [keep_ref[2 * h], keep_ref[2 * h + 1]]
        keep_next = keep_next_ref[h]
        for first, last in tiles_of(0, C5):
            width = last - first
            total = None
            for step in range(2):
                if first < ND:
                    part = act_v[2 * h + step, :, first:last].astype(F32)
                else:
                    at = slice(first - ND, last - ND)
                    shifted = z_v[2 * h + step, :, at] * vec[0:1, at] + vec[1:2, at]
                    part = (shifted * sigmoid(shifted) * keeps[step]).astype(BF16).astype(F32)
                total = part if total is None else total + part
            summed[:, 0:width] = total
            for time in range(extent):
                mean = None
                for offset in (2 * time, 2 * time + 1, 8 + 2 * time, 9 + 2 * time):
                    part = summed[pl.ds(offset, wide, stride=16), :]
                    mean = part if mean is None else mean + part
                picked[pl.ds(time, wide, stride=extent), :] = mean * 0.125
            mean = picked[...].astype(BF16).astype(F32) * keep_next
            x_ref[h, :, first:last] = mean[:, 0:width].astype(BF16)
        return carry

    lax.fori_loop(0, planes, pooling, 0)
    value = x_ref[...].reshape(planes * rows, channels)
    out = lax.dot_general(
        value, ordered[...], (((1,), (1,)), ((), ())), preferred_element_type=F32
    )
    z_next_ref[...] = out.reshape(planes, rows, NB1)
    pool[...] = out[:, B0:ND].reshape(planes, rows, B3)
    acc[...] = jnp.zeros_like(acc)

    def put(h, value):
        z_next_ref[h, :, B0:ND] = value
        plane_stats(z_next_ref, h, keep_next_ref[h], acc)

    window_sums(pool, between, extent, put)
    put_stats(stat_ref, acc, jnp.sum(keep_next_ref[...]))


def between_blocks(totals, second_out, keep, params, act, first_mom, keep_next, weight, peers):
    planes, rows = keep_next.shape[:2]
    above, source_rows = second_out.shape[:2]
    return call(
        between_body,
        [
            shape_of(planes, rows, C5, dtype=BF16),
            shape_of(planes, rows, NB1),
            shape_of(peers, 3, NB1),
            shape_of(2, NB2),
        ],
        "vvvv",
        [
            pltpu.VMEM((8, NB2), F32),
            pltpu.VMEM(second_out.shape, F32),
            pltpu.VMEM(act.shape, BF16),
            pltpu.VMEM((source_rows, 128), F32),
            pltpu.VMEM((rows, 128), F32),
            pltpu.VMEM((NB1, C5), BF16),
            pltpu.VMEM((planes, rows, B3), F32),
            pltpu.VMEM((planes + 2, rows, B3), F32),
            pltpu.VMEM((2, 8, NB1), F32),
            DMA((above,)),
            DMA((above,)),
        ],
        (totals, second_out, keep, params[3], params[4], act, first_mom, keep_next, weight),
        "vavvvavvv",
        "between_blocks",
        flops=2 * planes * rows * C5 * NB1,
        mib=16,
    )


def turn_body(
    clip_ref,
    tot_ref,
    z_ref,
    keep_ref,
    gain_ref,
    bias_ref,
    act_ref,
    first_mom_ref,
    grad_ref,
    out_ref,
    slope_ref,
    direct_ref,
    stat_ref,
    mom_ref,
    vec,
    grad,
    result,
    acc,
):
    planes, rows, unused = z_ref.shape
    unused, unused, width, extent, unused = grad_ref.shape
    clip = clip_ref[0]
    put_moments(tot_ref, mom_ref, first_mom_ref[2:3, 0:NB2])
    second_rows(vec, gain_ref, bias_ref, mom_ref)
    acc[...] = jnp.zeros_like(acc)
    grad[...] = jnp.zeros_like(grad)

    def plane(h, carry):
        keep = keep_ref[h]
        for column in range(width):
            at = slice(column * extent, (column + 1) * extent)
            grad[at, :] = grad_ref[clip, h, column].astype(F32)
        direct_ref[h, :, 0:B0] = grad[:, 0:B0].astype(BF16)
        direct_ref[h, :, B0:ND] = grad[:, C5 - B3 :].astype(BF16)
        result[:, 0:B0] = act_ref[h, :, 0:B0].astype(F32)
        result[:, C5 - B3 :] = act_ref[h, :, B0:ND].astype(F32)
        for inner, outer, size in SECOND_PIECES:
            at = slice(inner, inner + size)
            place = slice(B0 + outer, B0 + outer + size)
            value = z_ref[h, :, at]
            shifted = value * vec[0:1, at] + vec[1:2, at]
            gate = sigmoid(shifted)
            result[:, place] = shifted * gate * keep
            slope = grad[:, place] * keep * gate * (1.0 + shifted * (1.0 - gate))
            slope_ref[h, :, at] = slope
            acc[0, :, at] += rows_summed(slope)
            acc[1, :, at] += rows_summed(slope * (value * vec[2:3, at] + vec[3:4, at]))
        for column in range(width):
            at = slice(column * extent, (column + 1) * extent)
            out_ref[h, column] = result[at, :].astype(BF16)
        return carry

    lax.fori_loop(0, planes, plane, 0)
    put_stats(stat_ref, acc)


def turn(totals, second_out, keep, params, act, first_mom, cotangent, own_clip, peers):
    planes, rows, unused = second_out.shape
    return call(
        turn_body,
        [
            shape_of(*cotangent.shape[1:], dtype=BF16),
            shape_of(planes, rows, NB2),
            shape_of(planes, rows, ND, dtype=BF16),
            shape_of(peers, 2, NB2),
            shape_of(2, NB2),
        ],
        "vvvvv",
        [
            pltpu.VMEM((8, NB2), F32),
            pltpu.VMEM((rows, C5), F32),
            pltpu.VMEM((rows, C5), F32),
            pltpu.VMEM((2, 8, NB2), F32),
        ],
        (totals, second_out, keep, params[3], params[4], act, first_mom, cotangent),
        "vvvvvvvv",
        "turn",
        (own_clip,),
        mib=8,
    )


def slope_plane(
    upstream, z_ref, h, vec, keep, slope_ref, slope_at, acc, tiles
):
    for first, last in tiles:
        at = slice(first, last)
        value = z_ref[h, :, at]
        shifted = value * vec[0:1, at] + vec[1:2, at]
        gate = sigmoid(shifted)
        slope = upstream(first, last) * keep * gate * (1.0 + shifted * (1.0 - gate))
        slope_ref[slope_at, :, at] = slope
        acc[0, :, at] += rows_summed(slope)
        acc[1, :, at] += rows_summed(slope * (value * vec[2:3, at] + vec[3:4, at]))


def put_halves(section, packed, kept_hbm, sent_hbm, sems):
    half = packed.shape[0] // 2
    copies = [
        pltpu.make_async_copy(
            packed.at[pl.ds(pl.multiple_of(which * half, 16), half)],
            target.at[pl.ds(0, half)],
            sems.at[place],
        )
        for place, (which, target) in enumerate(((section, kept_hbm), (1 - section, sent_hbm)))
    ]
    for copy in copies:
        copy.start()
    return copies


def conv_grad_body(
    extent,
    section_ref,
    tot_ref,
    slope_hbm,
    z_hbm,
    mid_hbm,
    keep_ref,
    gain_ref,
    bias_ref,
    first_mom_ref,
    mom_ref,
    more_kept_hbm,
    more_sent_hbm,
    grad_hbm,
    kept_hbm,
    sent_hbm,
    norm_ref,
    vec,
    slope_v,
    z_v,
    mid_v,
    grad_v,
    im_wide,
    im_narrow,
    turned,
    packed,
    more_v,
    slope_sem,
    z_sem,
    mid_sem,
    grad_sem,
    half_sem,
):
    planes, rows, unused = z_v.shape
    slope_in = Planes(slope_hbm, slope_v, slope_sem)
    z_in = Planes(z_hbm, z_v, z_sem)
    mid_in = Planes(mid_hbm, mid_v, mid_sem)
    grad_out = Outwards(grad_v, grad_hbm, grad_sem)
    for h in range(planes):
        mid_in.start(h)
        slope_in.start(h)
        z_in.start(h)
    half_rows = packed.shape[0] // 2
    more = kept_hbm.shape[0] - half_rows
    beside = [
        (
            pltpu.make_async_copy(source, more_v.at[place], half_sem.at[2 + place]),
            pltpu.make_async_copy(
                more_v.at[place], target.at[pl.ds(half_rows, more)], half_sem.at[4 + place]
            ),
        )
        for place, (source, target) in enumerate(
            ((more_kept_hbm, kept_hbm), (more_sent_hbm, sent_hbm))
        )
        if more
    ]
    for arriving, leaving in beside:
        arriving.start()
    total = jnp.sum(tot_ref[...], axis=0)
    put_original(norm_ref, 0, total[1:2], SECOND_PIECES)
    put_original(norm_ref, 1, total[0:1], SECOND_PIECES)
    second_rows(vec, gain_ref, bias_ref, mom_ref)
    back_rows(vec, total, first_mom_ref[2:3, 0:NB2])
    targets = ((im_wide, 0, B1A), (im_narrow, B1A, NM))
    clear_ends(targets, (0, planes + 1))
    times = times_of(rows, 128, extent)

    def gradient(h, carry):
        mid_in.wait(h)
        for first, last in tiles_of(0, NM):
            value = mid_v[h, :, first:last].astype(F32)
            spread_plane(value, first, times, extent, targets, h + 1)
        slope_in.wait(h)
        z_in.wait(h)
        keep = keep_ref[h]
        for first, last in tiles_of(0, NB2):
            at = slice(first, last)
            value = slope_v[h, :, at] * vec[0:1, at] + z_v[h, :, at] * vec[7:8, at] + vec[6:7, at]
            grad_v[h, :, at] = (value * keep).astype(BF16)
        grad_out.start(h)
        return carry

    lax.fori_loop(0, planes, gradient, 0)
    for arriving, leaving in beside:
        arriving.wait()
        leaving.start()
    turned[...] = grad_v[...].reshape(planes * rows, NB2).T
    wide_rows = 27 * B1A
    half = wide_rows // 2
    used = CONV_NARROW + 27 * B2A
    packed[used:, :] = jnp.zeros((packed.shape[0] - used, 128), BF16)
    step = 3 * B1A
    for high in range(3):
        value = im_wide[high : high + planes].reshape(planes * rows, 9 * B1A)
        part = jnp.dot(turned[B2:NB2, :], value, preferred_element_type=F32)
        part = part.T.astype(BF16)
        value = im_narrow[high : high + planes].reshape(planes * rows, 9 * B2A)
        small = jnp.dot(turned[0:B2, :], value, preferred_element_type=F32)
        small = small.T.astype(BF16)
        for time in range(3):
            chunk = time * 3 + high
            row = chunk * step
            piece = part[time * step : (time + 1) * step]
            packed[row : row + step, :] = piece[:, 0:128]
            packed[wide_rows + row : wide_rows + row + step, :] = piece[:, 128:256]
            low = max(0, min(step, half - row))
            tail = 2 * wide_rows + row
            if low > 0:
                packed[tail : tail + low, 0:64] = piece[:low, 256:B1]
            if low < step:
                tail = tail + low - half
                packed[tail : tail + step - low, 64:128] = piece[low:, 256:B1]
            row = CONV_NARROW + chunk * 3 * B2A
            packed[row : row + 3 * B2A, :] = small[time * 3 * B2A : (time + 1) * 3 * B2A]
    copies = put_halves(section_ref[0], packed, kept_hbm, sent_hbm, half_sem)
    grad_out.wait_all()
    for copy in copies + [leaving for arriving, leaving in beside]:
        copy.wait()


def conv_grad(
    totals, slope, second_out, mid, keep, params, first_mom, mom, extent, section, peers, more=None
):
    planes, rows, unused = second_out.shape
    packed = conv_rows(peers)
    half = packed // 2
    if more is None:
        more = (mid, mid)
    else:
        half += more[0].shape[0]
    return call(
        functools.partial(conv_grad_body, extent),
        [
            shape_of(planes, rows, NB2, dtype=BF16),
            shape_of(half, 128, dtype=BF16),
            shape_of(half, 128, dtype=BF16),
            shape_of(2, NB2),
        ],
        "aaav",
        [
            pltpu.VMEM((8, NB2), F32),
            pltpu.VMEM((planes, rows, NB2), F32),
            pltpu.VMEM((planes, rows, NB2), F32),
            pltpu.VMEM((planes, rows, NM), BF16),
            pltpu.VMEM((planes, rows, NB2), BF16),
            pltpu.VMEM((planes + 2, rows, 9 * B1A), BF16),
            pltpu.VMEM((planes + 2, rows, 9 * B2A), BF16),
            pltpu.VMEM((NB2, planes * rows), BF16),
            pltpu.VMEM((packed, 128), BF16),
            pltpu.VMEM((2, max(half - packed // 2, 16), 128), BF16),
            DMA((planes,)),
            DMA((planes,)),
            DMA((planes,)),
            DMA((planes,)),
            DMA((6,)),
        ],
        (totals, slope, second_out, mid, keep, params[3], params[4], first_mom, mom, *more),
        "vaaavvvvvaa",
        "conv_grad",
        (section,),
        flops=2 * planes * rows * 27 * (B1A * B1 + B2A * B2),
        mib=30,
    )


def prepare_body(wide_ref, narrow_ref, turned_hbm, weights, sems):
    weights[...] = jnp.zeros_like(weights)
    copies = []
    for height in range(3):
        for place in range(9):
            source = 26 - ((place // 3) * 9 + height * 3 + place % 3)
            weights[height, 0:B1A, place * NB2 + B2 : (place + 1) * NB2] = wide_ref[source]
            weights[height, B1A:NM, place * NB2 : place * NB2 + B2] = narrow_ref[source]
        copies.append(
            pltpu.make_async_copy(weights.at[height], turned_hbm.at[height], sems.at[height])
        )
        copies[-1].start()
    for copy in copies:
        copy.wait()


def prepare(conv_mid, conv_small):
    return call(
        prepare_body,
        [shape_of(3, NM, TURNED, dtype=BF16)],
        "a",
        [pltpu.VMEM((3, NM, TURNED), BF16), DMA((3,))],
        (conv_mid, conv_small),
        "vv",
        "prepare",
        mib=24,
    )[0]


def back_conv_body(
    extent,
    halved,
    start,
    grad_hbm,
    z_hbm,
    keep_ref,
    gain_ref,
    bias_ref,
    first_mom_ref,
    direct_hbm,
    turned_hbm,
    before_ref,
    slope_hbm,
    stat_ref,
    acc,
    vec,
    grad_v,
    z_v,
    direct_v,
    slope_v,
    windows,
    weights,
    grad_sem,
    z_sem,
    direct_sem,
    weight_sem,
    slope_sem,
):
    planes = grad_hbm.shape[0]
    count, rows, unused = z_v.shape
    low = 1 if start == 0 else 0
    high = count + 1 if start + count == planes else count + 2
    grad_in = Planes(grad_hbm, grad_v, grad_sem, start - 1)
    for j in range(low, high):
        grad_in.start(j)
    weights_in = Planes(turned_hbm, weights, weight_sem)
    weights_in.start_all()
    z_in = Planes(z_hbm, z_v, z_sem, start)
    z_in.start_all()
    direct_in = Planes(direct_hbm, direct_v, direct_sem)
    direct_in.start_all()
    slope_out = Outwards(slope_v, slope_hbm, slope_sem)
    first_rows(vec, gain_ref, bias_ref, first_mom_ref)
    targets = ((windows, 0, NB2),)
    clear_ends(targets, [0] * low + [count + 1] * (count + 2 - high))
    times = times_of(rows, 128, extent)

    def shift(j, carry):
        grad_in.wait(j)
        for first, last in tiles_of(0, NB2):
            value = grad_v[j, :, first:last].astype(F32)
            spread_plane(value, first, times, extent, targets, j)
        return carry

    lax.fori_loop(low, high, shift, 0)
    weights_in.wait_all()
    total = None
    for height in range(3):
        value = windows[height : height + count].reshape(count * rows, 9 * NB2)
        part = lax.dot_general(
            value,
            weights[height, :, 0 : 9 * NB2],
            (((1,), (1,)), ((), ())),
            preferred_element_type=F32,
        )
        total = part if total is None else total + part
    slope_v[:, :, ND:NB1] = total.reshape(count, rows, NM)
    acc[...] = before_ref[...]
    direct_in.wait_all()

    def slopes(h, carry):
        z_in.wait(h)

        def upstream(first, last):
            if first >= ND:
                return slope_v[h, :, first:last]
            if halved:
                return direct_v[(start + h) // 2, :, first:last].astype(F32) * 0.125
            return direct_v[start + h, :, first:last].astype(F32)

        slope_plane(upstream, z_v, h, vec, keep_ref[start + h], slope_v, h, acc, tiles_of(0, NB1))
        slope_out.start(h)
        return carry

    lax.fori_loop(0, count, slopes, 0)
    put_stats(stat_ref, acc)
    slope_out.wait_all()


def back_conv(
    grad, first_out, keep, params, turned, first_mom, direct, halved, extent, peers, part, before
):
    unused, unused, unused, gain, bias = params
    planes, rows, unused = first_out.shape
    start, count = part
    return call(
        functools.partial(back_conv_body, extent, halved, start),
        [shape_of(count, rows, NB1), shape_of(peers, 2, NB1), shape_of(2, 8, NB1)],
        "avv",
        [
            pltpu.VMEM((8, NB1), F32),
            pltpu.VMEM((count + 2, rows, NB2), BF16),
            pltpu.VMEM((count, rows, NB1), F32),
            pltpu.VMEM(direct.shape, BF16),
            pltpu.VMEM((count, rows, NB1), F32),
            pltpu.VMEM((count + 2, rows, 9 * NB2), BF16),
            pltpu.VMEM((3, NM, TURNED), BF16),
            DMA((count + 2,)),
            DMA((count,)),
            DMA((direct.shape[0],)),
            DMA((3,)),
            DMA((count,)),
        ],
        (grad, first_out, keep, gain, bias, first_mom, direct, turned, before),
        "aavvvvaav",
        "back_conv",
        flops=2 * count * rows * 27 * (B1A * B1 + B2A * B2),
        mib=30,
    )


def first_gradient(slope_of, z_ref, keep_ref, vec, grad_ref, pool_ref, between_ref, extent, done):
    planes, rows, unused = z_ref.shape

    def gradient(h, carry):
        slope = slope_of(h)
        keep = keep_ref[h]
        for first, last in tiles_of(0, NB1):
            at = slice(first, last)
            value = (
                slope[h, :, at] * vec[0:1, at] + z_ref[h, :, at] * vec[7:8, at] + vec[6:7, at]
            ) * keep
            if first == B0:
                pool_ref[h] = value
            else:
                grad_ref[h, :, at] = value.astype(BF16)
        return carry

    lax.fori_loop(0, planes, gradient, 0)

    def put(h, value):
        grad_ref[h, :, B0:ND] = value.astype(BF16)
        done(h)

    window_sums(pool_ref, between_ref, extent, put)


def put_norms(norm_ref, total, pieces):
    put_original(norm_ref, 0, total[1:2], pieces)
    put_original(norm_ref, 1, total[0:1], pieces)


def last_gradient_body(
    tot_ref,
    low_hbm,
    high_hbm,
    z_hbm,
    keep_ref,
    gain_ref,
    bias_ref,
    mom_ref,
    grad_hbm,
    norm_ref,
    vec,
    slope_v,
    z_v,
    grad_v,
    pool,
    between,
    slope_sem,
    z_sem,
    grad_sem,
):
    planes, rows, unused = z_v.shape
    low_planes = low_hbm.shape[0]
    z_in = Planes(z_hbm, z_v, z_sem)
    grad_out = Outwards(grad_v, grad_hbm, grad_sem)
    for h in range(planes):
        source = low_hbm.at[h] if h < low_planes else high_hbm.at[h - low_planes]
        pltpu.make_async_copy(source, slope_v.at[h], slope_sem.at[h]).start()
        z_in.start(h)
    first_rows(vec, gain_ref, bias_ref, mom_ref)
    total = jnp.sum(tot_ref[...], axis=0)
    put_norms(norm_ref, total, FIRST_PIECES)
    back_rows(vec, total, mom_ref[2:3, :])

    def slope_of(h):
        pltpu.make_async_copy(low_hbm.at[0], slope_v.at[h], slope_sem.at[h]).wait()
        z_in.wait(h)
        return slope_v

    first_gradient(slope_of, z_v, keep_ref, vec, grad_v, pool, between, 8, grad_out.start)
    grad_out.wait_all()


def last_gradient(totals, slopes, first_out, keep, params, mom):
    planes, rows, unused = first_out.shape
    return call(
        last_gradient_body,
        [shape_of(planes, rows, NB1, dtype=BF16), shape_of(2, NB1)],
        "av",
        [
            pltpu.VMEM((8, NB1), F32),
            pltpu.VMEM((planes, rows, NB1), F32),
            pltpu.VMEM((planes, rows, NB1), F32),
            pltpu.VMEM((planes, rows, NB1), BF16),
            pltpu.VMEM((planes, rows, B3), F32),
            pltpu.VMEM((planes + 2, rows, B3), F32),
            DMA((planes,)),
            DMA((planes,)),
            DMA((planes,)),
        ],
        (totals, *slopes, first_out, keep, params[3], params[4], mom),
        "vaaavvvv",
        "last_gradient",
        flops=planes * rows * NB1 * 200,
        mib=22,
    )


def clip_inproj_body(
    clip_ref,
    section_ref,
    x_hbm,
    grad_hbm,
    keep_ref,
    kept_hbm,
    sent_hbm,
    x_v,
    grad_v,
    product,
    ordered,
    packed,
    x_sem,
    grad_sem,
    half_sem,
):
    planes, rows, channels = x_v.shape
    x_in = Planes(x_hbm.at[clip_ref[0]], x_v, x_sem)
    grad_in = Planes(grad_hbm, grad_v, grad_sem)
    x_in.start_all()
    grad_in.start_all()

    def masked(h, carry):
        x_in.wait(h)
        x_v[h] = x_v[h] * keep_ref[h].astype(BF16)
        return carry

    lax.fori_loop(0, planes, masked, 0)
    grad_in.wait_all()
    product[...] = lax.dot_general(
        x_v[...].reshape(planes * rows, channels),
        grad_v[...].reshape(planes * rows, NB1),
        (((0,), (0,)), ((), ())),
        preferred_element_type=F32,
    )
    for inner, outer, width in FIRST_PIECES:
        ordered[:, outer : outer + width] = product[:, inner : inner + width]
    pack_inproj(ordered, packed)
    for copy in put_halves(section_ref[0], packed, kept_hbm, sent_hbm, half_sem):
        copy.wait()


def clip_inproj(clips, grad, keep, own_clip, section, peers):
    unused, planes, rows, channels = clips.shape
    packed = padded_rows(inproj_rows(channels)[1], peers)
    return call(
        clip_inproj_body,
        [shape_of(packed // 2, 128), shape_of(packed // 2, 128)],
        "aa",
        [
            pltpu.VMEM((planes, rows, channels), BF16),
            pltpu.VMEM((planes, rows, NB1), BF16),
            pltpu.VMEM((channels, NB1), F32),
            pltpu.VMEM((channels, NB1), F32),
            pltpu.VMEM((packed, 128), F32),
            DMA((planes,)),
            DMA((planes,)),
            DMA((2,)),
        ],
        (clips, grad, keep),
        "aav",
        "clip_inproj",
        (own_clip, section),
        flops=2 * planes * rows * channels * NB1,
        mib=20,
    )


def clip_gradient_body(
    section_ref,
    grad_hbm,
    keep_ref,
    weight_ref,
    kept_hbm,
    sent_hbm,
    grad_v,
    du_v,
    kept_v,
    sent_v,
    ordered,
    grad_sem,
    kept_sem,
    sent_sem,
):
    planes, rows, channels = du_v.shape
    unused, width, half, unused = kept_v.shape
    later = section_ref[0] == 1
    grad_in = Planes(grad_hbm, grad_v, grad_sem)
    kept_out = Outwards(kept_v, kept_hbm, kept_sem)
    sent_out = Outwards(sent_v, sent_hbm, sent_sem)
    grad_in.start_all()
    weight_ordered(weight_ref, ordered)
    together, steps = step_planes(planes)

    def product(i, carry):
        def ready(k, carry):
            grad_in.wait(i * together + k)
            return carry

        lax.fori_loop(0, together, ready, 0)
        at = pl.ds(i * together, together)
        value = grad_v[at].reshape(together * rows, NB1)
        out = lax.dot_general(
            value, ordered[...], (((1,), (1,)), ((), ())), preferred_element_type=F32
        )
        du_v[at] = out.reshape(together, rows, channels) * keep_ref[at]

        def sent(k, carry):
            h = i * together + k
            for column in range(width):
                start = 2 * half * column
                early = du_v[h, start : start + half, :]
                late = du_v[h, start + half : start + 2 * half, :]
                kept_v[h, column] = jnp.where(later, late, early).astype(BF16)
                sent_v[h, column] = jnp.where(later, early, late).astype(BF16)
            kept_out.start(h)
            sent_out.start(h)
            return carry

        lax.fori_loop(0, together, sent, 0)
        return carry

    lax.fori_loop(0, steps, product, 0)
    kept_out.wait_all()
    sent_out.wait_all()


def clip_gradient(grad, keep, inproj, width, section):
    planes, rows, unused = grad.shape
    channels = inproj.shape[0]
    half = (planes, width, rows // width // 2, channels)
    return call(
        clip_gradient_body,
        [shape_of(*half, dtype=BF16)] * 2,
        "aa",
        [
            pltpu.VMEM((planes, rows, NB1), BF16),
            pltpu.VMEM((planes, rows, channels), F32),
            pltpu.VMEM(half, BF16),
            pltpu.VMEM(half, BF16),
            pltpu.VMEM((channels, NB1), BF16),
            DMA((planes,)),
            DMA((planes,)),
            DMA((planes,)),
        ],
        (grad, keep, inproj),
        "avv",
        "clip_gradient",
        (section,),
        flops=2 * planes * rows * channels * NB1,
        mib=24,
    )


def both_clips_body(own_ref, kept_ref, got_ref, out_ref):
    own = own_ref[0]
    out_ref[own] = kept_ref[...]
    out_ref[1 - own] = got_ref[...]


def both_clips(kept, got, own_clip):
    return call(
        both_clips_body,
        [shape_of(2, *kept.shape, dtype=BF16)],
        "v",
        [],
        (kept, got),
        "vv",
        "both_clips",
        (own_clip,),
        mib=24,
    )[0]


def back_between_body(
    tot_ref,
    slope_ref,
    z_ref,
    keep_ref,
    gain_ref,
    bias_ref,
    mom_ref,
    weight_ref,
    z_hbm,
    keep_prev,
    gain_prev,
    bias_prev,
    mom_prev,
    up_hbm,
    grad_ref,
    slope_hbm,
    stat_ref,
    norm_ref,
    vec,
    vec_prev,
    ordered,
    pool,
    between,
    single,
    double,
    up_v,
    z_v,
    slope_v,
    acc,
    z_sem,
    up_sem,
    slope_sem,
):
    planes, rows, unused = z_ref.shape
    extent = 4
    wide = z_v.shape[1] // 16
    z_in = Planes(z_hbm, z_v, z_sem)
    z_in.start_all()
    up_out = Outwards(up_v, up_hbm, up_sem)
    slope_out = Outwards(slope_v, slope_hbm, slope_sem)
    first_rows(vec, gain_ref, bias_ref, mom_ref)
    second_rows(vec_prev, gain_prev, bias_prev, mom_prev)
    total = jnp.sum(tot_ref[...], axis=0)
    put_norms(norm_ref, total, FIRST_PIECES)
    back_rows(vec, total, mom_ref[2:3, :])
    turned_ordered(weight_ref, ordered)
    first_gradient(
        lambda h: slope_ref, z_ref, keep_ref, vec, grad_ref, pool, between, extent, lambda h: None
    )
    value = grad_ref[...].reshape(planes * rows, NB1)
    out = lax.dot_general(
        value, ordered[...], (((1,), (0,)), ((), ())), preferred_element_type=F32
    )
    for h in range(planes):
        keep = keep_ref[h]
        for first, last in tiles_of(0, C5):
            width = last - first
            single[:, 0:width] = (
                (out[h * rows : (h + 1) * rows, first:last] * keep).astype(BF16).astype(F32)
            )
            for time in range(extent):
                row = single[pl.ds(time, wide, stride=extent), :]
                for offset in (2 * time, 2 * time + 1, 8 + 2 * time, 9 + 2 * time):
                    double[pl.ds(offset, wide, stride=16), :] = row
            up_v[h, :, first:last] = double[:, 0:width].astype(BF16)
        up_out.start(h)
    acc[...] = jnp.zeros_like(acc)

    def slopes(h, carry):
        z_in.wait(h)

        def upstream(first, last):
            return up_v[h // 2, :, ND + first : ND + last].astype(F32) * 0.125

        slope_plane(upstream, z_v, h, vec_prev, keep_prev[h], slope_v, h, acc, tiles_of(0, NB2))
        slope_out.start(h)
        return carry

    lax.fori_loop(0, 2 * planes, slopes, 0)
    put_stats(stat_ref, acc)
    up_out.wait_all()
    slope_out.wait_all()


def back_between(
    totals, slope, first_out, keep, params, mom, second_prev, keep_prev, params_prev, mom_prev, peers
):
    inproj, unused, unused, gain, bias = params
    planes, rows, unused = first_out.shape
    above, rows_prev, unused = second_prev.shape
    return call(
        back_between_body,
        [
            shape_of(planes, rows_prev, C5, dtype=BF16),
            shape_of(planes, rows, NB1, dtype=BF16),
            shape_of(*second_prev.shape),
            shape_of(peers, 2, NB2),
            shape_of(2, NB1),
        ],
        "avavv",
        [
            pltpu.VMEM((8, NB1), F32),
            pltpu.VMEM((8, NB2), F32),
            pltpu.VMEM((NB1, C5), BF16),
            pltpu.VMEM((planes, rows, B3), F32),
            pltpu.VMEM((planes + 2, rows, B3), F32),
            pltpu.VMEM((rows, 128), F32),
            pltpu.VMEM((rows_prev, 128), F32),
            pltpu.VMEM((planes, rows_prev, C5), BF16),
            pltpu.VMEM(second_prev.shape, F32),
            pltpu.VMEM(second_prev.shape, F32),
            pltpu.VMEM((2, 8, NB2), F32),
            DMA((above,)),
            DMA((planes,)),
            DMA((above,)),
        ],
        (
            totals,
            slope,
            first_out,
            keep,
            gain,
            bias,
            mom,
            inproj,
            second_prev,
            keep_prev,
            params_prev[3],
            params_prev[4],
            mom_prev,
        ),
        "vvvvvvvvavvvv",
        "back_between",
        flops=2 * planes * rows * C5 * NB1,
        mib=20,
    )


def inproj_rows(channels):
    first = -(-channels // 32) * 16
    return first, 4 * channels + first


def pack_inproj(ordered, packed):
    channels = ordered.shape[0]
    first, used = inproj_rows(channels)
    padded = packed.shape[0]
    for place in range(4):
        packed[place * channels : (place + 1) * channels, :] = ordered[
            :, place * 128 : (place + 1) * 128
        ]
    start = 4 * channels
    packed[start : start + first, 0:64] = ordered[0:first, 512:NB1]
    packed[start : start + channels - first, 64:128] = ordered[first:channels, 512:NB1]
    if 2 * first > channels:
        packed[start + channels - first : start + first, 64:128] = jnp.zeros(
            (2 * first - channels, 64), packed.dtype
        )
    if padded > used:
        packed[used:padded, :] = jnp.zeros((padded - used, 128), packed.dtype)


def inproj_grad_body(
    section_ref, x_ref, grad_ref, kept_hbm, sent_hbm, product, ordered, packed, half_sem
):
    planes, rows, channels = x_ref.shape
    product[...] = lax.dot_general(
        x_ref[...].reshape(planes * rows, channels),
        grad_ref[...].reshape(planes * rows, NB1),
        (((0,), (0,)), ((), ())),
        preferred_element_type=F32,
    ).astype(BF16)
    for row_to, row_from, height in RESULT_PIECES:
        for inner, outer, width in FIRST_PIECES:
            ordered[row_from : row_from + height, outer : outer + width] = product[
                row_to : row_to + height, inner : inner + width
            ]
    pack_inproj(ordered, packed)
    for copy in put_halves(section_ref[0], packed, kept_hbm, sent_hbm, half_sem):
        copy.wait()


def inproj_grad(x, grad, section, peers):
    planes, rows, channels = x.shape
    packed = padded_rows(inproj_rows(channels)[1], peers)
    return call(
        inproj_grad_body,
        [shape_of(packed // 2, 128, dtype=BF16)] * 2,
        "aa",
        [
            pltpu.VMEM((channels, NB1), BF16),
            pltpu.VMEM((channels, NB1), BF16),
            pltpu.VMEM((packed, 128), BF16),
            DMA((2,)),
        ],
        (x, grad),
        "vv",
        "inproj_grad",
        (section,),
        flops=2 * planes * rows * channels * NB1,
        mib=12,
    )


def unpack_conv(packed_ref, wide_ref, narrow_ref):
    step = 27 * B1A
    half = step // 2
    wide_ref[:, 0:128] = packed_ref[0:step, :].astype(F32)
    wide_ref[:, 128:256] = packed_ref[step : 2 * step, :].astype(F32)
    wide_ref[0:half, 256:B1] = packed_ref[2 * step : 2 * step + half, 0:64].astype(F32)
    wide_ref[half:step, 256:B1] = packed_ref[2 * step : 2 * step + half, 64:128].astype(F32)
    narrow_ref[...] = packed_ref[CONV_NARROW : CONV_NARROW + 27 * B2A, :].astype(F32)


def unpack_inproj(packed_ref, out_ref):
    channels = out_ref.shape[0]
    first = inproj_rows(channels)[0]
    for place in range(4):
        out_ref[:, place * 128 : (place + 1) * 128] = packed_ref[
            place * channels : (place + 1) * channels, :
        ].astype(F32)
    start = 4 * channels
    out_ref[0:first, 512:NB1] = packed_ref[start : start + first, 0:64].astype(F32)
    out_ref[first:channels, 512:NB1] = packed_ref[start : start + channels - first, 64:128].astype(
        F32
    )


def unpack_alone_body(section_ref, value_ref, got_ref, wide_ref, narrow_ref, packed_ref):
    half = value_ref.shape[0]
    section = section_ref[0]
    packed_ref[pl.ds(pl.multiple_of(section * half, 16), half), :] = value_ref[...]
    packed_ref[pl.ds(pl.multiple_of((1 - section) * half, 16), half), :] = got_ref[...]
    unpack_conv(packed_ref, wide_ref, narrow_ref)


def unpack_alone(value, got, section):
    return call(
        unpack_alone_body,
        [shape_of(27 * B1A, B1), shape_of(27 * B2A, B2)],
        "vv",
        [pltpu.VMEM((2 * value.shape[0], 128), BF16)],
        (value, got),
        "vv",
        "unpack_alone",
        (section,),
        mib=24,
    )


def halves_placed(section_ref, value_ref, got_ref, pieces):
    section = section_ref[0]
    for half_ref, half in ((value_ref, section), (got_ref, 1 - section)):
        for packed_ref, first, last in pieces:
            size = last - first
            packed_ref[pl.ds(pl.multiple_of(half * size, 16), size), :] = half_ref[first:last, :]


def unpack_joined_body(
    section_ref, value_ref, got_ref, wide_ref, narrow_ref, next_ref, conv_packed, next_packed, next_out
):
    half = conv_packed.shape[0] // 2
    halves_placed(
        section_ref,
        value_ref,
        got_ref,
        ((conv_packed, 0, half), (next_packed, half, value_ref.shape[0])),
    )
    unpack_conv(conv_packed, wide_ref, narrow_ref)
    unpack_inproj(next_packed, next_out)
    next_ref[...] = next_out[...].T


def unpack_joined(value, got, section, channels, peers):
    return call(
        unpack_joined_body,
        [shape_of(27 * B1A, B1), shape_of(27 * B2A, B2), shape_of(NB1, channels)],
        "vvv",
        [
            pltpu.VMEM((conv_rows(peers), 128), BF16),
            pltpu.VMEM((padded_rows(inproj_rows(channels)[1], peers), 128), BF16),
            pltpu.VMEM((channels, NB1), F32),
        ],
        (value, got),
        "vv",
        "unpack_joined",
        (section,),
        mib=32,
    )


def share_places(peers):
    pairs = distance_pairs(peers)
    places = []
    for section in range(2):
        order = [pair[section] for pair in pairs]
        places.append(
            [
                sum(
                    ((place // distance) % 2) << (len(order) - 1 - level)
                    for level, distance in enumerate(order)
                )
                for place in range(peers)
            ]
        )
    return places


def unpack_inproj_body(section_ref, value_ref, got_ref, out_ref, packed):
    section = section_ref[0]
    peers, share, unused = value_ref.shape
    places = share_places(peers)
    for half_ref, half in ((value_ref, section), (got_ref, 1 - section)):
        for place in range(peers):
            at = jnp.where(half == 0, places[0][place], places[1][place]) + half * peers
            packed[pl.ds(pl.multiple_of(at * share, 16), share), :] = half_ref[place]
    unpack_inproj(packed, out_ref)


def unpack_inproj_alone(value, got, section, channels):
    return call(
        unpack_inproj_body,
        [shape_of(channels, NB1)],
        "v",
        [pltpu.VMEM((2 * value.shape[0] * value.shape[1], 128), BF16)],
        (value, got),
        "vv",
        "unpack_inproj",
        (section,),
        mib=12,
    )[0]


def sent_to_all(spread):
    return lax.all_to_all(spread, "dp", 0, 0)


def swapped(value):
    return lax.ppermute(value, "section", [(0, 1), (1, 0)])


def distance_pairs(peers):
    distances = []
    while 2 ** len(distances) < peers:
        distances.append(2 ** len(distances))
    return list(zip(distances, [distances[1], distances[0]] + distances[2:]))


def distances_of():
    return distance_pairs(lax.axis_size("dp"))


def exchanged(value, pair):
    count = lax.axis_size("dp")
    links = [
        (section * count + place, section * count + (place ^ pair[section]))
        for section in range(2)
        for place in range(count)
    ]
    return lax.ppermute(value, ("section", "dp"), links)


def upper_half(pair):
    place = lax.axis_index("dp")
    distance = jnp.where(lax.axis_index("section") == 0, pair[0], pair[1])
    return ((place // distance) % 2).astype(jnp.int32).reshape(1)


def added(kept, got):
    return (kept.astype(F32) + got.astype(F32)).astype(kept.dtype)


def split_sum_body(upper_ref, kept_ref, got_ref, left_ref, sent_ref):
    half = left_ref.shape[0]
    upper = upper_ref[0]
    for target, which in ((left_ref, upper), (sent_ref, 1 - upper)):
        at = pl.ds(pl.multiple_of(which * half, 16), half)
        target[...] = added(kept_ref[at, :], got_ref[at, :])


def split_sum(kept, got, pair):
    half = shape_of(kept.shape[0] // 2, 128, dtype=kept.dtype)
    return call(
        split_sum_body, [half, half], "vv", [], (kept, got), "vv", "split_sum", (upper_half(pair),)
    )


def placed_body(upper_ref, value_ref, got_ref, out_ref):
    half = value_ref.shape[0]
    upper = upper_ref[0]
    out_ref[pl.ds(pl.multiple_of(upper * half, 16), half), :] = value_ref[...]
    out_ref[pl.ds(pl.multiple_of((1 - upper) * half, 16), half), :] = got_ref[...]


def placed(value, got, pair):
    whole = shape_of(value.shape[0] * 2, 128, dtype=value.dtype)
    return call(
        placed_body, [whole], "v", [], (value, got), "vv", "placed", (upper_half(pair),)
    )[0]


class Scatter:
    def __init__(self, kept, sent):
        self.kept = kept
        self.pairs = distances_of()
        self.place = 0
        self.got = swapped(sent)

    def step(self):
        pair = self.pairs[self.place]
        self.kept, sent = split_sum(self.kept, self.got, pair)
        self.got = exchanged(sent, pair)
        self.place += 1

    def result(self):
        while self.place < len(self.pairs):
            self.step()
        return added(self.kept, self.got)


class Gather:
    def __init__(self, value):
        self.value = value
        self.pairs = distances_of()[::-1]
        self.place = 0
        self.got = exchanged(value, self.pairs[0])

    def step(self):
        self.value = placed(self.value, self.got, self.pairs[self.place])
        self.place += 1
        if self.place < len(self.pairs):
            self.got = exchanged(self.value, self.pairs[self.place])
        else:
            self.got = swapped(self.value)

    def result(self):
        while self.place < len(self.pairs):
            self.step()
        return self.value, self.got


def lockstep(one, other):
    one.got, other.got = lax.optimization_barrier((one.got, other.got))


def tied(value, *exchanges):
    both = lax.optimization_barrier((value,) + tuple(e.got for e in exchanges))
    for exchange, got in zip(exchanges, both[1:]):
        exchange.got = got
    return both[0]


def small_body(first_a, second_a, first_b, second_b, norm1_a, norm2_a, norm1_b, norm2_b, out_ref):
    for row, first, second in ((0, first_a, second_a), (2, first_b, second_b)):
        for line in range(2):
            for pieces, source, offset in ((FIRST_PIECES, first, 0), (SECOND_PIECES, second, NB1)):
                for inner, outer, width in pieces:
                    start = offset + outer
                    out_ref[row + line : row + line + 1, start : start + width] = source[
                        line : line + 1, inner : inner + width
                    ]
    for row, first, second in ((4, norm1_a, norm2_a), (6, norm1_b, norm2_b)):
        out_ref[row : row + 2, 0:NB1] = first[...]
        out_ref[row : row + 2, NB1:NB] = second[...]


def small_out_body(section_ref, own_ref, other_ref, norm_a, mom_a, norm_b, mom_b):
    section = section_ref[0]
    own, other = own_ref[...], other_ref[...]
    norms = own[4:8] + other[4:8]
    norm_a[...] = norms[0:2]
    norm_b[...] = norms[2:4]
    low = jnp.where(section == 0, own, other)
    high = jnp.where(section == 0, other, own)
    mom_a[0] = low[0:2]
    mom_a[1] = high[0:2]
    mom_b[0] = low[2:4]
    mom_b[1] = high[2:4]


def small_outputs(rows, section):
    own = call(small_body, [shape_of(8, NB)], "v", [], rows, "vvvvvvvv", "small")[0]
    return call(
        small_out_body,
        [shape_of(2, NB), shape_of(2, 2, NB), shape_of(2, NB), shape_of(2, 2, NB)],
        "vvvv",
        [],
        (own, swapped(own)),
        "vv",
        "small_out",
        (section,),
    )


def local(
    clips_in,
    frames,
    voxel_mask,
    micro_order,
    inproj_4f,
    conv_mid_4f,
    conv_small_4f,
    gain_4f,
    bias_4f,
    inproj_5b,
    conv_mid_5b,
    conv_small_5b,
    gain_5b,
    bias_5b,
    cotangent,
):
    section = lax.axis_index("section")
    peers = lax.axis_size("dp")
    own = micro_order[0, section]
    own_clip = own.reshape(1)
    which = section.astype(jnp.int32).reshape(1)
    count, depth, height, width, channels = clips_in.shape
    clips = jnp.transpose(clips_in, (0, 2, 3, 1, 4)).reshape(count, height, width * depth, channels)
    upstream = jnp.transpose(cotangent, (0, 2, 3, 1, 4))

    keep, keep_next = masks(own_clip, frames, jnp.transpose(voxel_mask, (0, 2, 1, 3)))
    first = (inproj_4f, conv_mid_4f, conv_small_4f, gain_4f.reshape(1, NB), bias_4f.reshape(1, NB))
    second = (inproj_5b.T, conv_mid_5b, conv_small_5b, gain_5b.reshape(1, NB), bias_5b.reshape(1, NB))
    long, short = depth, depth // 2

    z1_a, stat = project_first(clips, own_clip, keep, inproj_4f, peers)
    turned_a = prepare(conv_mid_4f, conv_small_4f)
    act_a, mid_a, z2_a, stat, mom1_a = second_level(
        sent_to_all(stat), z1_a, keep, first, long, peers
    )
    totals = sent_to_all(stat)
    turned_b = prepare(conv_mid_5b, conv_small_5b)
    totals, turned_a, turned_b = lax.optimization_barrier((totals, turned_a, turned_b))
    x_b, z1_b, stat, mom2_a = between_blocks(
        totals, z2_a, keep, first, act_a, mom1_a, keep_next, second[0], peers
    )
    act_b, mid_b, z2_b, stat, mom1_b = second_level(
        sent_to_all(stat), z1_b, keep_next, second, short, peers
    )
    result, slope, direct, stat, mom2_b = turn(
        sent_to_all(stat), z2_b, keep_next, second, act_b, mom1_b, upstream, own_clip, peers
    )
    dz2_b, kept, sent, norm2_b = conv_grad(
        sent_to_all(stat), slope, z2_b, mid_b, keep_next, second, mom1_b, mom2_b, short, which, peers
    )
    sum_b = Scatter(kept, sent)
    nothing = jnp.zeros((2, 8, NB1), F32)
    slope, stat, unused = back_conv(
        dz2_b,
        z1_b,
        keep_next,
        second,
        turned_b,
        mom1_b,
        direct,
        False,
        short,
        peers,
        (0, height // 2),
        nothing,
    )
    stat = tied(stat, sum_b)
    sum_b.step()
    totals = sent_to_all(stat)
    half = result.shape[2] // 2
    early, late = result[:, :, :half], result[:, :, half:]
    kept = jnp.where(section == 0, early, late)
    block_out = both_clips(kept, swapped(jnp.where(section == 0, late, early)), own_clip)
    totals, block_out = lax.optimization_barrier((totals, block_out))
    totals = tied(totals, sum_b)
    sum_b.step()
    up, dz1_b, slope, stat, norm1_b = back_between(
        totals, slope, z1_b, keep_next, second, mom1_b, z2_a, keep, first, mom2_a, peers
    )
    stat = tied(stat, sum_b)
    sum_b.step()
    totals = sent_to_all(stat)
    inproj_halves = inproj_grad(x_b, dz1_b, which, peers)
    totals = tied(totals, sum_b)
    sum_b.step()
    dz2_a, kept, sent, norm2_a = conv_grad(
        totals,
        slope,
        z2_a,
        mid_a,
        keep,
        first,
        mom1_a,
        mom2_a,
        long,
        which,
        peers,
        inproj_halves,
    )
    sent = tied(sent, sum_b)
    sum_a = Scatter(kept, sent)
    gather_b = Gather(sum_b.result())
    dz2_a = tied(dz2_a, sum_a)
    sum_a.step()
    half = height // 2
    back = (z1_a, keep, first, turned_a, mom1_a, up, True, long, peers)
    slope_low, unused, part = back_conv(dz2_a, *back, (0, half), nothing)
    part = tied(part, sum_a, gather_b)
    sum_a.step()
    gather_b.step()
    slope_high, stat, unused = back_conv(dz2_a, *back, (half, height - half), part)
    stat = tied(stat, sum_a, gather_b)
    sum_a.step()
    gather_b.step()
    totals = sent_to_all(stat)
    totals = tied(totals, sum_a, gather_b)
    sum_a.step()
    gather_b.step()
    dz1_a, norm1_a = last_gradient(totals, (slope_low, slope_high), z1_a, keep, first, mom1_a)
    dz1_a = tied(dz1_a, sum_a)
    gather_a = Gather(sum_a.result())
    kept, sent = clip_inproj(clips, dz1_a, keep, own_clip, which, peers)
    sent = tied(sent, gather_a, gather_b)
    sum_i = Scatter(kept, sent)
    gather_a.step()
    gather_b.step()
    dz1_a, sum_i.got, gather_b.got = lax.optimization_barrier((dz1_a, sum_i.got, gather_b.got))
    sum_i.step()
    kept, sent = clip_gradient(dz1_a, keep, inproj_4f, width, which)
    sent, sum_i.got = lax.optimization_barrier((sent, sum_i.got))
    sum_i.step()
    clips_grad = both_clips(kept, swapped(sent), own_clip)
    small = small_outputs(
        (mom1_a, mom2_a, mom1_b, mom2_b, norm1_a, norm2_a, norm1_b, norm2_b), which
    )
    conv_b = unpack_alone(*gather_b.result(), which)
    lockstep(gather_a, sum_i)
    gather_a.got, clips_grad, small, conv_b = lax.optimization_barrier(
        (gather_a.got, clips_grad, small, conv_b)
    )
    gather_a.step()
    sum_i.step()
    sum_i.step()
    lockstep(gather_a, sum_i)
    gather_a.step()
    shares = jnp.broadcast_to(sum_i.result().astype(BF16)[None], (peers, *sum_i.kept.shape))
    whole = sent_to_all(shares)
    whole, gather_a.got = lax.optimization_barrier((whole, gather_a.got))
    gather_a.step()
    inproj_a = unpack_inproj_alone(whole, swapped(whole), which, inproj_4f.shape[0])
    wide_a, narrow_a, inproj_b = unpack_joined(
        *gather_a.result(), which, inproj_5b.shape[0], peers
    )
    return (
        jnp.transpose(block_out, (0, 3, 1, 2, 4)),
        jnp.transpose(clips_grad, (0, 3, 1, 2, 4)),
        inproj_a,
        wide_a.reshape(conv_mid_4f.shape),
        narrow_a.reshape(conv_small_4f.shape),
        small[0],
        small[1],
        inproj_b.T,
        conv_b[0].reshape(conv_mid_5b.shape),
        conv_b[1].reshape(conv_small_5b.shape),
        small[2],
        small[3],
    )


def solution(mesh):
    placed = (
        P("dp", None, None, None, None),
        P("dp"),
        P("dp", None, None, None),
        P("dp", None),
        P(),
        P(),
        P(),
        P(),
        P(),
        P(),
        P(),
        P(),
        P(),
        P(),
        P("dp", None, None, None, None),
    )
    return jax.shard_map(
        local,
        mesh=mesh,
        in_specs=placed,
        out_specs=(
            P("dp", "section", None, None, None),
            P("dp", "section", None, None, None),
            P(),
            P(),
            P(),
            P(),
            P(),
            P(),
            P(),
            P(),
            P(),
            P(),
        ),
        check_vma=False,
    )
```

```python
import functools

import jax
import jax.numpy as jnp
from jax import lax
from jax.experimental import pallas as pl
from jax.experimental.pallas import tpu as pltpu
from jax.sharding import PartitionSpec as P

B0 = 256
B1A = 160
B1 = 320
B2A = 32
B2 = 128
B3 = 128
C5 = 832
NX = 448
NB1 = 576
NB = 1024
NB2 = NB - NB1
NM = B1A + B2A
ND = B0 + B3

EPSILON = 0.001
F32 = jnp.float32
BF16 = jnp.bfloat16

FIRST_PIECES = ((0, 0, B0), (B0, NX, B3), (ND, B0, NM))
SECOND_PIECES = ((0, B1, B2), (B2, 0, B1))
RESULT_PIECES = ((0, 0, B0), (B0, C5 - B3, B3), (ND, B0 + B1, B2), (ND + B2, B0, B1))

CONV_NARROW = 10800
TURNED = 4096
DMA = pltpu.SemaphoreType.DMA


def padded_rows(rows, peers):
    whole = 32 * peers
    return -(-rows // whole) * whole


def conv_rows(peers):
    return padded_rows(CONV_NARROW + 27 * B2A, peers)


def shape_of(*dims, dtype=F32):
    return jax.ShapeDtypeStruct(dims, dtype)


def tiles_of(start, stop):
    return [(first, min(first + 128, stop)) for first in range(start, stop, 128)]


def call(body, outs, out_spaces, scratch, args, spaces, name, scalars=(), flops=0, mib=12):
    def spec(array, space):
        return pl.BlockSpec(memory_space=pltpu.VMEM if space == "v" else pltpu.HBM)

    assert len(args) == len(spaces) and len(outs) == len(out_spaces)
    return pl.pallas_call(
        body,
        out_shape=[
            pltpu.HBM(o.shape, o.dtype) if s == "a" else o for o, s in zip(outs, out_spaces)
        ],
        grid_spec=pltpu.PrefetchScalarGridSpec(
            num_scalar_prefetch=len(scalars),
            grid=(1,),
            in_specs=[spec(a, s) for a, s in zip(args, spaces)],
            out_specs=[spec(o, s) for o, s in zip(outs, out_spaces)],
            scratch_shapes=scratch,
        ),
        compiler_params=pltpu.CompilerParams(vmem_limit_bytes=mib * 2**20),
        cost_estimate=pl.CostEstimate(
            flops=flops,
            transcendentals=0,
            bytes_accessed=sum(a.size * a.dtype.itemsize for a in list(args) + list(outs)),
        ),
        name=name,
    )(
        *scalars,
        *[
            pltpu.with_memory_space_constraint(a, pltpu.HBM) if s == "a" else a
            for a, s in zip(args, spaces)
        ],
    )


class Planes:
    def __init__(self, source, target, sem, start=0):
        self.source, self.target, self.sem, self.start_at = source, target, sem, start

    def copy(self, h):
        return pltpu.make_async_copy(
            self.source.at[h + self.start_at], self.target.at[h], self.sem.at[h]
        )

    def start(self, h):
        self.copy(h).start()

    def wait(self, h):
        self.copy(h).wait()

    def start_all(self):
        for h in range(self.sem.shape[0]):
            self.start(h)

    def wait_all(self):
        for h in range(self.sem.shape[0]):
            self.wait(h)


class Parts:
    def __init__(self, sources, target, sem):
        self.target, self.sem = target, sem
        self.places = [source.at[h] for source in sources for h in range(source.shape[0])]

    def start_all(self):
        for h, source in enumerate(self.places):
            pltpu.make_async_copy(source, self.target.at[h], self.sem.at[h]).start()

    def wait(self, h):
        pltpu.make_async_copy(self.places[0], self.target.at[h], self.sem.at[h]).wait()


class Outwards(Planes):
    def copy(self, h):
        return pltpu.make_async_copy(
            self.source.at[h], self.target.at[h + self.start_at], self.sem.at[h]
        )


def sigmoid(value):
    return 0.5 * jnp.tanh(0.5 * value) + 0.5


def rows_summed(value):
    return value.reshape(value.shape[0] // 8, 8, value.shape[1]).sum(0)


def put_permuted(target, row, source, pieces, offset=0):
    for inner, outer, width in pieces:
        target[row : row + 1, inner : inner + width] = source[
            :, offset + outer : offset + outer + width
        ]


def put_original(target, row, value, pieces):
    for inner, outer, width in pieces:
        target[row : row + 1, outer : outer + width] = value[:, inner : inner + width]


def put_stats(stat_ref, acc_ref, count=None):
    peers, rows, width = stat_ref.shape
    for row in range(2):
        line = jnp.sum(acc_ref[row], axis=0, keepdims=True)
        stat_ref[:, row : row + 1, :] = jnp.broadcast_to(line[None], (peers, 1, width))
    if count is not None:
        stat_ref[:, 2:3, :] = jnp.broadcast_to(count.reshape(1, 1, 1), (peers, 1, width))


def plane_stats(value_ref, h, keep, acc_ref):
    for first, last in tiles_of(0, value_ref.shape[2]):
        value = value_ref[h, :, first:last]
        masked = value * keep
        acc_ref[0, :, first:last] += rows_summed(masked)
        acc_ref[1, :, first:last] += rows_summed(masked * value)


def times_of(rows, width, extent):
    return lax.broadcasted_iota(jnp.int32, (rows, width), 0) & (extent - 1)


def time_shifted(value, times, extent):
    rows = value.shape[0]
    earlier = jnp.where(times != 0, pltpu.roll(value, 1, 0), 0.0)
    later = jnp.where(times != extent - 1, pltpu.roll(value, rows - 1, 0), 0.0)
    return earlier, value, later


def width_shifted(value, extent):
    rows = value.shape[0]
    if extent % 8 == 0:
        edge = jnp.zeros((extent, value.shape[1]), value.dtype)
        left = jnp.concatenate([edge, value[:-extent]], 0)
        right = jnp.concatenate([value[extent:], edge], 0)
    else:
        left = pltpu.roll(value, extent, 0)
        right = pltpu.roll(value, rows - extent, 0)
    return left, value, right


def window_sums(source_ref, between_ref, extent, put):
    planes, rows, width = source_ref.shape
    between_ref[0] = jnp.zeros((rows, width), F32)
    between_ref[planes + 1] = jnp.zeros((rows, width), F32)
    times = times_of(rows, width, extent)

    def plane(h, carry):
        before, here, after = time_shifted(source_ref[h], times, extent)
        left, here, right = width_shifted(before + here + after, extent)
        between_ref[h + 1] = left + here + right
        return carry

    lax.fori_loop(0, planes, plane, 0)

    def through(h, carry):
        put(h, (between_ref[h] + between_ref[h + 1] + between_ref[h + 2]) * (1.0 / 27.0))
        return carry

    lax.fori_loop(0, planes, through, 0)


def turned_ordered(turned_ref, ordered_ref):
    for row_to, row_from, height in FIRST_PIECES:
        for inner, outer, width in RESULT_PIECES:
            ordered_ref[row_to : row_to + height, inner : inner + width] = turned_ref[
                row_from : row_from + height, outer : outer + width
            ]


def weight_ordered(weight_ref, ordered_ref):
    for inner, outer, width in FIRST_PIECES:
        ordered_ref[:, inner : inner + width] = weight_ref[:, outer : outer + width]


def step_planes(planes):
    return (planes // 2, 2) if planes % 2 == 0 else (planes, 1)


def put_masks(valid, mask_ref, keep_ref, next_ref):
    planes, rows, unused = keep_ref.shape
    unused, extent, width = mask_ref.shape

    def one_hot(shape, picked):
        places = lax.broadcasted_iota(jnp.int32, shape, 1)
        index = lax.broadcasted_iota(jnp.int32, shape, 0)
        return (places == picked(index)).astype(F32)

    times = one_hot((rows, extent), lambda r: r & (extent - 1))
    columns = one_hot((rows, width), lambda r: r // extent)
    frame = lax.broadcasted_iota(jnp.int32, (extent, width), 0)
    for h in range(planes):
        plane = jnp.where(frame < valid, mask_ref[h], 0).astype(F32)
        picked = jnp.dot(times, plane, preferred_element_type=F32) * columns
        keep_ref[h] = jnp.sum(picked, axis=1, keepdims=True)
    rows_next = next_ref.shape[1]
    half = extent // 2
    index = lax.broadcasted_iota(jnp.int32, (rows_next, rows), 0)
    places = lax.broadcasted_iota(jnp.int32, (rows_next, rows), 1)
    same_time = (places & (extent - 1)) // 2 == (index & (half - 1))
    same_column = places // (2 * extent) == index // half
    pooled = (same_time & same_column).astype(F32)
    for h in range(next_ref.shape[0]):
        both = jnp.broadcast_to(keep_ref[2 * h] + keep_ref[2 * h + 1], (rows, 128))
        held = jnp.dot(pooled, both, preferred_element_type=F32)
        next_ref[h] = jnp.where(held[:, 0:1] > 0.5, 1.0, 0.0)


def project_body(
    order_ref,
    section_ref,
    frames_ref,
    x_hbm,
    mask_hbm,
    weight_hbm,
    z_hbm,
    stat_ref,
    keep_ref,
    next_ref,
    x_v,
    mask_v,
    weight_v,
    z_v,
    ordered,
    pool,
    between,
    acc,
    x_sem,
    z_sem,
    weight_sem,
):
    planes, rows, channels = x_v.shape
    extent = 8
    clip = order_ref[section_ref[0]]
    arriving = Planes(x_hbm.at[clip], x_v, x_sem)
    leaving = Outwards(z_v, z_hbm, z_sem)
    weight_in = pltpu.make_async_copy(weight_hbm, weight_v, weight_sem.at[0])
    mask_in = pltpu.make_async_copy(mask_hbm.at[clip], mask_v, weight_sem.at[1])
    mask_in.start()
    weight_in.start()
    arriving.start_all()
    mask_in.wait()
    put_masks(frames_ref[clip], mask_v, keep_ref, next_ref)
    weight_in.wait()
    weight_ordered(weight_v, ordered)
    together, steps = step_planes(planes)

    def product(i, carry):
        def masked(k, carry):
            h = i * together + k
            arriving.wait(h)
            x_v[h] = x_v[h] * keep_ref[h].astype(BF16)
            return carry

        lax.fori_loop(0, together, masked, 0)
        at = pl.ds(i * together, together)
        value = x_v[at].reshape(together * rows, channels)
        out = jnp.dot(value, ordered[...], preferred_element_type=F32)
        z_v[at] = out.reshape(together, rows, NB1)
        pool[at] = out[:, B0:ND].reshape(together, rows, B3)
        return carry

    lax.fori_loop(0, steps, product, 0)
    acc[...] = jnp.zeros_like(acc)

    def put(h, value):
        z_v[h, :, B0:ND] = value
        leaving.start(h)
        plane_stats(z_v, h, keep_ref[h], acc)

    window_sums(pool, between, extent, put)
    put_stats(stat_ref, acc, jnp.sum(keep_ref[...]))
    leaving.wait_all()


def project_first(clips, order, section, frames, voxel_mask, weight, peers):
    unused, planes, rows, channels = clips.shape
    unused, unused, extent, width = voxel_mask.shape
    return call(
        project_body,
        [
            shape_of(planes, rows, NB1),
            shape_of(peers, 3, NB1),
            shape_of(planes, rows, 1),
            shape_of(planes // 2, (width // 2 + 1) * extent // 2, 1),
        ],
        "avvv",
        [
            pltpu.VMEM((planes, rows, channels), BF16),
            pltpu.VMEM(voxel_mask.shape[1:], jnp.int32),
            pltpu.VMEM((channels, NB1), BF16),
            pltpu.VMEM((planes, rows, NB1), F32),
            pltpu.VMEM((channels, NB1), BF16),
            pltpu.VMEM((planes, rows, B3), F32),
            pltpu.VMEM((planes + 2, rows, B3), F32),
            pltpu.VMEM((2, 8, NB1), F32),
            DMA((planes,)),
            DMA((planes,)),
            DMA((2,)),
        ],
        (clips, voxel_mask, weight),
        "aaa",
        "project_first",
        (order, section, frames),
        flops=2 * planes * rows * channels * NB1,
        mib=16,
    )


def level_rows(vec, gain_ref, bias_ref, mom_ref, pieces, offset):
    put_permuted(vec, 4, gain_ref, pieces, offset)
    put_permuted(vec, 5, bias_ref, pieces, offset)
    mean, var = mom_ref[0:1, :], mom_ref[1:2, :]
    inverse = lax.rsqrt(var + EPSILON)
    scale = vec[4:5, :] * inverse
    vec[0:1, :] = scale
    vec[1:2, :] = vec[5:6, :] - mean * scale
    vec[2:3, :] = inverse
    vec[3:4, :] = -mean * inverse


def first_rows(vec, gain_ref, bias_ref, mom_ref):
    level_rows(vec, gain_ref, bias_ref, mom_ref, FIRST_PIECES, 0)


def second_rows(vec, gain_ref, bias_ref, mom_ref):
    level_rows(vec, gain_ref, bias_ref, mom_ref, SECOND_PIECES, NB1)


def back_rows(vec, total, count):
    cross = vec[0:1, :] * total[1:2] / count
    vec[6:7, :] = -(vec[0:1, :] * total[0:1] / count) - cross * vec[3:4, :]
    vec[7:8, :] = -cross * vec[2:3, :]


def put_moments(tot_ref, mom_ref, count):
    total = jnp.sum(tot_ref[...], axis=0)
    if count is None:
        count = total[2:3, :]
        mom_ref[2:3, :] = count
    mean = total[0:1, :] / count
    mom_ref[0:1, :] = mean
    mom_ref[1:2, :] = total[1:2, :] / count - mean * mean


def spread_plane(value, first, times, extent, targets, index):
    width = value.shape[1]
    for early, shifted in enumerate(time_shifted(value, times[:, 0:width], extent)):
        for side, moved in enumerate(width_shifted(shifted, extent)):
            place = early * 3 + side
            moved = moved.astype(BF16)
            for target, low, high in targets:
                begin, end = max(low, first), min(high, first + width)
                if begin < end:
                    start = place * (high - low) + begin - low
                    target[index, :, start : start + end - begin] = moved[
                        :, begin - first : end - first
                    ]


def clear_ends(targets, ends):
    for target, unused, unused in targets:
        for end in ends:
            target[end] = jnp.zeros(target.shape[1:], BF16)


def weight_copies(source, target, sems):
    return [
        pltpu.make_async_copy(
            source.at[pl.ds(time * 9 + height * 3, 3)],
            target.at[height, pl.ds(time * 3, 3)],
            sems.at[height * 3 + time],
        )
        for height in range(3)
        for time in range(3)
    ]


def second_body(
    extent,
    tot_ref,
    z_hbm,
    keep_ref,
    gain_ref,
    bias_ref,
    wide_hbm,
    narrow_hbm,
    act_hbm,
    mid_hbm,
    out_hbm,
    stat_ref,
    mom_ref,
    vec,
    z_v,
    act_v,
    mid_v,
    out_v,
    wide_v,
    narrow_v,
    im_wide,
    im_narrow,
    acc,
    z_sem,
    wide_sem,
    narrow_sem,
    act_sem,
    mid_sem,
    out_sem,
):
    planes, rows, unused = z_v.shape
    arriving = Planes(z_hbm, z_v, z_sem)
    arriving.start_all()
    weights = weight_copies(wide_hbm, wide_v, wide_sem) + weight_copies(
        narrow_hbm, narrow_v, narrow_sem
    )
    for copy in weights:
        copy.start()
    act_out = Outwards(act_v, act_hbm, act_sem)
    mid_out = Outwards(mid_v, mid_hbm, mid_sem)
    out_out = Outwards(out_v, out_hbm, out_sem)
    put_moments(tot_ref, mom_ref, None)
    first_rows(vec, gain_ref, bias_ref, mom_ref)
    targets = ((im_wide, 0, B1A), (im_narrow, B1A, NM))
    clear_ends(targets, (0, planes + 1))
    times = times_of(rows, 128, extent)

    def activate(h, carry):
        arriving.wait(h)
        keep = keep_ref[h]
        for first, last in tiles_of(0, NB1):
            shifted = z_v[h, :, first:last] * vec[0:1, first:last] + vec[1:2, first:last]
            value = shifted * sigmoid(shifted) * keep
            if first < ND:
                act_v[h, :, first:last] = value.astype(BF16)
            else:
                mid_v[h, :, first - ND : last - ND] = value.astype(BF16)
                spread_plane(value, first - ND, times, extent, targets, h + 1)
        act_out.start(h)
        mid_out.start(h)
        return carry

    lax.fori_loop(0, planes, activate, 0)
    for copy in weights:
        copy.wait()
    acc[...] = jnp.zeros_like(acc)
    together, steps = step_planes(planes)

    def convolve(i, carry):
        at = pl.ds(i * together, together)
        for im_ref, weight_ref, first, last in (
            (im_narrow, narrow_v, 0, B2),
            (im_wide, wide_v, B2, NB2),
        ):
            total = None
            for high in range(3):
                value = im_ref[pl.ds(i * together + high, together)]
                value = value.reshape(together * rows, value.shape[2])
                weight = weight_ref[high].reshape(value.shape[1], last - first)
                part = jnp.dot(value, weight, preferred_element_type=F32)
                total = part if total is None else total + part
            out_v[at, :, first:last] = total.reshape(together, rows, last - first)

        def finish(k, carry):
            h = i * together + k
            out_out.start(h)
            plane_stats(out_v, h, keep_ref[h], acc)
            return carry

        lax.fori_loop(0, together, finish, 0)
        return carry

    lax.fori_loop(0, steps, convolve, 0)
    put_stats(stat_ref, acc)
    act_out.wait_all()
    mid_out.wait_all()
    out_out.wait_all()


def second_level(totals, first_out, keep, params, extent, peers):
    unused, conv_mid, conv_small, gain, bias = params
    planes, rows, unused = first_out.shape
    return call(
        functools.partial(second_body, extent),
        [
            shape_of(planes, rows, ND, dtype=BF16),
            shape_of(planes, rows, NM, dtype=BF16),
            shape_of(planes, rows, NB2),
            shape_of(peers, 2, NB2),
            shape_of(3, NB1),
        ],
        "aaavv",
        [
            pltpu.VMEM((8, NB1), F32),
            pltpu.VMEM((planes, rows, NB1), F32),
            pltpu.VMEM((planes, rows, ND), BF16),
            pltpu.VMEM((planes, rows, NM), BF16),
            pltpu.VMEM((planes, rows, NB2), F32),
            pltpu.VMEM((3, 9, B1A, B1), BF16),
            pltpu.VMEM((3, 9, B2A, B2), BF16),
            pltpu.VMEM((planes + 2, rows, 9 * B1A), BF16),
            pltpu.VMEM((planes + 2, rows, 9 * B2A), BF16),
            pltpu.VMEM((2, 8, NB2), F32),
            DMA((planes,)),
            DMA((9,)),
            DMA((9,)),
            DMA((planes,)),
            DMA((planes,)),
            DMA((planes,)),
        ],
        (totals, first_out, keep, gain, bias, conv_mid, conv_small),
        "vavvvaa",
        "second_level",
        flops=2 * planes * rows * 27 * (B1A * B1 + B2A * B2),
        mib=30,
    )


def cell_of(shape, axis, rows):
    row = lax.broadcasted_iota(jnp.int32, shape, axis)
    row = jnp.where(row >= rows, row - rows, row)
    return (row // 16) * 4 + (row % 8) // 2


def between_body(
    tot_ref,
    z_hbm,
    keep_ref,
    gain_ref,
    bias_ref,
    act_hbm,
    first_mom_ref,
    keep_next_ref,
    weight_ref,
    x_ref,
    z_next_ref,
    stat_ref,
    mom_ref,
    vec,
    z_v,
    act_v,
    both,
    ordered,
    pool,
    between,
    acc,
    z_sem,
    act_sem,
):
    planes, rows, channels = x_ref.shape
    z_in = Planes(z_hbm, z_v, z_sem)
    act_in = Planes(act_hbm, act_v, act_sem)
    for h in range(2 * planes):
        act_in.start(h)
        z_in.start(h)
    put_moments(tot_ref, mom_ref, first_mom_ref[2:3, 0:NB2])
    second_rows(vec, gain_ref, bias_ref, mom_ref)
    turned_ordered(weight_ref, ordered)
    extent = 4
    source_rows = z_v.shape[1]
    shape = (rows, 2 * source_rows)
    cells = cell_of(shape, 1, source_rows) == lax.broadcasted_iota(jnp.int32, shape, 0)
    pooled = jnp.where(cells, 1.0, 0.0).astype(BF16)

    def pooling(h, carry):
        for step in range(2):
            act_in.wait(2 * h + step)
            z_in.wait(2 * h + step)
        keeps = [keep_ref[2 * h], keep_ref[2 * h + 1]]
        keep_next = keep_next_ref[h]
        for first, last in tiles_of(0, C5):
            for step in range(2):
                if first < ND:
                    part = act_v[2 * h + step, :, first:last]
                else:
                    at = slice(first - ND, last - ND)
                    shifted = z_v[2 * h + step, :, at] * vec[0:1, at] + vec[1:2, at]
                    part = (shifted * sigmoid(shifted) * keeps[step]).astype(BF16)
                both[step * source_rows : (step + 1) * source_rows, first:last] = part
        mean = jnp.dot(pooled, both[...], preferred_element_type=F32) * 0.125
        x_ref[h] = (mean.astype(BF16).astype(F32) * keep_next).astype(BF16)
        return carry

    lax.fori_loop(0, planes, pooling, 0)
    value = x_ref[...].reshape(planes * rows, channels)
    out = lax.dot_general(
        value, ordered[...], (((1,), (1,)), ((), ())), preferred_element_type=F32
    )
    z_next_ref[...] = out.reshape(planes, rows, NB1)
    pool[...] = out[:, B0:ND].reshape(planes, rows, B3)
    acc[...] = jnp.zeros_like(acc)

    def put(h, value):
        z_next_ref[h, :, B0:ND] = value
        plane_stats(z_next_ref, h, keep_next_ref[h], acc)

    window_sums(pool, between, extent, put)
    put_stats(stat_ref, acc, jnp.sum(keep_next_ref[...]))


def between_blocks(totals, second_out, keep, params, act, first_mom, keep_next, weight, peers):
    planes, rows = keep_next.shape[:2]
    above, source_rows = second_out.shape[:2]
    return call(
        between_body,
        [
            shape_of(planes, rows, C5, dtype=BF16),
            shape_of(planes, rows, NB1),
            shape_of(peers, 3, NB1),
            shape_of(2, NB2),
        ],
        "vvvv",
        [
            pltpu.VMEM((8, NB2), F32),
            pltpu.VMEM(second_out.shape, F32),
            pltpu.VMEM(act.shape, BF16),
            pltpu.VMEM((2 * source_rows, C5), BF16),
            pltpu.VMEM((NB1, C5), BF16),
            pltpu.VMEM((planes, rows, B3), F32),
            pltpu.VMEM((planes + 2, rows, B3), F32),
            pltpu.VMEM((2, 8, NB1), F32),
            DMA((above,)),
            DMA((above,)),
        ],
        (totals, second_out, keep, params[3], params[4], act, first_mom, keep_next, weight),
        "vavvvavvv",
        "between_blocks",
        flops=2 * planes * rows * C5 * NB1,
        mib=16,
    )


def turn_body(
    clip_ref,
    section_ref,
    tot_ref,
    z_hbm,
    keep_ref,
    gain_ref,
    bias_ref,
    act_hbm,
    first_mom_ref,
    grad_hbm,
    kept_ref,
    sent_ref,
    slope_hbm,
    direct_hbm,
    stat_ref,
    mom_ref,
    vec,
    z_v,
    act_v,
    grad_v,
    slope_v,
    direct_v,
    grad,
    result,
    acc,
    z_sem,
    act_sem,
    grad_sem,
    slope_sem,
    direct_sem,
):
    planes, rows, unused = z_v.shape
    unused, width, extent, unused = grad_v.shape
    half = extent // 2
    later = section_ref[0] == 1
    z_in = Planes(z_hbm, z_v, z_sem)
    act_in = Planes(act_hbm, act_v, act_sem)
    grad_in = Planes(grad_hbm.at[clip_ref[0]], grad_v, grad_sem)
    for h in range(planes):
        grad_in.start(h)
        act_in.start(h)
        z_in.start(h)
    slope_out = Outwards(slope_v, slope_hbm, slope_sem)
    direct_out = Outwards(direct_v, direct_hbm, direct_sem)
    put_moments(tot_ref, mom_ref, first_mom_ref[2:3, 0:NB2])
    second_rows(vec, gain_ref, bias_ref, mom_ref)
    acc[...] = jnp.zeros_like(acc)
    grad[...] = jnp.zeros_like(grad)

    def plane(h, carry):
        keep = keep_ref[h]
        grad_in.wait(h)
        act_in.wait(h)
        z_in.wait(h)
        for column in range(width):
            at = slice(column * extent, (column + 1) * extent)
            grad[at, :] = grad_v[h, column].astype(F32)
        direct_v[h, :, 0:B0] = grad[:, 0:B0].astype(BF16)
        direct_v[h, :, B0:ND] = grad[:, C5 - B3 :].astype(BF16)
        result[:, 0:B0] = act_v[h, :, 0:B0].astype(F32)
        result[:, C5 - B3 :] = act_v[h, :, B0:ND].astype(F32)
        for inner, outer, size in SECOND_PIECES:
            at = slice(inner, inner + size)
            place = slice(B0 + outer, B0 + outer + size)
            value = z_v[h, :, at]
            shifted = value * vec[0:1, at] + vec[1:2, at]
            gate = sigmoid(shifted)
            result[:, place] = shifted * gate * keep
            slope = grad[:, place] * keep * gate * (1.0 + shifted * (1.0 - gate))
            slope_v[h, :, at] = slope
            acc[0, :, at] += rows_summed(slope)
            acc[1, :, at] += rows_summed(slope * (value * vec[2:3, at] + vec[3:4, at]))
        slope_out.start(h)
        direct_out.start(h)
        for column in range(width):
            start = column * extent
            early = result[start : start + half, :]
            late = result[start + half : start + extent, :]
            kept_ref[h, column] = jnp.where(later, late, early).astype(BF16)
            sent_ref[h, column] = jnp.where(later, early, late).astype(BF16)
        return carry

    lax.fori_loop(0, planes, plane, 0)
    put_stats(stat_ref, acc)
    slope_out.wait_all()
    direct_out.wait_all()


def turn(
    totals, second_out, keep, params, act, first_mom, cotangent, own_clip, section, peers
):
    planes, rows, unused = second_out.shape
    unused, unused, width, extent, unused = cotangent.shape
    half = (planes, width, extent // 2, C5)
    return call(
        turn_body,
        [
            shape_of(*half, dtype=BF16),
            shape_of(*half, dtype=BF16),
            shape_of(planes, rows, NB2),
            shape_of(planes, rows, ND, dtype=BF16),
            shape_of(peers, 2, NB2),
            shape_of(2, NB2),
        ],
        "vvaavv",
        [
            pltpu.VMEM((8, NB2), F32),
            pltpu.VMEM((planes, rows, NB2), F32),
            pltpu.VMEM((planes, rows, ND), BF16),
            pltpu.VMEM(cotangent.shape[1:], BF16),
            pltpu.VMEM((planes, rows, NB2), F32),
            pltpu.VMEM((planes, rows, ND), BF16),
            pltpu.VMEM((rows, C5), F32),
            pltpu.VMEM((rows, C5), F32),
            pltpu.VMEM((2, 8, NB2), F32),
            DMA((planes,)),
            DMA((planes,)),
            DMA((planes,)),
            DMA((planes,)),
            DMA((planes,)),
        ],
        (totals, second_out, keep, params[3], params[4], act, first_mom, cotangent),
        "vavvvava",
        "turn",
        (own_clip, section),
        mib=12,
    )


def slope_plane(
    upstream, z_ref, h, vec, keep, slope_ref, slope_at, acc, tiles
):
    for first, last in tiles:
        at = slice(first, last)
        value = z_ref[h, :, at]
        shifted = value * vec[0:1, at] + vec[1:2, at]
        gate = sigmoid(shifted)
        slope = upstream(first, last) * keep * gate * (1.0 + shifted * (1.0 - gate))
        slope_ref[slope_at, :, at] = slope
        acc[0, :, at] += rows_summed(slope)
        acc[1, :, at] += rows_summed(slope * (value * vec[2:3, at] + vec[3:4, at]))


def put_halves(section, packed, kept_hbm, sent_hbm, sems):
    half = packed.shape[0] // 2
    copies = [
        pltpu.make_async_copy(
            packed.at[pl.ds(pl.multiple_of(which * half, 16), half)],
            target.at[pl.ds(0, half)],
            sems.at[place],
        )
        for place, (which, target) in enumerate(((section, kept_hbm), (1 - section, sent_hbm)))
    ]
    for copy in copies:
        copy.start()
    return copies


def conv_grad_body(
    extent,
    section_ref,
    tot_ref,
    slope_hbm,
    z_hbm,
    mid_hbm,
    keep_ref,
    gain_ref,
    bias_ref,
    first_mom_ref,
    mom_ref,
    more_kept_hbm,
    more_sent_hbm,
    grad_hbm,
    kept_hbm,
    sent_hbm,
    norm_ref,
    vec,
    slope_v,
    z_v,
    mid_v,
    grad_v,
    im_wide,
    im_narrow,
    turned,
    packed,
    more_v,
    slope_sem,
    z_sem,
    mid_sem,
    grad_sem,
    half_sem,
):
    planes, rows, unused = z_v.shape
    slope_in = Planes(slope_hbm, slope_v, slope_sem)
    z_in = Planes(z_hbm, z_v, z_sem)
    mid_in = Planes(mid_hbm, mid_v, mid_sem)
    grad_out = Outwards(grad_v, grad_hbm, grad_sem)
    for h in range(planes):
        mid_in.start(h)
        slope_in.start(h)
        z_in.start(h)
    half_rows = packed.shape[0] // 2
    more = kept_hbm.shape[0] - half_rows
    beside = [
        (
            pltpu.make_async_copy(source, more_v.at[place], half_sem.at[2 + place]),
            pltpu.make_async_copy(
                more_v.at[place], target.at[pl.ds(half_rows, more)], half_sem.at[4 + place]
            ),
        )
        for place, (source, target) in enumerate(
            ((more_kept_hbm, kept_hbm), (more_sent_hbm, sent_hbm))
        )
        if more
    ]
    for arriving, leaving in beside:
        arriving.start()
    total = jnp.sum(tot_ref[...], axis=0)
    put_original(norm_ref, 0, total[1:2], SECOND_PIECES)
    put_original(norm_ref, 1, total[0:1], SECOND_PIECES)
    second_rows(vec, gain_ref, bias_ref, mom_ref)
    back_rows(vec, total, first_mom_ref[2:3, 0:NB2])
    targets = ((im_wide, 0, B1A), (im_narrow, B1A, NM))
    clear_ends(targets, (0, planes + 1))
    times = times_of(rows, 128, extent)

    def gradient(h, carry):
        mid_in.wait(h)
        for first, last in tiles_of(0, NM):
            value = mid_v[h, :, first:last].astype(F32)
            spread_plane(value, first, times, extent, targets, h + 1)
        slope_in.wait(h)
        z_in.wait(h)
        keep = keep_ref[h]
        for first, last in tiles_of(0, NB2):
            at = slice(first, last)
            value = slope_v[h, :, at] * vec[0:1, at] + z_v[h, :, at] * vec[7:8, at] + vec[6:7, at]
            grad_v[h, :, at] = (value * keep).astype(BF16)
        grad_out.start(h)
        return carry

    lax.fori_loop(0, planes, gradient, 0)
    for arriving, leaving in beside:
        arriving.wait()
        leaving.start()
    turned[...] = grad_v[...].reshape(planes * rows, NB2).T
    wide_rows = 27 * B1A
    half = wide_rows // 2
    used = CONV_NARROW + 27 * B2A
    packed[used:, :] = jnp.zeros((packed.shape[0] - used, 128), BF16)
    step = 3 * B1A
    for high in range(3):
        value = im_wide[high : high + planes].reshape(planes * rows, 9 * B1A)
        part = jnp.dot(turned[B2:NB2, :], value, preferred_element_type=F32)
        part = part.T.astype(BF16)
        value = im_narrow[high : high + planes].reshape(planes * rows, 9 * B2A)
        small = jnp.dot(turned[0:B2, :], value, preferred_element_type=F32)
        small = small.T.astype(BF16)
        for time in range(3):
            chunk = time * 3 + high
            row = chunk * step
            piece = part[time * step : (time + 1) * step]
            packed[row : row + step, :] = piece[:, 0:128]
            packed[wide_rows + row : wide_rows + row + step, :] = piece[:, 128:256]
            low = max(0, min(step, half - row))
            tail = 2 * wide_rows + row
            if low > 0:
                packed[tail : tail + low, 0:64] = piece[:low, 256:B1]
            if low < step:
                tail = tail + low - half
                packed[tail : tail + step - low, 64:128] = piece[low:, 256:B1]
            row = CONV_NARROW + chunk * 3 * B2A
            packed[row : row + 3 * B2A, :] = small[time * 3 * B2A : (time + 1) * 3 * B2A]
    copies = put_halves(section_ref[0], packed, kept_hbm, sent_hbm, half_sem)
    grad_out.wait_all()
    for copy in copies + [leaving for arriving, leaving in beside]:
        copy.wait()


def conv_grad(
    totals, slope, second_out, mid, keep, params, first_mom, mom, extent, section, peers, more=None
):
    planes, rows, unused = second_out.shape
    packed = conv_rows(peers)
    half = packed // 2
    if more is None:
        more = (mid, mid)
    else:
        half += more[0].shape[0]
    return call(
        functools.partial(conv_grad_body, extent),
        [
            shape_of(planes, rows, NB2, dtype=BF16),
            shape_of(half, 128, dtype=BF16),
            shape_of(half, 128, dtype=BF16),
            shape_of(2, NB2),
        ],
        "aaav",
        [
            pltpu.VMEM((8, NB2), F32),
            pltpu.VMEM((planes, rows, NB2), F32),
            pltpu.VMEM((planes, rows, NB2), F32),
            pltpu.VMEM((planes, rows, NM), BF16),
            pltpu.VMEM((planes, rows, NB2), BF16),
            pltpu.VMEM((planes + 2, rows, 9 * B1A), BF16),
            pltpu.VMEM((planes + 2, rows, 9 * B2A), BF16),
            pltpu.VMEM((NB2, planes * rows), BF16),
            pltpu.VMEM((packed, 128), BF16),
            pltpu.VMEM((2, max(half - packed // 2, 16), 128), BF16),
            DMA((planes,)),
            DMA((planes,)),
            DMA((planes,)),
            DMA((planes,)),
            DMA((6,)),
        ],
        (totals, slope, second_out, mid, keep, params[3], params[4], first_mom, mom, *more),
        "vaaavvvvvaa",
        "conv_grad",
        (section,),
        flops=2 * planes * rows * 27 * (B1A * B1 + B2A * B2),
        mib=30,
    )


def prepare_body(wide_ref, narrow_ref, turned_hbm, weights, sems):
    weights[...] = jnp.zeros_like(weights)
    copies = []
    for height in range(3):
        for place in range(9):
            source = 26 - ((place // 3) * 9 + height * 3 + place % 3)
            weights[height, 0:B1A, place * NB2 + B2 : (place + 1) * NB2] = wide_ref[source]
            weights[height, B1A:NM, place * NB2 : place * NB2 + B2] = narrow_ref[source]
        copies.append(
            pltpu.make_async_copy(weights.at[height], turned_hbm.at[height], sems.at[height])
        )
        copies[-1].start()
    for copy in copies:
        copy.wait()


def prepare(conv_mid, conv_small):
    return call(
        prepare_body,
        [shape_of(3, NM, TURNED, dtype=BF16)],
        "a",
        [pltpu.VMEM((3, NM, TURNED), BF16), DMA((3,))],
        (conv_mid, conv_small),
        "vv",
        "prepare",
        mib=24,
    )[0]


def back_conv_body(
    extent,
    halved,
    start,
    grad_hbm,
    z_hbm,
    keep_ref,
    gain_ref,
    bias_ref,
    first_mom_ref,
    direct_hbm,
    turned_hbm,
    before_ref,
    slope_hbm,
    stat_ref,
    acc,
    vec,
    grad_v,
    z_v,
    direct_v,
    slope_v,
    windows,
    weights,
    grad_sem,
    z_sem,
    direct_sem,
    weight_sem,
    slope_sem,
):
    planes = grad_hbm.shape[0]
    count, rows, unused = z_v.shape
    low = 1 if start == 0 else 0
    high = count + 1 if start + count == planes else count + 2
    grad_in = Planes(grad_hbm, grad_v, grad_sem, start - 1)
    for j in range(low, high):
        grad_in.start(j)
    weights_in = Planes(turned_hbm, weights, weight_sem)
    weights_in.start_all()
    z_in = Planes(z_hbm, z_v, z_sem, start)
    z_in.start_all()
    direct_in = Planes(direct_hbm, direct_v, direct_sem)
    direct_in.start_all()
    slope_out = Outwards(slope_v, slope_hbm, slope_sem)
    first_rows(vec, gain_ref, bias_ref, first_mom_ref)
    targets = ((windows, 0, NB2),)
    clear_ends(targets, [0] * low + [count + 1] * (count + 2 - high))
    times = times_of(rows, 128, extent)

    def shift(j, carry):
        grad_in.wait(j)
        for first, last in tiles_of(0, NB2):
            value = grad_v[j, :, first:last].astype(F32)
            spread_plane(value, first, times, extent, targets, j)
        return carry

    lax.fori_loop(low, high, shift, 0)
    weights_in.wait_all()
    total = None
    for height in range(3):
        value = windows[height : height + count].reshape(count * rows, 9 * NB2)
        part = lax.dot_general(
            value,
            weights[height, :, 0 : 9 * NB2],
            (((1,), (1,)), ((), ())),
            preferred_element_type=F32,
        )
        total = part if total is None else total + part
    slope_v[:, :, ND:NB1] = total.reshape(count, rows, NM)
    acc[...] = before_ref[...]
    direct_in.wait_all()

    def slopes(h, carry):
        z_in.wait(h)

        def upstream(first, last):
            if first >= ND:
                return slope_v[h, :, first:last]
            if halved:
                return direct_v[(start + h) // 2, :, first:last].astype(F32) * 0.125
            return direct_v[start + h, :, first:last].astype(F32)

        slope_plane(upstream, z_v, h, vec, keep_ref[start + h], slope_v, h, acc, tiles_of(0, NB1))
        slope_out.start(h)
        return carry

    lax.fori_loop(0, count, slopes, 0)
    put_stats(stat_ref, acc)
    slope_out.wait_all()


def back_conv(
    grad, first_out, keep, params, turned, first_mom, direct, halved, extent, peers, part, before
):
    unused, unused, unused, gain, bias = params
    planes, rows, unused = first_out.shape
    start, count = part
    return call(
        functools.partial(back_conv_body, extent, halved, start),
        [shape_of(count, rows, NB1), shape_of(peers, 2, NB1), shape_of(2, 8, NB1)],
        "avv",
        [
            pltpu.VMEM((8, NB1), F32),
            pltpu.VMEM((count + 2, rows, NB2), BF16),
            pltpu.VMEM((count, rows, NB1), F32),
            pltpu.VMEM(direct.shape, BF16),
            pltpu.VMEM((count, rows, NB1), F32),
            pltpu.VMEM((count + 2, rows, 9 * NB2), BF16),
            pltpu.VMEM((3, NM, TURNED), BF16),
            DMA((count + 2,)),
            DMA((count,)),
            DMA((direct.shape[0],)),
            DMA((3,)),
            DMA((count,)),
        ],
        (grad, first_out, keep, gain, bias, first_mom, direct, turned, before),
        "aavvvvaav",
        "back_conv",
        flops=2 * count * rows * 27 * (B1A * B1 + B2A * B2),
        mib=30,
    )


def first_gradient(slope_of, z_ref, keep_ref, vec, grad_ref, pool_ref, between_ref, extent, done):
    planes, rows, unused = z_ref.shape

    def gradient(h, carry):
        slope = slope_of(h)
        keep = keep_ref[h]
        for first, last in tiles_of(0, NB1):
            at = slice(first, last)
            value = (
                slope[h, :, at] * vec[0:1, at] + z_ref[h, :, at] * vec[7:8, at] + vec[6:7, at]
            ) * keep
            if first == B0:
                pool_ref[h] = value
            else:
                grad_ref[h, :, at] = value.astype(BF16)
        return carry

    lax.fori_loop(0, planes, gradient, 0)

    def put(h, value):
        grad_ref[h, :, B0:ND] = value.astype(BF16)
        done(h)

    window_sums(pool_ref, between_ref, extent, put)


def put_norms(norm_ref, total, pieces):
    put_original(norm_ref, 0, total[1:2], pieces)
    put_original(norm_ref, 1, total[0:1], pieces)


def last_gradient_body(
    tot_ref,
    slope_0,
    slope_1,
    z_hbm,
    keep_ref,
    gain_ref,
    bias_ref,
    mom_ref,
    grad_hbm,
    norm_ref,
    vec,
    slope_v,
    z_v,
    grad_v,
    pool,
    between,
    slope_sem,
    z_sem,
    grad_sem,
):
    planes, rows, unused = z_v.shape
    z_in = Planes(z_hbm, z_v, z_sem)
    slope_in = Parts((slope_0, slope_1), slope_v, slope_sem)
    grad_out = Outwards(grad_v, grad_hbm, grad_sem)
    slope_in.start_all()
    z_in.start_all()
    first_rows(vec, gain_ref, bias_ref, mom_ref)
    total = jnp.sum(tot_ref[...], axis=0)
    put_norms(norm_ref, total, FIRST_PIECES)
    back_rows(vec, total, mom_ref[2:3, :])

    def slope_of(h):
        slope_in.wait(h)
        z_in.wait(h)
        return slope_v

    first_gradient(slope_of, z_v, keep_ref, vec, grad_v, pool, between, 8, grad_out.start)
    grad_out.wait_all()


def last_gradient(totals, slopes, first_out, keep, params, mom):
    planes, rows, unused = first_out.shape
    return call(
        last_gradient_body,
        [shape_of(planes, rows, NB1, dtype=BF16), shape_of(2, NB1)],
        "av",
        [
            pltpu.VMEM((8, NB1), F32),
            pltpu.VMEM((planes, rows, NB1), F32),
            pltpu.VMEM((planes, rows, NB1), F32),
            pltpu.VMEM((planes, rows, NB1), BF16),
            pltpu.VMEM((planes, rows, B3), F32),
            pltpu.VMEM((planes + 2, rows, B3), F32),
            DMA((planes,)),
            DMA((planes,)),
            DMA((planes,)),
        ],
        (totals, *slopes, first_out, keep, params[3], params[4], mom),
        "vaaavvvv",
        "last_gradient",
        flops=planes * rows * NB1 * 200,
        mib=22,
    )


def clip_inproj_body(
    clip_ref,
    section_ref,
    x_hbm,
    grad_hbm,
    keep_ref,
    kept_hbm,
    sent_hbm,
    x_v,
    grad_v,
    product,
    ordered,
    packed,
    x_sem,
    grad_sem,
    half_sem,
):
    planes, rows, channels = x_v.shape
    x_in = Planes(x_hbm.at[clip_ref[0]], x_v, x_sem)
    grad_in = Planes(grad_hbm, grad_v, grad_sem)
    x_in.start_all()
    grad_in.start_all()

    def masked(h, carry):
        x_in.wait(h)
        x_v[h] = x_v[h] * keep_ref[h].astype(BF16)
        return carry

    lax.fori_loop(0, planes, masked, 0)
    grad_in.wait_all()
    product[...] = lax.dot_general(
        x_v[...].reshape(planes * rows, channels),
        grad_v[...].reshape(planes * rows, NB1),
        (((0,), (0,)), ((), ())),
        preferred_element_type=F32,
    )
    for inner, outer, width in FIRST_PIECES:
        ordered[:, outer : outer + width] = product[:, inner : inner + width]
    pack_inproj(ordered, packed)
    for copy in put_halves(section_ref[0], packed, kept_hbm, sent_hbm, half_sem):
        copy.wait()


def clip_inproj(clips, grad, keep, own_clip, section, peers):
    unused, planes, rows, channels = clips.shape
    packed = padded_rows(inproj_rows(channels)[1], peers)
    return call(
        clip_inproj_body,
        [shape_of(packed // 2, 128), shape_of(packed // 2, 128)],
        "aa",
        [
            pltpu.VMEM((planes, rows, channels), BF16),
            pltpu.VMEM((planes, rows, NB1), BF16),
            pltpu.VMEM((channels, NB1), F32),
            pltpu.VMEM((channels, NB1), F32),
            pltpu.VMEM((packed, 128), F32),
            DMA((planes,)),
            DMA((planes,)),
            DMA((2,)),
        ],
        (clips, grad, keep),
        "aav",
        "clip_inproj",
        (own_clip, section),
        flops=2 * planes * rows * channels * NB1,
        mib=20,
    )


def clip_gradient_body(
    section_ref,
    grad_hbm,
    keep_ref,
    weight_ref,
    kept_hbm,
    sent_hbm,
    grad_v,
    du_v,
    kept_v,
    sent_v,
    ordered,
    grad_sem,
    kept_sem,
    sent_sem,
):
    planes, rows, channels = du_v.shape
    unused, width, half, unused = kept_v.shape
    later = section_ref[0] == 1
    grad_in = Planes(grad_hbm, grad_v, grad_sem)
    kept_out = Outwards(kept_v, kept_hbm, kept_sem)
    sent_out = Outwards(sent_v, sent_hbm, sent_sem)
    grad_in.start_all()
    weight_ordered(weight_ref, ordered)
    together, steps = step_planes(planes)

    def product(i, carry):
        def ready(k, carry):
            grad_in.wait(i * together + k)
            return carry

        lax.fori_loop(0, together, ready, 0)
        at = pl.ds(i * together, together)
        value = grad_v[at].reshape(together * rows, NB1)
        out = lax.dot_general(
            value, ordered[...], (((1,), (1,)), ((), ())), preferred_element_type=F32
        )
        du_v[at] = out.reshape(together, rows, channels) * keep_ref[at]

        def sent(k, carry):
            h = i * together + k
            for column in range(width):
                start = 2 * half * column
                early = du_v[h, start : start + half, :]
                late = du_v[h, start + half : start + 2 * half, :]
                kept_v[h, column] = jnp.where(later, late, early).astype(BF16)
                sent_v[h, column] = jnp.where(later, early, late).astype(BF16)
            kept_out.start(h)
            sent_out.start(h)
            return carry

        lax.fori_loop(0, together, sent, 0)
        return carry

    lax.fori_loop(0, steps, product, 0)
    kept_out.wait_all()
    sent_out.wait_all()


def clip_gradient(grad, keep, inproj, width, section):
    planes, rows, unused = grad.shape
    channels = inproj.shape[0]
    half = (planes, width, rows // width // 2, channels)
    return call(
        clip_gradient_body,
        [shape_of(*half, dtype=BF16)] * 2,
        "aa",
        [
            pltpu.VMEM((planes, rows, NB1), BF16),
            pltpu.VMEM((planes, rows, channels), F32),
            pltpu.VMEM(half, BF16),
            pltpu.VMEM(half, BF16),
            pltpu.VMEM((channels, NB1), BF16),
            DMA((planes,)),
            DMA((planes,)),
            DMA((planes,)),
        ],
        (grad, keep, inproj),
        "avv",
        "clip_gradient",
        (section,),
        flops=2 * planes * rows * channels * NB1,
        mib=24,
    )


def both_clips_body(own_ref, kept_ref, got_ref, out_ref):
    own = own_ref[0]
    out_ref[own] = kept_ref[...]
    out_ref[1 - own] = got_ref[...]


def both_clips(kept, got, own_clip):
    return call(
        both_clips_body,
        [shape_of(2, *kept.shape, dtype=BF16)],
        "v",
        [],
        (kept, got),
        "vv",
        "both_clips",
        (own_clip,),
        mib=24,
    )[0]


def back_between_body(
    tot_ref,
    slope_ref,
    z_ref,
    keep_ref,
    gain_ref,
    bias_ref,
    mom_ref,
    weight_ref,
    z_hbm,
    keep_prev,
    gain_prev,
    bias_prev,
    mom_prev,
    up_hbm,
    grad_ref,
    slope_hbm,
    stat_ref,
    norm_ref,
    vec,
    vec_prev,
    ordered,
    pool,
    between,
    up_v,
    z_v,
    slope_v,
    acc,
    z_sem,
    up_sem,
    slope_sem,
):
    planes, rows, unused = z_ref.shape
    extent = 4
    z_in = Planes(z_hbm, z_v, z_sem)
    z_in.start_all()
    up_out = Outwards(up_v, up_hbm, up_sem)
    slope_out = Outwards(slope_v, slope_hbm, slope_sem)
    first_rows(vec, gain_ref, bias_ref, mom_ref)
    second_rows(vec_prev, gain_prev, bias_prev, mom_prev)
    total = jnp.sum(tot_ref[...], axis=0)
    put_norms(norm_ref, total, FIRST_PIECES)
    back_rows(vec, total, mom_ref[2:3, :])
    turned_ordered(weight_ref, ordered)
    first_gradient(
        lambda h: slope_ref, z_ref, keep_ref, vec, grad_ref, pool, between, extent, lambda h: None
    )
    value = grad_ref[...].reshape(planes * rows, NB1)
    out = lax.dot_general(
        value, ordered[...], (((1,), (0,)), ((), ())), preferred_element_type=F32
    )
    rows_prev = z_v.shape[1]
    cells = cell_of((rows_prev, rows), 0, rows_prev) == lax.broadcasted_iota(jnp.int32, (rows_prev, rows), 1)
    doubled = jnp.where(cells, 1.0, 0.0).astype(BF16)
    for h in range(planes):
        single = (out[h * rows : (h + 1) * rows] * keep_ref[h]).astype(BF16)
        up_v[h] = jnp.dot(doubled, single, preferred_element_type=F32).astype(BF16)
        up_out.start(h)
    acc[...] = jnp.zeros_like(acc)

    def slopes(h, carry):
        z_in.wait(h)

        def upstream(first, last):
            return up_v[h // 2, :, ND + first : ND + last].astype(F32) * 0.125

        slope_plane(upstream, z_v, h, vec_prev, keep_prev[h], slope_v, h, acc, tiles_of(0, NB2))
        slope_out.start(h)
        return carry

    lax.fori_loop(0, 2 * planes, slopes, 0)
    put_stats(stat_ref, acc)
    up_out.wait_all()
    slope_out.wait_all()


def back_between(
    totals, slope, first_out, keep, params, mom, second_prev, keep_prev, params_prev, mom_prev, peers
):
    inproj, unused, unused, gain, bias = params
    planes, rows, unused = first_out.shape
    above, rows_prev, unused = second_prev.shape
    return call(
        back_between_body,
        [
            shape_of(planes, rows_prev, C5, dtype=BF16),
            shape_of(planes, rows, NB1, dtype=BF16),
            shape_of(*second_prev.shape),
            shape_of(peers, 2, NB2),
            shape_of(2, NB1),
        ],
        "avavv",
        [
            pltpu.VMEM((8, NB1), F32),
            pltpu.VMEM((8, NB2), F32),
            pltpu.VMEM((NB1, C5), BF16),
            pltpu.VMEM((planes, rows, B3), F32),
            pltpu.VMEM((planes + 2, rows, B3), F32),
            pltpu.VMEM((planes, rows_prev, C5), BF16),
            pltpu.VMEM(second_prev.shape, F32),
            pltpu.VMEM(second_prev.shape, F32),
            pltpu.VMEM((2, 8, NB2), F32),
            DMA((above,)),
            DMA((planes,)),
            DMA((above,)),
        ],
        (
            totals,
            slope,
            first_out,
            keep,
            gain,
            bias,
            mom,
            inproj,
            second_prev,
            keep_prev,
            params_prev[3],
            params_prev[4],
            mom_prev,
        ),
        "vvvvvvvvavvvv",
        "back_between",
        flops=2 * planes * rows * C5 * NB1,
        mib=20,
    )


def inproj_rows(channels):
    first = -(-channels // 32) * 16
    return first, 4 * channels + first


def pack_inproj(ordered, packed):
    channels = ordered.shape[0]
    first, used = inproj_rows(channels)
    padded = packed.shape[0]
    for place in range(4):
        packed[place * channels : (place + 1) * channels, :] = ordered[
            :, place * 128 : (place + 1) * 128
        ]
    start = 4 * channels
    packed[start : start + first, 0:64] = ordered[0:first, 512:NB1]
    packed[start : start + channels - first, 64:128] = ordered[first:channels, 512:NB1]
    if 2 * first > channels:
        packed[start + channels - first : start + first, 64:128] = jnp.zeros(
            (2 * first - channels, 64), packed.dtype
        )
    if padded > used:
        packed[used:padded, :] = jnp.zeros((padded - used, 128), packed.dtype)


def inproj_grad_body(
    section_ref, x_ref, grad_ref, kept_hbm, sent_hbm, product, ordered, packed, half_sem
):
    planes, rows, channels = x_ref.shape
    product[...] = lax.dot_general(
        x_ref[...].reshape(planes * rows, channels),
        grad_ref[...].reshape(planes * rows, NB1),
        (((0,), (0,)), ((), ())),
        preferred_element_type=F32,
    ).astype(BF16)
    for row_to, row_from, height in RESULT_PIECES:
        for inner, outer, width in FIRST_PIECES:
            ordered[row_from : row_from + height, outer : outer + width] = product[
                row_to : row_to + height, inner : inner + width
            ]
    pack_inproj(ordered, packed)
    for copy in put_halves(section_ref[0], packed, kept_hbm, sent_hbm, half_sem):
        copy.wait()


def inproj_grad(x, grad, section, peers):
    planes, rows, channels = x.shape
    packed = padded_rows(inproj_rows(channels)[1], peers)
    return call(
        inproj_grad_body,
        [shape_of(packed // 2, 128, dtype=BF16)] * 2,
        "aa",
        [
            pltpu.VMEM((channels, NB1), BF16),
            pltpu.VMEM((channels, NB1), BF16),
            pltpu.VMEM((packed, 128), BF16),
            DMA((2,)),
        ],
        (x, grad),
        "vv",
        "inproj_grad",
        (section,),
        flops=2 * planes * rows * channels * NB1,
        mib=12,
    )


def unpack_conv(packed_ref, wide_ref, narrow_ref):
    step = 27 * B1A
    half = step // 2
    wide_ref[:, 0:128] = packed_ref[0:step, :].astype(F32)
    wide_ref[:, 128:256] = packed_ref[step : 2 * step, :].astype(F32)
    wide_ref[0:half, 256:B1] = packed_ref[2 * step : 2 * step + half, 0:64].astype(F32)
    wide_ref[half:step, 256:B1] = packed_ref[2 * step : 2 * step + half, 64:128].astype(F32)
    narrow_ref[...] = packed_ref[CONV_NARROW : CONV_NARROW + 27 * B2A, :].astype(F32)


def unpack_inproj(packed_ref, out_ref):
    channels = out_ref.shape[0]
    first = inproj_rows(channels)[0]
    for place in range(4):
        out_ref[:, place * 128 : (place + 1) * 128] = packed_ref[
            place * channels : (place + 1) * channels, :
        ].astype(F32)
    start = 4 * channels
    out_ref[0:first, 512:NB1] = packed_ref[start : start + first, 0:64].astype(F32)
    out_ref[first:channels, 512:NB1] = packed_ref[start : start + channels - first, 64:128].astype(
        F32
    )


def unpack_alone_body(section_ref, value_ref, got_ref, wide_ref, narrow_ref, packed_ref):
    half = value_ref.shape[0]
    section = section_ref[0]
    packed_ref[pl.ds(pl.multiple_of(section * half, 16), half), :] = value_ref[...]
    packed_ref[pl.ds(pl.multiple_of((1 - section) * half, 16), half), :] = got_ref[...]
    unpack_conv(packed_ref, wide_ref, narrow_ref)


def unpack_alone(value, got, section):
    return call(
        unpack_alone_body,
        [shape_of(27 * B1A, B1), shape_of(27 * B2A, B2)],
        "vv",
        [pltpu.VMEM((2 * value.shape[0], 128), BF16)],
        (value, got),
        "vv",
        "unpack_alone",
        (section,),
        mib=24,
    )


def halves_placed(section_ref, value_ref, got_ref, pieces):
    section = section_ref[0]
    for half_ref, half in ((value_ref, section), (got_ref, 1 - section)):
        for packed_ref, first, last in pieces:
            size = last - first
            packed_ref[pl.ds(pl.multiple_of(half * size, 16), size), :] = half_ref[first:last, :]


def unpack_joined_body(
    section_ref, value_ref, got_ref, wide_ref, narrow_ref, next_ref, conv_packed, next_packed, next_out
):
    half = conv_packed.shape[0] // 2
    halves_placed(
        section_ref,
        value_ref,
        got_ref,
        ((conv_packed, 0, half), (next_packed, half, value_ref.shape[0])),
    )
    unpack_conv(conv_packed, wide_ref, narrow_ref)
    unpack_inproj(next_packed, next_out)
    next_ref[...] = next_out[...].T


def unpack_joined(value, got, section, channels, peers):
    return call(
        unpack_joined_body,
        [shape_of(27 * B1A, B1), shape_of(27 * B2A, B2), shape_of(NB1, channels)],
        "vvv",
        [
            pltpu.VMEM((conv_rows(peers), 128), BF16),
            pltpu.VMEM((padded_rows(inproj_rows(channels)[1], peers), 128), BF16),
            pltpu.VMEM((channels, NB1), F32),
        ],
        (value, got),
        "vv",
        "unpack_joined",
        (section,),
        mib=32,
    )


def share_places(peers):
    pairs = distance_pairs(peers)
    places = []
    for section in range(2):
        order = [pair[section] for pair in pairs]
        places.append(
            [
                sum(
                    ((place // distance) % 2) << (len(order) - 1 - level)
                    for level, distance in enumerate(order)
                )
                for place in range(peers)
            ]
        )
    return places


def unpack_inproj_body(section_ref, value_ref, got_ref, out_ref, packed):
    section = section_ref[0]
    peers, share, unused = value_ref.shape
    places = share_places(peers)
    for half_ref, half in ((value_ref, section), (got_ref, 1 - section)):
        for place in range(peers):
            at = jnp.where(half == 0, places[0][place], places[1][place]) + half * peers
            packed[pl.ds(pl.multiple_of(at * share, 16), share), :] = half_ref[place]
    unpack_inproj(packed, out_ref)


def unpack_inproj_alone(value, got, section, channels):
    return call(
        unpack_inproj_body,
        [shape_of(channels, NB1)],
        "v",
        [pltpu.VMEM((2 * value.shape[0] * value.shape[1], 128), BF16)],
        (value, got),
        "vv",
        "unpack_inproj",
        (section,),
        mib=12,
    )[0]


def sent_to_all(spread):
    return lax.all_to_all(spread, "dp", 0, 0)


def swapped(value):
    return lax.ppermute(value, "section", [(0, 1), (1, 0)])


def distance_pairs(peers):
    distances = []
    while 2 ** len(distances) < peers:
        distances.append(2 ** len(distances))
    return list(zip(distances, [distances[1], distances[0]] + distances[2:]))


def distances_of():
    return distance_pairs(lax.axis_size("dp"))


def exchanged(value, pair):
    count = lax.axis_size("dp")
    links = [
        (section * count + place, section * count + (place ^ pair[section]))
        for section in range(2)
        for place in range(count)
    ]
    return lax.ppermute(value, ("section", "dp"), links)


def upper_half(pair):
    place = lax.axis_index("dp")
    distance = jnp.where(lax.axis_index("section") == 0, pair[0], pair[1])
    return ((place // distance) % 2).astype(jnp.int32).reshape(1)


def added(kept, got):
    return (kept.astype(F32) + got.astype(F32)).astype(kept.dtype)


def split_sum_body(upper_ref, kept_ref, got_ref, left_ref, sent_ref):
    half = left_ref.shape[0]
    upper = upper_ref[0]
    for target, which in ((left_ref, upper), (sent_ref, 1 - upper)):
        at = pl.ds(pl.multiple_of(which * half, 16), half)
        target[...] = added(kept_ref[at, :], got_ref[at, :])


def split_sum(kept, got, pair):
    half = shape_of(kept.shape[0] // 2, 128, dtype=kept.dtype)
    return call(
        split_sum_body, [half, half], "vv", [], (kept, got), "vv", "split_sum", (upper_half(pair),)
    )


def placed_body(upper_ref, value_ref, got_ref, out_ref):
    half = value_ref.shape[0]
    upper = upper_ref[0]
    out_ref[pl.ds(pl.multiple_of(upper * half, 16), half), :] = value_ref[...]
    out_ref[pl.ds(pl.multiple_of((1 - upper) * half, 16), half), :] = got_ref[...]


def placed(value, got, pair):
    whole = shape_of(value.shape[0] * 2, 128, dtype=value.dtype)
    return call(
        placed_body, [whole], "v", [], (value, got), "vv", "placed", (upper_half(pair),)
    )[0]


class Scatter:
    def __init__(self, kept, sent):
        self.kept = kept
        self.pairs = distances_of()
        self.place = 0
        self.got = swapped(sent)

    def step(self):
        pair = self.pairs[self.place]
        self.kept, sent = split_sum(self.kept, self.got, pair)
        self.got = exchanged(sent, pair)
        self.place += 1

    def result(self):
        while self.place < len(self.pairs):
            self.step()
        return added(self.kept, self.got)


class Gather:
    def __init__(self, value):
        self.value = value
        self.pairs = distances_of()[::-1]
        self.place = 0
        self.got = exchanged(value, self.pairs[0])

    def step(self):
        self.value = placed(self.value, self.got, self.pairs[self.place])
        self.place += 1
        if self.place < len(self.pairs):
            self.got = exchanged(self.value, self.pairs[self.place])
        else:
            self.got = swapped(self.value)

    def result(self):
        while self.place < len(self.pairs):
            self.step()
        return self.value, self.got


def lockstep(one, other):
    one.got, other.got = lax.optimization_barrier((one.got, other.got))


def tied(value, *exchanges):
    both = lax.optimization_barrier((value,) + tuple(e.got for e in exchanges))
    for exchange, got in zip(exchanges, both[1:]):
        exchange.got = got
    return both[0]


def small_body(first_a, second_a, first_b, second_b, norm1_a, norm2_a, norm1_b, norm2_b, out_ref):
    for row, first, second in ((0, first_a, second_a), (2, first_b, second_b)):
        for line in range(2):
            for pieces, source, offset in ((FIRST_PIECES, first, 0), (SECOND_PIECES, second, NB1)):
                for inner, outer, width in pieces:
                    start = offset + outer
                    out_ref[row + line : row + line + 1, start : start + width] = source[
                        line : line + 1, inner : inner + width
                    ]
    for row, first, second in ((4, norm1_a, norm2_a), (6, norm1_b, norm2_b)):
        out_ref[row : row + 2, 0:NB1] = first[...]
        out_ref[row : row + 2, NB1:NB] = second[...]


def small_out_body(section_ref, own_ref, other_ref, norm_a, mom_a, norm_b, mom_b):
    section = section_ref[0]
    own, other = own_ref[...], other_ref[...]
    norms = own[4:8] + other[4:8]
    norm_a[...] = norms[0:2]
    norm_b[...] = norms[2:4]
    low = jnp.where(section == 0, own, other)
    high = jnp.where(section == 0, other, own)
    mom_a[0] = low[0:2]
    mom_a[1] = high[0:2]
    mom_b[0] = low[2:4]
    mom_b[1] = high[2:4]


def small_outputs(rows, section):
    own = call(small_body, [shape_of(8, NB)], "v", [], rows, "vvvvvvvv", "small")[0]
    return call(
        small_out_body,
        [shape_of(2, NB), shape_of(2, 2, NB), shape_of(2, NB), shape_of(2, 2, NB)],
        "vvvv",
        [],
        (own, swapped(own)),
        "vv",
        "small_out",
        (section,),
    )


def local(
    clips_in,
    frames,
    voxel_mask,
    micro_order,
    inproj_4f,
    conv_mid_4f,
    conv_small_4f,
    gain_4f,
    bias_4f,
    inproj_5b,
    conv_mid_5b,
    conv_small_5b,
    gain_5b,
    bias_5b,
    cotangent,
):
    section = lax.axis_index("section")
    peers = lax.axis_size("dp")
    own = micro_order[0, section]
    own_clip = own.reshape(1)
    which = section.astype(jnp.int32).reshape(1)
    count, depth, height, width, channels = clips_in.shape
    clips = jnp.transpose(clips_in, (0, 2, 3, 1, 4)).reshape(count, height, width * depth, channels)
    upstream = jnp.transpose(cotangent, (0, 2, 3, 1, 4))

    first = (inproj_4f, conv_mid_4f, conv_small_4f, gain_4f.reshape(1, NB), bias_4f.reshape(1, NB))
    second = (inproj_5b.T, conv_mid_5b, conv_small_5b, gain_5b.reshape(1, NB), bias_5b.reshape(1, NB))
    long, short = depth, depth // 2

    z1_a, stat, keep, keep_next = project_first(
        clips,
        micro_order.reshape(-1),
        which,
        frames,
        jnp.transpose(voxel_mask, (0, 2, 1, 3)),
        inproj_4f,
        peers,
    )
    act_a, mid_a, z2_a, stat, mom1_a = second_level(
        sent_to_all(stat), z1_a, keep, first, long, peers
    )
    totals = sent_to_all(stat)
    x_b, z1_b, stat, mom2_a = between_blocks(
        totals, z2_a, keep, first, act_a, mom1_a, keep_next, second[0], peers
    )
    act_b, mid_b, z2_b, stat, mom1_b = second_level(
        sent_to_all(stat), z1_b, keep_next, second, short, peers
    )
    totals = sent_to_all(stat)
    turned_b = prepare(conv_mid_5b, conv_small_5b)
    totals, turned_b = lax.optimization_barrier((totals, turned_b))
    kept, sent, slope, direct, stat, mom2_b = turn(
        totals, z2_b, keep_next, second, act_b, mom1_b, upstream, own_clip, which, peers
    )
    totals = sent_to_all(stat)
    result = (kept, swapped(sent))
    turned_a = prepare(conv_mid_4f, conv_small_4f)
    totals, turned_a = lax.optimization_barrier((totals, turned_a))
    dz2_b, kept, sent, norm2_b = conv_grad(
        totals, slope, z2_b, mid_b, keep_next, second, mom1_b, mom2_b, short, which, peers
    )
    sum_b = Scatter(kept, sent)
    nothing = jnp.zeros((2, 8, NB1), F32)
    slope, stat, unused = back_conv(
        dz2_b,
        z1_b,
        keep_next,
        second,
        turned_b,
        mom1_b,
        direct,
        False,
        short,
        peers,
        (0, height // 2),
        nothing,
    )
    stat = tied(stat, sum_b)
    sum_b.step()
    totals = sent_to_all(stat)
    block_out = both_clips(*result, own_clip)
    totals, block_out = lax.optimization_barrier((totals, block_out))
    totals = tied(totals, sum_b)
    sum_b.step()
    up, dz1_b, slope, stat, norm1_b = back_between(
        totals, slope, z1_b, keep_next, second, mom1_b, z2_a, keep, first, mom2_a, peers
    )
    stat = tied(stat, sum_b)
    sum_b.step()
    totals = sent_to_all(stat)
    inproj_halves = inproj_grad(x_b, dz1_b, which, peers)
    totals = tied(totals, sum_b)
    sum_b.step()
    dz2_a, kept, sent, norm2_a = conv_grad(
        totals,
        slope,
        z2_a,
        mid_a,
        keep,
        first,
        mom1_a,
        mom2_a,
        long,
        which,
        peers,
        inproj_halves,
    )
    sent = tied(sent, sum_b)
    sum_a = Scatter(kept, sent)
    gather_b = Gather(sum_b.result())
    dz2_a = tied(dz2_a, sum_a)
    sum_a.step()
    half = height // 2
    back = (z1_a, keep, first, turned_a, mom1_a, up, True, long, peers)
    slope_low, unused, part = back_conv(dz2_a, *back, (0, half), nothing)
    part = tied(part, sum_a, gather_b)
    sum_a.step()
    gather_b.step()
    slope_high, stat, unused = back_conv(dz2_a, *back, (half, height - half), part)
    stat = tied(stat, sum_a, gather_b)
    sum_a.step()
    gather_b.step()
    totals = sent_to_all(stat)
    totals = tied(totals, sum_a, gather_b)
    sum_a.step()
    gather_b.step()
    dz1_a, norm1_a = last_gradient(totals, (slope_low, slope_high), z1_a, keep, first, mom1_a)
    dz1_a = tied(dz1_a, sum_a)
    gather_a = Gather(sum_a.result())
    kept, sent = clip_inproj(clips, dz1_a, keep, own_clip, which, peers)
    sent = tied(sent, gather_a, gather_b)
    sum_i = Scatter(kept, sent)
    gather_a.step()
    gather_b.step()
    dz1_a, sum_i.got, gather_b.got = lax.optimization_barrier((dz1_a, sum_i.got, gather_b.got))
    sum_i.step()
    kept, sent = clip_gradient(dz1_a, keep, inproj_4f, width, which)
    sent = tied(sent, sum_i)
    sum_i.step()
    lockstep(gather_a, sum_i)
    gather_a.step()
    sum_i.step()
    conv_b = unpack_alone(*gather_b.result(), which)
    sum_i.got, conv_b = lax.optimization_barrier((sum_i.got, conv_b))
    sum_i.step()
    lockstep(gather_a, sum_i)
    gather_a.step()
    shares = jnp.broadcast_to(sum_i.result().astype(BF16)[None], (peers, *sum_i.kept.shape))
    shares, sent = lax.optimization_barrier((shares, sent))
    whole = sent_to_all(shares)
    clips_grad = both_clips(kept, swapped(sent), own_clip)
    small = small_outputs(
        (mom1_a, mom2_a, mom1_b, mom2_b, norm1_a, norm2_a, norm1_b, norm2_b), which
    )
    whole, gather_a.got, clips_grad, small = lax.optimization_barrier(
        (whole, gather_a.got, clips_grad, small)
    )
    gather_a.step()
    inproj_a = unpack_inproj_alone(whole, swapped(whole), which, inproj_4f.shape[0])
    gather_a.got, inproj_a = lax.optimization_barrier((gather_a.got, inproj_a))
    wide_a, narrow_a, inproj_b = unpack_joined(
        *gather_a.result(), which, inproj_5b.shape[0], peers
    )
    return (
        jnp.transpose(block_out, (0, 3, 1, 2, 4)),
        jnp.transpose(clips_grad, (0, 3, 1, 2, 4)),
        inproj_a,
        wide_a.reshape(conv_mid_4f.shape),
        narrow_a.reshape(conv_small_4f.shape),
        small[0],
        small[1],
        inproj_b.T,
        conv_b[0].reshape(conv_mid_5b.shape),
        conv_b[1].reshape(conv_small_5b.shape),
        small[2],
        small[3],
    )


def solution(mesh):
    placed = (
        P("dp", None, None, None, None),
        P("dp"),
        P("dp", None, None, None),
        P("dp", None),
        P(),
        P(),
        P(),
        P(),
        P(),
        P(),
        P(),
        P(),
        P(),
        P(),
        P("dp", None, None, None, None),
    )
    return jax.shard_map(
        local,
        mesh=mesh,
        in_specs=placed,
        out_specs=(
            P("dp", "section", None, None, None),
            P("dp", "section", None, None, None),
            P(),
            P(),
            P(),
            P(),
            P(),
            P(),
            P(),
            P(),
            P(),
            P(),
        ),
        check_vma=False,
    )
```

```python
import functools

import jax
import jax.numpy as jnp
from jax import lax
from jax.experimental import pallas as pl
from jax.experimental.pallas import tpu as pltpu
from jax.sharding import PartitionSpec as P

B0 = 256
B1A = 160
B1 = 320
B2A = 32
B2 = 128
B3 = 128
C5 = 832
NX = 448
NB1 = 576
NB = 1024
NB2 = NB - NB1
NM = B1A + B2A
ND = B0 + B3

EPSILON = 0.001
F32 = jnp.float32
BF16 = jnp.bfloat16

FIRST_PIECES = ((0, 0, B0), (B0, NX, B3), (ND, B0, NM))
SECOND_PIECES = ((0, B1, B2), (B2, 0, B1))
RESULT_PIECES = ((0, 0, B0), (B0, C5 - B3, B3), (ND, B0 + B1, B2), (ND + B2, B0, B1))

CONV_NARROW = 10800
TURNED = 4096
DMA = pltpu.SemaphoreType.DMA


def padded_rows(rows, peers):
    whole = 32 * peers
    return -(-rows // whole) * whole


def conv_rows(peers):
    return padded_rows(CONV_NARROW + 27 * B2A, peers)


def shape_of(*dims, dtype=F32):
    return jax.ShapeDtypeStruct(dims, dtype)


def tiles_of(start, stop):
    return [(first, min(first + 128, stop)) for first in range(start, stop, 128)]


PINNED = {"a": pltpu.HBM, "p": pltpu.VMEM}


def call(body, outs, out_spaces, scratch, args, spaces, name, scalars=(), flops=0, mib=12):
    def spec(array, space):
        return pl.BlockSpec(memory_space=pltpu.HBM if space == "a" else pltpu.VMEM)

    assert len(args) == len(spaces) and len(outs) == len(out_spaces)
    return pl.pallas_call(
        body,
        out_shape=[
            PINNED[s](o.shape, o.dtype) if s in PINNED else o for o, s in zip(outs, out_spaces)
        ],
        grid_spec=pltpu.PrefetchScalarGridSpec(
            num_scalar_prefetch=len(scalars),
            grid=(1,),
            in_specs=[spec(a, s) for a, s in zip(args, spaces)],
            out_specs=[spec(o, s) for o, s in zip(outs, out_spaces)],
            scratch_shapes=scratch,
        ),
        compiler_params=pltpu.CompilerParams(vmem_limit_bytes=mib * 2**20),
        cost_estimate=pl.CostEstimate(
            flops=flops,
            transcendentals=0,
            bytes_accessed=sum(a.size * a.dtype.itemsize for a in list(args) + list(outs)),
        ),
        name=name,
    )(
        *scalars,
        *[
            pltpu.with_memory_space_constraint(a, pltpu.HBM) if s == "a" else a
            for a, s in zip(args, spaces)
        ],
    )


class Planes:
    def __init__(self, source, target, sem, start=0):
        self.source, self.target, self.sem, self.start_at = source, target, sem, start

    def copy(self, h):
        return pltpu.make_async_copy(
            self.source.at[h + self.start_at], self.target.at[h], self.sem.at[h]
        )

    def start(self, h):
        self.copy(h).start()

    def wait(self, h):
        self.copy(h).wait()

    def start_all(self):
        for h in range(self.sem.shape[0]):
            self.start(h)

    def wait_all(self):
        for h in range(self.sem.shape[0]):
            self.wait(h)


class Parts:
    def __init__(self, sources, target, sem):
        self.target, self.sem = target, sem
        self.places = [source.at[h] for source in sources for h in range(source.shape[0])]

    def start_all(self):
        for h, source in enumerate(self.places):
            pltpu.make_async_copy(source, self.target.at[h], self.sem.at[h]).start()

    def wait(self, h):
        pltpu.make_async_copy(self.places[0], self.target.at[h], self.sem.at[h]).wait()


class Outwards(Planes):
    def copy(self, h):
        return pltpu.make_async_copy(
            self.source.at[h], self.target.at[h + self.start_at], self.sem.at[h]
        )


def sigmoid(value):
    return 0.5 * jnp.tanh(0.5 * value) + 0.5


def rows_summed(value):
    return value.reshape(value.shape[0] // 8, 8, value.shape[1]).sum(0)


def put_permuted(target, row, source, pieces, offset=0):
    for inner, outer, width in pieces:
        target[row : row + 1, inner : inner + width] = source[
            :, offset + outer : offset + outer + width
        ]


def put_original(target, row, value, pieces):
    for inner, outer, width in pieces:
        target[row : row + 1, outer : outer + width] = value[:, inner : inner + width]


def put_stats(stat_ref, acc_ref, count=None):
    peers, rows, width = stat_ref.shape
    for row in range(2):
        line = jnp.sum(acc_ref[row], axis=0, keepdims=True)
        stat_ref[:, row : row + 1, :] = jnp.broadcast_to(line[None], (peers, 1, width))
    if count is not None:
        stat_ref[:, 2:3, :] = jnp.broadcast_to(count.reshape(1, 1, 1), (peers, 1, width))


def plane_stats(value_ref, h, keep, acc_ref):
    for first, last in tiles_of(0, value_ref.shape[2]):
        value = value_ref[h, :, first:last]
        masked = value * keep
        acc_ref[0, :, first:last] += rows_summed(masked)
        acc_ref[1, :, first:last] += rows_summed(masked * value)


def times_of(rows, width, extent):
    return lax.broadcasted_iota(jnp.int32, (rows, width), 0) & (extent - 1)


def time_shifted(value, times, extent):
    rows = value.shape[0]
    earlier = jnp.where(times != 0, pltpu.roll(value, 1, 0), 0.0)
    later = jnp.where(times != extent - 1, pltpu.roll(value, rows - 1, 0), 0.0)
    return earlier, value, later


def width_shifted(value, extent):
    rows = value.shape[0]
    if extent % 8 == 0:
        edge = jnp.zeros((extent, value.shape[1]), value.dtype)
        left = jnp.concatenate([edge, value[:-extent]], 0)
        right = jnp.concatenate([value[extent:], edge], 0)
    else:
        left = pltpu.roll(value, extent, 0)
        right = pltpu.roll(value, rows - extent, 0)
    return left, value, right


def window_sums(source_ref, between_ref, extent, put):
    planes, rows, width = source_ref.shape
    between_ref[0] = jnp.zeros((rows, width), F32)
    between_ref[planes + 1] = jnp.zeros((rows, width), F32)
    times = times_of(rows, width, extent)

    def plane(h, carry):
        before, here, after = time_shifted(source_ref[h], times, extent)
        left, here, right = width_shifted(before + here + after, extent)
        between_ref[h + 1] = left + here + right
        return carry

    lax.fori_loop(0, planes, plane, 0)

    def through(h, carry):
        put(h, (between_ref[h] + between_ref[h + 1] + between_ref[h + 2]) * (1.0 / 27.0))
        return carry

    lax.fori_loop(0, planes, through, 0)


def turned_ordered(turned_ref, ordered_ref):
    for row_to, row_from, height in FIRST_PIECES:
        for inner, outer, width in RESULT_PIECES:
            ordered_ref[row_to : row_to + height, inner : inner + width] = turned_ref[
                row_from : row_from + height, outer : outer + width
            ]


def weight_ordered(weight_ref, ordered_ref):
    for inner, outer, width in FIRST_PIECES:
        ordered_ref[:, inner : inner + width] = weight_ref[:, outer : outer + width]


def step_planes(planes):
    return (planes // 2, 2) if planes % 2 == 0 else (planes, 1)


def put_masks(valid, mask_ref, keep_ref, next_ref):
    planes, rows, unused = keep_ref.shape
    unused, extent, width = mask_ref.shape

    def one_hot(shape, picked):
        places = lax.broadcasted_iota(jnp.int32, shape, 1)
        index = lax.broadcasted_iota(jnp.int32, shape, 0)
        return jnp.where(places == picked(index), 1.0, 0.0)

    times = one_hot((rows, extent), lambda r: r & (extent - 1))
    columns = one_hot((rows, width), lambda r: r // extent)
    frame = lax.broadcasted_iota(jnp.int32, (extent, width), 0)
    for h in range(planes):
        plane = jnp.where(frame < valid, mask_ref[h], 0).astype(F32)
        picked = jnp.dot(times.astype(BF16), plane.astype(BF16), preferred_element_type=F32)
        picked = picked * columns
        keep_ref[h] = jnp.sum(picked, axis=1, keepdims=True)
    rows_next = next_ref.shape[1]
    half = extent // 2
    index = lax.broadcasted_iota(jnp.int32, (rows_next, rows), 0)
    places = lax.broadcasted_iota(jnp.int32, (rows_next, rows), 1)
    same_time = (places & (extent - 1)) // 2 == (index & (half - 1))
    same_column = places // (2 * extent) == index // half
    pooled = jnp.where(same_time & same_column, 1.0, 0.0).astype(BF16)
    for h in range(next_ref.shape[0]):
        both = jnp.broadcast_to(keep_ref[2 * h] + keep_ref[2 * h + 1], (rows, 128))
        held = jnp.dot(pooled, both.astype(BF16), preferred_element_type=F32)
        next_ref[h] = jnp.where(held[:, 0:1] > 0.5, 1.0, 0.0)


def project_body(
    order_ref,
    section_ref,
    frames_ref,
    x_hbm,
    mask_hbm,
    weight_hbm,
    z_hbm,
    z_v,
    stat_ref,
    keep_ref,
    next_ref,
    x_v,
    mask_v,
    weight_v,
    ordered,
    pool,
    between,
    acc,
    x_sem,
    z_sem,
    weight_sem,
):
    planes, rows, channels = x_v.shape
    extent = 8
    clip = order_ref[section_ref[0]]
    arriving = Planes(x_hbm.at[clip], x_v, x_sem)
    leaving = Outwards(z_v, z_hbm, z_sem)
    weight_in = pltpu.make_async_copy(weight_hbm, weight_v, weight_sem.at[0])
    mask_in = pltpu.make_async_copy(mask_hbm.at[clip], mask_v, weight_sem.at[1])
    mask_in.start()
    weight_in.start()
    arriving.start_all()
    mask_in.wait()
    put_masks(frames_ref[clip], mask_v, keep_ref, next_ref)
    weight_in.wait()
    weight_ordered(weight_v, ordered)
    together, steps = step_planes(planes)

    def product(i, carry):
        def masked(k, carry):
            h = i * together + k
            arriving.wait(h)
            x_v[h] = x_v[h] * keep_ref[h].astype(BF16)
            return carry

        lax.fori_loop(0, together, masked, 0)
        at = pl.ds(i * together, together)
        value = x_v[at].reshape(together * rows, channels)
        out = jnp.dot(value, ordered[...], preferred_element_type=F32)
        z_v[at] = out.reshape(together, rows, NB1)
        pool[at] = out[:, B0:ND].reshape(together, rows, B3)
        return carry

    lax.fori_loop(0, steps, product, 0)
    acc[...] = jnp.zeros_like(acc)

    def put(h, value):
        z_v[h, :, B0:ND] = value
        leaving.start(h)
        plane_stats(z_v, h, keep_ref[h], acc)

    window_sums(pool, between, extent, put)
    put_stats(stat_ref, acc, jnp.sum(keep_ref[...]))
    leaving.wait_all()


def project_first(clips, order, section, frames, voxel_mask, weight, peers):
    unused, planes, rows, channels = clips.shape
    unused, unused, extent, width = voxel_mask.shape
    return call(
        project_body,
        [
            shape_of(planes, rows, NB1),
            shape_of(planes, rows, NB1),
            shape_of(peers, 3, NB1),
            shape_of(planes, rows, 1),
            shape_of(planes // 2, (width // 2 + 1) * extent // 2, 1),
        ],
        "apvvv",
        [
            pltpu.VMEM((planes, rows, channels), BF16),
            pltpu.VMEM(voxel_mask.shape[1:], jnp.int32),
            pltpu.VMEM((channels, NB1), BF16),
            pltpu.VMEM((channels, NB1), BF16),
            pltpu.VMEM((planes, rows, B3), F32),
            pltpu.VMEM((planes + 2, rows, B3), F32),
            pltpu.VMEM((2, 8, NB1), F32),
            DMA((planes,)),
            DMA((planes,)),
            DMA((2,)),
        ],
        (clips, voxel_mask, weight),
        "aaa",
        "project_first",
        (order, section, frames),
        flops=2 * planes * rows * channels * NB1,
        mib=16,
    )


def level_rows(vec, gain_ref, bias_ref, mom_ref, pieces, offset):
    put_permuted(vec, 4, gain_ref, pieces, offset)
    put_permuted(vec, 5, bias_ref, pieces, offset)
    mean, var = mom_ref[0:1, :], mom_ref[1:2, :]
    inverse = lax.rsqrt(var + EPSILON)
    scale = vec[4:5, :] * inverse
    vec[0:1, :] = scale
    vec[1:2, :] = vec[5:6, :] - mean * scale
    vec[2:3, :] = inverse
    vec[3:4, :] = -mean * inverse


def first_rows(vec, gain_ref, bias_ref, mom_ref):
    level_rows(vec, gain_ref, bias_ref, mom_ref, FIRST_PIECES, 0)


def second_rows(vec, gain_ref, bias_ref, mom_ref):
    level_rows(vec, gain_ref, bias_ref, mom_ref, SECOND_PIECES, NB1)


def back_rows(vec, total, count):
    cross = vec[0:1, :] * total[1:2] / count
    vec[6:7, :] = -(vec[0:1, :] * total[0:1] / count) - cross * vec[3:4, :]
    vec[7:8, :] = -cross * vec[2:3, :]


def put_moments(tot_ref, mom_ref, count):
    total = jnp.sum(tot_ref[...], axis=0)
    if count is None:
        count = total[2:3, :]
        mom_ref[2:3, :] = count
    mean = total[0:1, :] / count
    mom_ref[0:1, :] = mean
    mom_ref[1:2, :] = total[1:2, :] / count - mean * mean


def spread_plane(value, first, times, extent, targets, index):
    width = value.shape[1]
    for early, shifted in enumerate(time_shifted(value, times[:, 0:width], extent)):
        for side, moved in enumerate(width_shifted(shifted, extent)):
            place = early * 3 + side
            moved = moved.astype(BF16)
            for target, low, high in targets:
                begin, end = max(low, first), min(high, first + width)
                if begin < end:
                    start = place * (high - low) + begin - low
                    target[index, :, start : start + end - begin] = moved[
                        :, begin - first : end - first
                    ]


def clear_ends(targets, ends):
    for target, unused, unused in targets:
        for end in ends:
            target[end] = jnp.zeros(target.shape[1:], BF16)


def weight_copies(source, target, sems):
    return [
        pltpu.make_async_copy(
            source.at[pl.ds(time * 9 + height * 3, 3)],
            target.at[height, pl.ds(time * 3, 3)],
            sems.at[height * 3 + time],
        )
        for height in range(3)
        for time in range(3)
    ]


def second_body(
    extent,
    tot_ref,
    z_v,
    keep_ref,
    gain_ref,
    bias_ref,
    wide_hbm,
    narrow_hbm,
    act_v,
    mid_hbm,
    out_hbm,
    out_v,
    stat_ref,
    mom_ref,
    vec,
    mid_v,
    wide_v,
    narrow_v,
    im_wide,
    im_narrow,
    acc,
    wide_sem,
    narrow_sem,
    mid_sem,
    out_sem,
):
    planes, rows, unused = z_v.shape
    weights = weight_copies(wide_hbm, wide_v, wide_sem) + weight_copies(
        narrow_hbm, narrow_v, narrow_sem
    )
    for copy in weights:
        copy.start()
    mid_out = Outwards(mid_v, mid_hbm, mid_sem)
    out_out = Outwards(out_v, out_hbm, out_sem)
    put_moments(tot_ref, mom_ref, None)
    first_rows(vec, gain_ref, bias_ref, mom_ref)
    targets = ((im_wide, 0, B1A), (im_narrow, B1A, NM))
    clear_ends(targets, (0, planes + 1))
    times = times_of(rows, 128, extent)

    def activate(h, carry):
        keep = keep_ref[h]
        for first, last in tiles_of(0, NB1):
            shifted = z_v[h, :, first:last] * vec[0:1, first:last] + vec[1:2, first:last]
            value = shifted * sigmoid(shifted) * keep
            if first < ND:
                act_v[h, :, first:last] = value.astype(BF16)
            else:
                mid_v[h, :, first - ND : last - ND] = value.astype(BF16)
                spread_plane(value, first - ND, times, extent, targets, h + 1)
        mid_out.start(h)
        return carry

    lax.fori_loop(0, planes, activate, 0)
    for copy in weights:
        copy.wait()
    acc[...] = jnp.zeros_like(acc)
    together, steps = step_planes(planes)

    def convolve(i, carry):
        at = pl.ds(i * together, together)
        for im_ref, weight_ref, first, last in (
            (im_narrow, narrow_v, 0, B2),
            (im_wide, wide_v, B2, NB2),
        ):
            total = None
            for high in range(3):
                value = im_ref[pl.ds(i * together + high, together)]
                value = value.reshape(together * rows, value.shape[2])
                weight = weight_ref[high].reshape(value.shape[1], last - first)
                part = jnp.dot(value, weight, preferred_element_type=F32)
                total = part if total is None else total + part
            out_v[at, :, first:last] = total.reshape(together, rows, last - first)

        def finish(k, carry):
            h = i * together + k
            out_out.start(h)
            plane_stats(out_v, h, keep_ref[h], acc)
            return carry

        lax.fori_loop(0, together, finish, 0)
        return carry

    lax.fori_loop(0, steps, convolve, 0)
    put_stats(stat_ref, acc)
    mid_out.wait_all()
    out_out.wait_all()


def second_level(totals, first_out, keep, params, extent, peers):
    unused, conv_mid, conv_small, gain, bias = params
    planes, rows, unused = first_out.shape
    return call(
        functools.partial(second_body, extent),
        [
            shape_of(planes, rows, ND, dtype=BF16),
            shape_of(planes, rows, NM, dtype=BF16),
            shape_of(planes, rows, NB2),
            shape_of(planes, rows, NB2),
            shape_of(peers, 2, NB2),
            shape_of(3, NB1),
        ],
        "paapvv",
        [
            pltpu.VMEM((8, NB1), F32),
            pltpu.VMEM((planes, rows, NM), BF16),
            pltpu.VMEM((3, 9, B1A, B1), BF16),
            pltpu.VMEM((3, 9, B2A, B2), BF16),
            pltpu.VMEM((planes + 2, rows, 9 * B1A), BF16),
            pltpu.VMEM((planes + 2, rows, 9 * B2A), BF16),
            pltpu.VMEM((2, 8, NB2), F32),
            DMA((9,)),
            DMA((9,)),
            DMA((planes,)),
            DMA((planes,)),
        ],
        (totals, first_out, keep, gain, bias, conv_mid, conv_small),
        "vpvvvaa",
        "second_level",
        flops=2 * planes * rows * 27 * (B1A * B1 + B2A * B2),
        mib=30,
    )


def cell_of(shape, axis, rows):
    row = lax.broadcasted_iota(jnp.int32, shape, axis)
    row = jnp.where(row >= rows, row - rows, row)
    return (row // 16) * 4 + (row % 8) // 2


def between_body(
    tot_ref,
    z_v,
    keep_ref,
    gain_ref,
    bias_ref,
    act_v,
    first_mom_ref,
    keep_next_ref,
    weight_ref,
    x_hbm,
    z_next_hbm,
    z_next_ref,
    stat_ref,
    mom_ref,
    vec,
    x_ref,
    both,
    ordered,
    pool,
    between,
    acc,
    x_sem,
    z_next_sem,
):
    planes, rows, channels = x_ref.shape
    x_out = Outwards(x_ref, x_hbm, x_sem)
    z_next_out = Outwards(z_next_ref, z_next_hbm, z_next_sem)
    put_moments(tot_ref, mom_ref, first_mom_ref[2:3, 0:NB2])
    second_rows(vec, gain_ref, bias_ref, mom_ref)
    turned_ordered(weight_ref, ordered)
    extent = 4
    source_rows = z_v.shape[1]
    shape = (rows, 2 * source_rows)
    cells = cell_of(shape, 1, source_rows) == lax.broadcasted_iota(jnp.int32, shape, 0)
    pooled = jnp.where(cells, 1.0, 0.0).astype(BF16)

    def pooling(h, carry):
        keeps = [keep_ref[2 * h], keep_ref[2 * h + 1]]
        keep_next = keep_next_ref[h]
        for first, last in tiles_of(0, C5):
            for step in range(2):
                if first < ND:
                    part = act_v[2 * h + step, :, first:last]
                else:
                    at = slice(first - ND, last - ND)
                    shifted = z_v[2 * h + step, :, at] * vec[0:1, at] + vec[1:2, at]
                    part = (shifted * sigmoid(shifted) * keeps[step]).astype(BF16)
                both[step * source_rows : (step + 1) * source_rows, first:last] = part
        mean = jnp.dot(pooled, both[...], preferred_element_type=F32) * 0.125
        x_ref[h] = (mean.astype(BF16).astype(F32) * keep_next).astype(BF16)
        x_out.start(h)
        return carry

    lax.fori_loop(0, planes, pooling, 0)
    value = x_ref[...].reshape(planes * rows, channels)
    out = lax.dot_general(
        value, ordered[...], (((1,), (1,)), ((), ())), preferred_element_type=F32
    )
    z_next_ref[...] = out.reshape(planes, rows, NB1)
    pool[...] = out[:, B0:ND].reshape(planes, rows, B3)
    acc[...] = jnp.zeros_like(acc)

    def put(h, value):
        z_next_ref[h, :, B0:ND] = value
        z_next_out.start(h)
        plane_stats(z_next_ref, h, keep_next_ref[h], acc)

    window_sums(pool, between, extent, put)
    put_stats(stat_ref, acc, jnp.sum(keep_next_ref[...]))
    x_out.wait_all()
    z_next_out.wait_all()


def between_blocks(totals, second_out, keep, params, act, first_mom, keep_next, weight, peers):
    planes, rows = keep_next.shape[:2]
    above, source_rows = second_out.shape[:2]
    return call(
        between_body,
        [
            shape_of(planes, rows, C5, dtype=BF16),
            shape_of(planes, rows, NB1),
            shape_of(planes, rows, NB1),
            shape_of(peers, 3, NB1),
            shape_of(2, NB2),
        ],
        "aapvv",
        [
            pltpu.VMEM((8, NB2), F32),
            pltpu.VMEM((planes, rows, C5), BF16),
            pltpu.VMEM((2 * source_rows, C5), BF16),
            pltpu.VMEM((NB1, C5), BF16),
            pltpu.VMEM((planes, rows, B3), F32),
            pltpu.VMEM((planes + 2, rows, B3), F32),
            pltpu.VMEM((2, 8, NB1), F32),
            DMA((planes,)),
            DMA((planes,)),
        ],
        (totals, second_out, keep, params[3], params[4], act, first_mom, keep_next, weight),
        "vpvvvpvvv",
        "between_blocks",
        flops=2 * planes * rows * C5 * NB1,
        mib=16,
    )


def turn_body(
    clip_ref,
    section_ref,
    tot_ref,
    z_v,
    keep_ref,
    gain_ref,
    bias_ref,
    act_v,
    first_mom_ref,
    grad_hbm,
    kept_ref,
    sent_ref,
    slope_hbm,
    direct_v,
    stat_ref,
    mom_ref,
    vec,
    slope_v,
    grad_v,
    grad,
    result,
    acc,
    grad_sem,
    slope_sem,
):
    planes, rows, unused = z_v.shape
    unused, width, extent, unused = grad_v.shape
    half = extent // 2
    later = section_ref[0] == 1
    grad_in = Planes(grad_hbm.at[clip_ref[0]], grad_v, grad_sem)
    for h in range(planes):
        grad_in.start(h)
    slope_out = Outwards(slope_v, slope_hbm, slope_sem)
    put_moments(tot_ref, mom_ref, first_mom_ref[2:3, 0:NB2])
    second_rows(vec, gain_ref, bias_ref, mom_ref)
    acc[...] = jnp.zeros_like(acc)
    grad[...] = jnp.zeros_like(grad)

    def plane(h, carry):
        keep = keep_ref[h]
        grad_in.wait(h)
        for column in range(width):
            at = slice(column * extent, (column + 1) * extent)
            grad[at, :] = grad_v[h, column].astype(F32)
        direct_v[h, :, 0:B0] = grad[:, 0:B0].astype(BF16)
        direct_v[h, :, B0:ND] = grad[:, C5 - B3 :].astype(BF16)
        result[:, 0:B0] = act_v[h, :, 0:B0].astype(F32)
        result[:, C5 - B3 :] = act_v[h, :, B0:ND].astype(F32)
        for inner, outer, size in SECOND_PIECES:
            at = slice(inner, inner + size)
            place = slice(B0 + outer, B0 + outer + size)
            value = z_v[h, :, at]
            shifted = value * vec[0:1, at] + vec[1:2, at]
            gate = sigmoid(shifted)
            result[:, place] = shifted * gate * keep
            slope = grad[:, place] * keep * gate * (1.0 + shifted * (1.0 - gate))
            slope_v[h, :, at] = slope
            acc[0, :, at] += rows_summed(slope)
            acc[1, :, at] += rows_summed(slope * (value * vec[2:3, at] + vec[3:4, at]))
        slope_out.start(h)
        for column in range(width):
            start = column * extent
            early = result[start : start + half, :]
            late = result[start + half : start + extent, :]
            kept_ref[h, column] = jnp.where(later, late, early).astype(BF16)
            sent_ref[h, column] = jnp.where(later, early, late).astype(BF16)
        return carry

    lax.fori_loop(0, planes, plane, 0)
    put_stats(stat_ref, acc)
    slope_out.wait_all()


def turn(
    totals, second_out, keep, params, act, first_mom, cotangent, own_clip, section, peers
):
    planes, rows, unused = second_out.shape
    unused, unused, width, extent, unused = cotangent.shape
    half = (planes, width, extent // 2, C5)
    return call(
        turn_body,
        [
            shape_of(*half, dtype=BF16),
            shape_of(*half, dtype=BF16),
            shape_of(planes, rows, NB2),
            shape_of(planes, rows, ND, dtype=BF16),
            shape_of(peers, 2, NB2),
            shape_of(2, NB2),
        ],
        "vvapvv",
        [
            pltpu.VMEM((8, NB2), F32),
            pltpu.VMEM((planes, rows, NB2), F32),
            pltpu.VMEM(cotangent.shape[1:], BF16),
            pltpu.VMEM((rows, C5), F32),
            pltpu.VMEM((rows, C5), F32),
            pltpu.VMEM((2, 8, NB2), F32),
            DMA((planes,)),
            DMA((planes,)),
        ],
        (totals, second_out, keep, params[3], params[4], act, first_mom, cotangent),
        "vpvvvpva",
        "turn",
        (own_clip, section),
        mib=12,
    )


def slope_plane(
    upstream, z_ref, h, vec, keep, slope_ref, slope_at, acc, tiles
):
    for first, last in tiles:
        at = slice(first, last)
        value = z_ref[h, :, at]
        shifted = value * vec[0:1, at] + vec[1:2, at]
        gate = sigmoid(shifted)
        slope = upstream(first, last) * keep * gate * (1.0 + shifted * (1.0 - gate))
        slope_ref[slope_at, :, at] = slope
        acc[0, :, at] += rows_summed(slope)
        acc[1, :, at] += rows_summed(slope * (value * vec[2:3, at] + vec[3:4, at]))


def put_halves(section, packed, kept_hbm, sent_hbm, sems):
    half = packed.shape[0] // 2
    copies = [
        pltpu.make_async_copy(
            packed.at[pl.ds(pl.multiple_of(which * half, 16), half)],
            target.at[pl.ds(0, half)],
            sems.at[place],
        )
        for place, (which, target) in enumerate(((section, kept_hbm), (1 - section, sent_hbm)))
    ]
    for copy in copies:
        copy.start()
    return copies


def conv_grad_body(
    extent,
    section_ref,
    tot_ref,
    slope_hbm,
    z_hbm,
    mid_hbm,
    keep_ref,
    gain_ref,
    bias_ref,
    first_mom_ref,
    mom_ref,
    more_kept_hbm,
    more_sent_hbm,
    grad_v,
    kept_hbm,
    sent_hbm,
    norm_ref,
    vec,
    slope_v,
    z_v,
    mid_v,
    im_wide,
    im_narrow,
    turned,
    packed,
    more_v,
    slope_sem,
    z_sem,
    mid_sem,
    half_sem,
):
    planes, rows, unused = z_v.shape
    slope_in = Planes(slope_hbm, slope_v, slope_sem)
    z_in = Planes(z_hbm, z_v, z_sem)
    mid_in = Planes(mid_hbm, mid_v, mid_sem)
    for h in range(planes):
        mid_in.start(h)
        slope_in.start(h)
        z_in.start(h)
    half_rows = packed.shape[0] // 2
    more = kept_hbm.shape[0] - half_rows
    beside = [
        (
            pltpu.make_async_copy(source, more_v.at[place], half_sem.at[2 + place]),
            pltpu.make_async_copy(
                more_v.at[place], target.at[pl.ds(half_rows, more)], half_sem.at[4 + place]
            ),
        )
        for place, (source, target) in enumerate(
            ((more_kept_hbm, kept_hbm), (more_sent_hbm, sent_hbm))
        )
        if more
    ]
    for arriving, leaving in beside:
        arriving.start()
    total = jnp.sum(tot_ref[...], axis=0)
    put_original(norm_ref, 0, total[1:2], SECOND_PIECES)
    put_original(norm_ref, 1, total[0:1], SECOND_PIECES)
    second_rows(vec, gain_ref, bias_ref, mom_ref)
    back_rows(vec, total, first_mom_ref[2:3, 0:NB2])
    targets = ((im_wide, 0, B1A), (im_narrow, B1A, NM))
    clear_ends(targets, (0, planes + 1))
    times = times_of(rows, 128, extent)

    def gradient(h, carry):
        mid_in.wait(h)
        for first, last in tiles_of(0, NM):
            value = mid_v[h, :, first:last].astype(F32)
            spread_plane(value, first, times, extent, targets, h + 1)
        slope_in.wait(h)
        z_in.wait(h)
        keep = keep_ref[h]
        for first, last in tiles_of(0, NB2):
            at = slice(first, last)
            value = slope_v[h, :, at] * vec[0:1, at] + z_v[h, :, at] * vec[7:8, at] + vec[6:7, at]
            grad_v[h, :, at] = (value * keep).astype(BF16)
        return carry

    lax.fori_loop(0, planes, gradient, 0)
    for arriving, leaving in beside:
        arriving.wait()
        leaving.start()
    turned[...] = grad_v[...].reshape(planes * rows, NB2).T
    wide_rows = 27 * B1A
    half = wide_rows // 2
    used = CONV_NARROW + 27 * B2A
    packed[used:, :] = jnp.zeros((packed.shape[0] - used, 128), BF16)
    step = 3 * B1A
    for high in range(3):
        value = im_wide[high : high + planes].reshape(planes * rows, 9 * B1A)
        part = jnp.dot(turned[B2:NB2, :], value, preferred_element_type=F32)
        part = part.T.astype(BF16)
        value = im_narrow[high : high + planes].reshape(planes * rows, 9 * B2A)
        small = jnp.dot(turned[0:B2, :], value, preferred_element_type=F32)
        small = small.T.astype(BF16)
        for time in range(3):
            chunk = time * 3 + high
            row = chunk * step
            piece = part[time * step : (time + 1) * step]
            packed[row : row + step, :] = piece[:, 0:128]
            packed[wide_rows + row : wide_rows + row + step, :] = piece[:, 128:256]
            low = max(0, min(step, half - row))
            tail = 2 * wide_rows + row
            if low > 0:
                packed[tail : tail + low, 0:64] = piece[:low, 256:B1]
            if low < step:
                tail = tail + low - half
                packed[tail : tail + step - low, 64:128] = piece[low:, 256:B1]
            row = CONV_NARROW + chunk * 3 * B2A
            packed[row : row + 3 * B2A, :] = small[time * 3 * B2A : (time + 1) * 3 * B2A]
    copies = put_halves(section_ref[0], packed, kept_hbm, sent_hbm, half_sem)
    for copy in copies + [leaving for arriving, leaving in beside]:
        copy.wait()


def conv_grad(
    totals, slope, second_out, mid, keep, params, first_mom, mom, extent, section, peers, more=None
):
    planes, rows, unused = second_out.shape
    packed = conv_rows(peers)
    half = packed // 2
    if more is None:
        more = (mid, mid)
    else:
        half += more[0].shape[0]
    return call(
        functools.partial(conv_grad_body, extent),
        [
            shape_of(planes, rows, NB2, dtype=BF16),
            shape_of(half, 128, dtype=BF16),
            shape_of(half, 128, dtype=BF16),
            shape_of(2, NB2),
        ],
        "paav",
        [
            pltpu.VMEM((8, NB2), F32),
            pltpu.VMEM((planes, rows, NB2), F32),
            pltpu.VMEM((planes, rows, NB2), F32),
            pltpu.VMEM((planes, rows, NM), BF16),
            pltpu.VMEM((planes + 2, rows, 9 * B1A), BF16),
            pltpu.VMEM((planes + 2, rows, 9 * B2A), BF16),
            pltpu.VMEM((NB2, planes * rows), BF16),
            pltpu.VMEM((packed, 128), BF16),
            pltpu.VMEM((2, max(half - packed // 2, 16), 128), BF16),
            DMA((planes,)),
            DMA((planes,)),
            DMA((planes,)),
            DMA((6,)),
        ],
        (totals, slope, second_out, mid, keep, params[3], params[4], first_mom, mom, *more),
        "vaaavvvvvaa",
        "conv_grad",
        (section,),
        flops=2 * planes * rows * 27 * (B1A * B1 + B2A * B2),
        mib=30,
    )


def prepare_body(wide_ref, narrow_ref, turned_hbm, weights, sems):
    weights[...] = jnp.zeros_like(weights)
    copies = []
    for height in range(3):
        for place in range(9):
            source = 26 - ((place // 3) * 9 + height * 3 + place % 3)
            weights[height, 0:B1A, place * NB2 + B2 : (place + 1) * NB2] = wide_ref[source]
            weights[height, B1A:NM, place * NB2 : place * NB2 + B2] = narrow_ref[source]
        copies.append(
            pltpu.make_async_copy(weights.at[height], turned_hbm.at[height], sems.at[height])
        )
        copies[-1].start()
    for copy in copies:
        copy.wait()


def prepare(conv_mid, conv_small):
    return call(
        prepare_body,
        [shape_of(3, NM, TURNED, dtype=BF16)],
        "a",
        [pltpu.VMEM((3, NM, TURNED), BF16), DMA((3,))],
        (conv_mid, conv_small),
        "vv",
        "prepare",
        mib=24,
    )[0]


def back_conv_body(
    extent,
    halved,
    start,
    grad_ref,
    z_hbm,
    keep_ref,
    gain_ref,
    bias_ref,
    first_mom_ref,
    direct_v,
    turned_hbm,
    before_ref,
    slope_v,
    stat_ref,
    acc,
    vec,
    z_v,
    windows,
    weights,
    z_sem,
    weight_sem,
):
    planes = grad_ref.shape[0]
    count, rows, unused = z_v.shape
    low = 1 if start == 0 else 0
    high = count + 1 if start + count == planes else count + 2
    weights_in = Planes(turned_hbm, weights, weight_sem)
    weights_in.start_all()
    z_in = Planes(z_hbm, z_v, z_sem, start)
    z_in.start_all()
    first_rows(vec, gain_ref, bias_ref, first_mom_ref)
    targets = ((windows, 0, NB2),)
    clear_ends(targets, [0] * low + [count + 1] * (count + 2 - high))
    times = times_of(rows, 128, extent)

    def shift(j, carry):
        for first, last in tiles_of(0, NB2):
            value = grad_ref[start - 1 + j, :, first:last].astype(F32)
            spread_plane(value, first, times, extent, targets, j)
        return carry

    lax.fori_loop(low, high, shift, 0)
    weights_in.wait_all()
    total = None
    for height in range(3):
        value = windows[height : height + count].reshape(count * rows, 9 * NB2)
        part = lax.dot_general(
            value,
            weights[height, :, 0 : 9 * NB2],
            (((1,), (1,)), ((), ())),
            preferred_element_type=F32,
        )
        total = part if total is None else total + part
    slope_v[:, :, ND:NB1] = total.reshape(count, rows, NM)
    acc[...] = before_ref[...]

    def slopes(h, carry):
        z_in.wait(h)

        def upstream(first, last):
            if first >= ND:
                return slope_v[h, :, first:last]
            if halved:
                return direct_v[(start + h) // 2, :, first:last].astype(F32) * 0.125
            return direct_v[start + h, :, first:last].astype(F32)

        slope_plane(upstream, z_v, h, vec, keep_ref[start + h], slope_v, h, acc, tiles_of(0, NB1))
        return carry

    lax.fori_loop(0, count, slopes, 0)
    put_stats(stat_ref, acc)


def back_conv(
    grad, first_out, keep, params, turned, first_mom, direct, halved, extent, peers, part, before
):
    unused, unused, unused, gain, bias = params
    planes, rows, unused = first_out.shape
    start, count = part
    return call(
        functools.partial(back_conv_body, extent, halved, start),
        [shape_of(count, rows, NB1), shape_of(peers, 2, NB1), shape_of(2, 8, NB1)],
        "pvv",
        [
            pltpu.VMEM((8, NB1), F32),
            pltpu.VMEM((count, rows, NB1), F32),
            pltpu.VMEM((count + 2, rows, 9 * NB2), BF16),
            pltpu.VMEM((3, NM, TURNED), BF16),
            DMA((count,)),
            DMA((3,)),
        ],
        (grad, first_out, keep, gain, bias, first_mom, direct, turned, before),
        "pavvvvpav",
        "back_conv",
        flops=2 * count * rows * 27 * (B1A * B1 + B2A * B2),
        mib=30,
    )


def first_gradient(
    slope_refs, ready, z_ref, keep_ref, vec, grad_ref, pool_ref, between_ref, extent, done
):
    begin = 0
    for slope_ref in slope_refs:

        def gradient(t, carry, begin=begin, slope_ref=slope_ref):
            h = begin + t
            ready(h)
            keep = keep_ref[h]
            for first, last in tiles_of(0, NB1):
                at = slice(first, last)
                value = (
                    slope_ref[t, :, at] * vec[0:1, at] + z_ref[h, :, at] * vec[7:8, at] + vec[6:7, at]
                ) * keep
                if first == B0:
                    pool_ref[h] = value
                else:
                    grad_ref[h, :, at] = value.astype(BF16)
            return carry

        lax.fori_loop(0, slope_ref.shape[0], gradient, 0)
        begin += slope_ref.shape[0]

    def put(h, value):
        grad_ref[h, :, B0:ND] = value.astype(BF16)
        done(h)

    window_sums(pool_ref, between_ref, extent, put)


def put_norms(norm_ref, total, pieces):
    put_original(norm_ref, 0, total[1:2], pieces)
    put_original(norm_ref, 1, total[0:1], pieces)


def last_gradient_body(
    clip_ref,
    section_ref,
    tot_ref,
    slope_0,
    slope_1,
    z_hbm,
    x_hbm,
    keep_ref,
    gain_ref,
    bias_ref,
    mom_ref,
    grad_v,
    kept_hbm,
    sent_hbm,
    norm_ref,
    vec,
    z_v,
    x_v,
    pool,
    between,
    product,
    ordered,
    packed,
    z_sem,
    x_sem,
    half_sem,
):
    planes, rows, channels = x_v.shape
    z_in = Planes(z_hbm, z_v, z_sem)
    x_in = Planes(x_hbm.at[clip_ref[0]], x_v, x_sem)
    for h in range(planes):
        z_in.start(h)
    x_in.start_all()
    first_rows(vec, gain_ref, bias_ref, mom_ref)
    total = jnp.sum(tot_ref[...], axis=0)
    put_norms(norm_ref, total, FIRST_PIECES)
    back_rows(vec, total, mom_ref[2:3, :])

    def done(h):
        x_in.wait(h)
        x_v[h] = x_v[h] * keep_ref[h].astype(BF16)

    first_gradient(
        (slope_0, slope_1), z_in.wait, z_v, keep_ref, vec, grad_v, pool, between, 8, done
    )
    product[...] = lax.dot_general(
        x_v[...].reshape(planes * rows, channels),
        grad_v[...].reshape(planes * rows, NB1),
        (((0,), (0,)), ((), ())),
        preferred_element_type=F32,
    )
    for inner, outer, width in FIRST_PIECES:
        ordered[:, outer : outer + width] = product[:, inner : inner + width]
    pack_inproj(ordered, packed)
    copies = put_halves(section_ref[0], packed, kept_hbm, sent_hbm, half_sem)
    for copy in copies:
        copy.wait()


def last_gradient(totals, slopes, first_out, clips, keep, params, mom, own_clip, section, peers):
    planes, rows, unused = first_out.shape
    channels = clips.shape[3]
    packed = padded_rows(inproj_rows(channels)[1], peers)
    return call(
        last_gradient_body,
        [
            shape_of(planes, rows, NB1, dtype=BF16),
            shape_of(packed // 2, 128),
            shape_of(packed // 2, 128),
            shape_of(2, NB1),
        ],
        "paav",
        [
            pltpu.VMEM((8, NB1), F32),
            pltpu.VMEM((planes, rows, NB1), F32),
            pltpu.VMEM((planes, rows, channels), BF16),
            pltpu.VMEM((planes, rows, B3), F32),
            pltpu.VMEM((planes + 2, rows, B3), F32),
            pltpu.VMEM((channels, NB1), F32),
            pltpu.VMEM((channels, NB1), F32),
            pltpu.VMEM((packed, 128), F32),
            DMA((planes,)),
            DMA((planes,)),
            DMA((2,)),
        ],
        (totals, *slopes, first_out, clips, keep, params[3], params[4], mom),
        "vppaavvvv",
        "last_gradient",
        (own_clip, section),
        flops=2 * planes * rows * channels * NB1,
        mib=28,
    )


def clip_gradient_body(
    section_ref,
    grad_v,
    keep_ref,
    weight_ref,
    kept_hbm,
    sent_hbm,
    du_v,
    kept_v,
    sent_v,
    ordered,
    kept_sem,
    sent_sem,
):
    planes, rows, channels = du_v.shape
    unused, width, half, unused = kept_v.shape
    later = section_ref[0] == 1
    kept_out = Outwards(kept_v, kept_hbm, kept_sem)
    sent_out = Outwards(sent_v, sent_hbm, sent_sem)
    weight_ordered(weight_ref, ordered)
    together, steps = step_planes(planes)

    def product(i, carry):
        at = pl.ds(i * together, together)
        value = grad_v[at].reshape(together * rows, NB1)
        out = lax.dot_general(
            value, ordered[...], (((1,), (1,)), ((), ())), preferred_element_type=F32
        )
        du_v[at] = out.reshape(together, rows, channels) * keep_ref[at]

        def sent(k, carry):
            h = i * together + k
            for column in range(width):
                start = 2 * half * column
                early = du_v[h, start : start + half, :]
                late = du_v[h, start + half : start + 2 * half, :]
                kept_v[h, column] = jnp.where(later, late, early).astype(BF16)
                sent_v[h, column] = jnp.where(later, early, late).astype(BF16)
            kept_out.start(h)
            sent_out.start(h)
            return carry

        lax.fori_loop(0, together, sent, 0)
        return carry

    lax.fori_loop(0, steps, product, 0)
    kept_out.wait_all()
    sent_out.wait_all()


def clip_gradient(grad, keep, inproj, width, section):
    planes, rows, unused = grad.shape
    channels = inproj.shape[0]
    half = (planes, width, rows // width // 2, channels)
    return call(
        clip_gradient_body,
        [shape_of(*half, dtype=BF16)] * 2,
        "aa",
        [
            pltpu.VMEM((planes, rows, channels), F32),
            pltpu.VMEM(half, BF16),
            pltpu.VMEM(half, BF16),
            pltpu.VMEM((channels, NB1), BF16),
            DMA((planes,)),
            DMA((planes,)),
        ],
        (grad, keep, inproj),
        "pvv",
        "clip_gradient",
        (section,),
        flops=2 * planes * rows * channels * NB1,
        mib=24,
    )


def both_clips_body(own_ref, kept_ref, got_ref, out_ref):
    own = own_ref[0]
    out_ref[own] = kept_ref[...]
    out_ref[1 - own] = got_ref[...]


def both_clips(kept, got, own_clip):
    return call(
        both_clips_body,
        [shape_of(2, *kept.shape, dtype=BF16)],
        "v",
        [],
        (kept, got),
        "vv",
        "both_clips",
        (own_clip,),
        mib=24,
    )[0]


def back_between_body(
    tot_ref,
    own_slope_hbm,
    own_z_hbm,
    keep_ref,
    gain_ref,
    bias_ref,
    mom_ref,
    weight_ref,
    z_hbm,
    keep_prev,
    gain_prev,
    bias_prev,
    mom_prev,
    up_v,
    grad_ref,
    slope_hbm,
    stat_ref,
    norm_ref,
    vec,
    vec_prev,
    slope_ref,
    z_ref,
    ordered,
    pool,
    between,
    z_v,
    slope_v,
    acc,
    z_sem,
    slope_sem,
    own_sem,
):
    planes, rows, unused = z_ref.shape
    extent = 4
    own = [
        pltpu.make_async_copy(own_slope_hbm, slope_ref, own_sem.at[0]),
        pltpu.make_async_copy(own_z_hbm, z_ref, own_sem.at[1]),
    ]
    for copy in own:
        copy.start()
    z_in = Planes(z_hbm, z_v, z_sem)
    slope_out = Outwards(slope_v, slope_hbm, slope_sem)
    first_rows(vec, gain_ref, bias_ref, mom_ref)
    second_rows(vec_prev, gain_prev, bias_prev, mom_prev)
    total = jnp.sum(tot_ref[...], axis=0)
    put_norms(norm_ref, total, FIRST_PIECES)
    back_rows(vec, total, mom_ref[2:3, :])
    turned_ordered(weight_ref, ordered)
    for copy in own:
        copy.wait()
    z_in.start_all()
    first_gradient(
        (slope_ref,),
        lambda h: None,
        z_ref,
        keep_ref,
        vec,
        grad_ref,
        pool,
        between,
        extent,
        lambda h: None,
    )
    value = grad_ref[...].reshape(planes * rows, NB1)
    out = lax.dot_general(
        value, ordered[...], (((1,), (0,)), ((), ())), preferred_element_type=F32
    )
    rows_prev = z_v.shape[1]
    cells = cell_of((rows_prev, rows), 0, rows_prev) == lax.broadcasted_iota(jnp.int32, (rows_prev, rows), 1)
    doubled = jnp.where(cells, 1.0, 0.0).astype(BF16)
    for h in range(planes):
        single = (out[h * rows : (h + 1) * rows] * keep_ref[h]).astype(BF16)
        up_v[h] = jnp.dot(doubled, single, preferred_element_type=F32).astype(BF16)
    acc[...] = jnp.zeros_like(acc)

    def slopes(h, carry):
        z_in.wait(h)

        def upstream(first, last):
            return up_v[h // 2, :, ND + first : ND + last].astype(F32) * 0.125

        slope_plane(upstream, z_v, h, vec_prev, keep_prev[h], slope_v, h, acc, tiles_of(0, NB2))
        slope_out.start(h)
        return carry

    lax.fori_loop(0, 2 * planes, slopes, 0)
    put_stats(stat_ref, acc)
    slope_out.wait_all()


def back_between(
    totals, slope, first_out, keep, params, mom, second_prev, keep_prev, params_prev, mom_prev, peers
):
    inproj, unused, unused, gain, bias = params
    planes, rows, unused = first_out.shape
    above, rows_prev, unused = second_prev.shape
    return call(
        back_between_body,
        [
            shape_of(planes, rows_prev, C5, dtype=BF16),
            shape_of(planes, rows, NB1, dtype=BF16),
            shape_of(*second_prev.shape),
            shape_of(peers, 2, NB2),
            shape_of(2, NB1),
        ],
        "pvavv",
        [
            pltpu.VMEM((8, NB1), F32),
            pltpu.VMEM((8, NB2), F32),
            pltpu.VMEM((planes, rows, NB1), F32),
            pltpu.VMEM((planes, rows, NB1), F32),
            pltpu.VMEM((NB1, C5), BF16),
            pltpu.VMEM((planes, rows, B3), F32),
            pltpu.VMEM((planes + 2, rows, B3), F32),
            pltpu.VMEM(second_prev.shape, F32),
            pltpu.VMEM(second_prev.shape, F32),
            pltpu.VMEM((2, 8, NB2), F32),
            DMA((above,)),
            DMA((above,)),
            DMA((2,)),
        ],
        (
            totals,
            slope,
            first_out,
            keep,
            gain,
            bias,
            mom,
            inproj,
            second_prev,
            keep_prev,
            params_prev[3],
            params_prev[4],
            mom_prev,
        ),
        "vaavvvvvavvvv",
        "back_between",
        flops=2 * planes * rows * C5 * NB1,
        mib=20,
    )


def inproj_rows(channels):
    first = -(-channels // 32) * 16
    return first, 4 * channels + first


def pack_inproj(ordered, packed):
    channels = ordered.shape[0]
    first, used = inproj_rows(channels)
    padded = packed.shape[0]
    for place in range(4):
        packed[place * channels : (place + 1) * channels, :] = ordered[
            :, place * 128 : (place + 1) * 128
        ]
    start = 4 * channels
    packed[start : start + first, 0:64] = ordered[0:first, 512:NB1]
    packed[start : start + channels - first, 64:128] = ordered[first:channels, 512:NB1]
    if 2 * first > channels:
        packed[start + channels - first : start + first, 64:128] = jnp.zeros(
            (2 * first - channels, 64), packed.dtype
        )
    if padded > used:
        packed[used:padded, :] = jnp.zeros((padded - used, 128), packed.dtype)


def inproj_grad_body(
    section_ref, x_ref, grad_ref, kept_hbm, sent_hbm, product, ordered, packed, half_sem
):
    planes, rows, channels = x_ref.shape
    product[...] = lax.dot_general(
        x_ref[...].reshape(planes * rows, channels),
        grad_ref[...].reshape(planes * rows, NB1),
        (((0,), (0,)), ((), ())),
        preferred_element_type=F32,
    ).astype(BF16)
    for row_to, row_from, height in RESULT_PIECES:
        for inner, outer, width in FIRST_PIECES:
            ordered[row_from : row_from + height, outer : outer + width] = product[
                row_to : row_to + height, inner : inner + width
            ]
    pack_inproj(ordered, packed)
    for copy in put_halves(section_ref[0], packed, kept_hbm, sent_hbm, half_sem):
        copy.wait()


def inproj_grad(x, grad, section, peers):
    planes, rows, channels = x.shape
    packed = padded_rows(inproj_rows(channels)[1], peers)
    return call(
        inproj_grad_body,
        [shape_of(packed // 2, 128, dtype=BF16)] * 2,
        "aa",
        [
            pltpu.VMEM((channels, NB1), BF16),
            pltpu.VMEM((channels, NB1), BF16),
            pltpu.VMEM((packed, 128), BF16),
            DMA((2,)),
        ],
        (x, grad),
        "vv",
        "inproj_grad",
        (section,),
        flops=2 * planes * rows * channels * NB1,
        mib=12,
    )


def unpack_conv(packed_ref, wide_ref, narrow_ref):
    step = 27 * B1A
    half = step // 2
    wide_ref[:, 0:128] = packed_ref[0:step, :].astype(F32)
    wide_ref[:, 128:256] = packed_ref[step : 2 * step, :].astype(F32)
    wide_ref[0:half, 256:B1] = packed_ref[2 * step : 2 * step + half, 0:64].astype(F32)
    wide_ref[half:step, 256:B1] = packed_ref[2 * step : 2 * step + half, 64:128].astype(F32)
    narrow_ref[...] = packed_ref[CONV_NARROW : CONV_NARROW + 27 * B2A, :].astype(F32)


def unpack_inproj(packed_ref, out_ref):
    channels = out_ref.shape[0]
    first = inproj_rows(channels)[0]
    for place in range(4):
        out_ref[:, place * 128 : (place + 1) * 128] = packed_ref[
            place * channels : (place + 1) * channels, :
        ].astype(F32)
    start = 4 * channels
    out_ref[0:first, 512:NB1] = packed_ref[start : start + first, 0:64].astype(F32)
    out_ref[first:channels, 512:NB1] = packed_ref[start : start + channels - first, 64:128].astype(
        F32
    )


def unpack_alone_body(section_ref, value_ref, got_ref, wide_ref, narrow_ref, packed_ref):
    half = value_ref.shape[0]
    section = section_ref[0]
    packed_ref[pl.ds(pl.multiple_of(section * half, 16), half), :] = value_ref[...]
    packed_ref[pl.ds(pl.multiple_of((1 - section) * half, 16), half), :] = got_ref[...]
    unpack_conv(packed_ref, wide_ref, narrow_ref)


def unpack_alone(value, got, section):
    return call(
        unpack_alone_body,
        [shape_of(27 * B1A, B1), shape_of(27 * B2A, B2)],
        "vv",
        [pltpu.VMEM((2 * value.shape[0], 128), BF16)],
        (value, got),
        "vv",
        "unpack_alone",
        (section,),
        mib=24,
    )


def halves_placed(section_ref, value_ref, got_ref, pieces):
    section = section_ref[0]
    for half_ref, half in ((value_ref, section), (got_ref, 1 - section)):
        for packed_ref, first, last in pieces:
            size = last - first
            packed_ref[pl.ds(pl.multiple_of(half * size, 16), size), :] = half_ref[first:last, :]


def unpack_joined_body(
    section_ref,
    value_ref,
    got_ref,
    wide_hbm,
    narrow_hbm,
    next_hbm,
    wide_ref,
    narrow_ref,
    next_ref,
    conv_packed,
    next_packed,
    next_out,
    sems,
):
    half = conv_packed.shape[0] // 2
    halves_placed(
        section_ref,
        value_ref,
        got_ref,
        ((conv_packed, 0, half), (next_packed, half, value_ref.shape[0])),
    )
    step = 3 * B1A
    rows, halfway = 9 * step, 9 * step // 2
    copies = []
    for chunk in range(9):
        row = chunk * step
        at = slice(row, row + step)
        wide_ref[at, 0:128] = conv_packed[at, :].astype(F32)
        wide_ref[at, 128:256] = conv_packed[rows + row : rows + row + step, :].astype(F32)
        low = max(0, min(step, halfway - row))
        tail = 2 * rows + row
        if low > 0:
            wide_ref[row : row + low, 256:B1] = conv_packed[tail : tail + low, 0:64].astype(F32)
        if low < step:
            tail += low - halfway
            wide_ref[row + low : row + step, 256:B1] = conv_packed[
                tail : tail + step - low, 64:128
            ].astype(F32)
        copies.append(
            pltpu.make_async_copy(
                wide_ref.at[pl.ds(row, step)], wide_hbm.at[pl.ds(row, step)], sems.at[chunk]
            )
        )
        copies[-1].start()
    narrow_ref[...] = conv_packed[CONV_NARROW : CONV_NARROW + 27 * B2A, :].astype(F32)
    copies.append(pltpu.make_async_copy(narrow_ref, narrow_hbm, sems.at[9]))
    copies[-1].start()
    unpack_inproj(next_packed, next_out)
    next_ref[...] = next_out[...].T
    copies.append(pltpu.make_async_copy(next_ref, next_hbm, sems.at[10]))
    copies[-1].start()
    for copy in copies:
        copy.wait()


def unpack_joined(value, got, section, channels, peers):
    return call(
        unpack_joined_body,
        [shape_of(27 * B1A, B1), shape_of(27 * B2A, B2), shape_of(NB1, channels)],
        "aaa",
        [
            pltpu.VMEM((27 * B1A, B1), F32),
            pltpu.VMEM((27 * B2A, B2), F32),
            pltpu.VMEM((NB1, channels), F32),
            pltpu.VMEM((conv_rows(peers), 128), BF16),
            pltpu.VMEM((padded_rows(inproj_rows(channels)[1], peers), 128), BF16),
            pltpu.VMEM((channels, NB1), F32),
            DMA((11,)),
        ],
        (value, got),
        "vv",
        "unpack_joined",
        (section,),
        mib=32,
    )


def share_places(peers):
    pairs = distance_pairs(peers)
    places = []
    for section in range(2):
        order = [pair[section] for pair in pairs]
        places.append(
            [
                sum(
                    ((place // distance) % 2) << (len(order) - 1 - level)
                    for level, distance in enumerate(order)
                )
                for place in range(peers)
            ]
        )
    return places


def unpack_inproj_body(section_ref, value_ref, got_ref, out_ref, packed):
    section = section_ref[0]
    peers, share, unused = value_ref.shape
    places = share_places(peers)
    for half_ref, half in ((value_ref, section), (got_ref, 1 - section)):
        for place in range(peers):
            at = jnp.where(half == 0, places[0][place], places[1][place]) + half * peers
            packed[pl.ds(pl.multiple_of(at * share, 16), share), :] = half_ref[place]
    unpack_inproj(packed, out_ref)


def unpack_inproj_alone(value, got, section, channels):
    return call(
        unpack_inproj_body,
        [shape_of(channels, NB1)],
        "v",
        [pltpu.VMEM((2 * value.shape[0] * value.shape[1], 128), BF16)],
        (value, got),
        "vv",
        "unpack_inproj",
        (section,),
        mib=12,
    )[0]


def sent_to_all(spread):
    return lax.all_to_all(spread, "dp", 0, 0)


def swapped(value):
    return lax.ppermute(value, "section", [(0, 1), (1, 0)])


def distance_pairs(peers):
    distances = []
    while 2 ** len(distances) < peers:
        distances.append(2 ** len(distances))
    return list(zip(distances, [distances[1], distances[0]] + distances[2:]))


def distances_of():
    return distance_pairs(lax.axis_size("dp"))


def exchanged(value, pair):
    count = lax.axis_size("dp")
    links = [
        (section * count + place, section * count + (place ^ pair[section]))
        for section in range(2)
        for place in range(count)
    ]
    return lax.ppermute(value, ("section", "dp"), links)


def upper_half(pair):
    place = lax.axis_index("dp")
    distance = jnp.where(lax.axis_index("section") == 0, pair[0], pair[1])
    return ((place // distance) % 2).astype(jnp.int32).reshape(1)


def added(kept, got):
    return (kept.astype(F32) + got.astype(F32)).astype(kept.dtype)


def split_sum_body(upper_ref, kept_ref, got_ref, left_ref, sent_ref):
    half = left_ref.shape[0]
    upper = upper_ref[0]
    for target, which in ((left_ref, upper), (sent_ref, 1 - upper)):
        at = pl.ds(pl.multiple_of(which * half, 16), half)
        target[...] = added(kept_ref[at, :], got_ref[at, :])


def split_sum(kept, got, pair):
    half = shape_of(kept.shape[0] // 2, 128, dtype=kept.dtype)
    return call(
        split_sum_body, [half, half], "vv", [], (kept, got), "vv", "split_sum", (upper_half(pair),)
    )


def placed_body(upper_ref, value_ref, got_ref, out_ref):
    half = value_ref.shape[0]
    upper = upper_ref[0]
    out_ref[pl.ds(pl.multiple_of(upper * half, 16), half), :] = value_ref[...]
    out_ref[pl.ds(pl.multiple_of((1 - upper) * half, 16), half), :] = got_ref[...]


def placed(value, got, pair):
    whole = shape_of(value.shape[0] * 2, 128, dtype=value.dtype)
    return call(
        placed_body, [whole], "v", [], (value, got), "vv", "placed", (upper_half(pair),)
    )[0]


def staged_body(source_hbm, target_ref, sem):
    copy = pltpu.make_async_copy(source_hbm, target_ref, sem.at[0])
    copy.start()
    copy.wait()


def staged(value):
    whole = shape_of(*value.shape, dtype=value.dtype)
    return call(staged_body, [whole], "p", [DMA((1,))], (value,), "a", "staged", mib=6)[0]


class Scatter:
    def __init__(self, kept, sent, stage=True):
        self.pairs = distances_of()
        self.place = 0
        self.got = swapped(sent)
        self.kept = staged(kept) if stage else kept

    def step(self):
        pair = self.pairs[self.place]
        self.kept, sent = split_sum(self.kept, self.got, pair)
        self.got = exchanged(sent, pair)
        self.place += 1

    def result(self):
        while self.place < len(self.pairs):
            self.step()
        return added(self.kept, self.got)


class Gather:
    def __init__(self, value):
        self.value = value
        self.pairs = distances_of()[::-1]
        self.place = 0
        self.got = exchanged(value, self.pairs[0])

    def step(self):
        self.value = placed(self.value, self.got, self.pairs[self.place])
        self.place += 1
        if self.place < len(self.pairs):
            self.got = exchanged(self.value, self.pairs[self.place])
        else:
            self.got = swapped(self.value)

    def result(self):
        while self.place < len(self.pairs):
            self.step()
        return self.value, self.got


def lockstep(one, other):
    one.got, other.got = lax.optimization_barrier((one.got, other.got))


def tied(value, *exchanges):
    both = lax.optimization_barrier((value,) + tuple(e.got for e in exchanges))
    for exchange, got in zip(exchanges, both[1:]):
        exchange.got = got
    return both[0]


def small_body(first_a, second_a, first_b, second_b, norm1_a, norm2_a, norm1_b, norm2_b, out_ref):
    for row, first, second in ((0, first_a, second_a), (2, first_b, second_b)):
        for line in range(2):
            for pieces, source, offset in ((FIRST_PIECES, first, 0), (SECOND_PIECES, second, NB1)):
                for inner, outer, width in pieces:
                    start = offset + outer
                    out_ref[row + line : row + line + 1, start : start + width] = source[
                        line : line + 1, inner : inner + width
                    ]
    for row, first, second in ((4, norm1_a, norm2_a), (6, norm1_b, norm2_b)):
        out_ref[row : row + 2, 0:NB1] = first[...]
        out_ref[row : row + 2, NB1:NB] = second[...]


def small_out_body(section_ref, own_ref, other_ref, norm_a, mom_a, norm_b, mom_b):
    section = section_ref[0]
    own, other = own_ref[...], other_ref[...]
    norms = own[4:8] + other[4:8]
    norm_a[...] = norms[0:2]
    norm_b[...] = norms[2:4]
    low = jnp.where(section == 0, own, other)
    high = jnp.where(section == 0, other, own)
    mom_a[0] = low[0:2]
    mom_a[1] = high[0:2]
    mom_b[0] = low[2:4]
    mom_b[1] = high[2:4]


def small_outputs(rows, section):
    own = call(small_body, [shape_of(8, NB)], "v", [], rows, "vvvvvvvv", "small")[0]
    return call(
        small_out_body,
        [shape_of(2, NB), shape_of(2, 2, NB), shape_of(2, NB), shape_of(2, 2, NB)],
        "vvvv",
        [],
        (own, swapped(own)),
        "vv",
        "small_out",
        (section,),
    )


def local(
    clips_in,
    frames,
    voxel_mask,
    micro_order,
    inproj_4f,
    conv_mid_4f,
    conv_small_4f,
    gain_4f,
    bias_4f,
    inproj_5b,
    conv_mid_5b,
    conv_small_5b,
    gain_5b,
    bias_5b,
    cotangent,
):
    section = lax.axis_index("section")
    peers = lax.axis_size("dp")
    own = micro_order[0, section]
    own_clip = own.reshape(1)
    which = section.astype(jnp.int32).reshape(1)
    count, depth, height, width, channels = clips_in.shape
    clips = jnp.transpose(clips_in, (0, 2, 3, 1, 4)).reshape(count, height, width * depth, channels)
    upstream = jnp.transpose(cotangent, (0, 2, 3, 1, 4))

    first = (inproj_4f, conv_mid_4f, conv_small_4f, gain_4f.reshape(1, NB), bias_4f.reshape(1, NB))
    second = (inproj_5b.T, conv_mid_5b, conv_small_5b, gain_5b.reshape(1, NB), bias_5b.reshape(1, NB))
    long, short = depth, depth // 2

    z1_a, z1_here, stat, keep, keep_next = project_first(
        clips,
        micro_order.reshape(-1),
        which,
        frames,
        jnp.transpose(voxel_mask, (0, 2, 1, 3)),
        inproj_4f,
        peers,
    )
    totals = sent_to_all(stat)
    act_a, mid_a, z2_a, z2_here, stat, mom1_a = second_level(
        totals, z1_here, keep, first, long, peers
    )
    totals = sent_to_all(stat)
    x_b, z1_b, z1_here, stat, mom2_a = between_blocks(
        totals, z2_here, keep, first, act_a, mom1_a, keep_next, second[0], peers
    )
    act_b, mid_b, z2_b, z2_here, stat, mom1_b = second_level(
        sent_to_all(stat), z1_here, keep_next, second, short, peers
    )
    totals = sent_to_all(stat)
    kept, sent, slope, direct, stat, mom2_b = turn(
        totals, z2_here, keep_next, second, act_b, mom1_b, upstream, own_clip, which, peers
    )
    totals = sent_to_all(stat)
    result = (kept, swapped(sent))
    turned_b = prepare(conv_mid_5b, conv_small_5b)
    totals, turned_b = lax.optimization_barrier((totals, turned_b))
    dz2_b, kept, sent, norm2_b = conv_grad(
        totals, slope, z2_b, mid_b, keep_next, second, mom1_b, mom2_b, short, which, peers
    )
    sum_b = Scatter(kept, sent, False)
    nothing = jnp.zeros((2, 8, NB1), F32)
    slope, stat, unused = back_conv(
        dz2_b,
        z1_b,
        keep_next,
        second,
        turned_b,
        mom1_b,
        direct,
        False,
        short,
        peers,
        (0, height // 2),
        nothing,
    )
    stat = tied(stat, sum_b)
    sum_b.step()
    totals = sent_to_all(stat)
    block_out = both_clips(*result, own_clip)
    turned_a = prepare(conv_mid_4f, conv_small_4f)
    totals, turned_a = lax.optimization_barrier((totals, turned_a))
    totals, block_out = lax.optimization_barrier((totals, block_out))
    totals = tied(totals, sum_b)
    sum_b.step()
    up, dz1_b, slope, stat, norm1_b = back_between(
        totals, slope, z1_b, keep_next, second, mom1_b, z2_a, keep, first, mom2_a, peers
    )
    stat = tied(stat, sum_b)
    sum_b.step()
    totals = sent_to_all(stat)
    inproj_halves = inproj_grad(x_b, dz1_b, which, peers)
    totals = tied(totals, sum_b)
    sum_b.step()
    dz2_a, kept, sent, norm2_a = conv_grad(
        totals,
        slope,
        z2_a,
        mid_a,
        keep,
        first,
        mom1_a,
        mom2_a,
        long,
        which,
        peers,
        inproj_halves,
    )
    sent = tied(sent, sum_b)
    sum_a = Scatter(kept, sent)
    gather_b = Gather(sum_b.result())
    dz2_a = tied(dz2_a, sum_a)
    sum_a.step()
    half = height // 2
    back = (z1_a, keep, first, turned_a, mom1_a, up, True, long, peers)
    slope_low, unused, part = back_conv(dz2_a, *back, (0, half), nothing)
    part = tied(part, sum_a, gather_b)
    sum_a.step()
    gather_b.step()
    slope_high, stat, unused = back_conv(dz2_a, *back, (half, height - half), part)
    stat = tied(stat, sum_a, gather_b)
    sum_a.step()
    gather_b.step()
    totals = sent_to_all(stat)
    totals = tied(totals, sum_a, gather_b)
    sum_a.step()
    gather_b.step()
    dz1_a, kept, sent, norm1_a = last_gradient(
        totals,
        (slope_low, slope_high),
        z1_a,
        clips,
        keep,
        first,
        mom1_a,
        own_clip,
        which,
        peers,
    )
    sent = tied(sent, sum_a, gather_b)
    gather_a = Gather(sum_a.result())
    sum_i = Scatter(kept, sent)
    gather_b.step()
    dz1_a = tied(dz1_a, sum_i)
    sum_i.step()
    kept, sent = clip_gradient(dz1_a, keep, inproj_4f, width, which)
    sent = tied(sent, sum_i, gather_a)
    sum_i.step()
    gather_a.step()
    lockstep(gather_a, sum_i)
    sum_i.step()
    gather_a.step()
    lockstep(gather_a, sum_i)
    sum_i.step()
    gather_a.step()
    shares = jnp.broadcast_to(sum_i.result().astype(BF16)[None], (peers, *sum_i.kept.shape))
    shares, sent = lax.optimization_barrier((shares, sent))
    whole = sent_to_all(shares)
    clips_grad = both_clips(kept, swapped(sent), own_clip)
    small = small_outputs(
        (mom1_a, mom2_a, mom1_b, mom2_b, norm1_a, norm2_a, norm1_b, norm2_b), which
    )
    conv_b = unpack_alone(*gather_b.result(), which)
    whole, gather_a.got, clips_grad, small, conv_b = lax.optimization_barrier(
        (whole, gather_a.got, clips_grad, small, conv_b)
    )
    gather_a.step()
    inproj_a = unpack_inproj_alone(whole, swapped(whole), which, inproj_4f.shape[0])
    gather_a.got, inproj_a = lax.optimization_barrier((gather_a.got, inproj_a))
    wide_a, narrow_a, inproj_b = unpack_joined(
        *gather_a.result(), which, inproj_5b.shape[0], peers
    )
    return (
        jnp.transpose(block_out, (0, 3, 1, 2, 4)),
        jnp.transpose(clips_grad, (0, 3, 1, 2, 4)),
        inproj_a,
        wide_a.reshape(conv_mid_4f.shape),
        narrow_a.reshape(conv_small_4f.shape),
        small[0],
        small[1],
        inproj_b.T,
        conv_b[0].reshape(conv_mid_5b.shape),
        conv_b[1].reshape(conv_small_5b.shape),
        small[2],
        small[3],
    )


def solution(mesh):
    placed = (
        P("dp", None, None, None, None),
        P("dp"),
        P("dp", None, None, None),
        P("dp", None),
        P(),
        P(),
        P(),
        P(),
        P(),
        P(),
        P(),
        P(),
        P(),
        P(),
        P("dp", None, None, None, None),
    )
    return jax.shard_map(
        local,
        mesh=mesh,
        in_specs=placed,
        out_specs=(
            P("dp", "section", None, None, None),
            P("dp", "section", None, None, None),
            P(),
            P(),
            P(),
            P(),
            P(),
            P(),
            P(),
            P(),
            P(),
            P(),
        ),
        check_vma=False,
    )
```

```python
import functools

import jax
import jax.numpy as jnp
from jax import lax
from jax.experimental import pallas as pl
from jax.experimental.pallas import tpu as pltpu
from jax.sharding import PartitionSpec as P

B0 = 256
B1A = 160
B1 = 320
B2A = 32
B2 = 128
B3 = 128
C5 = 832
NX = 448
NB1 = 576
NB = 1024
NB2 = NB - NB1
NM = B1A + B2A
ND = B0 + B3

EPSILON = 0.001
F32 = jnp.float32
BF16 = jnp.bfloat16

FIRST_PIECES = ((0, 0, B0), (B0, NX, B3), (ND, B0, NM))
SECOND_PIECES = ((0, B1, B2), (B2, 0, B1))
RESULT_PIECES = ((0, 0, B0), (B0, C5 - B3, B3), (ND, B0 + B1, B2), (ND + B2, B0, B1))

CONV_NARROW = 10800
TURNED = 4096
DMA = pltpu.SemaphoreType.DMA


def padded_rows(rows, peers):
    whole = 32 * peers
    return -(-rows // whole) * whole


def conv_rows(peers):
    return padded_rows(CONV_NARROW + 27 * B2A, peers)


def shape_of(*dims, dtype=F32):
    return jax.ShapeDtypeStruct(dims, dtype)


def tiles_of(start, stop):
    return [(first, min(first + 128, stop)) for first in range(start, stop, 128)]


PINNED = {"a": pltpu.HBM, "p": pltpu.VMEM}


def call(body, outs, out_spaces, scratch, args, spaces, name, scalars=(), flops=0, mib=12):
    def spec(array, space):
        return pl.BlockSpec(memory_space=pltpu.HBM if space == "a" else pltpu.VMEM)

    assert len(args) == len(spaces) and len(outs) == len(out_spaces)
    return pl.pallas_call(
        body,
        out_shape=[
            PINNED[s](o.shape, o.dtype) if s in PINNED else o for o, s in zip(outs, out_spaces)
        ],
        grid_spec=pltpu.PrefetchScalarGridSpec(
            num_scalar_prefetch=len(scalars),
            grid=(1,),
            in_specs=[spec(a, s) for a, s in zip(args, spaces)],
            out_specs=[spec(o, s) for o, s in zip(outs, out_spaces)],
            scratch_shapes=scratch,
        ),
        compiler_params=pltpu.CompilerParams(vmem_limit_bytes=mib * 2**20),
        cost_estimate=pl.CostEstimate(
            flops=flops,
            transcendentals=0,
            bytes_accessed=sum(a.size * a.dtype.itemsize for a in list(args) + list(outs)),
        ),
        name=name,
    )(
        *scalars,
        *[
            pltpu.with_memory_space_constraint(a, pltpu.HBM) if s == "a" else a
            for a, s in zip(args, spaces)
        ],
    )


class Planes:
    def __init__(self, source, target, sem, start=0):
        self.source, self.target, self.sem, self.start_at = source, target, sem, start

    def copy(self, h):
        return pltpu.make_async_copy(
            self.source.at[h + self.start_at], self.target.at[h], self.sem.at[h]
        )

    def start(self, h):
        self.copy(h).start()

    def wait(self, h):
        self.copy(h).wait()

    def start_all(self):
        for h in range(self.sem.shape[0]):
            self.start(h)

    def wait_all(self):
        for h in range(self.sem.shape[0]):
            self.wait(h)


class Parts:
    def __init__(self, sources, target, sem):
        self.target, self.sem = target, sem
        self.places = [source.at[h] for source in sources for h in range(source.shape[0])]

    def start_all(self):
        for h, source in enumerate(self.places):
            pltpu.make_async_copy(source, self.target.at[h], self.sem.at[h]).start()

    def wait(self, h):
        pltpu.make_async_copy(self.places[0], self.target.at[h], self.sem.at[h]).wait()


class Outwards(Planes):
    def copy(self, h):
        return pltpu.make_async_copy(
            self.source.at[h], self.target.at[h + self.start_at], self.sem.at[h]
        )


def sigmoid(value):
    return 0.5 * jnp.tanh(0.5 * value) + 0.5


def rows_summed(value):
    return value.reshape(value.shape[0] // 8, 8, value.shape[1]).sum(0)


def put_permuted(target, row, source, pieces, offset=0):
    for inner, outer, width in pieces:
        target[row : row + 1, inner : inner + width] = source[
            :, offset + outer : offset + outer + width
        ]


def put_original(target, row, value, pieces):
    for inner, outer, width in pieces:
        target[row : row + 1, outer : outer + width] = value[:, inner : inner + width]


def put_stats(stat_ref, acc_ref, count=None):
    peers, rows, width = stat_ref.shape
    for row in range(2):
        line = jnp.sum(acc_ref[row], axis=0, keepdims=True)
        stat_ref[:, row : row + 1, :] = jnp.broadcast_to(line[None], (peers, 1, width))
    if count is not None:
        stat_ref[:, 2:3, :] = jnp.broadcast_to(count.reshape(1, 1, 1), (peers, 1, width))


def plane_stats(value_ref, h, keep, acc_ref):
    for first, last in tiles_of(0, value_ref.shape[2]):
        value = value_ref[h, :, first:last]
        masked = value * keep
        acc_ref[0, :, first:last] += rows_summed(masked)
        acc_ref[1, :, first:last] += rows_summed(masked * value)


def times_of(rows, width, extent):
    return lax.broadcasted_iota(jnp.int32, (rows, width), 0) & (extent - 1)


def time_shifted(value, times, extent):
    rows = value.shape[0]
    earlier = jnp.where(times != 0, pltpu.roll(value, 1, 0), 0.0)
    later = jnp.where(times != extent - 1, pltpu.roll(value, rows - 1, 0), 0.0)
    return earlier, value, later


def width_shifted(value, extent):
    rows = value.shape[0]
    if extent % 8 == 0:
        edge = jnp.zeros((extent, value.shape[1]), value.dtype)
        left = jnp.concatenate([edge, value[:-extent]], 0)
        right = jnp.concatenate([value[extent:], edge], 0)
    else:
        left = pltpu.roll(value, extent, 0)
        right = pltpu.roll(value, rows - extent, 0)
    return left, value, right


def window_sums(source_ref, between_ref, extent, put):
    planes, rows, width = source_ref.shape
    between_ref[0] = jnp.zeros((rows, width), F32)
    between_ref[planes + 1] = jnp.zeros((rows, width), F32)
    times = times_of(rows, width, extent)

    def plane(h, carry):
        before, here, after = time_shifted(source_ref[h], times, extent)
        left, here, right = width_shifted(before + here + after, extent)
        between_ref[h + 1] = left + here + right
        return carry

    lax.fori_loop(0, planes, plane, 0)

    def through(h, carry):
        put(h, (between_ref[h] + between_ref[h + 1] + between_ref[h + 2]) * (1.0 / 27.0))
        return carry

    lax.fori_loop(0, planes, through, 0)


def turned_ordered(turned_ref, ordered_ref):
    for row_to, row_from, height in FIRST_PIECES:
        for inner, outer, width in RESULT_PIECES:
            ordered_ref[row_to : row_to + height, inner : inner + width] = turned_ref[
                row_from : row_from + height, outer : outer + width
            ]


def weight_ordered(weight_ref, ordered_ref):
    for inner, outer, width in FIRST_PIECES:
        ordered_ref[:, inner : inner + width] = weight_ref[:, outer : outer + width]


def step_planes(planes):
    return (planes // 2, 2) if planes % 2 == 0 else (planes, 1)


def put_masks(valid, mask_ref, keep_ref, next_ref, lanes_ref):
    planes, rows, unused = keep_ref.shape
    unused, extent, width = mask_ref.shape
    frame = lax.broadcasted_iota(jnp.int32, (extent, width), 0)
    lanes_ref[...] = jnp.zeros_like(lanes_ref)
    for h in range(planes):
        plane = jnp.where(frame < valid, mask_ref[h], 0).astype(F32)
        lanes_ref[:, 16 * h : 16 * h + width] = plane
    total = lanes_ref.shape[1]

    def chosen(condition):
        return jnp.where(condition, 1.0, 0.0)

    def places(shape, axis):
        return lax.broadcasted_iota(jnp.int32, shape, axis)

    shape = (rows, extent)
    times = chosen(places(shape, 1) == places(shape, 0) & (extent - 1)).astype(BF16)
    picked = jnp.dot(times, lanes_ref[...].astype(BF16), preferred_element_type=F32)
    shape = (rows, total)
    picked = picked * chosen(places(shape, 1) & 15 == places(shape, 0) // extent)
    shape = (total, 128)
    group = chosen(places(shape, 0) // 16 == places(shape, 1)).astype(BF16)
    keeps = jnp.dot(picked.astype(BF16), group, preferred_element_type=F32)
    rows_next = next_ref.shape[1]
    half = extent // 2
    shape = (rows_next, rows)
    cell, row = places(shape, 0), places(shape, 1)
    same_time = (row & (extent - 1)) // 2 == (cell & (half - 1))
    same_column = row // (2 * extent) == cell // half
    pooled = chosen(same_time & same_column).astype(BF16)
    held = jnp.dot(pooled, keeps.astype(BF16), preferred_element_type=F32)
    for h in range(planes):
        keep_ref[h] = keeps[:, h : h + 1]
    for h in range(next_ref.shape[0]):
        both = held[:, 2 * h : 2 * h + 1] + held[:, 2 * h + 1 : 2 * h + 2]
        next_ref[h] = jnp.where(both > 0.5, 1.0, 0.0)


def project_body(
    order_ref,
    section_ref,
    frames_ref,
    x_hbm,
    mask_hbm,
    weight_hbm,
    z_hbm,
    z_v,
    stat_ref,
    keep_ref,
    next_ref,
    x_v,
    mask_v,
    mask_lanes,
    weight_v,
    ordered,
    pool,
    between,
    acc,
    x_sem,
    z_sem,
    weight_sem,
):
    planes, rows, channels = x_v.shape
    extent = 8
    clip = order_ref[section_ref[0]]
    arriving = Planes(x_hbm.at[clip], x_v, x_sem)
    leaving = Outwards(z_v, z_hbm, z_sem)
    weight_in = pltpu.make_async_copy(weight_hbm, weight_v, weight_sem.at[0])
    mask_in = pltpu.make_async_copy(mask_hbm.at[clip], mask_v, weight_sem.at[1])
    mask_in.start()
    weight_in.start()
    arriving.start_all()
    mask_in.wait()
    put_masks(frames_ref[clip], mask_v, keep_ref, next_ref, mask_lanes)
    weight_in.wait()
    weight_ordered(weight_v, ordered)
    together, steps = step_planes(planes)

    def product(i, carry):
        def masked(k, carry):
            h = i * together + k
            arriving.wait(h)
            x_v[h] = x_v[h] * keep_ref[h].astype(BF16)
            return carry

        lax.fori_loop(0, together, masked, 0)
        at = pl.ds(i * together, together)
        value = x_v[at].reshape(together * rows, channels)
        out = jnp.dot(value, ordered[...], preferred_element_type=F32)
        z_v[at] = out.reshape(together, rows, NB1)
        pool[at] = out[:, B0:ND].reshape(together, rows, B3)
        return carry

    lax.fori_loop(0, steps, product, 0)
    acc[...] = jnp.zeros_like(acc)

    def put(h, value):
        z_v[h, :, B0:ND] = value
        leaving.start(h)
        plane_stats(z_v, h, keep_ref[h], acc)

    window_sums(pool, between, extent, put)
    put_stats(stat_ref, acc, jnp.sum(keep_ref[...]))
    leaving.wait_all()


def project_first(clips, order, section, frames, voxel_mask, weight, peers):
    unused, planes, rows, channels = clips.shape
    unused, unused, extent, width = voxel_mask.shape
    return call(
        project_body,
        [
            shape_of(planes, rows, NB1),
            shape_of(planes, rows, NB1),
            shape_of(peers, 3, NB1),
            shape_of(planes, rows, 1),
            shape_of(planes // 2, (width // 2 + 1) * extent // 2, 1),
        ],
        "apvvv",
        [
            pltpu.VMEM((planes, rows, channels), BF16),
            pltpu.VMEM(voxel_mask.shape[1:], jnp.int32),
            pltpu.VMEM((extent, -(-planes // 8) * 128), F32),
            pltpu.VMEM((channels, NB1), BF16),
            pltpu.VMEM((channels, NB1), BF16),
            pltpu.VMEM((planes, rows, B3), F32),
            pltpu.VMEM((planes + 2, rows, B3), F32),
            pltpu.VMEM((2, 8, NB1), F32),
            DMA((planes,)),
            DMA((planes,)),
            DMA((2,)),
        ],
        (clips, voxel_mask, weight),
        "aaa",
        "project_first",
        (order, section, frames),
        flops=2 * planes * rows * channels * NB1,
        mib=16,
    )


def level_rows(vec, gain_ref, bias_ref, mom_ref, pieces, offset):
    put_permuted(vec, 4, gain_ref, pieces, offset)
    put_permuted(vec, 5, bias_ref, pieces, offset)
    mean, var = mom_ref[0:1, :], mom_ref[1:2, :]
    inverse = lax.rsqrt(var + EPSILON)
    scale = vec[4:5, :] * inverse
    vec[0:1, :] = scale
    vec[1:2, :] = vec[5:6, :] - mean * scale
    vec[2:3, :] = inverse
    vec[3:4, :] = -mean * inverse


def first_rows(vec, gain_ref, bias_ref, mom_ref):
    level_rows(vec, gain_ref, bias_ref, mom_ref, FIRST_PIECES, 0)


def second_rows(vec, gain_ref, bias_ref, mom_ref):
    level_rows(vec, gain_ref, bias_ref, mom_ref, SECOND_PIECES, NB1)


def back_rows(vec, total, count):
    cross = vec[0:1, :] * total[1:2] / count
    vec[6:7, :] = -(vec[0:1, :] * total[0:1] / count) - cross * vec[3:4, :]
    vec[7:8, :] = -cross * vec[2:3, :]


def put_moments(tot_ref, mom_ref, count):
    total = jnp.sum(tot_ref[...], axis=0)
    if count is None:
        count = total[2:3, :]
        mom_ref[2:3, :] = count
    mean = total[0:1, :] / count
    mom_ref[0:1, :] = mean
    mom_ref[1:2, :] = total[1:2, :] / count - mean * mean


def spread_plane(value, first, times, extent, targets, index):
    width = value.shape[1]
    for early, shifted in enumerate(time_shifted(value, times[:, 0:width], extent)):
        for side, moved in enumerate(width_shifted(shifted, extent)):
            place = early * 3 + side
            moved = moved.astype(BF16)
            for target, low, high in targets:
                begin, end = max(low, first), min(high, first + width)
                if begin < end:
                    start = place * (high - low) + begin - low
                    target[index, :, start : start + end - begin] = moved[
                        :, begin - first : end - first
                    ]


def clear_ends(targets, ends):
    for target, unused, unused in targets:
        for end in ends:
            target[end] = jnp.zeros(target.shape[1:], BF16)


def weight_copies(source, target, sems):
    return [
        pltpu.make_async_copy(
            source.at[pl.ds(time * 9 + height * 3, 3)],
            target.at[height, pl.ds(time * 3, 3)],
            sems.at[height * 3 + time],
        )
        for height in range(3)
        for time in range(3)
    ]


def second_body(
    extent,
    tot_ref,
    z_v,
    keep_ref,
    gain_ref,
    bias_ref,
    wide_hbm,
    narrow_hbm,
    act_v,
    mid_hbm,
    out_hbm,
    out_v,
    stat_ref,
    mom_ref,
    vec,
    mid_v,
    wide_v,
    narrow_v,
    im_wide,
    im_narrow,
    acc,
    wide_sem,
    narrow_sem,
    mid_sem,
    out_sem,
):
    planes, rows, unused = z_v.shape
    weights = weight_copies(wide_hbm, wide_v, wide_sem) + weight_copies(
        narrow_hbm, narrow_v, narrow_sem
    )
    for copy in weights:
        copy.start()
    mid_out = Outwards(mid_v, mid_hbm, mid_sem)
    out_out = Outwards(out_v, out_hbm, out_sem)
    put_moments(tot_ref, mom_ref, None)
    first_rows(vec, gain_ref, bias_ref, mom_ref)
    targets = ((im_wide, 0, B1A), (im_narrow, B1A, NM))
    clear_ends(targets, (0, planes + 1))
    times = times_of(rows, 128, extent)

    def activate(h, carry):
        keep = keep_ref[h]
        for first, last in tiles_of(0, NB1):
            shifted = z_v[h, :, first:last] * vec[0:1, first:last] + vec[1:2, first:last]
            value = shifted * sigmoid(shifted) * keep
            if first < ND:
                act_v[h, :, first:last] = value.astype(BF16)
            else:
                mid_v[h, :, first - ND : last - ND] = value.astype(BF16)
                spread_plane(value, first - ND, times, extent, targets, h + 1)
        mid_out.start(h)
        return carry

    lax.fori_loop(0, planes, activate, 0)
    for copy in weights:
        copy.wait()
    acc[...] = jnp.zeros_like(acc)
    together, steps = step_planes(planes)

    def convolve(i, carry):
        at = pl.ds(i * together, together)
        for im_ref, weight_ref, first, last in (
            (im_narrow, narrow_v, 0, B2),
            (im_wide, wide_v, B2, NB2),
        ):
            total = None
            for high in range(3):
                value = im_ref[pl.ds(i * together + high, together)]
                value = value.reshape(together * rows, value.shape[2])
                weight = weight_ref[high].reshape(value.shape[1], last - first)
                part = jnp.dot(value, weight, preferred_element_type=F32)
                total = part if total is None else total + part
            out_v[at, :, first:last] = total.reshape(together, rows, last - first)

        def finish(k, carry):
            h = i * together + k
            out_out.start(h)
            plane_stats(out_v, h, keep_ref[h], acc)
            return carry

        lax.fori_loop(0, together, finish, 0)
        return carry

    lax.fori_loop(0, steps, convolve, 0)
    put_stats(stat_ref, acc)
    mid_out.wait_all()
    out_out.wait_all()


def second_level(totals, first_out, keep, params, extent, peers):
    unused, conv_mid, conv_small, gain, bias = params
    planes, rows, unused = first_out.shape
    return call(
        functools.partial(second_body, extent),
        [
            shape_of(planes, rows, ND, dtype=BF16),
            shape_of(planes, rows, NM, dtype=BF16),
            shape_of(planes, rows, NB2),
            shape_of(planes, rows, NB2),
            shape_of(peers, 2, NB2),
            shape_of(3, NB1),
        ],
        "paapvv",
        [
            pltpu.VMEM((8, NB1), F32),
            pltpu.VMEM((planes, rows, NM), BF16),
            pltpu.VMEM((3, 9, B1A, B1), BF16),
            pltpu.VMEM((3, 9, B2A, B2), BF16),
            pltpu.VMEM((planes + 2, rows, 9 * B1A), BF16),
            pltpu.VMEM((planes + 2, rows, 9 * B2A), BF16),
            pltpu.VMEM((2, 8, NB2), F32),
            DMA((9,)),
            DMA((9,)),
            DMA((planes,)),
            DMA((planes,)),
        ],
        (totals, first_out, keep, gain, bias, conv_mid, conv_small),
        "vpvvvaa",
        "second_level",
        flops=2 * planes * rows * 27 * (B1A * B1 + B2A * B2),
        mib=30,
    )


def cell_of(shape, axis, rows):
    row = lax.broadcasted_iota(jnp.int32, shape, axis)
    row = jnp.where(row >= rows, row - rows, row)
    return (row // 16) * 4 + (row % 8) // 2


def between_body(
    tot_ref,
    z_v,
    keep_ref,
    gain_ref,
    bias_ref,
    act_v,
    first_mom_ref,
    keep_next_ref,
    weight_ref,
    x_hbm,
    z_next_hbm,
    z_next_ref,
    stat_ref,
    mom_ref,
    vec,
    x_ref,
    both,
    ordered,
    pool,
    between,
    acc,
    x_sem,
    z_next_sem,
):
    planes, rows, channels = x_ref.shape
    x_out = Outwards(x_ref, x_hbm, x_sem)
    z_next_out = Outwards(z_next_ref, z_next_hbm, z_next_sem)
    put_moments(tot_ref, mom_ref, first_mom_ref[2:3, 0:NB2])
    second_rows(vec, gain_ref, bias_ref, mom_ref)
    turned_ordered(weight_ref, ordered)
    extent = 4
    source_rows = z_v.shape[1]
    shape = (rows, 2 * source_rows)
    cells = cell_of(shape, 1, source_rows) == lax.broadcasted_iota(jnp.int32, shape, 0)
    pooled = jnp.where(cells, 1.0, 0.0).astype(BF16)

    def pooling(h, carry):
        keeps = [keep_ref[2 * h], keep_ref[2 * h + 1]]
        keep_next = keep_next_ref[h]
        for first, last in tiles_of(0, C5):
            for step in range(2):
                if first < ND:
                    part = act_v[2 * h + step, :, first:last]
                else:
                    at = slice(first - ND, last - ND)
                    shifted = z_v[2 * h + step, :, at] * vec[0:1, at] + vec[1:2, at]
                    part = (shifted * sigmoid(shifted) * keeps[step]).astype(BF16)
                both[step * source_rows : (step + 1) * source_rows, first:last] = part
        mean = jnp.dot(pooled, both[...], preferred_element_type=F32) * 0.125
        x_ref[h] = (mean.astype(BF16).astype(F32) * keep_next).astype(BF16)
        x_out.start(h)
        return carry

    lax.fori_loop(0, planes, pooling, 0)
    value = x_ref[...].reshape(planes * rows, channels)
    out = lax.dot_general(
        value, ordered[...], (((1,), (1,)), ((), ())), preferred_element_type=F32
    )
    z_next_ref[...] = out.reshape(planes, rows, NB1)
    pool[...] = out[:, B0:ND].reshape(planes, rows, B3)
    acc[...] = jnp.zeros_like(acc)

    def put(h, value):
        z_next_ref[h, :, B0:ND] = value
        z_next_out.start(h)
        plane_stats(z_next_ref, h, keep_next_ref[h], acc)

    window_sums(pool, between, extent, put)
    put_stats(stat_ref, acc, jnp.sum(keep_next_ref[...]))
    x_out.wait_all()
    z_next_out.wait_all()


def between_blocks(totals, second_out, keep, params, act, first_mom, keep_next, weight, peers):
    planes, rows = keep_next.shape[:2]
    above, source_rows = second_out.shape[:2]
    return call(
        between_body,
        [
            shape_of(planes, rows, C5, dtype=BF16),
            shape_of(planes, rows, NB1),
            shape_of(planes, rows, NB1),
            shape_of(peers, 3, NB1),
            shape_of(2, NB2),
        ],
        "aapvv",
        [
            pltpu.VMEM((8, NB2), F32),
            pltpu.VMEM((planes, rows, C5), BF16),
            pltpu.VMEM((2 * source_rows, C5), BF16),
            pltpu.VMEM((NB1, C5), BF16),
            pltpu.VMEM((planes, rows, B3), F32),
            pltpu.VMEM((planes + 2, rows, B3), F32),
            pltpu.VMEM((2, 8, NB1), F32),
            DMA((planes,)),
            DMA((planes,)),
        ],
        (totals, second_out, keep, params[3], params[4], act, first_mom, keep_next, weight),
        "vpvvvpvvv",
        "between_blocks",
        flops=2 * planes * rows * C5 * NB1,
        mib=16,
    )


def turn_body(
    clip_ref,
    section_ref,
    tot_ref,
    z_v,
    keep_ref,
    gain_ref,
    bias_ref,
    act_v,
    first_mom_ref,
    grad_hbm,
    kept_ref,
    sent_ref,
    slope_hbm,
    direct_v,
    stat_ref,
    mom_ref,
    vec,
    slope_v,
    grad_v,
    grad,
    result,
    acc,
    grad_sem,
    slope_sem,
):
    planes, rows, unused = z_v.shape
    unused, width, extent, unused = grad_v.shape
    half = extent // 2
    later = section_ref[0] == 1
    grad_in = Planes(grad_hbm.at[clip_ref[0]], grad_v, grad_sem)
    for h in range(planes):
        grad_in.start(h)
    slope_out = Outwards(slope_v, slope_hbm, slope_sem)
    put_moments(tot_ref, mom_ref, first_mom_ref[2:3, 0:NB2])
    second_rows(vec, gain_ref, bias_ref, mom_ref)
    acc[...] = jnp.zeros_like(acc)
    grad[...] = jnp.zeros_like(grad)

    def plane(h, carry):
        keep = keep_ref[h]
        grad_in.wait(h)
        for column in range(width):
            at = slice(column * extent, (column + 1) * extent)
            grad[at, :] = grad_v[h, column].astype(F32)
        direct_v[h, :, 0:B0] = grad[:, 0:B0].astype(BF16)
        direct_v[h, :, B0:ND] = grad[:, C5 - B3 :].astype(BF16)
        result[:, 0:B0] = act_v[h, :, 0:B0].astype(F32)
        result[:, C5 - B3 :] = act_v[h, :, B0:ND].astype(F32)
        for inner, outer, size in SECOND_PIECES:
            at = slice(inner, inner + size)
            place = slice(B0 + outer, B0 + outer + size)
            value = z_v[h, :, at]
            shifted = value * vec[0:1, at] + vec[1:2, at]
            gate = sigmoid(shifted)
            result[:, place] = shifted * gate * keep
            slope = grad[:, place] * keep * gate * (1.0 + shifted * (1.0 - gate))
            slope_v[h, :, at] = slope
            acc[0, :, at] += rows_summed(slope)
            acc[1, :, at] += rows_summed(slope * (value * vec[2:3, at] + vec[3:4, at]))
        slope_out.start(h)
        for column in range(width):
            start = column * extent
            early = result[start : start + half, :]
            late = result[start + half : start + extent, :]
            kept_ref[h, column] = jnp.where(later, late, early).astype(BF16)
            sent_ref[h, column] = jnp.where(later, early, late).astype(BF16)
        return carry

    lax.fori_loop(0, planes, plane, 0)
    put_stats(stat_ref, acc)
    slope_out.wait_all()


def turn(
    totals, second_out, keep, params, act, first_mom, cotangent, own_clip, section, peers
):
    planes, rows, unused = second_out.shape
    unused, unused, width, extent, unused = cotangent.shape
    half = (planes, width, extent // 2, C5)
    return call(
        turn_body,
        [
            shape_of(*half, dtype=BF16),
            shape_of(*half, dtype=BF16),
            shape_of(planes, rows, NB2),
            shape_of(planes, rows, ND, dtype=BF16),
            shape_of(peers, 2, NB2),
            shape_of(2, NB2),
        ],
        "vvapvv",
        [
            pltpu.VMEM((8, NB2), F32),
            pltpu.VMEM((planes, rows, NB2), F32),
            pltpu.VMEM(cotangent.shape[1:], BF16),
            pltpu.VMEM((rows, C5), F32),
            pltpu.VMEM((rows, C5), F32),
            pltpu.VMEM((2, 8, NB2), F32),
            DMA((planes,)),
            DMA((planes,)),
        ],
        (totals, second_out, keep, params[3], params[4], act, first_mom, cotangent),
        "vpvvvpva",
        "turn",
        (own_clip, section),
        mib=12,
    )


def slope_plane(
    upstream, z_ref, h, vec, keep, slope_ref, slope_at, acc, tiles
):
    for first, last in tiles:
        at = slice(first, last)
        value = z_ref[h, :, at]
        shifted = value * vec[0:1, at] + vec[1:2, at]
        gate = sigmoid(shifted)
        slope = upstream(first, last) * keep * gate * (1.0 + shifted * (1.0 - gate))
        slope_ref[slope_at, :, at] = slope
        acc[0, :, at] += rows_summed(slope)
        acc[1, :, at] += rows_summed(slope * (value * vec[2:3, at] + vec[3:4, at]))


def put_halves(section, packed, kept_hbm, sent_hbm, sems):
    half = packed.shape[0] // 2
    copies = [
        pltpu.make_async_copy(
            packed.at[pl.ds(pl.multiple_of(which * half, 16), half)],
            target.at[pl.ds(0, half)],
            sems.at[place],
        )
        for place, (which, target) in enumerate(((section, kept_hbm), (1 - section, sent_hbm)))
    ]
    for copy in copies:
        copy.start()
    return copies


def conv_grad_body(
    extent,
    section_ref,
    tot_ref,
    slope_hbm,
    z_hbm,
    mid_hbm,
    keep_ref,
    gain_ref,
    bias_ref,
    first_mom_ref,
    mom_ref,
    more_kept_hbm,
    more_sent_hbm,
    grad_v,
    kept_hbm,
    sent_hbm,
    norm_ref,
    vec,
    slope_v,
    z_v,
    mid_v,
    im_wide,
    im_narrow,
    turned,
    packed,
    more_v,
    slope_sem,
    z_sem,
    mid_sem,
    half_sem,
):
    planes, rows, unused = z_v.shape
    slope_in = Planes(slope_hbm, slope_v, slope_sem)
    z_in = Planes(z_hbm, z_v, z_sem)
    mid_in = Planes(mid_hbm, mid_v, mid_sem)
    for h in range(planes):
        mid_in.start(h)
        slope_in.start(h)
        z_in.start(h)
    half_rows = packed.shape[0] // 2
    more = kept_hbm.shape[0] - half_rows
    beside = [
        (
            pltpu.make_async_copy(source, more_v.at[place], half_sem.at[2 + place]),
            pltpu.make_async_copy(
                more_v.at[place], target.at[pl.ds(half_rows, more)], half_sem.at[4 + place]
            ),
        )
        for place, (source, target) in enumerate(
            ((more_kept_hbm, kept_hbm), (more_sent_hbm, sent_hbm))
        )
        if more
    ]
    for arriving, leaving in beside:
        arriving.start()
    total = jnp.sum(tot_ref[...], axis=0)
    put_original(norm_ref, 0, total[1:2], SECOND_PIECES)
    put_original(norm_ref, 1, total[0:1], SECOND_PIECES)
    second_rows(vec, gain_ref, bias_ref, mom_ref)
    back_rows(vec, total, first_mom_ref[2:3, 0:NB2])
    targets = ((im_wide, 0, B1A), (im_narrow, B1A, NM))
    clear_ends(targets, (0, planes + 1))
    times = times_of(rows, 128, extent)

    def gradient(h, carry):
        mid_in.wait(h)
        for first, last in tiles_of(0, NM):
            value = mid_v[h, :, first:last].astype(F32)
            spread_plane(value, first, times, extent, targets, h + 1)
        slope_in.wait(h)
        z_in.wait(h)
        keep = keep_ref[h]
        for first, last in tiles_of(0, NB2):
            at = slice(first, last)
            value = slope_v[h, :, at] * vec[0:1, at] + z_v[h, :, at] * vec[7:8, at] + vec[6:7, at]
            grad_v[h, :, at] = (value * keep).astype(BF16)
        return carry

    lax.fori_loop(0, planes, gradient, 0)
    for arriving, leaving in beside:
        arriving.wait()
        leaving.start()
    turned[...] = grad_v[...].reshape(planes * rows, NB2).T
    wide_rows = 27 * B1A
    half = wide_rows // 2
    used = CONV_NARROW + 27 * B2A
    packed[used:, :] = jnp.zeros((packed.shape[0] - used, 128), BF16)
    step = 3 * B1A
    for high in range(3):
        value = im_wide[high : high + planes].reshape(planes * rows, 9 * B1A)
        part = jnp.dot(turned[B2:NB2, :], value, preferred_element_type=F32)
        part = part.T.astype(BF16)
        value = im_narrow[high : high + planes].reshape(planes * rows, 9 * B2A)
        small = jnp.dot(turned[0:B2, :], value, preferred_element_type=F32)
        small = small.T.astype(BF16)
        for time in range(3):
            chunk = time * 3 + high
            row = chunk * step
            piece = part[time * step : (time + 1) * step]
            packed[row : row + step, :] = piece[:, 0:128]
            packed[wide_rows + row : wide_rows + row + step, :] = piece[:, 128:256]
            low = max(0, min(step, half - row))
            tail = 2 * wide_rows + row
            if low > 0:
                packed[tail : tail + low, 0:64] = piece[:low, 256:B1]
            if low < step:
                tail = tail + low - half
                packed[tail : tail + step - low, 64:128] = piece[low:, 256:B1]
            row = CONV_NARROW + chunk * 3 * B2A
            packed[row : row + 3 * B2A, :] = small[time * 3 * B2A : (time + 1) * 3 * B2A]
    copies = put_halves(section_ref[0], packed, kept_hbm, sent_hbm, half_sem)
    for copy in copies + [leaving for arriving, leaving in beside]:
        copy.wait()


def conv_grad(
    totals, slope, second_out, mid, keep, params, first_mom, mom, extent, section, peers, more=None
):
    planes, rows, unused = second_out.shape
    packed = conv_rows(peers)
    half = packed // 2
    if more is None:
        more = (mid, mid)
    else:
        half += more[0].shape[0]
    return call(
        functools.partial(conv_grad_body, extent),
        [
            shape_of(planes, rows, NB2, dtype=BF16),
            shape_of(half, 128, dtype=BF16),
            shape_of(half, 128, dtype=BF16),
            shape_of(2, NB2),
        ],
        "paav",
        [
            pltpu.VMEM((8, NB2), F32),
            pltpu.VMEM((planes, rows, NB2), F32),
            pltpu.VMEM((planes, rows, NB2), F32),
            pltpu.VMEM((planes, rows, NM), BF16),
            pltpu.VMEM((planes + 2, rows, 9 * B1A), BF16),
            pltpu.VMEM((planes + 2, rows, 9 * B2A), BF16),
            pltpu.VMEM((NB2, planes * rows), BF16),
            pltpu.VMEM((packed, 128), BF16),
            pltpu.VMEM((2, max(half - packed // 2, 16), 128), BF16),
            DMA((planes,)),
            DMA((planes,)),
            DMA((planes,)),
            DMA((6,)),
        ],
        (totals, slope, second_out, mid, keep, params[3], params[4], first_mom, mom, *more),
        "vaaavvvvvaa",
        "conv_grad",
        (section,),
        flops=2 * planes * rows * 27 * (B1A * B1 + B2A * B2),
        mib=30,
    )


def prepare_body(wide_ref, narrow_ref, turned_hbm, weights, sems):
    weights[...] = jnp.zeros_like(weights)
    copies = []
    for height in range(3):
        for place in range(9):
            source = 26 - ((place // 3) * 9 + height * 3 + place % 3)
            weights[height, 0:B1A, place * NB2 + B2 : (place + 1) * NB2] = wide_ref[source]
            weights[height, B1A:NM, place * NB2 : place * NB2 + B2] = narrow_ref[source]
        copies.append(
            pltpu.make_async_copy(weights.at[height], turned_hbm.at[height], sems.at[height])
        )
        copies[-1].start()
    for copy in copies:
        copy.wait()


def prepare(conv_mid, conv_small):
    return call(
        prepare_body,
        [shape_of(3, NM, TURNED, dtype=BF16)],
        "a",
        [pltpu.VMEM((3, NM, TURNED), BF16), DMA((3,))],
        (conv_mid, conv_small),
        "vv",
        "prepare",
        mib=24,
    )[0]


def back_conv_body(
    extent,
    halved,
    start,
    grad_ref,
    z_hbm,
    keep_ref,
    gain_ref,
    bias_ref,
    first_mom_ref,
    direct_v,
    turned_hbm,
    before_ref,
    slope_v,
    stat_ref,
    acc,
    vec,
    z_v,
    windows,
    weights,
    z_sem,
    weight_sem,
):
    planes = grad_ref.shape[0]
    count, rows, unused = z_v.shape
    low = 1 if start == 0 else 0
    high = count + 1 if start + count == planes else count + 2
    weights_in = Planes(turned_hbm, weights, weight_sem)
    weights_in.start_all()
    z_in = Planes(z_hbm, z_v, z_sem, start)
    z_in.start_all()
    first_rows(vec, gain_ref, bias_ref, first_mom_ref)
    targets = ((windows, 0, NB2),)
    clear_ends(targets, [0] * low + [count + 1] * (count + 2 - high))
    times = times_of(rows, 128, extent)

    def shift(j, carry):
        for first, last in tiles_of(0, NB2):
            value = grad_ref[start - 1 + j, :, first:last].astype(F32)
            spread_plane(value, first, times, extent, targets, j)
        return carry

    lax.fori_loop(low, high, shift, 0)
    weights_in.wait_all()
    total = None
    for height in range(3):
        value = windows[height : height + count].reshape(count * rows, 9 * NB2)
        part = lax.dot_general(
            value,
            weights[height, :, 0 : 9 * NB2],
            (((1,), (1,)), ((), ())),
            preferred_element_type=F32,
        )
        total = part if total is None else total + part
    slope_v[:, :, ND:NB1] = total.reshape(count, rows, NM)
    acc[...] = before_ref[...]

    def slopes(h, carry):
        z_in.wait(h)

        def upstream(first, last):
            if first >= ND:
                return slope_v[h, :, first:last]
            if halved:
                return direct_v[(start + h) // 2, :, first:last].astype(F32) * 0.125
            return direct_v[start + h, :, first:last].astype(F32)

        slope_plane(upstream, z_v, h, vec, keep_ref[start + h], slope_v, h, acc, tiles_of(0, NB1))
        return carry

    lax.fori_loop(0, count, slopes, 0)
    put_stats(stat_ref, acc)


def back_conv(
    grad, first_out, keep, params, turned, first_mom, direct, halved, extent, peers, part, before
):
    unused, unused, unused, gain, bias = params
    planes, rows, unused = first_out.shape
    start, count = part
    return call(
        functools.partial(back_conv_body, extent, halved, start),
        [shape_of(count, rows, NB1), shape_of(peers, 2, NB1), shape_of(2, 8, NB1)],
        "pvv",
        [
            pltpu.VMEM((8, NB1), F32),
            pltpu.VMEM((count, rows, NB1), F32),
            pltpu.VMEM((count + 2, rows, 9 * NB2), BF16),
            pltpu.VMEM((3, NM, TURNED), BF16),
            DMA((count,)),
            DMA((3,)),
        ],
        (grad, first_out, keep, gain, bias, first_mom, direct, turned, before),
        "pavvvvpav",
        "back_conv",
        flops=2 * count * rows * 27 * (B1A * B1 + B2A * B2),
        mib=30,
    )


def first_gradient(
    slope_refs, ready, z_ref, keep_ref, vec, grad_ref, pool_ref, between_ref, extent, done
):
    begin = 0
    for slope_ref in slope_refs:

        def gradient(t, carry, begin=begin, slope_ref=slope_ref):
            h = begin + t
            ready(h)
            keep = keep_ref[h]
            for first, last in tiles_of(0, NB1):
                at = slice(first, last)
                value = (
                    slope_ref[t, :, at] * vec[0:1, at] + z_ref[h, :, at] * vec[7:8, at] + vec[6:7, at]
                ) * keep
                if first == B0:
                    pool_ref[h] = value
                else:
                    grad_ref[h, :, at] = value.astype(BF16)
            return carry

        lax.fori_loop(0, slope_ref.shape[0], gradient, 0)
        begin += slope_ref.shape[0]

    def put(h, value):
        grad_ref[h, :, B0:ND] = value.astype(BF16)
        done(h)

    window_sums(pool_ref, between_ref, extent, put)


def put_norms(norm_ref, total, pieces):
    put_original(norm_ref, 0, total[1:2], pieces)
    put_original(norm_ref, 1, total[0:1], pieces)


def last_gradient_body(
    clip_ref,
    section_ref,
    tot_ref,
    slope_0,
    slope_1,
    z_hbm,
    x_hbm,
    keep_ref,
    gain_ref,
    bias_ref,
    mom_ref,
    grad_v,
    kept_hbm,
    sent_hbm,
    norm_ref,
    vec,
    z_v,
    x_v,
    pool,
    between,
    product,
    ordered,
    packed,
    z_sem,
    x_sem,
    half_sem,
):
    planes, rows, channels = x_v.shape
    z_in = Planes(z_hbm, z_v, z_sem)
    x_in = Planes(x_hbm.at[clip_ref[0]], x_v, x_sem)
    for h in range(planes):
        z_in.start(h)
    x_in.start_all()
    first_rows(vec, gain_ref, bias_ref, mom_ref)
    total = jnp.sum(tot_ref[...], axis=0)
    put_norms(norm_ref, total, FIRST_PIECES)
    back_rows(vec, total, mom_ref[2:3, :])

    def done(h):
        x_in.wait(h)
        x_v[h] = x_v[h] * keep_ref[h].astype(BF16)

    first_gradient(
        (slope_0, slope_1), z_in.wait, z_v, keep_ref, vec, grad_v, pool, between, 8, done
    )
    product[...] = lax.dot_general(
        x_v[...].reshape(planes * rows, channels),
        grad_v[...].reshape(planes * rows, NB1),
        (((0,), (0,)), ((), ())),
        preferred_element_type=F32,
    )
    for inner, outer, width in FIRST_PIECES:
        ordered[:, outer : outer + width] = product[:, inner : inner + width]
    pack_inproj(ordered, packed)
    copies = put_halves(section_ref[0], packed, kept_hbm, sent_hbm, half_sem)
    for copy in copies:
        copy.wait()


def last_gradient(totals, slopes, first_out, clips, keep, params, mom, own_clip, section, peers):
    planes, rows, unused = first_out.shape
    channels = clips.shape[3]
    packed = padded_rows(inproj_rows(channels)[1], peers)
    return call(
        last_gradient_body,
        [
            shape_of(planes, rows, NB1, dtype=BF16),
            shape_of(packed // 2, 128),
            shape_of(packed // 2, 128),
            shape_of(2, NB1),
        ],
        "paav",
        [
            pltpu.VMEM((8, NB1), F32),
            pltpu.VMEM((planes, rows, NB1), F32),
            pltpu.VMEM((planes, rows, channels), BF16),
            pltpu.VMEM((planes, rows, B3), F32),
            pltpu.VMEM((planes + 2, rows, B3), F32),
            pltpu.VMEM((channels, NB1), F32),
            pltpu.VMEM((channels, NB1), F32),
            pltpu.VMEM((packed, 128), F32),
            DMA((planes,)),
            DMA((planes,)),
            DMA((2,)),
        ],
        (totals, *slopes, first_out, clips, keep, params[3], params[4], mom),
        "vppaavvvv",
        "last_gradient",
        (own_clip, section),
        flops=2 * planes * rows * channels * NB1,
        mib=28,
    )


def clip_gradient_body(
    section_ref,
    grad_v,
    keep_ref,
    weight_ref,
    kept_hbm,
    sent_hbm,
    du_v,
    kept_v,
    sent_v,
    ordered,
    kept_sem,
    sent_sem,
):
    planes, rows, channels = du_v.shape
    unused, width, half, unused = kept_v.shape
    later = section_ref[0] == 1
    kept_out = Outwards(kept_v, kept_hbm, kept_sem)
    sent_out = Outwards(sent_v, sent_hbm, sent_sem)
    weight_ordered(weight_ref, ordered)
    together, steps = step_planes(planes)

    def product(i, carry):
        at = pl.ds(i * together, together)
        value = grad_v[at].reshape(together * rows, NB1)
        out = lax.dot_general(
            value, ordered[...], (((1,), (1,)), ((), ())), preferred_element_type=F32
        )
        du_v[at] = out.reshape(together, rows, channels) * keep_ref[at]

        def sent(k, carry):
            h = i * together + k
            for column in range(width):
                start = 2 * half * column
                early = du_v[h, start : start + half, :]
                late = du_v[h, start + half : start + 2 * half, :]
                kept_v[h, column] = jnp.where(later, late, early).astype(BF16)
                sent_v[h, column] = jnp.where(later, early, late).astype(BF16)
            kept_out.start(h)
            sent_out.start(h)
            return carry

        lax.fori_loop(0, together, sent, 0)
        return carry

    lax.fori_loop(0, steps, product, 0)
    kept_out.wait_all()
    sent_out.wait_all()


def clip_gradient(grad, keep, inproj, width, section):
    planes, rows, unused = grad.shape
    channels = inproj.shape[0]
    half = (planes, width, rows // width // 2, channels)
    return call(
        clip_gradient_body,
        [shape_of(*half, dtype=BF16)] * 2,
        "aa",
        [
            pltpu.VMEM((planes, rows, channels), F32),
            pltpu.VMEM(half, BF16),
            pltpu.VMEM(half, BF16),
            pltpu.VMEM((channels, NB1), BF16),
            DMA((planes,)),
            DMA((planes,)),
        ],
        (grad, keep, inproj),
        "pvv",
        "clip_gradient",
        (section,),
        flops=2 * planes * rows * channels * NB1,
        mib=24,
    )


def both_clips_body(own_ref, kept_ref, got_ref, out_ref):
    own = own_ref[0]
    out_ref[own] = kept_ref[...]
    out_ref[1 - own] = got_ref[...]


def both_clips(kept, got, own_clip):
    return call(
        both_clips_body,
        [shape_of(2, *kept.shape, dtype=BF16)],
        "v",
        [],
        (kept, got),
        "vv",
        "both_clips",
        (own_clip,),
        mib=24,
    )[0]


def back_between_body(
    tot_ref,
    own_slope_hbm,
    own_z_hbm,
    keep_ref,
    gain_ref,
    bias_ref,
    mom_ref,
    weight_ref,
    z_hbm,
    keep_prev,
    gain_prev,
    bias_prev,
    mom_prev,
    up_v,
    grad_ref,
    slope_hbm,
    stat_ref,
    norm_ref,
    vec,
    vec_prev,
    slope_ref,
    z_ref,
    ordered,
    pool,
    between,
    z_v,
    slope_v,
    acc,
    z_sem,
    slope_sem,
    own_sem,
):
    planes, rows, unused = z_ref.shape
    extent = 4
    own = [
        pltpu.make_async_copy(own_slope_hbm, slope_ref, own_sem.at[0]),
        pltpu.make_async_copy(own_z_hbm, z_ref, own_sem.at[1]),
    ]
    for copy in own:
        copy.start()
    z_in = Planes(z_hbm, z_v, z_sem)
    slope_out = Outwards(slope_v, slope_hbm, slope_sem)
    first_rows(vec, gain_ref, bias_ref, mom_ref)
    second_rows(vec_prev, gain_prev, bias_prev, mom_prev)
    total = jnp.sum(tot_ref[...], axis=0)
    put_norms(norm_ref, total, FIRST_PIECES)
    back_rows(vec, total, mom_ref[2:3, :])
    turned_ordered(weight_ref, ordered)
    for copy in own:
        copy.wait()
    z_in.start_all()
    first_gradient(
        (slope_ref,),
        lambda h: None,
        z_ref,
        keep_ref,
        vec,
        grad_ref,
        pool,
        between,
        extent,
        lambda h: None,
    )
    value = grad_ref[...].reshape(planes * rows, NB1)
    out = lax.dot_general(
        value, ordered[...], (((1,), (0,)), ((), ())), preferred_element_type=F32
    )
    rows_prev = z_v.shape[1]
    cells = cell_of((rows_prev, rows), 0, rows_prev) == lax.broadcasted_iota(jnp.int32, (rows_prev, rows), 1)
    doubled = jnp.where(cells, 1.0, 0.0).astype(BF16)
    for h in range(planes):
        single = (out[h * rows : (h + 1) * rows] * keep_ref[h]).astype(BF16)
        up_v[h] = jnp.dot(doubled, single, preferred_element_type=F32).astype(BF16)
    acc[...] = jnp.zeros_like(acc)

    def slopes(h, carry):
        z_in.wait(h)

        def upstream(first, last):
            return up_v[h // 2, :, ND + first : ND + last].astype(F32) * 0.125

        slope_plane(upstream, z_v, h, vec_prev, keep_prev[h], slope_v, h, acc, tiles_of(0, NB2))
        slope_out.start(h)
        return carry

    lax.fori_loop(0, 2 * planes, slopes, 0)
    put_stats(stat_ref, acc)
    slope_out.wait_all()


def back_between(
    totals, slope, first_out, keep, params, mom, second_prev, keep_prev, params_prev, mom_prev, peers
):
    inproj, unused, unused, gain, bias = params
    planes, rows, unused = first_out.shape
    above, rows_prev, unused = second_prev.shape
    return call(
        back_between_body,
        [
            shape_of(planes, rows_prev, C5, dtype=BF16),
            shape_of(planes, rows, NB1, dtype=BF16),
            shape_of(*second_prev.shape),
            shape_of(peers, 2, NB2),
            shape_of(2, NB1),
        ],
        "pvavv",
        [
            pltpu.VMEM((8, NB1), F32),
            pltpu.VMEM((8, NB2), F32),
            pltpu.VMEM((planes, rows, NB1), F32),
            pltpu.VMEM((planes, rows, NB1), F32),
            pltpu.VMEM((NB1, C5), BF16),
            pltpu.VMEM((planes, rows, B3), F32),
            pltpu.VMEM((planes + 2, rows, B3), F32),
            pltpu.VMEM(second_prev.shape, F32),
            pltpu.VMEM(second_prev.shape, F32),
            pltpu.VMEM((2, 8, NB2), F32),
            DMA((above,)),
            DMA((above,)),
            DMA((2,)),
        ],
        (
            totals,
            slope,
            first_out,
            keep,
            gain,
            bias,
            mom,
            inproj,
            second_prev,
            keep_prev,
            params_prev[3],
            params_prev[4],
            mom_prev,
        ),
        "vaavvvvvavvvv",
        "back_between",
        flops=2 * planes * rows * C5 * NB1,
        mib=20,
    )


def inproj_rows(channels):
    first = -(-channels // 32) * 16
    return first, 4 * channels + first


def pack_inproj(ordered, packed):
    channels = ordered.shape[0]
    first, used = inproj_rows(channels)
    padded = packed.shape[0]
    for place in range(4):
        packed[place * channels : (place + 1) * channels, :] = ordered[
            :, place * 128 : (place + 1) * 128
        ]
    start = 4 * channels
    packed[start : start + first, 0:64] = ordered[0:first, 512:NB1]
    packed[start : start + channels - first, 64:128] = ordered[first:channels, 512:NB1]
    if 2 * first > channels:
        packed[start + channels - first : start + first, 64:128] = jnp.zeros(
            (2 * first - channels, 64), packed.dtype
        )
    if padded > used:
        packed[used:padded, :] = jnp.zeros((padded - used, 128), packed.dtype)


def inproj_grad_body(
    section_ref, x_ref, grad_ref, kept_hbm, sent_hbm, product, ordered, packed, half_sem
):
    planes, rows, channels = x_ref.shape
    product[...] = lax.dot_general(
        x_ref[...].reshape(planes * rows, channels),
        grad_ref[...].reshape(planes * rows, NB1),
        (((0,), (0,)), ((), ())),
        preferred_element_type=F32,
    ).astype(BF16)
    for row_to, row_from, height in RESULT_PIECES:
        for inner, outer, width in FIRST_PIECES:
            ordered[row_from : row_from + height, outer : outer + width] = product[
                row_to : row_to + height, inner : inner + width
            ]
    pack_inproj(ordered, packed)
    for copy in put_halves(section_ref[0], packed, kept_hbm, sent_hbm, half_sem):
        copy.wait()


def inproj_grad(x, grad, section, peers):
    planes, rows, channels = x.shape
    packed = padded_rows(inproj_rows(channels)[1], peers)
    return call(
        inproj_grad_body,
        [shape_of(packed // 2, 128, dtype=BF16)] * 2,
        "aa",
        [
            pltpu.VMEM((channels, NB1), BF16),
            pltpu.VMEM((channels, NB1), BF16),
            pltpu.VMEM((packed, 128), BF16),
            DMA((2,)),
        ],
        (x, grad),
        "vv",
        "inproj_grad",
        (section,),
        flops=2 * planes * rows * channels * NB1,
        mib=12,
    )


def unpack_conv(packed_ref, wide_ref, narrow_ref):
    step = 27 * B1A
    half = step // 2
    wide_ref[:, 0:128] = packed_ref[0:step, :].astype(F32)
    wide_ref[:, 128:256] = packed_ref[step : 2 * step, :].astype(F32)
    wide_ref[0:half, 256:B1] = packed_ref[2 * step : 2 * step + half, 0:64].astype(F32)
    wide_ref[half:step, 256:B1] = packed_ref[2 * step : 2 * step + half, 64:128].astype(F32)
    narrow_ref[...] = packed_ref[CONV_NARROW : CONV_NARROW + 27 * B2A, :].astype(F32)


def unpack_inproj(packed_ref, out_ref):
    channels = out_ref.shape[0]
    first = inproj_rows(channels)[0]
    for place in range(4):
        out_ref[:, place * 128 : (place + 1) * 128] = packed_ref[
            place * channels : (place + 1) * channels, :
        ].astype(F32)
    start = 4 * channels
    out_ref[0:first, 512:NB1] = packed_ref[start : start + first, 0:64].astype(F32)
    out_ref[first:channels, 512:NB1] = packed_ref[start : start + channels - first, 64:128].astype(
        F32
    )


def unpack_alone_body(section_ref, value_ref, got_ref, wide_ref, narrow_ref, packed_ref):
    half = value_ref.shape[0]
    section = section_ref[0]
    packed_ref[pl.ds(pl.multiple_of(section * half, 16), half), :] = value_ref[...]
    packed_ref[pl.ds(pl.multiple_of((1 - section) * half, 16), half), :] = got_ref[...]
    unpack_conv(packed_ref, wide_ref, narrow_ref)


def unpack_alone(value, got, section):
    return call(
        unpack_alone_body,
        [shape_of(27 * B1A, B1), shape_of(27 * B2A, B2)],
        "vv",
        [pltpu.VMEM((2 * value.shape[0], 128), BF16)],
        (value, got),
        "vv",
        "unpack_alone",
        (section,),
        mib=24,
    )


def share_places(peers):
    pairs = distance_pairs(peers)
    places = []
    for section in range(2):
        order = [pair[section] for pair in pairs]
        places.append(
            [
                sum(
                    ((place // distance) % 2) << (len(order) - 1 - level)
                    for level, distance in enumerate(order)
                )
                for place in range(peers)
            ]
        )
    return places


def quarters_placed(half, upper, sources, conv_packed, next_packed):
    quarter = sources[0].shape[0]
    conv, rest = conv_packed.shape[0] // 2, next_packed.shape[0] // 2
    for place in range(2):
        first, last = place * quarter, (place + 1) * quarter
        split = min(max(conv - first, 0), quarter)
        for which, source in enumerate(sources):

            @pl.when(upper == (place ^ which))
            def put(source=source, first=first, split=split):
                if split > 0:
                    at = pl.multiple_of(half * conv + first, 16)
                    conv_packed[pl.ds(at, split), :] = source[0:split, :]
                if split < quarter:
                    at = pl.multiple_of(half * rest + first + split - conv, 16)
                    next_packed[pl.ds(at, quarter - split), :] = source[split:quarter, :]


def unpack_joined_body(
    section_ref,
    own_upper_ref,
    other_upper_ref,
    own_ref,
    own_got_ref,
    other_ref,
    other_got_ref,
    shares_ref,
    other_shares_ref,
    wide_hbm,
    narrow_hbm,
    next_hbm,
    inproj_ref,
    wide_ref,
    narrow_ref,
    next_ref,
    conv_packed,
    next_packed,
    next_out,
    inproj_packed,
    sems,
):
    section = section_ref[0]
    quarters_placed(
        section, own_upper_ref[0], (own_ref, own_got_ref), conv_packed, next_packed
    )
    quarters_placed(
        1 - section, other_upper_ref[0], (other_ref, other_got_ref), conv_packed, next_packed
    )
    step = 3 * B1A
    rows, halfway = 9 * step, 9 * step // 2
    copies = []
    for chunk in range(9):
        row = chunk * step
        at = slice(row, row + step)
        wide_ref[at, 0:128] = conv_packed[at, :].astype(F32)
        wide_ref[at, 128:256] = conv_packed[rows + row : rows + row + step, :].astype(F32)
        low = max(0, min(step, halfway - row))
        tail = 2 * rows + row
        if low > 0:
            wide_ref[row : row + low, 256:B1] = conv_packed[tail : tail + low, 0:64].astype(F32)
        if low < step:
            tail += low - halfway
            wide_ref[row + low : row + step, 256:B1] = conv_packed[
                tail : tail + step - low, 64:128
            ].astype(F32)
        copies.append(
            pltpu.make_async_copy(
                wide_ref.at[pl.ds(row, step)], wide_hbm.at[pl.ds(row, step)], sems.at[chunk]
            )
        )
        copies[-1].start()
    narrow_ref[...] = conv_packed[CONV_NARROW : CONV_NARROW + 27 * B2A, :].astype(F32)
    copies.append(pltpu.make_async_copy(narrow_ref, narrow_hbm, sems.at[9]))
    copies[-1].start()
    unpack_inproj(next_packed, next_out)
    next_ref[...] = next_out[...].T
    copies.append(pltpu.make_async_copy(next_ref, next_hbm, sems.at[10]))
    copies[-1].start()
    peers, share, unused = shares_ref.shape
    places = share_places(peers)
    for half_ref, half in ((shares_ref, section), (other_shares_ref, 1 - section)):
        for place in range(peers):
            at = jnp.where(half == 0, places[0][place], places[1][place]) + half * peers
            inproj_packed[pl.ds(pl.multiple_of(at * share, 16), share), :] = half_ref[place]
    unpack_inproj(inproj_packed, inproj_ref)
    for copy in copies:
        copy.wait()


def unpack_joined(quarters, uppers, shares, section, channels, next_channels):
    peers, share, unused = shares[0].shape
    return call(
        unpack_joined_body,
        [
            shape_of(27 * B1A, B1),
            shape_of(27 * B2A, B2),
            shape_of(NB1, next_channels),
            shape_of(channels, NB1),
        ],
        "aaav",
        [
            pltpu.VMEM((27 * B1A, B1), F32),
            pltpu.VMEM((27 * B2A, B2), F32),
            pltpu.VMEM((NB1, next_channels), F32),
            pltpu.VMEM((conv_rows(peers), 128), BF16),
            pltpu.VMEM((padded_rows(inproj_rows(next_channels)[1], peers), 128), BF16),
            pltpu.VMEM((next_channels, NB1), F32),
            pltpu.VMEM((2 * peers * share, 128), BF16),
            DMA((11,)),
        ],
        (*quarters, *shares),
        "vvvvvv",
        "unpack_joined",
        (section, *uppers),
        mib=32,
    )


def sent_to_all(spread):
    return lax.all_to_all(spread, "dp", 0, 0)


def swapped(value):
    return lax.ppermute(value, "section", [(0, 1), (1, 0)])


def distance_pairs(peers):
    distances = []
    while 2 ** len(distances) < peers:
        distances.append(2 ** len(distances))
    return list(zip(distances, [distances[1], distances[0]] + distances[2:]))


def distances_of():
    return distance_pairs(lax.axis_size("dp"))


def exchanged(value, pair):
    count = lax.axis_size("dp")
    links = [
        (section * count + place, section * count + (place ^ pair[section]))
        for section in range(2)
        for place in range(count)
    ]
    return lax.ppermute(value, ("section", "dp"), links)


def upper_half(pair, other=0):
    place = lax.axis_index("dp")
    distance = jnp.where(lax.axis_index("section") == other, pair[0], pair[1])
    return ((place // distance) % 2).astype(jnp.int32).reshape(1)


def added(kept, got):
    return (kept.astype(F32) + got.astype(F32)).astype(kept.dtype)


def split_sum_body(upper_ref, kept_ref, got_ref, left_ref, sent_ref):
    half = left_ref.shape[0]
    upper = upper_ref[0]
    for target, which in ((left_ref, upper), (sent_ref, 1 - upper)):
        at = pl.ds(pl.multiple_of(which * half, 16), half)
        target[...] = added(kept_ref[at, :], got_ref[at, :])


def split_sum(kept, got, pair):
    half = shape_of(kept.shape[0] // 2, 128, dtype=kept.dtype)
    return call(
        split_sum_body, [half, half], "vv", [], (kept, got), "vv", "split_sum", (upper_half(pair),)
    )


def placed_body(upper_ref, value_ref, got_ref, out_ref):
    half = value_ref.shape[0]
    upper = upper_ref[0]
    out_ref[pl.ds(pl.multiple_of(upper * half, 16), half), :] = value_ref[...]
    out_ref[pl.ds(pl.multiple_of((1 - upper) * half, 16), half), :] = got_ref[...]


def placed(value, got, pair):
    whole = shape_of(value.shape[0] * 2, 128, dtype=value.dtype)
    return call(
        placed_body, [whole], "v", [], (value, got), "vv", "placed", (upper_half(pair),)
    )[0]


def staged_body(source_hbm, target_ref, sem):
    copy = pltpu.make_async_copy(source_hbm, target_ref, sem.at[0])
    copy.start()
    copy.wait()


def staged(value):
    whole = shape_of(*value.shape, dtype=value.dtype)
    return call(staged_body, [whole], "p", [DMA((1,))], (value,), "a", "staged", mib=6)[0]


class Scatter:
    def __init__(self, kept, sent, stage=True):
        self.pairs = distances_of()
        self.place = 0
        self.got = swapped(sent)
        self.kept = staged(kept) if stage else kept

    def step(self):
        pair = self.pairs[self.place]
        self.kept, sent = split_sum(self.kept, self.got, pair)
        self.got = exchanged(sent, pair)
        self.place += 1

    def result(self):
        while self.place < len(self.pairs):
            self.step()
        return added(self.kept, self.got)


class Gather:
    def __init__(self, value):
        self.value = value
        self.pairs = distances_of()[::-1]
        self.place = 0
        self.got = exchanged(value, self.pairs[0])

    def step(self):
        self.value = placed(self.value, self.got, self.pairs[self.place])
        self.place += 1
        if self.place < len(self.pairs):
            self.got = exchanged(self.value, self.pairs[self.place])
        else:
            self.got = swapped(self.value)

    def result(self):
        while self.place < len(self.pairs):
            self.step()
        return self.value, self.got


def lockstep(one, other):
    one.got, other.got = lax.optimization_barrier((one.got, other.got))


def tied(value, *exchanges):
    both = lax.optimization_barrier((value,) + tuple(e.got for e in exchanges))
    for exchange, got in zip(exchanges, both[1:]):
        exchange.got = got
    return both[0]


def small_body(first_a, second_a, first_b, second_b, norm1_a, norm2_a, norm1_b, norm2_b, out_ref):
    for row, first, second in ((0, first_a, second_a), (2, first_b, second_b)):
        for line in range(2):
            for pieces, source, offset in ((FIRST_PIECES, first, 0), (SECOND_PIECES, second, NB1)):
                for inner, outer, width in pieces:
                    start = offset + outer
                    out_ref[row + line : row + line + 1, start : start + width] = source[
                        line : line + 1, inner : inner + width
                    ]
    for row, first, second in ((4, norm1_a, norm2_a), (6, norm1_b, norm2_b)):
        out_ref[row : row + 2, 0:NB1] = first[...]
        out_ref[row : row + 2, NB1:NB] = second[...]


def small_out_body(section_ref, own_ref, other_ref, norm_a, mom_a, norm_b, mom_b):
    section = section_ref[0]
    own, other = own_ref[...], other_ref[...]
    norms = own[4:8] + other[4:8]
    norm_a[...] = norms[0:2]
    norm_b[...] = norms[2:4]
    low = jnp.where(section == 0, own, other)
    high = jnp.where(section == 0, other, own)
    mom_a[0] = low[0:2]
    mom_a[1] = high[0:2]
    mom_b[0] = low[2:4]
    mom_b[1] = high[2:4]


def small_outputs(rows, section):
    own = call(small_body, [shape_of(8, NB)], "v", [], rows, "vvvvvvvv", "small")[0]
    return call(
        small_out_body,
        [shape_of(2, NB), shape_of(2, 2, NB), shape_of(2, NB), shape_of(2, 2, NB)],
        "vvvv",
        [],
        (own, swapped(own)),
        "vv",
        "small_out",
        (section,),
    )


def local(
    clips_in,
    frames,
    voxel_mask,
    micro_order,
    inproj_4f,
    conv_mid_4f,
    conv_small_4f,
    gain_4f,
    bias_4f,
    inproj_5b,
    conv_mid_5b,
    conv_small_5b,
    gain_5b,
    bias_5b,
    cotangent,
):
    section = lax.axis_index("section")
    peers = lax.axis_size("dp")
    own = micro_order[0, section]
    own_clip = own.reshape(1)
    which = section.astype(jnp.int32).reshape(1)
    count, depth, height, width, channels = clips_in.shape
    clips = jnp.transpose(clips_in, (0, 2, 3, 1, 4)).reshape(count, height, width * depth, channels)
    upstream = jnp.transpose(cotangent, (0, 2, 3, 1, 4))

    first = (inproj_4f, conv_mid_4f, conv_small_4f, gain_4f.reshape(1, NB), bias_4f.reshape(1, NB))
    second = (inproj_5b.T, conv_mid_5b, conv_small_5b, gain_5b.reshape(1, NB), bias_5b.reshape(1, NB))
    long, short = depth, depth // 2

    z1_a, z1_here, stat, keep, keep_next = project_first(
        clips,
        micro_order.reshape(-1),
        which,
        frames,
        jnp.transpose(voxel_mask, (0, 2, 1, 3)),
        inproj_4f,
        peers,
    )
    totals = sent_to_all(stat)
    act_a, mid_a, z2_a, z2_here, stat, mom1_a = second_level(
        totals, z1_here, keep, first, long, peers
    )
    totals = sent_to_all(stat)
    x_b, z1_b, z1_here, stat, mom2_a = between_blocks(
        totals, z2_here, keep, first, act_a, mom1_a, keep_next, second[0], peers
    )
    act_b, mid_b, z2_b, z2_here, stat, mom1_b = second_level(
        sent_to_all(stat), z1_here, keep_next, second, short, peers
    )
    totals = sent_to_all(stat)
    kept, sent, slope, direct, stat, mom2_b = turn(
        totals, z2_here, keep_next, second, act_b, mom1_b, upstream, own_clip, which, peers
    )
    totals = sent_to_all(stat)
    result = (kept, swapped(sent))
    turned_b = prepare(conv_mid_5b, conv_small_5b)
    totals, turned_b = lax.optimization_barrier((totals, turned_b))
    dz2_b, kept, sent, norm2_b = conv_grad(
        totals, slope, z2_b, mid_b, keep_next, second, mom1_b, mom2_b, short, which, peers
    )
    sum_b = Scatter(kept, sent, False)
    nothing = jnp.zeros((2, 8, NB1), F32)
    slope, stat, unused = back_conv(
        dz2_b,
        z1_b,
        keep_next,
        second,
        turned_b,
        mom1_b,
        direct,
        False,
        short,
        peers,
        (0, height // 2),
        nothing,
    )
    stat = tied(stat, sum_b)
    sum_b.step()
    totals = sent_to_all(stat)
    block_out = both_clips(*result, own_clip)
    turned_a = prepare(conv_mid_4f, conv_small_4f)
    totals, turned_a = lax.optimization_barrier((totals, turned_a))
    totals, block_out = lax.optimization_barrier((totals, block_out))
    totals = tied(totals, sum_b)
    sum_b.step()
    up, dz1_b, slope, stat, norm1_b = back_between(
        totals, slope, z1_b, keep_next, second, mom1_b, z2_a, keep, first, mom2_a, peers
    )
    stat = tied(stat, sum_b)
    sum_b.step()
    totals = sent_to_all(stat)
    inproj_halves = inproj_grad(x_b, dz1_b, which, peers)
    totals = tied(totals, sum_b)
    sum_b.step()
    dz2_a, kept, sent, norm2_a = conv_grad(
        totals,
        slope,
        z2_a,
        mid_a,
        keep,
        first,
        mom1_a,
        mom2_a,
        long,
        which,
        peers,
        inproj_halves,
    )
    sent = tied(sent, sum_b)
    sum_a = Scatter(kept, sent)
    gather_b = Gather(sum_b.result())
    dz2_a = tied(dz2_a, sum_a)
    sum_a.step()
    half = height // 2
    back = (z1_a, keep, first, turned_a, mom1_a, up, True, long, peers)
    slope_low, unused, part = back_conv(dz2_a, *back, (0, half), nothing)
    part = tied(part, sum_a, gather_b)
    sum_a.step()
    gather_b.step()
    slope_high, stat, unused = back_conv(dz2_a, *back, (half, height - half), part)
    stat = tied(stat, sum_a, gather_b)
    sum_a.step()
    gather_b.step()
    totals = sent_to_all(stat)
    totals = tied(totals, sum_a, gather_b)
    sum_a.step()
    gather_b.step()
    dz1_a, kept, sent, norm1_a = last_gradient(
        totals,
        (slope_low, slope_high),
        z1_a,
        clips,
        keep,
        first,
        mom1_a,
        own_clip,
        which,
        peers,
    )
    sent = tied(sent, sum_a, gather_b)
    gather_a = Gather(sum_a.result())
    sum_i = Scatter(kept, sent)
    gather_b.step()
    dz1_a = tied(dz1_a, sum_i)
    sum_i.step()
    kept, sent = clip_gradient(dz1_a, keep, inproj_4f, width, which)
    sent = tied(sent, sum_i, gather_a)
    sum_i.step()
    gather_a.step()
    lockstep(gather_a, sum_i)
    sum_i.step()
    gather_a.step()
    lockstep(gather_a, sum_i)
    sum_i.step()
    gather_a.step()
    shares = jnp.broadcast_to(sum_i.result().astype(BF16)[None], (peers, *sum_i.kept.shape))
    shares, sent = lax.optimization_barrier((shares, sent))
    whole = sent_to_all(shares)
    own, own_got = gather_a.value, gather_a.got
    other = swapped(own)
    clips_grad = both_clips(kept, swapped(sent), own_clip)
    small = small_outputs(
        (mom1_a, mom2_a, mom1_b, mom2_b, norm1_a, norm2_a, norm1_b, norm2_b), which
    )
    conv_b = unpack_alone(*gather_b.result(), which)
    whole, own_got, other, clips_grad, small, conv_b = lax.optimization_barrier(
        (whole, own_got, other, clips_grad, small, conv_b)
    )
    last_pair = gather_a.pairs[-1]
    wide_a, narrow_a, inproj_b, inproj_a = unpack_joined(
        (own, own_got, other, swapped(own_got)),
        (upper_half(last_pair), upper_half(last_pair, 1)),
        (whole, swapped(whole)),
        which,
        inproj_4f.shape[0],
        inproj_5b.shape[0],
    )
    return (
        jnp.transpose(block_out, (0, 3, 1, 2, 4)),
        jnp.transpose(clips_grad, (0, 3, 1, 2, 4)),
        inproj_a,
        wide_a.reshape(conv_mid_4f.shape),
        narrow_a.reshape(conv_small_4f.shape),
        small[0],
        small[1],
        inproj_b.T,
        conv_b[0].reshape(conv_mid_5b.shape),
        conv_b[1].reshape(conv_small_5b.shape),
        small[2],
        small[3],
    )


def solution(mesh):
    placed = (
        P("dp", None, None, None, None),
        P("dp"),
        P("dp", None, None, None),
        P("dp", None),
        P(),
        P(),
        P(),
        P(),
        P(),
        P(),
        P(),
        P(),
        P(),
        P(),
        P("dp", None, None, None, None),
    )
    return jax.shard_map(
        local,
        mesh=mesh,
        in_specs=placed,
        out_specs=(
            P("dp", "section", None, None, None),
            P("dp", "section", None, None, None),
            P(),
            P(),
            P(),
            P(),
            P(),
            P(),
            P(),
            P(),
            P(),
            P(),
        ),
        check_vma=False,
    )
```

```python
import functools

import jax
import jax.numpy as jnp
from jax import lax
from jax.experimental import pallas as pl
from jax.experimental.pallas import tpu as pltpu
from jax.sharding import PartitionSpec as P

B0 = 256
B1A = 160
B1 = 320
B2A = 32
B2 = 128
B3 = 128
C5 = 832
NX = 448
NB1 = 576
NB = 1024
NB2 = NB - NB1
NM = B1A + B2A
ND = B0 + B3

EPSILON = 0.001
F32 = jnp.float32
BF16 = jnp.bfloat16

FIRST_PIECES = ((0, 0, B0), (B0, NX, B3), (ND, B0, NM))
SECOND_PIECES = ((0, B1, B2), (B2, 0, B1))
RESULT_PIECES = ((0, 0, B0), (B0, C5 - B3, B3), (ND, B0 + B1, B2), (ND + B2, B0, B1))

CONV_NARROW = 10800
TURNED = 4096
DMA = pltpu.SemaphoreType.DMA


def padded_rows(rows, peers):
    whole = 32 * peers
    return -(-rows // whole) * whole


def conv_rows(peers):
    return padded_rows(CONV_NARROW + 27 * B2A, peers)


def shape_of(*dims, dtype=F32):
    return jax.ShapeDtypeStruct(dims, dtype)


def tiles_of(start, stop):
    return [(first, min(first + 128, stop)) for first in range(start, stop, 128)]


PINNED = {"a": pltpu.HBM, "p": pltpu.VMEM}


def call(body, outs, out_spaces, scratch, args, spaces, name, scalars=(), flops=0, mib=12):
    def spec(array, space):
        return pl.BlockSpec(memory_space=pltpu.HBM if space == "a" else pltpu.VMEM)

    assert len(args) == len(spaces) and len(outs) == len(out_spaces)
    return pl.pallas_call(
        body,
        out_shape=[
            PINNED[s](o.shape, o.dtype) if s in PINNED else o for o, s in zip(outs, out_spaces)
        ],
        grid_spec=pltpu.PrefetchScalarGridSpec(
            num_scalar_prefetch=len(scalars),
            grid=(1,),
            in_specs=[spec(a, s) for a, s in zip(args, spaces)],
            out_specs=[spec(o, s) for o, s in zip(outs, out_spaces)],
            scratch_shapes=scratch,
        ),
        compiler_params=pltpu.CompilerParams(vmem_limit_bytes=mib * 2**20),
        cost_estimate=pl.CostEstimate(
            flops=flops,
            transcendentals=0,
            bytes_accessed=sum(a.size * a.dtype.itemsize for a in list(args) + list(outs)),
        ),
        name=name,
    )(
        *scalars,
        *[
            pltpu.with_memory_space_constraint(a, pltpu.HBM) if s == "a" else a
            for a, s in zip(args, spaces)
        ],
    )


class Planes:
    def __init__(self, source, target, sem, start=0):
        self.source, self.target, self.sem, self.start_at = source, target, sem, start

    def copy(self, h):
        return pltpu.make_async_copy(
            self.source.at[h + self.start_at], self.target.at[h], self.sem.at[h]
        )

    def start(self, h):
        self.copy(h).start()

    def wait(self, h):
        self.copy(h).wait()

    def start_all(self):
        for h in range(self.sem.shape[0]):
            self.start(h)

    def wait_all(self):
        for h in range(self.sem.shape[0]):
            self.wait(h)


class Parts:
    def __init__(self, sources, target, sem):
        self.target, self.sem = target, sem
        self.places = [source.at[h] for source in sources for h in range(source.shape[0])]

    def start_all(self):
        for h, source in enumerate(self.places):
            pltpu.make_async_copy(source, self.target.at[h], self.sem.at[h]).start()

    def wait(self, h):
        pltpu.make_async_copy(self.places[0], self.target.at[h], self.sem.at[h]).wait()


class Outwards(Planes):
    def copy(self, h):
        return pltpu.make_async_copy(
            self.source.at[h], self.target.at[h + self.start_at], self.sem.at[h]
        )


def sigmoid(value):
    return 0.5 * jnp.tanh(0.5 * value) + 0.5


def rows_summed(value):
    return value.reshape(value.shape[0] // 8, 8, value.shape[1]).sum(0)


def put_permuted(target, row, source, pieces, offset=0):
    for inner, outer, width in pieces:
        target[row : row + 1, inner : inner + width] = source[
            :, offset + outer : offset + outer + width
        ]


def put_original(target, row, value, pieces):
    for inner, outer, width in pieces:
        target[row : row + 1, outer : outer + width] = value[:, inner : inner + width]


def put_stats(stat_ref, acc_ref, count=None):
    peers, rows, width = stat_ref.shape
    for row in range(2):
        line = jnp.sum(acc_ref[row], axis=0, keepdims=True)
        stat_ref[:, row : row + 1, :] = jnp.broadcast_to(line[None], (peers, 1, width))
    if count is not None:
        stat_ref[:, 2:3, :] = jnp.broadcast_to(count.reshape(1, 1, 1), (peers, 1, width))


def plane_stats(value_ref, h, keep, acc_ref):
    for first, last in tiles_of(0, value_ref.shape[2]):
        value = value_ref[h, :, first:last]
        masked = value * keep
        acc_ref[0, :, first:last] += rows_summed(masked)
        acc_ref[1, :, first:last] += rows_summed(masked * value)


def times_of(rows, width, extent):
    return lax.broadcasted_iota(jnp.int32, (rows, width), 0) & (extent - 1)


def time_shifted(value, times, extent):
    rows = value.shape[0]
    earlier = jnp.where(times != 0, pltpu.roll(value, 1, 0), 0.0)
    later = jnp.where(times != extent - 1, pltpu.roll(value, rows - 1, 0), 0.0)
    return earlier, value, later


def width_shifted(value, extent):
    rows = value.shape[0]
    if extent % 8 == 0:
        edge = jnp.zeros((extent, value.shape[1]), value.dtype)
        left = jnp.concatenate([edge, value[:-extent]], 0)
        right = jnp.concatenate([value[extent:], edge], 0)
    else:
        left = pltpu.roll(value, extent, 0)
        right = pltpu.roll(value, rows - extent, 0)
    return left, value, right


def window_sums(source_ref, between_ref, extent, put):
    planes, rows, width = source_ref.shape
    between_ref[0] = jnp.zeros((rows, width), F32)
    between_ref[planes + 1] = jnp.zeros((rows, width), F32)
    times = times_of(rows, width, extent)

    def plane(h, carry):
        before, here, after = time_shifted(source_ref[h], times, extent)
        left, here, right = width_shifted(before + here + after, extent)
        between_ref[h + 1] = left + here + right
        return carry

    lax.fori_loop(0, planes, plane, 0)

    def through(h, carry):
        put(h, (between_ref[h] + between_ref[h + 1] + between_ref[h + 2]) * (1.0 / 27.0))
        return carry

    lax.fori_loop(0, planes, through, 0)


def turned_ordered(turned_ref, ordered_ref):
    for row_to, row_from, height in FIRST_PIECES:
        for inner, outer, width in RESULT_PIECES:
            ordered_ref[row_to : row_to + height, inner : inner + width] = turned_ref[
                row_from : row_from + height, outer : outer + width
            ]


def weight_ordered(weight_ref, ordered_ref):
    for inner, outer, width in FIRST_PIECES:
        ordered_ref[:, inner : inner + width] = weight_ref[:, outer : outer + width]


def step_planes(planes):
    return (planes // 2, 2) if planes % 2 == 0 else (planes, 1)


def put_masks(valid, mask_ref, keep_ref, next_ref, lanes_ref):
    planes, rows, unused = keep_ref.shape
    unused, extent, width = mask_ref.shape
    frame = lax.broadcasted_iota(jnp.int32, (extent, width), 0)
    lanes_ref[...] = jnp.zeros_like(lanes_ref)
    for h in range(planes):
        plane = jnp.where(frame < valid, mask_ref[h], 0).astype(F32)
        lanes_ref[:, 16 * h : 16 * h + width] = plane
    total = lanes_ref.shape[1]

    def chosen(condition):
        return jnp.where(condition, 1.0, 0.0)

    def places(shape, axis):
        return lax.broadcasted_iota(jnp.int32, shape, axis)

    shape = (rows, extent)
    times = chosen(places(shape, 1) == places(shape, 0) & (extent - 1)).astype(BF16)
    picked = jnp.dot(times, lanes_ref[...].astype(BF16), preferred_element_type=F32)
    shape = (rows, total)
    picked = picked * chosen(places(shape, 1) & 15 == places(shape, 0) // extent)
    shape = (total, 128)
    group = chosen(places(shape, 0) // 16 == places(shape, 1)).astype(BF16)
    keeps = jnp.dot(picked.astype(BF16), group, preferred_element_type=F32)
    rows_next = next_ref.shape[1]
    half = extent // 2
    shape = (rows_next, rows)
    cell, row = places(shape, 0), places(shape, 1)
    same_time = (row & (extent - 1)) // 2 == (cell & (half - 1))
    same_column = row // (2 * extent) == cell // half
    pooled = chosen(same_time & same_column).astype(BF16)
    held = jnp.dot(pooled, keeps.astype(BF16), preferred_element_type=F32)
    for h in range(planes):
        keep_ref[h] = keeps[:, h : h + 1]
    for h in range(next_ref.shape[0]):
        both = held[:, 2 * h : 2 * h + 1] + held[:, 2 * h + 1 : 2 * h + 2]
        next_ref[h] = jnp.where(both > 0.5, 1.0, 0.0)


def project_body(
    order_ref,
    section_ref,
    frames_ref,
    x_hbm,
    mask_hbm,
    weight_hbm,
    z_hbm,
    z_v,
    stat_ref,
    keep_ref,
    next_ref,
    x_v,
    mask_v,
    mask_lanes,
    weight_v,
    ordered,
    pool,
    between,
    acc,
    x_sem,
    z_sem,
    weight_sem,
):
    planes, rows, channels = x_v.shape
    extent = 8
    clip = order_ref[section_ref[0]]
    arriving = Planes(x_hbm.at[clip], x_v, x_sem)
    leaving = Outwards(z_v, z_hbm, z_sem)
    weight_in = pltpu.make_async_copy(weight_hbm, weight_v, weight_sem.at[0])
    mask_in = pltpu.make_async_copy(mask_hbm.at[clip], mask_v, weight_sem.at[1])
    mask_in.start()
    weight_in.start()
    arriving.start_all()
    mask_in.wait()
    put_masks(frames_ref[clip], mask_v, keep_ref, next_ref, mask_lanes)
    weight_in.wait()
    weight_ordered(weight_v, ordered)
    together, steps = step_planes(planes)

    def product(i, carry):
        def masked(k, carry):
            h = i * together + k
            arriving.wait(h)
            x_v[h] = x_v[h] * keep_ref[h].astype(BF16)
            return carry

        lax.fori_loop(0, together, masked, 0)
        at = pl.ds(i * together, together)
        value = x_v[at].reshape(together * rows, channels)
        out = jnp.dot(value, ordered[...], preferred_element_type=F32)
        z_v[at] = out.reshape(together, rows, NB1)
        pool[at] = out[:, B0:ND].reshape(together, rows, B3)
        return carry

    lax.fori_loop(0, steps, product, 0)
    acc[...] = jnp.zeros_like(acc)

    def put(h, value):
        z_v[h, :, B0:ND] = value
        leaving.start(h)
        plane_stats(z_v, h, keep_ref[h], acc)

    window_sums(pool, between, extent, put)
    put_stats(stat_ref, acc, jnp.sum(keep_ref[...]))
    leaving.wait_all()


def project_first(clips, order, section, frames, voxel_mask, weight, peers):
    unused, planes, rows, channels = clips.shape
    unused, unused, extent, width = voxel_mask.shape
    return call(
        project_body,
        [
            shape_of(planes, rows, NB1),
            shape_of(planes, rows, NB1),
            shape_of(peers, 3, NB1),
            shape_of(planes, rows, 1),
            shape_of(planes // 2, (width // 2 + 1) * extent // 2, 1),
        ],
        "apvvv",
        [
            pltpu.VMEM((planes, rows, channels), BF16),
            pltpu.VMEM(voxel_mask.shape[1:], jnp.int32),
            pltpu.VMEM((extent, -(-planes // 8) * 128), F32),
            pltpu.VMEM((channels, NB1), BF16),
            pltpu.VMEM((channels, NB1), BF16),
            pltpu.VMEM((planes, rows, B3), F32),
            pltpu.VMEM((planes + 2, rows, B3), F32),
            pltpu.VMEM((2, 8, NB1), F32),
            DMA((planes,)),
            DMA((planes,)),
            DMA((2,)),
        ],
        (clips, voxel_mask, weight),
        "aaa",
        "project_first",
        (order, section, frames),
        flops=2 * planes * rows * channels * NB1,
        mib=16,
    )


def level_rows(vec, gain_ref, bias_ref, mom_ref, pieces, offset):
    put_permuted(vec, 4, gain_ref, pieces, offset)
    put_permuted(vec, 5, bias_ref, pieces, offset)
    mean, var = mom_ref[0:1, :], mom_ref[1:2, :]
    inverse = lax.rsqrt(var + EPSILON)
    scale = vec[4:5, :] * inverse
    vec[0:1, :] = scale
    vec[1:2, :] = vec[5:6, :] - mean * scale
    vec[2:3, :] = inverse
    vec[3:4, :] = -mean * inverse


def first_rows(vec, gain_ref, bias_ref, mom_ref):
    level_rows(vec, gain_ref, bias_ref, mom_ref, FIRST_PIECES, 0)


def second_rows(vec, gain_ref, bias_ref, mom_ref):
    level_rows(vec, gain_ref, bias_ref, mom_ref, SECOND_PIECES, NB1)


def back_rows(vec, total, count):
    cross = vec[0:1, :] * total[1:2] / count
    vec[6:7, :] = -(vec[0:1, :] * total[0:1] / count) - cross * vec[3:4, :]
    vec[7:8, :] = -cross * vec[2:3, :]


def put_moments(tot_ref, mom_ref, count):
    total = jnp.sum(tot_ref[...], axis=0)
    if count is None:
        count = total[2:3, :]
        mom_ref[2:3, :] = count
    mean = total[0:1, :] / count
    mom_ref[0:1, :] = mean
    mom_ref[1:2, :] = total[1:2, :] / count - mean * mean


def spread_plane(value, first, times, extent, targets, index):
    width = value.shape[1]
    for early, shifted in enumerate(time_shifted(value, times[:, 0:width], extent)):
        for side, moved in enumerate(width_shifted(shifted, extent)):
            place = early * 3 + side
            moved = moved.astype(BF16)
            for target, low, high in targets:
                begin, end = max(low, first), min(high, first + width)
                if begin < end:
                    start = place * (high - low) + begin - low
                    target[index, :, start : start + end - begin] = moved[
                        :, begin - first : end - first
                    ]


def clear_ends(targets, ends):
    for target, unused, unused in targets:
        for end in ends:
            target[end] = jnp.zeros(target.shape[1:], BF16)


def weight_copies(source, target, sems):
    return [
        pltpu.make_async_copy(
            source.at[pl.ds(time * 9 + height * 3, 3)],
            target.at[height, pl.ds(time * 3, 3)],
            sems.at[height * 3 + time],
        )
        for height in range(3)
        for time in range(3)
    ]


def second_body(
    extent,
    tot_ref,
    z_v,
    keep_ref,
    gain_ref,
    bias_ref,
    wide_hbm,
    narrow_hbm,
    act_v,
    mid_hbm,
    out_hbm,
    out_v,
    stat_ref,
    mom_ref,
    vec,
    mid_v,
    wide_v,
    narrow_v,
    im_wide,
    im_narrow,
    acc,
    wide_sem,
    narrow_sem,
    mid_sem,
    out_sem,
):
    planes, rows, unused = z_v.shape
    weights = weight_copies(wide_hbm, wide_v, wide_sem) + weight_copies(
        narrow_hbm, narrow_v, narrow_sem
    )
    for copy in weights:
        copy.start()
    mid_out = Outwards(mid_v, mid_hbm, mid_sem)
    out_out = Outwards(out_v, out_hbm, out_sem)
    put_moments(tot_ref, mom_ref, None)
    first_rows(vec, gain_ref, bias_ref, mom_ref)
    targets = ((im_wide, 0, B1A), (im_narrow, B1A, NM))
    clear_ends(targets, (0, planes + 1))
    times = times_of(rows, 128, extent)

    def activate(h, carry):
        keep = keep_ref[h]
        for first, last in tiles_of(0, NB1):
            shifted = z_v[h, :, first:last] * vec[0:1, first:last] + vec[1:2, first:last]
            value = shifted * sigmoid(shifted) * keep
            if first < ND:
                act_v[h, :, first:last] = value.astype(BF16)
            else:
                mid_v[h, :, first - ND : last - ND] = value.astype(BF16)
                spread_plane(value, first - ND, times, extent, targets, h + 1)
        mid_out.start(h)
        return carry

    lax.fori_loop(0, planes, activate, 0)
    for copy in weights:
        copy.wait()
    acc[...] = jnp.zeros_like(acc)
    together, steps = step_planes(planes)

    def convolve(i, carry):
        at = pl.ds(i * together, together)
        for im_ref, weight_ref, first, last in (
            (im_narrow, narrow_v, 0, B2),
            (im_wide, wide_v, B2, NB2),
        ):
            total = None
            for high in range(3):
                value = im_ref[pl.ds(i * together + high, together)]
                value = value.reshape(together * rows, value.shape[2])
                weight = weight_ref[high].reshape(value.shape[1], last - first)
                part = jnp.dot(value, weight, preferred_element_type=F32)
                total = part if total is None else total + part
            out_v[at, :, first:last] = total.reshape(together, rows, last - first)

        def finish(k, carry):
            h = i * together + k
            out_out.start(h)
            plane_stats(out_v, h, keep_ref[h], acc)
            return carry

        lax.fori_loop(0, together, finish, 0)
        return carry

    lax.fori_loop(0, steps, convolve, 0)
    put_stats(stat_ref, acc)
    mid_out.wait_all()
    out_out.wait_all()


def second_level(totals, first_out, keep, params, extent, peers):
    unused, conv_mid, conv_small, gain, bias = params
    planes, rows, unused = first_out.shape
    return call(
        functools.partial(second_body, extent),
        [
            shape_of(planes, rows, ND, dtype=BF16),
            shape_of(planes, rows, NM, dtype=BF16),
            shape_of(planes, rows, NB2),
            shape_of(planes, rows, NB2),
            shape_of(peers, 2, NB2),
            shape_of(3, NB1),
        ],
        "paapvv",
        [
            pltpu.VMEM((8, NB1), F32),
            pltpu.VMEM((planes, rows, NM), BF16),
            pltpu.VMEM((3, 9, B1A, B1), BF16),
            pltpu.VMEM((3, 9, B2A, B2), BF16),
            pltpu.VMEM((planes + 2, rows, 9 * B1A), BF16),
            pltpu.VMEM((planes + 2, rows, 9 * B2A), BF16),
            pltpu.VMEM((2, 8, NB2), F32),
            DMA((9,)),
            DMA((9,)),
            DMA((planes,)),
            DMA((planes,)),
        ],
        (totals, first_out, keep, gain, bias, conv_mid, conv_small),
        "vpvvvaa",
        "second_level",
        flops=2 * planes * rows * 27 * (B1A * B1 + B2A * B2),
        mib=30,
    )


def cell_of(shape, axis, rows):
    row = lax.broadcasted_iota(jnp.int32, shape, axis)
    row = jnp.where(row >= rows, row - rows, row)
    return (row // 16) * 4 + (row % 8) // 2


def between_body(
    tot_ref,
    z_v,
    keep_ref,
    gain_ref,
    bias_ref,
    act_v,
    first_mom_ref,
    keep_next_ref,
    weight_ref,
    x_hbm,
    z_next_hbm,
    z_next_ref,
    stat_ref,
    mom_ref,
    vec,
    x_ref,
    both,
    ordered,
    pool,
    between,
    acc,
    x_sem,
    z_next_sem,
):
    planes, rows, channels = x_ref.shape
    x_out = Outwards(x_ref, x_hbm, x_sem)
    z_next_out = Outwards(z_next_ref, z_next_hbm, z_next_sem)
    put_moments(tot_ref, mom_ref, first_mom_ref[2:3, 0:NB2])
    second_rows(vec, gain_ref, bias_ref, mom_ref)
    turned_ordered(weight_ref, ordered)
    extent = 4
    source_rows = z_v.shape[1]
    shape = (rows, 2 * source_rows)
    cells = cell_of(shape, 1, source_rows) == lax.broadcasted_iota(jnp.int32, shape, 0)
    pooled = jnp.where(cells, 1.0, 0.0).astype(BF16)

    def pooling(h, carry):
        keeps = [keep_ref[2 * h], keep_ref[2 * h + 1]]
        keep_next = keep_next_ref[h]
        for first, last in tiles_of(0, C5):
            for step in range(2):
                if first < ND:
                    part = act_v[2 * h + step, :, first:last]
                else:
                    at = slice(first - ND, last - ND)
                    shifted = z_v[2 * h + step, :, at] * vec[0:1, at] + vec[1:2, at]
                    part = (shifted * sigmoid(shifted) * keeps[step]).astype(BF16)
                both[step * source_rows : (step + 1) * source_rows, first:last] = part
        mean = jnp.dot(pooled, both[...], preferred_element_type=F32) * 0.125
        x_ref[h] = (mean.astype(BF16).astype(F32) * keep_next).astype(BF16)
        x_out.start(h)
        return carry

    lax.fori_loop(0, planes, pooling, 0)
    value = x_ref[...].reshape(planes * rows, channels)
    out = lax.dot_general(
        value, ordered[...], (((1,), (1,)), ((), ())), preferred_element_type=F32
    )
    z_next_ref[...] = out.reshape(planes, rows, NB1)
    pool[...] = out[:, B0:ND].reshape(planes, rows, B3)
    acc[...] = jnp.zeros_like(acc)

    def put(h, value):
        z_next_ref[h, :, B0:ND] = value
        z_next_out.start(h)
        plane_stats(z_next_ref, h, keep_next_ref[h], acc)

    window_sums(pool, between, extent, put)
    put_stats(stat_ref, acc, jnp.sum(keep_next_ref[...]))
    x_out.wait_all()
    z_next_out.wait_all()


def between_blocks(totals, second_out, keep, params, act, first_mom, keep_next, weight, peers):
    planes, rows = keep_next.shape[:2]
    above, source_rows = second_out.shape[:2]
    return call(
        between_body,
        [
            shape_of(planes, rows, C5, dtype=BF16),
            shape_of(planes, rows, NB1),
            shape_of(planes, rows, NB1),
            shape_of(peers, 3, NB1),
            shape_of(2, NB2),
        ],
        "aapvv",
        [
            pltpu.VMEM((8, NB2), F32),
            pltpu.VMEM((planes, rows, C5), BF16),
            pltpu.VMEM((2 * source_rows, C5), BF16),
            pltpu.VMEM((NB1, C5), BF16),
            pltpu.VMEM((planes, rows, B3), F32),
            pltpu.VMEM((planes + 2, rows, B3), F32),
            pltpu.VMEM((2, 8, NB1), F32),
            DMA((planes,)),
            DMA((planes,)),
        ],
        (totals, second_out, keep, params[3], params[4], act, first_mom, keep_next, weight),
        "vpvvvpvvv",
        "between_blocks",
        flops=2 * planes * rows * C5 * NB1,
        mib=16,
    )


def turn_body(
    clip_ref,
    section_ref,
    tot_ref,
    z_v,
    keep_ref,
    gain_ref,
    bias_ref,
    act_v,
    first_mom_ref,
    grad_hbm,
    kept_ref,
    sent_ref,
    slope_hbm,
    direct_v,
    stat_ref,
    mom_ref,
    vec,
    slope_v,
    grad_v,
    grad,
    result,
    acc,
    grad_sem,
    slope_sem,
):
    planes, rows, unused = z_v.shape
    unused, width, extent, unused = grad_v.shape
    half = extent // 2
    later = section_ref[0] == 1
    grad_in = Planes(grad_hbm.at[clip_ref[0]], grad_v, grad_sem)
    for h in range(planes):
        grad_in.start(h)
    slope_out = Outwards(slope_v, slope_hbm, slope_sem)
    put_moments(tot_ref, mom_ref, first_mom_ref[2:3, 0:NB2])
    second_rows(vec, gain_ref, bias_ref, mom_ref)
    acc[...] = jnp.zeros_like(acc)
    grad[...] = jnp.zeros_like(grad)

    def plane(h, carry):
        keep = keep_ref[h]
        grad_in.wait(h)
        for column in range(width):
            at = slice(column * extent, (column + 1) * extent)
            grad[at, :] = grad_v[h, column].astype(F32)
        direct_v[h, :, 0:B0] = grad[:, 0:B0].astype(BF16)
        direct_v[h, :, B0:ND] = grad[:, C5 - B3 :].astype(BF16)
        result[:, 0:B0] = act_v[h, :, 0:B0].astype(F32)
        result[:, C5 - B3 :] = act_v[h, :, B0:ND].astype(F32)
        for inner, outer, size in SECOND_PIECES:
            at = slice(inner, inner + size)
            place = slice(B0 + outer, B0 + outer + size)
            value = z_v[h, :, at]
            shifted = value * vec[0:1, at] + vec[1:2, at]
            gate = sigmoid(shifted)
            result[:, place] = shifted * gate * keep
            slope = grad[:, place] * keep * gate * (1.0 + shifted * (1.0 - gate))
            slope_v[h, :, at] = slope
            acc[0, :, at] += rows_summed(slope)
            acc[1, :, at] += rows_summed(slope * (value * vec[2:3, at] + vec[3:4, at]))
        slope_out.start(h)
        for column in range(width):
            start = column * extent
            early = result[start : start + half, :]
            late = result[start + half : start + extent, :]
            kept_ref[h, column] = jnp.where(later, late, early).astype(BF16)
            sent_ref[h, column] = jnp.where(later, early, late).astype(BF16)
        return carry

    lax.fori_loop(0, planes, plane, 0)
    put_stats(stat_ref, acc)
    slope_out.wait_all()


def turn(
    totals, second_out, keep, params, act, first_mom, cotangent, own_clip, section, peers
):
    planes, rows, unused = second_out.shape
    unused, unused, width, extent, unused = cotangent.shape
    half = (planes, width, extent // 2, C5)
    return call(
        turn_body,
        [
            shape_of(*half, dtype=BF16),
            shape_of(*half, dtype=BF16),
            shape_of(planes, rows, NB2),
            shape_of(planes, rows, ND, dtype=BF16),
            shape_of(peers, 2, NB2),
            shape_of(2, NB2),
        ],
        "vvapvv",
        [
            pltpu.VMEM((8, NB2), F32),
            pltpu.VMEM((planes, rows, NB2), F32),
            pltpu.VMEM(cotangent.shape[1:], BF16),
            pltpu.VMEM((rows, C5), F32),
            pltpu.VMEM((rows, C5), F32),
            pltpu.VMEM((2, 8, NB2), F32),
            DMA((planes,)),
            DMA((planes,)),
        ],
        (totals, second_out, keep, params[3], params[4], act, first_mom, cotangent),
        "vpvvvpva",
        "turn",
        (own_clip, section),
        mib=12,
    )


def slope_plane(
    upstream, z_ref, h, vec, keep, slope_ref, slope_at, acc, tiles
):
    for first, last in tiles:
        at = slice(first, last)
        value = z_ref[h, :, at]
        shifted = value * vec[0:1, at] + vec[1:2, at]
        gate = sigmoid(shifted)
        slope = upstream(first, last) * keep * gate * (1.0 + shifted * (1.0 - gate))
        slope_ref[slope_at, :, at] = slope
        acc[0, :, at] += rows_summed(slope)
        acc[1, :, at] += rows_summed(slope * (value * vec[2:3, at] + vec[3:4, at]))


def put_halves(section, packed, kept_hbm, sent_hbm, sems):
    half = packed.shape[0] // 2
    copies = [
        pltpu.make_async_copy(
            packed.at[pl.ds(pl.multiple_of(which * half, 16), half)],
            target.at[pl.ds(0, half)],
            sems.at[place],
        )
        for place, (which, target) in enumerate(((section, kept_hbm), (1 - section, sent_hbm)))
    ]
    for copy in copies:
        copy.start()
    return copies


def conv_grad_body(
    extent,
    section_ref,
    tot_ref,
    slope_hbm,
    z_hbm,
    mid_hbm,
    keep_ref,
    gain_ref,
    bias_ref,
    first_mom_ref,
    mom_ref,
    more_kept_hbm,
    more_sent_hbm,
    grad_v,
    kept_hbm,
    sent_hbm,
    norm_ref,
    vec,
    slope_v,
    z_v,
    mid_v,
    im_wide,
    im_narrow,
    turned,
    packed,
    more_v,
    slope_sem,
    z_sem,
    mid_sem,
    half_sem,
):
    planes, rows, unused = z_v.shape
    slope_in = Planes(slope_hbm, slope_v, slope_sem)
    z_in = Planes(z_hbm, z_v, z_sem)
    mid_in = Planes(mid_hbm, mid_v, mid_sem)
    for h in range(planes):
        mid_in.start(h)
        slope_in.start(h)
        z_in.start(h)
    half_rows = packed.shape[0] // 2
    more = kept_hbm.shape[0] - half_rows
    beside = [
        (
            pltpu.make_async_copy(source, more_v.at[place], half_sem.at[2 + place]),
            pltpu.make_async_copy(
                more_v.at[place], target.at[pl.ds(half_rows, more)], half_sem.at[4 + place]
            ),
        )
        for place, (source, target) in enumerate(
            ((more_kept_hbm, kept_hbm), (more_sent_hbm, sent_hbm))
        )
        if more
    ]
    for arriving, leaving in beside:
        arriving.start()
    total = jnp.sum(tot_ref[...], axis=0)
    put_original(norm_ref, 0, total[1:2], SECOND_PIECES)
    put_original(norm_ref, 1, total[0:1], SECOND_PIECES)
    second_rows(vec, gain_ref, bias_ref, mom_ref)
    back_rows(vec, total, first_mom_ref[2:3, 0:NB2])
    targets = ((im_wide, 0, B1A), (im_narrow, B1A, NM))
    clear_ends(targets, (0, planes + 1))
    times = times_of(rows, 128, extent)

    def gradient(h, carry):
        mid_in.wait(h)
        for first, last in tiles_of(0, NM):
            value = mid_v[h, :, first:last].astype(F32)
            spread_plane(value, first, times, extent, targets, h + 1)
        slope_in.wait(h)
        z_in.wait(h)
        keep = keep_ref[h]
        for first, last in tiles_of(0, NB2):
            at = slice(first, last)
            value = slope_v[h, :, at] * vec[0:1, at] + z_v[h, :, at] * vec[7:8, at] + vec[6:7, at]
            grad_v[h, :, at] = (value * keep).astype(BF16)
        return carry

    lax.fori_loop(0, planes, gradient, 0)
    for arriving, leaving in beside:
        arriving.wait()
        leaving.start()
    turned[...] = grad_v[...].reshape(planes * rows, NB2).T
    wide_rows = 27 * B1A
    half = wide_rows // 2
    used = CONV_NARROW + 27 * B2A
    packed[used:, :] = jnp.zeros((packed.shape[0] - used, 128), BF16)
    step = 3 * B1A
    for high in range(3):
        value = im_wide[high : high + planes].reshape(planes * rows, 9 * B1A)
        part = jnp.dot(turned[B2:NB2, :], value, preferred_element_type=F32)
        part = part.T.astype(BF16)
        value = im_narrow[high : high + planes].reshape(planes * rows, 9 * B2A)
        small = jnp.dot(turned[0:B2, :], value, preferred_element_type=F32)
        small = small.T.astype(BF16)
        for time in range(3):
            chunk = time * 3 + high
            row = chunk * step
            piece = part[time * step : (time + 1) * step]
            packed[row : row + step, :] = piece[:, 0:128]
            packed[wide_rows + row : wide_rows + row + step, :] = piece[:, 128:256]
            low = max(0, min(step, half - row))
            tail = 2 * wide_rows + row
            if low > 0:
                packed[tail : tail + low, 0:64] = piece[:low, 256:B1]
            if low < step:
                tail = tail + low - half
                packed[tail : tail + step - low, 64:128] = piece[low:, 256:B1]
            row = CONV_NARROW + chunk * 3 * B2A
            packed[row : row + 3 * B2A, :] = small[time * 3 * B2A : (time + 1) * 3 * B2A]
    copies = put_halves(section_ref[0], packed, kept_hbm, sent_hbm, half_sem)
    for copy in copies + [leaving for arriving, leaving in beside]:
        copy.wait()


def conv_grad(
    totals, slope, second_out, mid, keep, params, first_mom, mom, extent, section, peers, more=None
):
    planes, rows, unused = second_out.shape
    packed = conv_rows(peers)
    half = packed // 2
    if more is None:
        more = (mid, mid)
    else:
        half += more[0].shape[0]
    return call(
        functools.partial(conv_grad_body, extent),
        [
            shape_of(planes, rows, NB2, dtype=BF16),
            shape_of(half, 128, dtype=BF16),
            shape_of(half, 128, dtype=BF16),
            shape_of(2, NB2),
        ],
        "paav",
        [
            pltpu.VMEM((8, NB2), F32),
            pltpu.VMEM((planes, rows, NB2), F32),
            pltpu.VMEM((planes, rows, NB2), F32),
            pltpu.VMEM((planes, rows, NM), BF16),
            pltpu.VMEM((planes + 2, rows, 9 * B1A), BF16),
            pltpu.VMEM((planes + 2, rows, 9 * B2A), BF16),
            pltpu.VMEM((NB2, planes * rows), BF16),
            pltpu.VMEM((packed, 128), BF16),
            pltpu.VMEM((2, max(half - packed // 2, 16), 128), BF16),
            DMA((planes,)),
            DMA((planes,)),
            DMA((planes,)),
            DMA((6,)),
        ],
        (totals, slope, second_out, mid, keep, params[3], params[4], first_mom, mom, *more),
        "vaaavvvvvaa",
        "conv_grad",
        (section,),
        flops=2 * planes * rows * 27 * (B1A * B1 + B2A * B2),
        mib=30,
    )


def prepare_body(wide_ref, narrow_ref, turned_hbm, weights, sems):
    weights[...] = jnp.zeros_like(weights)
    copies = []
    for height in range(3):
        for place in range(9):
            source = 26 - ((place // 3) * 9 + height * 3 + place % 3)
            weights[height, 0:B1A, place * NB2 + B2 : (place + 1) * NB2] = wide_ref[source]
            weights[height, B1A:NM, place * NB2 : place * NB2 + B2] = narrow_ref[source]
        copies.append(
            pltpu.make_async_copy(weights.at[height], turned_hbm.at[height], sems.at[height])
        )
        copies[-1].start()
    for copy in copies:
        copy.wait()


def prepare(conv_mid, conv_small):
    return call(
        prepare_body,
        [shape_of(3, NM, TURNED, dtype=BF16)],
        "a",
        [pltpu.VMEM((3, NM, TURNED), BF16), DMA((3,))],
        (conv_mid, conv_small),
        "vv",
        "prepare",
        mib=24,
    )[0]


def back_conv_body(
    extent,
    halved,
    start,
    grad_ref,
    z_hbm,
    keep_ref,
    gain_ref,
    bias_ref,
    first_mom_ref,
    direct_v,
    turned_hbm,
    before_ref,
    slope_v,
    stat_ref,
    acc,
    vec,
    z_v,
    windows,
    weights,
    z_sem,
    weight_sem,
):
    planes = grad_ref.shape[0]
    count, rows, unused = z_v.shape
    low = 1 if start == 0 else 0
    high = count + 1 if start + count == planes else count + 2
    weights_in = Planes(turned_hbm, weights, weight_sem)
    weights_in.start_all()
    z_in = Planes(z_hbm, z_v, z_sem, start)
    z_in.start_all()
    first_rows(vec, gain_ref, bias_ref, first_mom_ref)
    targets = ((windows, 0, NB2),)
    clear_ends(targets, [0] * low + [count + 1] * (count + 2 - high))
    times = times_of(rows, 128, extent)

    def shift(j, carry):
        for first, last in tiles_of(0, NB2):
            value = grad_ref[start - 1 + j, :, first:last].astype(F32)
            spread_plane(value, first, times, extent, targets, j)
        return carry

    lax.fori_loop(low, high, shift, 0)
    weights_in.wait_all()
    total = None
    for height in range(3):
        value = windows[height : height + count].reshape(count * rows, 9 * NB2)
        part = lax.dot_general(
            value,
            weights[height, :, 0 : 9 * NB2],
            (((1,), (1,)), ((), ())),
            preferred_element_type=F32,
        )
        total = part if total is None else total + part
    slope_v[:, :, ND:NB1] = total.reshape(count, rows, NM)
    acc[...] = before_ref[...]

    def slopes(h, carry):
        z_in.wait(h)

        def upstream(first, last):
            if first >= ND:
                return slope_v[h, :, first:last]
            if halved:
                return direct_v[(start + h) // 2, :, first:last].astype(F32) * 0.125
            return direct_v[start + h, :, first:last].astype(F32)

        slope_plane(upstream, z_v, h, vec, keep_ref[start + h], slope_v, h, acc, tiles_of(0, NB1))
        return carry

    lax.fori_loop(0, count, slopes, 0)
    put_stats(stat_ref, acc)


def back_conv(
    grad, first_out, keep, params, turned, first_mom, direct, halved, extent, peers, part, before
):
    unused, unused, unused, gain, bias = params
    planes, rows, unused = first_out.shape
    start, count = part
    return call(
        functools.partial(back_conv_body, extent, halved, start),
        [shape_of(count, rows, NB1), shape_of(peers, 2, NB1), shape_of(2, 8, NB1)],
        "pvv",
        [
            pltpu.VMEM((8, NB1), F32),
            pltpu.VMEM((count, rows, NB1), F32),
            pltpu.VMEM((count + 2, rows, 9 * NB2), BF16),
            pltpu.VMEM((3, NM, TURNED), BF16),
            DMA((count,)),
            DMA((3,)),
        ],
        (grad, first_out, keep, gain, bias, first_mom, direct, turned, before),
        "pavvvvpav",
        "back_conv",
        flops=2 * count * rows * 27 * (B1A * B1 + B2A * B2),
        mib=30,
    )


def first_gradient(
    slope_refs, ready, z_ref, keep_ref, vec, grad_ref, pool_ref, between_ref, extent, done
):
    begin = 0
    for slope_ref in slope_refs:

        def gradient(t, carry, begin=begin, slope_ref=slope_ref):
            h = begin + t
            ready(h)
            keep = keep_ref[h]
            for first, last in tiles_of(0, NB1):
                at = slice(first, last)
                value = (
                    slope_ref[t, :, at] * vec[0:1, at] + z_ref[h, :, at] * vec[7:8, at] + vec[6:7, at]
                ) * keep
                if first == B0:
                    pool_ref[h] = value
                else:
                    grad_ref[h, :, at] = value.astype(BF16)
            return carry

        lax.fori_loop(0, slope_ref.shape[0], gradient, 0)
        begin += slope_ref.shape[0]

    def put(h, value):
        grad_ref[h, :, B0:ND] = value.astype(BF16)
        done(h)

    window_sums(pool_ref, between_ref, extent, put)


def put_norms(norm_ref, total, pieces):
    put_original(norm_ref, 0, total[1:2], pieces)
    put_original(norm_ref, 1, total[0:1], pieces)


def last_gradient_body(
    clip_ref,
    section_ref,
    tot_ref,
    slope_0,
    slope_1,
    z_hbm,
    x_hbm,
    keep_ref,
    gain_ref,
    bias_ref,
    mom_ref,
    grad_v,
    kept_hbm,
    sent_hbm,
    norm_ref,
    vec,
    z_v,
    x_v,
    pool,
    between,
    product,
    ordered,
    packed,
    z_sem,
    x_sem,
    half_sem,
):
    planes, rows, channels = x_v.shape
    z_in = Planes(z_hbm, z_v, z_sem)
    x_in = Planes(x_hbm.at[clip_ref[0]], x_v, x_sem)
    for h in range(planes):
        z_in.start(h)
    x_in.start_all()
    first_rows(vec, gain_ref, bias_ref, mom_ref)
    total = jnp.sum(tot_ref[...], axis=0)
    put_norms(norm_ref, total, FIRST_PIECES)
    back_rows(vec, total, mom_ref[2:3, :])

    def done(h):
        x_in.wait(h)
        x_v[h] = x_v[h] * keep_ref[h].astype(BF16)

    first_gradient(
        (slope_0, slope_1), z_in.wait, z_v, keep_ref, vec, grad_v, pool, between, 8, done
    )
    product[...] = lax.dot_general(
        x_v[...].reshape(planes * rows, channels),
        grad_v[...].reshape(planes * rows, NB1),
        (((0,), (0,)), ((), ())),
        preferred_element_type=F32,
    )
    for inner, outer, width in FIRST_PIECES:
        ordered[:, outer : outer + width] = product[:, inner : inner + width]
    pack_inproj(ordered, packed)
    copies = put_halves(section_ref[0], packed, kept_hbm, sent_hbm, half_sem)
    for copy in copies:
        copy.wait()


def last_gradient(totals, slopes, first_out, clips, keep, params, mom, own_clip, section, peers):
    planes, rows, unused = first_out.shape
    channels = clips.shape[3]
    packed = padded_rows(inproj_rows(channels)[1], peers)
    return call(
        last_gradient_body,
        [
            shape_of(planes, rows, NB1, dtype=BF16),
            shape_of(packed // 2, 128),
            shape_of(packed // 2, 128),
            shape_of(2, NB1),
        ],
        "paav",
        [
            pltpu.VMEM((8, NB1), F32),
            pltpu.VMEM((planes, rows, NB1), F32),
            pltpu.VMEM((planes, rows, channels), BF16),
            pltpu.VMEM((planes, rows, B3), F32),
            pltpu.VMEM((planes + 2, rows, B3), F32),
            pltpu.VMEM((channels, NB1), F32),
            pltpu.VMEM((channels, NB1), F32),
            pltpu.VMEM((packed, 128), F32),
            DMA((planes,)),
            DMA((planes,)),
            DMA((2,)),
        ],
        (totals, *slopes, first_out, clips, keep, params[3], params[4], mom),
        "vppaavvvv",
        "last_gradient",
        (own_clip, section),
        flops=2 * planes * rows * channels * NB1,
        mib=28,
    )


def clip_gradient_body(
    section_ref,
    grad_v,
    keep_ref,
    weight_ref,
    kept_hbm,
    sent_hbm,
    du_v,
    kept_v,
    sent_v,
    ordered,
    kept_sem,
    sent_sem,
):
    planes, rows, channels = du_v.shape
    unused, width, half, unused = kept_v.shape
    later = section_ref[0] == 1
    kept_out = Outwards(kept_v, kept_hbm, kept_sem)
    sent_out = Outwards(sent_v, sent_hbm, sent_sem)
    weight_ordered(weight_ref, ordered)
    together, steps = step_planes(planes)

    def product(i, carry):
        at = pl.ds(i * together, together)
        value = grad_v[at].reshape(together * rows, NB1)
        out = lax.dot_general(
            value, ordered[...], (((1,), (1,)), ((), ())), preferred_element_type=F32
        )
        du_v[at] = out.reshape(together, rows, channels) * keep_ref[at]

        def sent(k, carry):
            h = i * together + k
            for column in range(width):
                start = 2 * half * column
                early = du_v[h, start : start + half, :]
                late = du_v[h, start + half : start + 2 * half, :]
                kept_v[h, column] = jnp.where(later, late, early).astype(BF16)
                sent_v[h, column] = jnp.where(later, early, late).astype(BF16)
            kept_out.start(h)
            sent_out.start(h)
            return carry

        lax.fori_loop(0, together, sent, 0)
        return carry

    lax.fori_loop(0, steps, product, 0)
    kept_out.wait_all()
    sent_out.wait_all()


def clip_gradient(grad, keep, inproj, width, section):
    planes, rows, unused = grad.shape
    channels = inproj.shape[0]
    half = (planes, width, rows // width // 2, channels)
    return call(
        clip_gradient_body,
        [shape_of(*half, dtype=BF16)] * 2,
        "aa",
        [
            pltpu.VMEM((planes, rows, channels), F32),
            pltpu.VMEM(half, BF16),
            pltpu.VMEM(half, BF16),
            pltpu.VMEM((channels, NB1), BF16),
            DMA((planes,)),
            DMA((planes,)),
        ],
        (grad, keep, inproj),
        "pvv",
        "clip_gradient",
        (section,),
        flops=2 * planes * rows * channels * NB1,
        mib=24,
    )


def both_clips_body(own_ref, kept_ref, got_ref, out_ref):
    own = own_ref[0]
    out_ref[own] = kept_ref[...]
    out_ref[1 - own] = got_ref[...]


def both_clips(kept, got, own_clip):
    return call(
        both_clips_body,
        [shape_of(2, *kept.shape, dtype=BF16)],
        "v",
        [],
        (kept, got),
        "vv",
        "both_clips",
        (own_clip,),
        mib=24,
    )[0]


def back_between_body(
    tot_ref,
    own_slope_hbm,
    own_z_hbm,
    keep_ref,
    gain_ref,
    bias_ref,
    mom_ref,
    weight_ref,
    z_hbm,
    keep_prev,
    gain_prev,
    bias_prev,
    mom_prev,
    up_v,
    grad_ref,
    slope_hbm,
    stat_ref,
    norm_ref,
    vec,
    vec_prev,
    slope_ref,
    z_ref,
    ordered,
    pool,
    between,
    z_v,
    slope_v,
    acc,
    z_sem,
    slope_sem,
    own_sem,
):
    planes, rows, unused = z_ref.shape
    extent = 4
    own = [
        pltpu.make_async_copy(own_slope_hbm, slope_ref, own_sem.at[0]),
        pltpu.make_async_copy(own_z_hbm, z_ref, own_sem.at[1]),
    ]
    for copy in own:
        copy.start()
    z_in = Planes(z_hbm, z_v, z_sem)
    slope_out = Outwards(slope_v, slope_hbm, slope_sem)
    first_rows(vec, gain_ref, bias_ref, mom_ref)
    second_rows(vec_prev, gain_prev, bias_prev, mom_prev)
    total = jnp.sum(tot_ref[...], axis=0)
    put_norms(norm_ref, total, FIRST_PIECES)
    back_rows(vec, total, mom_ref[2:3, :])
    turned_ordered(weight_ref, ordered)
    for copy in own:
        copy.wait()
    z_in.start_all()
    first_gradient(
        (slope_ref,),
        lambda h: None,
        z_ref,
        keep_ref,
        vec,
        grad_ref,
        pool,
        between,
        extent,
        lambda h: None,
    )
    value = grad_ref[...].reshape(planes * rows, NB1)
    out = lax.dot_general(
        value, ordered[...], (((1,), (0,)), ((), ())), preferred_element_type=F32
    )
    rows_prev = z_v.shape[1]
    cells = cell_of((rows_prev, rows), 0, rows_prev) == lax.broadcasted_iota(jnp.int32, (rows_prev, rows), 1)
    doubled = jnp.where(cells, 1.0, 0.0).astype(BF16)
    for h in range(planes):
        single = (out[h * rows : (h + 1) * rows] * keep_ref[h]).astype(BF16)
        up_v[h] = jnp.dot(doubled, single, preferred_element_type=F32).astype(BF16)
    acc[...] = jnp.zeros_like(acc)

    def slopes(h, carry):
        z_in.wait(h)

        def upstream(first, last):
            return up_v[h // 2, :, ND + first : ND + last].astype(F32) * 0.125

        slope_plane(upstream, z_v, h, vec_prev, keep_prev[h], slope_v, h, acc, tiles_of(0, NB2))
        slope_out.start(h)
        return carry

    lax.fori_loop(0, 2 * planes, slopes, 0)
    put_stats(stat_ref, acc)
    slope_out.wait_all()


def back_between(
    totals, slope, first_out, keep, params, mom, second_prev, keep_prev, params_prev, mom_prev, peers
):
    inproj, unused, unused, gain, bias = params
    planes, rows, unused = first_out.shape
    above, rows_prev, unused = second_prev.shape
    return call(
        back_between_body,
        [
            shape_of(planes, rows_prev, C5, dtype=BF16),
            shape_of(planes, rows, NB1, dtype=BF16),
            shape_of(*second_prev.shape),
            shape_of(peers, 2, NB2),
            shape_of(2, NB1),
        ],
        "pvavv",
        [
            pltpu.VMEM((8, NB1), F32),
            pltpu.VMEM((8, NB2), F32),
            pltpu.VMEM((planes, rows, NB1), F32),
            pltpu.VMEM((planes, rows, NB1), F32),
            pltpu.VMEM((NB1, C5), BF16),
            pltpu.VMEM((planes, rows, B3), F32),
            pltpu.VMEM((planes + 2, rows, B3), F32),
            pltpu.VMEM(second_prev.shape, F32),
            pltpu.VMEM(second_prev.shape, F32),
            pltpu.VMEM((2, 8, NB2), F32),
            DMA((above,)),
            DMA((above,)),
            DMA((2,)),
        ],
        (
            totals,
            slope,
            first_out,
            keep,
            gain,
            bias,
            mom,
            inproj,
            second_prev,
            keep_prev,
            params_prev[3],
            params_prev[4],
            mom_prev,
        ),
        "vaavvvvvavvvv",
        "back_between",
        flops=2 * planes * rows * C5 * NB1,
        mib=20,
    )


def inproj_rows(channels):
    first = -(-channels // 32) * 16
    return first, 4 * channels + first


def pack_inproj(ordered, packed):
    channels = ordered.shape[0]
    first, used = inproj_rows(channels)
    padded = packed.shape[0]
    for place in range(4):
        packed[place * channels : (place + 1) * channels, :] = ordered[
            :, place * 128 : (place + 1) * 128
        ]
    start = 4 * channels
    packed[start : start + first, 0:64] = ordered[0:first, 512:NB1]
    packed[start : start + channels - first, 64:128] = ordered[first:channels, 512:NB1]
    if 2 * first > channels:
        packed[start + channels - first : start + first, 64:128] = jnp.zeros(
            (2 * first - channels, 64), packed.dtype
        )
    if padded > used:
        packed[used:padded, :] = jnp.zeros((padded - used, 128), packed.dtype)


def inproj_grad_body(
    section_ref, x_ref, grad_ref, kept_hbm, sent_hbm, product, ordered, packed, half_sem
):
    planes, rows, channels = x_ref.shape
    product[...] = lax.dot_general(
        x_ref[...].reshape(planes * rows, channels),
        grad_ref[...].reshape(planes * rows, NB1),
        (((0,), (0,)), ((), ())),
        preferred_element_type=F32,
    ).astype(BF16)
    for row_to, row_from, height in RESULT_PIECES:
        for inner, outer, width in FIRST_PIECES:
            ordered[row_from : row_from + height, outer : outer + width] = product[
                row_to : row_to + height, inner : inner + width
            ]
    pack_inproj(ordered, packed)
    for copy in put_halves(section_ref[0], packed, kept_hbm, sent_hbm, half_sem):
        copy.wait()


def inproj_grad(x, grad, section, peers):
    planes, rows, channels = x.shape
    packed = padded_rows(inproj_rows(channels)[1], peers)
    return call(
        inproj_grad_body,
        [shape_of(packed // 2, 128, dtype=BF16)] * 2,
        "aa",
        [
            pltpu.VMEM((channels, NB1), BF16),
            pltpu.VMEM((channels, NB1), BF16),
            pltpu.VMEM((packed, 128), BF16),
            DMA((2,)),
        ],
        (x, grad),
        "vv",
        "inproj_grad",
        (section,),
        flops=2 * planes * rows * channels * NB1,
        mib=12,
    )


def unpack_conv(packed_ref, wide_ref, narrow_ref):
    step = 27 * B1A
    half = step // 2
    wide_ref[:, 0:128] = packed_ref[0:step, :].astype(F32)
    wide_ref[:, 128:256] = packed_ref[step : 2 * step, :].astype(F32)
    wide_ref[0:half, 256:B1] = packed_ref[2 * step : 2 * step + half, 0:64].astype(F32)
    wide_ref[half:step, 256:B1] = packed_ref[2 * step : 2 * step + half, 64:128].astype(F32)
    narrow_ref[...] = packed_ref[CONV_NARROW : CONV_NARROW + 27 * B2A, :].astype(F32)


def unpack_inproj(packed_ref, out_ref):
    channels = out_ref.shape[0]
    first = inproj_rows(channels)[0]
    for place in range(4):
        out_ref[:, place * 128 : (place + 1) * 128] = packed_ref[
            place * channels : (place + 1) * channels, :
        ].astype(F32)
    start = 4 * channels
    out_ref[0:first, 512:NB1] = packed_ref[start : start + first, 0:64].astype(F32)
    out_ref[first:channels, 512:NB1] = packed_ref[start : start + channels - first, 64:128].astype(
        F32
    )


def unpack_alone_body(section_ref, value_ref, got_ref, wide_ref, narrow_ref, packed_ref):
    half = value_ref.shape[0]
    section = section_ref[0]
    packed_ref[pl.ds(pl.multiple_of(section * half, 16), half), :] = value_ref[...]
    packed_ref[pl.ds(pl.multiple_of((1 - section) * half, 16), half), :] = got_ref[...]
    unpack_conv(packed_ref, wide_ref, narrow_ref)


def unpack_alone(value, got, section):
    return call(
        unpack_alone_body,
        [shape_of(27 * B1A, B1), shape_of(27 * B2A, B2)],
        "vv",
        [pltpu.VMEM((2 * value.shape[0], 128), BF16)],
        (value, got),
        "vv",
        "unpack_alone",
        (section,),
        mib=24,
    )


def share_places(peers):
    pairs = distance_pairs(peers)
    places = []
    for section in range(2):
        order = [pair[section] for pair in pairs]
        places.append(
            [
                sum(
                    ((place // distance) % 2) << (len(order) - 1 - level)
                    for level, distance in enumerate(order)
                )
                for place in range(peers)
            ]
        )
    return places


def quarters_placed(half, upper, sources, conv_packed, next_packed):
    quarter = sources[0].shape[0]
    conv, rest = conv_packed.shape[0] // 2, next_packed.shape[0] // 2
    for place in range(2):
        first, last = place * quarter, (place + 1) * quarter
        split = min(max(conv - first, 0), quarter)
        for which, source in enumerate(sources):

            @pl.when(upper == (place ^ which))
            def put(source=source, first=first, split=split):
                if split > 0:
                    at = pl.multiple_of(half * conv + first, 16)
                    conv_packed[pl.ds(at, split), :] = source[0:split, :]
                if split < quarter:
                    at = pl.multiple_of(half * rest + first + split - conv, 16)
                    next_packed[pl.ds(at, quarter - split), :] = source[split:quarter, :]


def unpack_joined_body(
    section_ref,
    own_upper_ref,
    other_upper_ref,
    own_ref,
    own_got_ref,
    other_ref,
    other_got_ref,
    shares_ref,
    other_shares_ref,
    wide_hbm,
    narrow_hbm,
    next_hbm,
    inproj_ref,
    wide_ref,
    narrow_ref,
    next_ref,
    conv_packed,
    next_packed,
    next_out,
    inproj_packed,
    sems,
):
    section = section_ref[0]
    quarters_placed(
        section, own_upper_ref[0], (own_ref, own_got_ref), conv_packed, next_packed
    )
    quarters_placed(
        1 - section, other_upper_ref[0], (other_ref, other_got_ref), conv_packed, next_packed
    )
    step = 3 * B1A
    rows, halfway = 9 * step, 9 * step // 2
    copies = []
    for chunk in range(9):
        row = chunk * step
        at = slice(row, row + step)
        wide_ref[at, 0:128] = conv_packed[at, :].astype(F32)
        wide_ref[at, 128:256] = conv_packed[rows + row : rows + row + step, :].astype(F32)
        low = max(0, min(step, halfway - row))
        tail = 2 * rows + row
        if low > 0:
            wide_ref[row : row + low, 256:B1] = conv_packed[tail : tail + low, 0:64].astype(F32)
        if low < step:
            tail += low - halfway
            wide_ref[row + low : row + step, 256:B1] = conv_packed[
                tail : tail + step - low, 64:128
            ].astype(F32)
        copies.append(
            pltpu.make_async_copy(
                wide_ref.at[pl.ds(row, step)], wide_hbm.at[pl.ds(row, step)], sems.at[chunk]
            )
        )
        copies[-1].start()
    narrow_ref[...] = conv_packed[CONV_NARROW : CONV_NARROW + 27 * B2A, :].astype(F32)
    copies.append(pltpu.make_async_copy(narrow_ref, narrow_hbm, sems.at[9]))
    copies[-1].start()
    unpack_inproj(next_packed, next_out)
    next_ref[...] = next_out[...].T
    copies.append(pltpu.make_async_copy(next_ref, next_hbm, sems.at[10]))
    copies[-1].start()
    peers, share, unused = shares_ref.shape
    places = share_places(peers)
    for half_ref, half in ((shares_ref, section), (other_shares_ref, 1 - section)):
        for place in range(peers):
            at = jnp.where(half == 0, places[0][place], places[1][place]) + half * peers
            inproj_packed[pl.ds(pl.multiple_of(at * share, 16), share), :] = half_ref[place]
    unpack_inproj(inproj_packed, inproj_ref)
    for copy in copies:
        copy.wait()


def unpack_joined(quarters, uppers, shares, section, channels, next_channels):
    peers, share, unused = shares[0].shape
    return call(
        unpack_joined_body,
        [
            shape_of(27 * B1A, B1),
            shape_of(27 * B2A, B2),
            shape_of(NB1, next_channels),
            shape_of(channels, NB1),
        ],
        "aaav",
        [
            pltpu.VMEM((27 * B1A, B1), F32),
            pltpu.VMEM((27 * B2A, B2), F32),
            pltpu.VMEM((NB1, next_channels), F32),
            pltpu.VMEM((conv_rows(peers), 128), BF16),
            pltpu.VMEM((padded_rows(inproj_rows(next_channels)[1], peers), 128), BF16),
            pltpu.VMEM((next_channels, NB1), F32),
            pltpu.VMEM((2 * peers * share, 128), BF16),
            DMA((11,)),
        ],
        (*quarters, *shares),
        "vvvvvv",
        "unpack_joined",
        (section, *uppers),
        mib=32,
    )


def sent_to_all(spread):
    return lax.all_to_all(spread, "dp", 0, 0)


def swapped(value):
    return lax.ppermute(value, "section", [(0, 1), (1, 0)])


def distance_pairs(peers):
    distances = []
    while 2 ** len(distances) < peers:
        distances.append(2 ** len(distances))
    return list(zip(distances, [distances[1], distances[0]] + distances[2:]))


def distances_of():
    return distance_pairs(lax.axis_size("dp"))


def exchanged(value, pair):
    count = lax.axis_size("dp")
    links = [
        (section * count + place, section * count + (place ^ pair[section]))
        for section in range(2)
        for place in range(count)
    ]
    return lax.ppermute(value, ("section", "dp"), links)


def upper_half(pair, other=0):
    place = lax.axis_index("dp")
    distance = jnp.where(lax.axis_index("section") == other, pair[0], pair[1])
    return ((place // distance) % 2).astype(jnp.int32).reshape(1)


def added(kept, got):
    return (kept.astype(F32) + got.astype(F32)).astype(kept.dtype)


def split_sum_body(upper_ref, kept_ref, got_ref, left_ref, sent_ref):
    half = left_ref.shape[0]
    upper = upper_ref[0]
    for target, which in ((left_ref, upper), (sent_ref, 1 - upper)):
        at = pl.ds(pl.multiple_of(which * half, 16), half)
        target[...] = added(kept_ref[at, :], got_ref[at, :])


def split_sum(kept, got, pair):
    half = shape_of(kept.shape[0] // 2, 128, dtype=kept.dtype)
    return call(
        split_sum_body, [half, half], "vv", [], (kept, got), "vv", "split_sum", (upper_half(pair),)
    )


def placed_body(upper_ref, value_ref, got_ref, out_ref):
    half = value_ref.shape[0]
    upper = upper_ref[0]
    out_ref[pl.ds(pl.multiple_of(upper * half, 16), half), :] = value_ref[...]
    out_ref[pl.ds(pl.multiple_of((1 - upper) * half, 16), half), :] = got_ref[...]


def placed(value, got, pair):
    whole = shape_of(value.shape[0] * 2, 128, dtype=value.dtype)
    return call(
        placed_body, [whole], "v", [], (value, got), "vv", "placed", (upper_half(pair),)
    )[0]


def staged_body(source_hbm, target_ref, sem):
    copy = pltpu.make_async_copy(source_hbm, target_ref, sem.at[0])
    copy.start()
    copy.wait()


def staged(value):
    whole = shape_of(*value.shape, dtype=value.dtype)
    return call(staged_body, [whole], "p", [DMA((1,))], (value,), "a", "staged", mib=6)[0]


class Scatter:
    def __init__(self, kept, sent, stage=True):
        self.pairs = distances_of()
        self.place = 0
        self.got = swapped(sent)
        self.kept = staged(kept) if stage else kept

    def step(self):
        pair = self.pairs[self.place]
        self.kept, sent = split_sum(self.kept, self.got, pair)
        self.got = exchanged(sent, pair)
        self.place += 1

    def result(self):
        while self.place < len(self.pairs):
            self.step()
        return added(self.kept, self.got)


class Gather:
    def __init__(self, value):
        self.value = value
        self.pairs = distances_of()[::-1]
        self.place = 0
        self.got = exchanged(value, self.pairs[0])

    def step(self):
        self.value = placed(self.value, self.got, self.pairs[self.place])
        self.place += 1
        if self.place < len(self.pairs):
            self.got = exchanged(self.value, self.pairs[self.place])
        else:
            self.got = swapped(self.value)

    def result(self):
        while self.place < len(self.pairs):
            self.step()
        return self.value, self.got


def lockstep(one, other):
    one.got, other.got = lax.optimization_barrier((one.got, other.got))


def tied(value, *exchanges):
    both = lax.optimization_barrier((value,) + tuple(e.got for e in exchanges))
    for exchange, got in zip(exchanges, both[1:]):
        exchange.got = got
    return both[0]


def small_body(first_a, second_a, first_b, second_b, norm1_a, norm2_a, norm1_b, norm2_b, out_ref):
    for row, first, second in ((0, first_a, second_a), (2, first_b, second_b)):
        for line in range(2):
            for pieces, source, offset in ((FIRST_PIECES, first, 0), (SECOND_PIECES, second, NB1)):
                for inner, outer, width in pieces:
                    start = offset + outer
                    out_ref[row + line : row + line + 1, start : start + width] = source[
                        line : line + 1, inner : inner + width
                    ]
    for row, first, second in ((4, norm1_a, norm2_a), (6, norm1_b, norm2_b)):
        out_ref[row : row + 2, 0:NB1] = first[...]
        out_ref[row : row + 2, NB1:NB] = second[...]


def small_out_body(section_ref, own_ref, other_ref, norm_a, mom_a, norm_b, mom_b):
    section = section_ref[0]
    own, other = own_ref[...], other_ref[...]
    norms = own[4:8] + other[4:8]
    norm_a[...] = norms[0:2]
    norm_b[...] = norms[2:4]
    low = jnp.where(section == 0, own, other)
    high = jnp.where(section == 0, other, own)
    mom_a[0] = low[0:2]
    mom_a[1] = high[0:2]
    mom_b[0] = low[2:4]
    mom_b[1] = high[2:4]


def small_outputs(rows, section):
    own = call(small_body, [shape_of(8, NB)], "v", [], rows, "vvvvvvvv", "small")[0]
    return call(
        small_out_body,
        [shape_of(2, NB), shape_of(2, 2, NB), shape_of(2, NB), shape_of(2, 2, NB)],
        "vvvv",
        [],
        (own, swapped(own)),
        "vv",
        "small_out",
        (section,),
    )


def local(
    clips_in,
    frames,
    voxel_mask,
    micro_order,
    inproj_4f,
    conv_mid_4f,
    conv_small_4f,
    gain_4f,
    bias_4f,
    inproj_5b,
    conv_mid_5b,
    conv_small_5b,
    gain_5b,
    bias_5b,
    cotangent,
):
    section = lax.axis_index("section")
    peers = lax.axis_size("dp")
    own = micro_order[0, section]
    own_clip = own.reshape(1)
    which = section.astype(jnp.int32).reshape(1)
    count, depth, height, width, channels = clips_in.shape
    clips = jnp.transpose(clips_in, (0, 2, 3, 1, 4)).reshape(count, height, width * depth, channels)
    upstream = jnp.transpose(cotangent, (0, 2, 3, 1, 4))

    first = (inproj_4f, conv_mid_4f, conv_small_4f, gain_4f.reshape(1, NB), bias_4f.reshape(1, NB))
    second = (inproj_5b.T, conv_mid_5b, conv_small_5b, gain_5b.reshape(1, NB), bias_5b.reshape(1, NB))
    long, short = depth, depth // 2

    z1_a, z1_here, stat, keep, keep_next = project_first(
        clips,
        micro_order.reshape(-1),
        which,
        frames,
        jnp.transpose(voxel_mask, (0, 2, 1, 3)),
        inproj_4f,
        peers,
    )
    totals = sent_to_all(stat)
    act_a, mid_a, z2_a, z2_here, stat, mom1_a = second_level(
        totals, z1_here, keep, first, long, peers
    )
    totals = sent_to_all(stat)
    x_b, z1_b, z1_here, stat, mom2_a = between_blocks(
        totals, z2_here, keep, first, act_a, mom1_a, keep_next, second[0], peers
    )
    act_b, mid_b, z2_b, z2_here, stat, mom1_b = second_level(
        sent_to_all(stat), z1_here, keep_next, second, short, peers
    )
    totals = sent_to_all(stat)
    kept, sent, slope, direct, stat, mom2_b = turn(
        totals, z2_here, keep_next, second, act_b, mom1_b, upstream, own_clip, which, peers
    )
    totals = sent_to_all(stat)
    result = (kept, swapped(sent))
    turned_b = prepare(conv_mid_5b, conv_small_5b)
    totals, turned_b = lax.optimization_barrier((totals, turned_b))
    dz2_b, kept, sent, norm2_b = conv_grad(
        totals, slope, z2_b, mid_b, keep_next, second, mom1_b, mom2_b, short, which, peers
    )
    sum_b = Scatter(kept, sent, False)
    nothing = jnp.zeros((2, 8, NB1), F32)
    slope, stat, unused = back_conv(
        dz2_b,
        z1_b,
        keep_next,
        second,
        turned_b,
        mom1_b,
        direct,
        False,
        short,
        peers,
        (0, height // 2),
        nothing,
    )
    stat = tied(stat, sum_b)
    sum_b.step()
    totals = sent_to_all(stat)
    block_out = both_clips(*result, own_clip)
    turned_a = prepare(conv_mid_4f, conv_small_4f)
    totals, turned_a = lax.optimization_barrier((totals, turned_a))
    totals, block_out = lax.optimization_barrier((totals, block_out))
    totals = tied(totals, sum_b)
    sum_b.step()
    up, dz1_b, slope, stat, norm1_b = back_between(
        totals, slope, z1_b, keep_next, second, mom1_b, z2_a, keep, first, mom2_a, peers
    )
    stat = tied(stat, sum_b)
    sum_b.step()
    totals = sent_to_all(stat)
    inproj_halves = inproj_grad(x_b, dz1_b, which, peers)
    totals = tied(totals, sum_b)
    sum_b.step()
    dz2_a, kept, sent, norm2_a = conv_grad(
        totals,
        slope,
        z2_a,
        mid_a,
        keep,
        first,
        mom1_a,
        mom2_a,
        long,
        which,
        peers,
        inproj_halves,
    )
    sent = tied(sent, sum_b)
    sum_a = Scatter(kept, sent)
    gather_b = Gather(sum_b.result())
    dz2_a = tied(dz2_a, sum_a)
    sum_a.step()
    half = height // 2
    back = (z1_a, keep, first, turned_a, mom1_a, up, True, long, peers)
    slope_low, unused, part = back_conv(dz2_a, *back, (0, half), nothing)
    part = tied(part, sum_a, gather_b)
    sum_a.step()
    gather_b.step()
    slope_high, stat, unused = back_conv(dz2_a, *back, (half, height - half), part)
    stat = tied(stat, sum_a, gather_b)
    sum_a.step()
    gather_b.step()
    totals = sent_to_all(stat)
    totals = tied(totals, sum_a, gather_b)
    sum_a.step()
    gather_b.step()
    dz1_a, kept, sent, norm1_a = last_gradient(
        totals,
        (slope_low, slope_high),
        z1_a,
        clips,
        keep,
        first,
        mom1_a,
        own_clip,
        which,
        peers,
    )
    sent = tied(sent, sum_a)
    gather_a = Gather(sum_a.result())
    sum_i = Scatter(kept, sent)
    dz1_a = tied(dz1_a, sum_i, gather_b)
    gather_b.step()
    sum_i.step()
    kept, sent = clip_gradient(dz1_a, keep, inproj_4f, width, which)
    sent = tied(sent, sum_i, gather_a)
    sum_i.step()
    gather_a.step()
    lockstep(gather_a, sum_i)
    sum_i.step()
    gather_a.step()
    lockstep(gather_a, sum_i)
    sum_i.step()
    gather_a.step()
    shares = jnp.broadcast_to(sum_i.result().astype(BF16)[None], (peers, *sum_i.kept.shape))
    shares, sent = lax.optimization_barrier((shares, sent))
    whole = sent_to_all(shares)
    own, own_got = gather_a.value, gather_a.got
    other = swapped(own)
    clips_grad = both_clips(kept, swapped(sent), own_clip)
    small = small_outputs(
        (mom1_a, mom2_a, mom1_b, mom2_b, norm1_a, norm2_a, norm1_b, norm2_b), which
    )
    conv_b = unpack_alone(*gather_b.result(), which)
    whole, own_got, other, clips_grad, small, conv_b = lax.optimization_barrier(
        (whole, own_got, other, clips_grad, small, conv_b)
    )
    last_pair = gather_a.pairs[-1]
    wide_a, narrow_a, inproj_b, inproj_a = unpack_joined(
        (own, own_got, other, swapped(own_got)),
        (upper_half(last_pair), upper_half(last_pair, 1)),
        (whole, swapped(whole)),
        which,
        inproj_4f.shape[0],
        inproj_5b.shape[0],
    )
    return (
        jnp.transpose(block_out, (0, 3, 1, 2, 4)),
        jnp.transpose(clips_grad, (0, 3, 1, 2, 4)),
        inproj_a,
        wide_a.reshape(conv_mid_4f.shape),
        narrow_a.reshape(conv_small_4f.shape),
        small[0],
        small[1],
        inproj_b.T,
        conv_b[0].reshape(conv_mid_5b.shape),
        conv_b[1].reshape(conv_small_5b.shape),
        small[2],
        small[3],
    )


def solution(mesh):
    placed = (
        P("dp", None, None, None, None),
        P("dp"),
        P("dp", None, None, None),
        P("dp", None),
        P(),
        P(),
        P(),
        P(),
        P(),
        P(),
        P(),
        P(),
        P(),
        P(),
        P("dp", None, None, None, None),
    )
    return jax.shard_map(
        local,
        mesh=mesh,
        in_specs=placed,
        out_specs=(
            P("dp", "section", None, None, None),
            P("dp", "section", None, None, None),
            P(),
            P(),
            P(),
            P(),
            P(),
            P(),
            P(),
            P(),
            P(),
            P(),
        ),
        check_vma=False,
    )
```
